32 devices in a mesh: gx: 8 (over z, y), gy: 4 (over x, core).
Axes of the slice: x: 2, y: 2, z: 4, core: 2. Of those that a mesh axis runs over, the one named last changes fastest.
Arguments:
- phi_init: float32 [64, 32768], P(('gx', 'gy')), may hold values from -12 to 12
- source: float32 [64, 32768], P(('gx', 'gy')), may hold values from -6 to 6
- tile_mat: int32 [64, 32768], P(('gx', 'gy')), may hold values from 0 to 3
- tile_pos: int32 [64, 3], replicated, may hold values from 0 to 7, as said below
- neighbours: int32 [64, 6], P(('gx', 'gy')), may hold values from -1 to 63, as said below
- sigma_table: float32 [4], replicated, may hold values from 0.5 to 4
- temp_init: float32 [256, 16384], P('gx', 'gy'), may hold values from -6 to 6
- slab_mat: int32 [256, 16384], P('gx', 'gy'), may hold values from 0 to 3
- k0_table: float32 [4], replicated, may hold values from 0.5 to 1
- beta_table: float32 [4], replicated, may hold values from 0.1 to 1
Outputs:
- potential: float32 [64, 32768], P(('gx', 'gy'))
- temperature: float32 [256, 16384], P('gx', 'gy')
- tile_temps: float32 [64, 32768], P(('gx', 'gy'))
The draws below stay inside these ranges and needn't reach their ends.
Inputs may be any that keep to these rules, and one draw needn't show every extreme that they name: `tile_pos`: tiles are listed in dealt order, 2 to a device, devices in mesh order (gx slowest). Positions are distinct; every tile dealt to gx index i has first coordinate in [i, (i+1)); third coordinate is 0 or 1. Of the tiles of one gx row, at most 4 lie within one slab of 1 x 2 x 2 tile positions, and some slab holds exactly 4 in every row. neighbours[t, d] is the list index of the tile at tile_pos[t] moved one step in direction d, or -1 where there is none.
All inputs are finite; a program needn't handle non-finite values.
Results may differ from the reference program's by a relative error of at most 0.00012.
Values sent between devices are 32-bit elements; how exact they have to be, the bound alone decides.
No kernel may reach another device: no remote copies, remote signals or barrier semaphores. Data moves between devices by JAX's collectives and lax.ppermute only.
A program may use at most 64 MiB of HBM per device.

```python
import math
import jax
import jax.numpy as jnp
from jax import lax

TE = 32
TX_DEV = 1
TY_DEV = 2
TILES_DEV = 2
SWEEPS = 4
CSWEEPS = 3
MATS = 4
SLOT = 4
NZ = 64
NX = 256
NY = 256
TILES = 64
N_GX = 8
N_GY = 4


def build_layout(key):
    row_tiles = TILES_DEV * N_GY
    per_slab = 2 * TX_DEV * TY_DEV

    def one_row(row_key, row_index):
        key_hot, key_perm, key_pick, key_deal = jax.random.split(row_key, 4)
        hottest = jax.random.randint(key_hot, (), 0, N_GY)
        ranked = jax.vmap(lambda sub: jax.random.permutation(sub, per_slab))(jax.random.split(key_perm, N_GY))
        hot_places = ranked[hottest, :SLOT]
        others = (hottest + 1 + jnp.arange(N_GY - 1, dtype=jnp.int32)) % N_GY
        cand_places = ranked[others, :SLOT - 1].reshape(-1)
        cand_slabs = jnp.repeat(others, SLOT - 1)
        chosen = jax.random.permutation(key_pick, (N_GY - 1) * (SLOT - 1))[:row_tiles - SLOT]
        slabs = jnp.concatenate([jnp.full((SLOT,), hottest, jnp.int32), cand_slabs[chosen]])
        places = jnp.concatenate([hot_places, cand_places[chosen]])
        dealt = jax.random.permutation(key_deal, row_tiles)
        slabs = slabs[dealt]
        places = places[dealt]
        along_x = places // (TY_DEV * 2)
        along_y = places // 2 % TY_DEV
        along_z = places % 2
        return jnp.stack([row_index * TX_DEV + along_x, slabs * TY_DEV + along_y, along_z], -1).astype(jnp.int32)
    rows = jax.vmap(one_row)(jax.random.split(key, N_GX), jnp.arange(N_GX, dtype=jnp.int32))
    positions = rows.reshape(TILES, 3)
    grid = jnp.full((N_GX * TX_DEV, N_GY * TY_DEV, 2), -1, jnp.int32)
    grid = grid.at[positions[:, 0], positions[:, 1], positions[:, 2]].set(jnp.arange(TILES, dtype=jnp.int32))
    offsets = ((-1, 0, 0), (1, 0, 0), (0, -1, 0), (0, 1, 0), (0, 0, -1), (0, 0, 1))
    columns = []
    for step_x, step_y, step_z in offsets:
        moved_x = positions[:, 0] + step_x
        moved_y = positions[:, 1] + step_y
        moved_z = positions[:, 2] + step_z
        inside = (moved_x >= 0) & (moved_x < N_GX * TX_DEV) & (moved_y >= 0) & (moved_y < N_GY * TY_DEV) & (moved_z >= 0) & (moved_z < 2)
        found = grid[jnp.clip(moved_x, 0, N_GX * TX_DEV - 1), jnp.clip(moved_y, 0, N_GY * TY_DEV - 1), jnp.clip(moved_z, 0, 1)]
        columns.append(jnp.where(inside, found, -1))
    return (positions, jnp.stack(columns, -1).astype(jnp.int32))


def draw_tile_pos(key, part):
    return build_layout(jax.random.fold_in(key, 7))[0]


def draw_neighbours(key, part):
    return build_layout(jax.random.fold_in(key, 7))[1]


def place_ends(values, own_key, least, top_value):
    place = [jax.random.randint(jax.random.fold_in(own_key, axis), (), 0, length) for axis, length in enumerate(values.shape)]
    longest = values.shape.index(max(values.shape))
    beside = place[:longest] + [(place[longest] + 1) % values.shape[longest]] + place[longest + 1:]
    return values.at[tuple(place)].set(least).at[tuple(beside)].set(top_value)


def block_levels(rng, dims, pieces, smallest, top_value):
    gain, own = 1.0, jax.random.fold_in(rng, 6)
    for axis_at, blocks in pieces:
        steps = jnp.exp(jax.random.uniform(jax.random.fold_in(own, axis_at), (blocks,), jnp.float32, smallest / len(pieces), top_value / len(pieces)))
        gain = gain * jnp.repeat(steps, dims[axis_at] // blocks).reshape([-1 if axis == axis_at else 1 for axis in range(len(dims))])
    return gain


def centred(rng, dims, spread, most, cuts=(), kind=jnp.bfloat16):
    values = jax.random.normal(rng, dims, jnp.float32) * spread
    if len(cuts) > 0:
        values = block_levels(rng, dims, cuts, -0.22, 0.18) * values
    return jnp.clip(values, min=-most, max=most).astype(kind)


def setup_inputs(seed: int = 0) -> dict:
    keys = jax.random.split(jax.random.key(seed), 11)
    phi_init = centred(keys[0], (TILES, TE ** 3), 2.0, 12.0, ((0, 32),), jnp.float32)
    source = centred(keys[1], (TILES, TE ** 3), 1.0, 6.0, ((0, 32),), jnp.float32)
    tile_mat = place_ends(jax.random.randint(keys[2], (TILES, TE ** 3), 0, MATS), jax.random.fold_in(keys[2], 1), 0, MATS - 1).astype(jnp.int32)
    tile_pos = draw_tile_pos(jax.random.fold_in(keys[10], 71), 0)
    neighbours = draw_neighbours(jax.random.fold_in(keys[10], 71), 0)
    sigma_table = jnp.clip(jnp.exp(jax.random.uniform(keys[5], (MATS,), jnp.float32, math.log(0.5), math.log(4.0))), 0.5, 4.0)
    temp_init = centred(keys[6], (NX, NY * NZ), 1.0, 6.0, ((0, 8), (1, 4)), jnp.float32)
    slab_mat = place_ends(jax.random.randint(keys[7], (NX, NY * NZ), 0, MATS), jax.random.fold_in(keys[7], 1), 0, MATS - 1).astype(jnp.int32)
    k0_table = jnp.clip(jnp.exp(jax.random.uniform(keys[8], (MATS,), jnp.float32, math.log(0.5), math.log(1.0))), 0.5, 1.0)
    beta_table = jnp.clip(jnp.exp(jax.random.uniform(keys[9], (MATS,), jnp.float32, math.log(0.1), math.log(1.0))), 0.1, 1.0)
    return {"phi_init": phi_init, "source": source, "tile_mat": tile_mat, "tile_pos": tile_pos, "neighbours": neighbours, "sigma_table": sigma_table, "temp_init": temp_init, "slab_mat": slab_mat, "k0_table": k0_table, "beta_table": beta_table}


FLIP = (1, 0, 3, 2, 5, 4)
EPS = 2.0
DT = 0.15


def lookup(table, ids):
    result = jnp.zeros(ids.shape, jnp.float32)
    for which in range(table.shape[0]):
        result = result + jnp.where(ids == which, table[which], jnp.float32(0.0))
    return result


def cheb_weight(step, count):
    return 1.0 / (1.0 + 0.75 * math.cos(math.pi * (2 * step + 1) / (2 * count)))


def tile_faces(field):
    count = field.shape[0]
    edge = field.shape[1]
    flat = (count, edge * edge)
    return jnp.stack([field[:, 0].reshape(flat), field[:, -1].reshape(flat),
                      field[:, :, 0].reshape(flat), field[:, :, -1].reshape(flat),
                      field[:, :, :, 0].reshape(flat), field[:, :, :, -1].reshape(flat)], axis=1)


def ghosts_from(source_faces, index):
    flipped = source_faces[:, jnp.array(FLIP, dtype=jnp.int32)]
    picked = flipped[jnp.maximum(index, 0), jnp.arange(6, dtype=jnp.int32)[None, :]]
    return picked * (index >= 0).astype(jnp.float32)[:, :, None]


def beside(field, ghost):
    count = field.shape[0]
    edge = field.shape[1]
    layers = ghost.reshape(count, 6, edge, edge)
    x_minus = jnp.concatenate([layers[:, 0][:, None], field[:, :-1]], 1)
    x_plus = jnp.concatenate([field[:, 1:], layers[:, 1][:, None]], 1)
    y_minus = jnp.concatenate([layers[:, 2][:, :, None], field[:, :, :-1]], 2)
    y_plus = jnp.concatenate([field[:, :, 1:], layers[:, 3][:, :, None]], 2)
    z_minus = jnp.concatenate([layers[:, 4][..., None], field[..., :-1]], 3)
    z_plus = jnp.concatenate([field[..., 1:], layers[:, 5][..., None]], 3)
    return x_minus, x_plus, y_minus, y_plus, z_minus, z_plus


def sweep(field, ghost, source, sigma, weight):
    parts = beside(field, ghost)
    total = parts[0] + parts[1] + parts[2] + parts[3] + parts[4] + parts[5]
    resid = source - sigma * ((6.0 + EPS) * field - total)
    return field + weight * resid / (sigma * (6.0 + EPS))


def joule(field, ghost, sigma):
    parts = beside(field, ghost)
    return sigma * ((parts[1] - field) ** 2 + (parts[3] - field) ** 2 + (parts[5] - field) ** 2)


def thermal_step(temp_pad, cond_pad, heat, anchor_x, anchor_y, total_x, total_y):
    size_a = temp_pad.shape[0] - 2
    size_b = temp_pad.shape[1] - 2
    coord_x = anchor_x + jnp.arange(size_a + 2, dtype=jnp.int32)
    valid_x = ((coord_x >= 0) & (coord_x < total_x)).astype(jnp.float32)
    face_x = valid_x[1:] * valid_x[:-1]
    coord_y = anchor_y + jnp.arange(size_b + 2, dtype=jnp.int32)
    valid_y = ((coord_y >= 0) & (coord_y < total_y)).astype(jnp.float32)
    face_y = valid_y[1:] * valid_y[:-1]
    flux_x = 0.5 * (cond_pad[1:] + cond_pad[:-1]) * (temp_pad[1:] - temp_pad[:-1]) * face_x[:, None, None]
    div_x = (flux_x[1:] - flux_x[:-1])[:, 1:-1]
    flux_y = 0.5 * (cond_pad[:, 1:] + cond_pad[:, :-1]) * (temp_pad[:, 1:] - temp_pad[:, :-1]) * face_y[None, :, None]
    div_y = (flux_y[:, 1:] - flux_y[:, :-1])[1:-1]
    center = temp_pad[1:-1, 1:-1]
    cond_c = cond_pad[1:-1, 1:-1]
    flux_z = 0.5 * (cond_c[..., 1:] + cond_c[..., :-1]) * (center[..., 1:] - center[..., :-1])
    zero_z = jnp.zeros_like(center[..., :1])
    div_z = jnp.concatenate([flux_z, zero_z], 2) - jnp.concatenate([zero_z, flux_z], 2)
    return center + DT * (div_x + div_y + div_z + heat)


def reference(phi_init, source, tile_mat, tile_pos, neighbours, sigma_table, temp_init, slab_mat, k0_table, beta_table):
    edge = TE
    shape4 = (TILES, edge, edge, edge)
    field = phi_init.reshape(shape4)
    src = source.reshape(shape4)
    sigma = lookup(sigma_table, tile_mat).reshape(shape4)
    for step in range(SWEEPS):
        ghost = ghosts_from(tile_faces(field), neighbours)
        field = sweep(field, ghost, src, sigma, cheb_weight(step, SWEEPS))
    ghost = ghosts_from(tile_faces(field), neighbours)
    heat = joule(field, ghost, sigma)

    def deposit(tile, grid):
        where = tile_pos[tile] * edge
        block = heat[tile]
        current = lax.dynamic_slice(grid, (where[0], where[1], where[2]), (edge, edge, edge))
        return lax.dynamic_update_slice(grid, current + block, (where[0], where[1], where[2]))

    heat_grid = lax.fori_loop(0, TILES, deposit, jnp.zeros((NX, NY, NZ), jnp.float32))
    temp = temp_init.reshape(NX, NY, NZ)
    mats = slab_mat.reshape(NX, NY, NZ)
    k_zero = lookup(k0_table, mats)
    k_beta = lookup(beta_table, mats)
    for step in range(CSWEEPS):
        cond = k_zero / (1.0 + k_beta * temp * temp)
        pads = ((1, 1), (1, 1), (0, 0))
        temp = thermal_step(jnp.pad(temp, pads), jnp.pad(cond, pads), heat_grid, -1, -1, NX, NY)

    def pick(where):
        scaled = where * edge
        return lax.dynamic_slice(temp, (scaled[0], scaled[1], scaled[2]), (edge, edge, edge)).reshape(edge ** 3)

    tile_temps = lax.map(pick, tile_pos)
    return field.reshape(TILES, edge ** 3), temp.reshape(NX, NY * NZ), tile_temps
```

```python
import functools
import math

import jax
import jax.numpy as jnp
from jax import lax
from jax.experimental import pallas as pl
from jax.experimental.pallas import tpu as pltpu
from jax.sharding import PartitionSpec as P

TE = 32
SWEEPS = 4
CSWEEPS = 3
NZ = 64
EPS = 2.0
DT = 0.15
LANES = 128
SUB = 8
TILES = 2
ROW = SUB * TILES

LOW = (SWEEPS + 2, SWEEPS + 1, 2)
HIGH = (SWEEPS + 3, SWEEPS + 2, 2)
LOW_ROWS = sum(LOW) * ROW
HIGH_ROWS = sum(HIGH) * ROW
SLABX = TE + SUB
HALO = CSWEEPS
PAD = 256


def cheb_weight(step, count):
    return 1.0 / (1.0 + 0.75 * math.cos(math.pi * (2 * step + 1) / (2 * count)))


def lookup(table, ids):
    out = jnp.full(ids.shape, table[3], jnp.float32)
    for which in (2, 1, 0):
        out = jnp.where(ids == which, table[which], out)
    return out


def prep_kernel(table, phi, src, mat, body, up, down):
    rows = TE * ROW
    sigma = lookup(table, mat[...])
    s = src[...] / sigma
    body[0:rows] = phi[...]
    body[rows : 2 * rows] = s
    body[2 * rows : 3 * rows] = sigma
    at_up, at_down = 0, 0
    for which in range(3):
        size = LOW[which] * ROW
        up[at_up : at_up + size] = body[(which + 1) * rows - size : (which + 1) * rows]
        at_up += size
        size = HIGH[which] * ROW
        down[at_down : at_down + size] = body[which * rows : which * rows + size]
        at_down += size


def slab_kernel(k0_table, beta_table, temp, mat, ylow, yhigh, xlow, xhigh, t_ext, k0_ext, b_ext):
    width = temp.shape[1]
    inner = slice(HALO, HALO + TE)
    high = slice(HALO + TE, 2 * HALO + TE)

    def fill(ref, which, own):
        wide = width + 2 * PAD
        ref[0:HALO, 0:wide] = xlow[which * HALO : (which + 1) * HALO, :]
        ref[inner, 0:PAD] = ylow[which]
        ref[inner, PAD : PAD + width] = own
        ref[inner, PAD + width : wide] = yhigh[which]
        ref[high, 0:wide] = xhigh[which * HALO : (which + 1) * HALO, :]
        ref[2 * HALO + TE :, 0:wide] = jnp.zeros((SLABX - TE - 2 * HALO, wide), jnp.float32)
        ref[:, wide:] = jnp.zeros((SLABX, ref.shape[1] - wide), jnp.float32)

    fill(t_ext, 0, temp[...])
    fill(b_ext, 1, mat[...].astype(jnp.float32))

    def block(at, carry):
        lanes = pl.ds(pl.multiple_of(at * LANES, LANES), LANES)
        ids = b_ext[:, lanes]
        k0_ext[:, lanes] = lookup(k0_table, ids)
        b_ext[:, lanes] = lookup(beta_table, ids)
        return carry

    lax.fori_loop(0, t_ext.shape[1] // LANES, block, 0)


def roll(value, by, axis):
    return pltpu.roll(value, by % value.shape[axis], axis)


def step_kernel(chips, pos, *refs):
    width_gy = 2 * chips
    tiles = width_gy * TILES
    none = tiles
    bodies = refs[:width_gy]
    halos = refs[width_gy : 2 * width_gy]
    t_in, k0_ext, b_ext = refs[2 * width_gy : 2 * width_gy + 3]
    outs = refs[2 * width_gy + 3 :]
    pot, temp_out = outs[:2]
    sends = outs[2 : 2 + width_gy]
    cell_at, cell_of, pa, pb, la, lb, ua, ub, s_c, s_l, s_u, g_c, g_l, g_u, heat, q_ext, t_ext, blocks = outs[
        2 + width_gy :
    ]
    i = lax.axis_index("gx")
    j = lax.axis_index("gy")
    rows_gx = lax.axis_size("gx")

    def clear_map(at, carry):
        for which in range(3):
            cell_at[which, at] = none
        return carry

    lax.fori_loop(0, 2 * (2 * width_gy + 2), clear_map, 0)
    mate = j + 1 - 2 * lax.rem(j, 2)
    for which, by in enumerate((0, -1, 1)):
        row = i + by
        valid = (row >= 0) & (row < rows_gx)
        first = jnp.clip(row, 0, rows_gx - 1) * tiles
        for part in range(width_gy):
            base = j if part < chips else mate
            dev = lax.rem(base - 2 * (part % chips) + width_gy, width_gy)
            for t in range(TILES):
                tile = first + dev * TILES + t
                cell = (pos[tile, 1] + 1) * 2 + pos[tile, 2]
                slot = part * TILES + t
                cell_of[which, slot] = cell
                cell_at[which, cell] = jnp.where(valid, slot, none)

    zero = jnp.zeros((SUB, LANES), jnp.float32)

    def unpack(source, start, t, target, first, count):
        def plane(p, carry):
            at = pl.multiple_of(p * ROW, ROW)
            target[first + p] = source[pl.ds(start + at + t, SUB, stride=TILES), :]
            return carry

        lax.fori_loop(0, count, plane, 0, unroll=min(count, 8))

    for part in range(width_gy):
        for t in range(TILES):
            slot = part * TILES + t
            for which, target in enumerate((pa, s_c, g_c)):
                unpack(bodies[part], which * TE * ROW, t, target, slot * TE, TE)
            at = 0
            for which, target in enumerate((la, s_l, g_l)):
                unpack(halos[part], at, t, target, slot * LOW[which], LOW[which])
                at += LOW[which] * ROW
            for which, target in enumerate((ua, s_u, g_u)):
                unpack(halos[part], at, t, target, slot * HIGH[which], HIGH[which])
                at += HIGH[which] * ROW
    for ref, count in ((pa, TE), (pb, TE), (la, LOW[0]), (lb, LOW[0]), (ua, HIGH[0]), (ub, HIGH[0])):
        for p in range(count):
            ref[none * count + p] = zero

    lane = lax.broadcasted_iota(jnp.int32, (SUB, LANES), 1)
    sub = lax.broadcasted_iota(jnp.int32, (SUB, LANES), 0)
    depth = lane % TE
    first_y, last_y = lane < TE, lane >= LANES - TE
    first_sub, last_sub = sub == 0, sub == SUB - 1
    first_z, last_z = depth == 0, depth == TE - 1

    def y_plus(own, ghost):
        turned = roll(jnp.where(first_sub, ghost, own), -1, 0)
        return roll(jnp.where(first_y, turned, own), -TE, 1)

    def y_minus(own, ghost):
        turned = roll(jnp.where(last_sub, ghost, own), 1, 0)
        return roll(jnp.where(last_y, turned, own), TE, 1)

    def z_plus(own, ghost):
        return jnp.where(last_z, roll(ghost, TE - 1, 1), roll(own, -1, 1))

    def z_minus(own, ghost):
        return jnp.where(first_z, roll(ghost, 1 - TE, 1), roll(own, 1, 1))

    def around(which, slot):
        cell = cell_of[which, slot]
        upper = cell % 2
        y_m = cell_at[which, cell - 2]
        y_p = cell_at[which, cell + 2]
        z_m = jnp.where(upper == 1, cell_at[which, cell - upper], none)
        z_p = jnp.where(upper == 0, cell_at[which, cell + 1 - upper], none)
        return cell, y_m, y_p, z_m, z_p

    bufs = ((pa, la, ua), (pb, lb, ub))
    for k in range(SWEEPS):
        weight = cheb_weight(k, SWEEPS)
        keep, gain = 1.0 - weight, weight / (6.0 + EPS)
        (c_src, l_src, u_src), (c_dst, l_dst, u_dst) = bufs[k % 2], bufs[(k + 1) % 2]

        def relax(field, size, slots, p, x_m, x_p, s):
            slot, y_m, y_p, z_m, z_p = slots
            own = field[slot * size + p]
            total = (x_m + x_p) + s
            total = total + y_minus(own, field[y_m * size + p])
            total = total + y_plus(own, field[y_p * size + p])
            total = total + z_minus(own, field[z_m * size + p])
            total = total + z_plus(own, field[z_p * size + p])
            return keep * own + gain * total

        def sweep_tile(slot, carry):
            cell, *near = around(0, slot)
            slots = (slot, *near)
            below, above = cell_at[1, cell], cell_at[2, cell]
            for p in range(TE):
                x_m = c_src[slot * TE + p - 1] if p > 0 else l_src[below * LOW[0] + LOW[0] - 1]
                x_p = c_src[slot * TE + p + 1] if p < TE - 1 else u_src[above * HIGH[0]]
                c_dst[slot * TE + p] = relax(c_src, TE, slots, p, x_m, x_p, s_c[slot * TE + p])
            cell, *near = around(1, slot)
            slots = (slot, *near)
            centre = cell_at[0, cell]
            for p in range(k + 1, LOW[0]):
                x_m = l_src[slot * LOW[0] + p - 1]
                x_p = l_src[slot * LOW[0] + p + 1] if p < LOW[0] - 1 else c_src[centre * TE]
                s = s_l[slot * LOW[1] + p - (LOW[0] - LOW[1])]
                l_dst[slot * LOW[0] + p] = relax(l_src, LOW[0], slots, p, x_m, x_p, s)
            cell, *near = around(2, slot)
            slots = (slot, *near)
            centre = cell_at[0, cell]
            for p in range(HIGH[0] - 1 - k):
                x_m = u_src[slot * HIGH[0] + p - 1] if p > 0 else c_src[centre * TE + TE - 1]
                x_p = u_src[slot * HIGH[0] + p + 1]
                u_dst[slot * HIGH[0] + p] = relax(u_src, HIGH[0], slots, p, x_m, x_p, s_u[slot * HIGH[1] + p])
            return carry

        lax.fori_loop(0, tiles, sweep_tile, 0)

    field, f_l, f_u = bufs[SWEEPS % 2]
    for t in range(TILES):
        for p in range(TE):
            pot[pl.ds(p * ROW + t, SUB, stride=TILES), :] = field[t * TE + p]

    def clear_heat(at, carry):
        heat[pl.ds(pl.multiple_of(at * SUB, SUB), SUB), :] = zero
        return carry

    lax.fori_loop(0, heat.shape[0] // SUB, clear_heat, 0, unroll=8)

    def joule(ref, size, slots, p, x_p, sigma):
        slot, _, y_p, _, z_p = slots
        own = ref[slot * size + p]
        d_x = x_p - own
        d_y = y_plus(own, ref[y_p * size + p]) - own
        d_z = z_plus(own, ref[z_p * size + p]) - own
        return sigma * (d_x * d_x + d_y * d_y + d_z * d_z)

    first_cell = 2 * (2 * j)

    def put_heat(local, x, value):
        heat[pl.ds(pl.multiple_of((local * SLABX + x) * SUB, SUB), SUB), :] = value

    def heat_tile(slot, carry):
        for which in range(3):
            cell, *near = around(which, slot)
            slots = (slot, *near)
            local = cell - first_cell
            inside = (local >= 0) & (local < 8)
            if which > 0:
                row = i - 1 if which == 1 else i + 1
                inside = inside & (row >= 0) & (row < rows_gx)

            @pl.when(inside)
            def _():
                if which == 0:
                    above = cell_at[2, cell]
                    for p in range(TE):
                        x_p = field[slot * TE + p + 1] if p < TE - 1 else f_u[above * HIGH[0]]
                        put_heat(local, HALO + p, joule(field, TE, slots, p, x_p, g_c[slot * TE + p]))
                elif which == 1:
                    centre = cell_at[0, cell]
                    for p in range(2):
                        q = LOW[0] - 2 + p
                        x_p = f_l[slot * LOW[0] + q + 1] if p < 1 else field[centre * TE]
                        put_heat(local, HALO - 2 + p, joule(f_l, LOW[0], slots, q, x_p, g_l[slot * LOW[2] + p]))
                else:
                    for p in range(2):
                        x_p = f_u[slot * HIGH[0] + p + 1]
                        put_heat(local, HALO + TE + p, joule(f_u, HIGH[0], slots, p, x_p, g_u[slot * HIGH[2] + p]))

        return carry

    lax.fori_loop(0, tiles, heat_tile, 0)

    quarter = [(lane >= q * TE) & (lane < (q + 1) * TE) for q in range(3)]

    def pick(parts):
        return jnp.where(
            quarter[0], parts[0], jnp.where(quarter[1], parts[1], jnp.where(quarter[2], parts[2], parts[3]))
        )

    quads = (t_in.shape[1] - LANES) // (2 * LANES)
    for m in range(quads):
        y0 = 4 * m - 4 + TE
        col, yq = y0 // TE, y0 % TE // 4
        for g in range(SLABX // SUB):
            a = heat[pl.ds((2 * col * SLABX + g * SUB) * SUB + yq, SUB, stride=SUB), :]
            b = heat[pl.ds(((2 * col + 1) * SLABX + g * SUB) * SUB + yq, SUB, stride=SUB), :]
            rows = slice(g * SUB, (g + 1) * SUB)
            q_ext[rows, 2 * m * LANES : (2 * m + 1) * LANES] = pick(
                (a, roll(b, TE, 1), roll(a, TE, 1), roll(b, 2 * TE, 1))
            )
            q_ext[rows, (2 * m + 1) * LANES : (2 * m + 2) * LANES] = pick(
                (roll(a, 2 * TE, 1), roll(b, -TE, 1), roll(a, -TE, 1), b)
            )

    wide = (SLABX, LANES)
    lane_w = lax.broadcasted_iota(jnp.int32, wide, 1)
    row_w = lax.broadcasted_iota(jnp.int32, wide, 0)
    half = lane_w < NZ
    no_z = lane_w % NZ == NZ - 1
    no_x = ((row_w == HALO - 1) & (i == 0)) | ((row_w == HALO + TE - 1) & (i == rows_gx - 1))
    nothing = jnp.zeros(wide, jnp.float32)
    count = 2 * quads
    low_block, high_block = PAD // LANES - 1, count - PAD // LANES - 1

    def load(ref, at):
        return ref[:, pl.ds(pl.multiple_of(at * LANES, LANES), LANES)]

    for step in range(CSWEEPS):
        source = t_in if step == 0 else t_ext

        def conduct(temp, at):
            return load(k0_ext, at) / (1.0 + load(b_ext, at) * temp * temp)

        def advance(at, carry):
            temp, cond, temp_r, cond_r, flux_before = carry
            temp_n = load(source, at + 1)
            cond_n = conduct(temp_n, at + 1)
            temp_nr, cond_nr = roll(temp_n, NZ, 1), roll(cond_n, NZ, 1)
            flux_y = (cond + jnp.where(half, cond_r, cond_nr)) * (jnp.where(half, temp_r, temp_nr) - temp)
            closed = ((at == low_block) & (j == 0)) | ((at == high_block) & (j == width_gy - 1))
            flux_y = jnp.where((lane_w >= NZ) & closed, 0.0, flux_y)
            flux_yr = roll(flux_y, NZ, 1)
            div = flux_y - jnp.where(half, flux_before, flux_yr)
            flux_x = (cond + roll(cond, -1, 0)) * (roll(temp, -1, 0) - temp)
            flux_x = jnp.where(no_x, 0.0, flux_x)
            div = div + (flux_x - roll(flux_x, 1, 0))
            flux_z = (cond + roll(cond, -1, 1)) * (roll(temp, -1, 1) - temp)
            flux_z = jnp.where(no_z, 0.0, flux_z)
            div = div + (flux_z - roll(flux_z, 1, 1))
            t_ext[:, pl.ds(pl.multiple_of(at * LANES, LANES), LANES)] = temp + DT * (0.5 * div + load(q_ext, at))
            return temp_n, cond_n, temp_nr, cond_nr, flux_yr

        temp_0 = load(source, 0)
        cond_0 = conduct(temp_0, 0)
        lax.fori_loop(
            0, count, advance, (temp_0, cond_0, roll(temp_0, NZ, 1), roll(cond_0, NZ, 1), nothing)
        )
        t_ext[:, count * LANES :] = nothing

    temp_out[...] = t_ext[HALO : HALO + TE, PAD : PAD + temp_out.shape[1]]

    for m in range(quads - 2):
        col, yq = 4 * m // TE, 4 * m % TE // 4
        for g in range(TE // SUB):
            rows = slice(g * SUB, (g + 1) * SUB)
            v = temp_out[rows, 2 * m * LANES : (2 * m + 1) * LANES]
            w = temp_out[rows, (2 * m + 1) * LANES : (2 * m + 2) * LANES]
            a = pick((v, roll(v, -TE, 1), roll(w, 2 * TE, 1), roll(w, TE, 1)))
            b = pick((roll(v, -TE, 1), roll(v, 2 * TE, 1), roll(w, TE, 1), w))
            blocks[pl.ds((2 * col * TE + g * SUB) * SUB + yq, SUB, stride=SUB), :] = a
            blocks[pl.ds(((2 * col + 1) * TE + g * SUB) * SUB + yq, SUB, stride=SUB), :] = b
    for shift in range(width_gy):
        dev = lax.rem(j + shift, width_gy)
        for t in range(TILES):
            tile = i * tiles + dev * TILES + t
            col = pos[tile, 1] - 2 * j
            cell = jnp.clip(col, 0, 1) * 2 + pos[tile, 2]
            here = (col >= 0) & (col < 2)

            def plane(p, carry):
                value = blocks[pl.ds(pl.multiple_of((cell * TE + p) * SUB, SUB), SUB), :]
                value = jnp.where(here, value, 0.0)
                sends[shift][pl.ds(pl.multiple_of(p * ROW, ROW) + t, SUB, stride=TILES), :] = value
                return carry

            lax.fori_loop(0, TE, plane, 0, unroll=8)


def shifted(value, axis, by, wrap=False):
    count = lax.axis_size(axis)
    pairs = [(d, (d + by) % count) for d in range(count) if wrap or 0 <= d + by < count]
    return lax.ppermute(value, axis, pairs)


def from_mate(value):
    return lax.ppermute(value, "gy", [(d, d ^ 1) for d in range(lax.axis_size("gy"))])


def to_rows(value):
    return value.reshape(TILES, -1, LANES).transpose(1, 0, 2).reshape(-1, LANES)


def from_rows(value):
    return value.reshape(-1, TILES, LANES).transpose(1, 0, 2).reshape(TILES, -1)


def everyone(value, chips):
    mine = [value] + [shifted(value, "gy", 2 * d, True) for d in range(1, chips)]
    return mine + [from_mate(part) for part in mine]


VMEM = pl.BlockSpec(memory_space=pltpu.VMEM)
SMEM = pl.BlockSpec(memory_space=pltpu.SMEM)
PARAMS = pltpu.CompilerParams(vmem_limit_bytes=48 * 1024 * 1024)


def on_device(
    phi_init,
    source,
    tile_mat,
    tile_pos,
    neighbours,
    sigma_table,
    temp_init,
    slab_mat,
    k0_table,
    beta_table,
):
    f32 = jnp.float32
    width_gy = lax.axis_size("gy")
    chips = width_gy // 2
    tiles = width_gy * TILES
    size_x, width = temp_init.shape
    wide = width + 2 * PAD
    shape = jax.ShapeDtypeStruct

    body, up, down = pl.pallas_call(
        prep_kernel,
        out_shape=(
            shape((3 * TE * ROW, LANES), f32),
            shape((LOW_ROWS, LANES), f32),
            shape((HIGH_ROWS, LANES), f32),
        ),
        in_specs=[SMEM, VMEM, VMEM, VMEM],
        out_specs=(VMEM, VMEM, VMEM),
        compiler_params=PARAMS,
        name="prep",
    )(sigma_table, to_rows(phi_init), to_rows(source), to_rows(tile_mat))
    bodies = everyone(body, chips)
    halo = jnp.concatenate([shifted(up, "gx", 1), shifted(down, "gx", -1)])
    halos = everyone(halo, chips)

    edge = lambda lanes: jnp.stack([temp_init[:, lanes], slab_mat[:, lanes].astype(f32)])
    ylow = shifted(edge(slice(width - PAD, None)), "gy", 1)
    yhigh = shifted(edge(slice(0, PAD)), "gy", -1)

    def x_edge(rows):
        temp = jnp.concatenate([ylow[0, rows], temp_init[rows], yhigh[0, rows]], axis=1)
        mat = jnp.concatenate([ylow[1, rows], slab_mat[rows].astype(f32), yhigh[1, rows]], axis=1)
        return jnp.concatenate([temp, mat])

    xlow = shifted(x_edge(slice(size_x - HALO, None)), "gx", 1)
    xhigh = shifted(x_edge(slice(0, HALO)), "gx", -1)

    ext = shape((SLABX, wide + LANES), f32)

    t_ext, k0_ext, b_ext = pl.pallas_call(
        slab_kernel,
        out_shape=(ext, ext, ext),
        in_specs=[SMEM, SMEM] + [VMEM] * 6,
        out_specs=(VMEM, VMEM, VMEM),
        compiler_params=PARAMS,
        name="slab_prep",
    )(k0_table, beta_table, temp_init, slab_mat, ylow, yhigh, xlow, xhigh)

    plane = (SUB, LANES)

    def planes(count):
        return pltpu.VMEM(((tiles + 1) * count, *plane), f32)

    cells = 2 * (2 * width_gy + 2)
    tile_rows = shape((TE * ROW, LANES), f32)
    results = pl.pallas_call(
        functools.partial(step_kernel, chips),
        out_shape=(tile_rows, shape((size_x, width), f32)) + (tile_rows,) * width_gy,
        in_specs=[SMEM] + [VMEM] * (2 * width_gy + 3),
        out_specs=(VMEM,) * (2 + width_gy),
        scratch_shapes=[
            pltpu.SMEM((3, cells), jnp.int32),
            pltpu.SMEM((3, tiles), jnp.int32),
            planes(TE), planes(TE), planes(LOW[0]), planes(LOW[0]), planes(HIGH[0]), planes(HIGH[0]),
            planes(TE), planes(LOW[1]), planes(HIGH[1]),
            planes(TE), planes(LOW[2]), planes(HIGH[2]),
            pltpu.VMEM((8 * SLABX * SUB, LANES), f32),
            pltpu.VMEM((SLABX, wide), f32),
            pltpu.VMEM((SLABX, wide + LANES), f32),
            pltpu.VMEM((4 * TE * SUB, LANES), f32),
        ],
        compiler_params=PARAMS,
        name="step",
    )(tile_pos, *bodies, *halos, t_ext, k0_ext, b_ext)
    pot, temp, sends = results[0], results[1], results[2:]
    tile_temps = sends[0]
    for by in range(1, width_gy):
        tile_temps = tile_temps + shifted(sends[by], "gy", by, True)
    return from_rows(pot), temp, from_rows(tile_temps)


def solution(mesh):
    placed = (
        P(("gx", "gy"), None),
        P(("gx", "gy"), None),
        P(("gx", "gy"), None),
        P(),
        P(("gx", "gy"), None),
        P(),
        P("gx", "gy"),
        P("gx", "gy"),
        P(),
        P(),
    )
    return jax.shard_map(
        on_device,
        mesh=mesh,
        in_specs=placed,
        out_specs=(P(("gx", "gy"), None), P("gx", "gy"), P(("gx", "gy"), None)),
        check_vma=False,
    )
```

```python
import functools
import math

import jax
import jax.numpy as jnp
from jax import lax
from jax.experimental import pallas as pl
from jax.experimental.pallas import tpu as pltpu
from jax.sharding import PartitionSpec as P

TE = 32
SWEEPS = 4
CSWEEPS = 3
NZ = 64
EPS = 2.0
DT = 0.15
LANES = 128
SUB = 8
TILES = 2
ROW = SUB * TILES

LOW = (SWEEPS + 2, SWEEPS + 1, 2)
HIGH = (SWEEPS + 3, SWEEPS + 2, 2)
LOW_ROWS = sum(LOW) * ROW
HIGH_ROWS = sum(HIGH) * ROW
SLABX = TE + SUB
HALO = CSWEEPS
PAD = 256


def cheb_weight(step, count):
    return 1.0 / (1.0 + 0.75 * math.cos(math.pi * (2 * step + 1) / (2 * count)))


def lookup(table, ids):
    out = jnp.full(ids.shape, table[3], jnp.float32)
    for which in (2, 1, 0):
        out = jnp.where(ids == which, table[which], out)
    return out


def roll(value, by, axis):
    return pltpu.roll(value, by % value.shape[axis], axis)


def prep_kernel(table, phi, src, mat, temp, slab, body, sigma, up, down, src_v, mat_v, ends_t, ends_m, sems):
    rows = TE * ROW
    size_x, width = temp.shape
    moves = [(phi, body.at[0:rows]), (src, src_v), (mat, mat_v)]
    for which, first in enumerate((0, size_x - SUB)):
        moves.append((temp.at[first : first + SUB], ends_t.at[which]))
        moves.append((slab.at[first : first + SUB], ends_m.at[which]))
    moves = [pltpu.make_async_copy(*move, sems.at[at]) for at, move in enumerate(moves)]
    for move in moves:
        move.start()
    for move in moves:
        move.wait()
    sigma[...] = lookup(table, mat_v[...])
    body[rows : 2 * rows] = src_v[...] / sigma[...]
    at_up, at_down = 0, 0
    for ref, first in ((body, 0), (body, rows), (sigma, 0)):
        which = (first // rows) if ref is body else 2
        size = LOW[which] * ROW
        up[at_up : at_up + size] = ref[first + rows - size : first + rows]
        at_up += size
        size = HIGH[which] * ROW
        down[at_down : at_down + size] = ref[first : first + size]
        at_down += size
    sub = lax.broadcasted_iota(jnp.int32, (SUB, LANES), 0)
    for at in range(width // LANES):
        lanes = slice(at * LANES, (at + 1) * LANES)
        t_low, m_low = ends_t[0, :, lanes], ends_m[0, :, lanes].astype(jnp.float32)
        t_high, m_high = ends_t[1, :, lanes], ends_m[1, :, lanes].astype(jnp.float32)
        first = at * SUB
        up[LOW_ROWS + first : LOW_ROWS + first + SUB] = jnp.where(sub < 4, roll(t_high, HALO, 0), roll(m_high, -1, 0))
        down[HIGH_ROWS + first : HIGH_ROWS + first + SUB] = jnp.where(sub < 4, t_low, roll(m_low, 4, 0))


def relay_kernel(low, high, temp, mat, halo, edge_low, edge_high):
    halo[0:LOW_ROWS] = low[0:LOW_ROWS]
    halo[LOW_ROWS : LOW_ROWS + HIGH_ROWS] = high[0:HIGH_ROWS]
    blocks = temp.shape[1] // LANES
    for edge, firsts in ((edge_low, (0, 1)), (edge_high, (blocks - 2, blocks - 1))):
        for at, block in enumerate(firsts):
            lanes = slice(at * LANES, (at + 1) * LANES)
            own = slice(block * LANES, (block + 1) * LANES)
            for which, value in enumerate((temp[:, own], mat[:, own].astype(jnp.float32))):
                edge[which, HALO : HALO + TE, lanes] = value
                first = LOW_ROWS + block * SUB + 4 * which
                edge[which, 0:HALO, lanes] = low[first : first + HALO, :]
                first = HIGH_ROWS + block * SUB + 4 * which
                edge[which, HALO + TE : 2 * HALO + TE, lanes] = high[first : first + HALO, :]
                rest = SLABX - TE - 2 * HALO
                edge[which, SLABX - rest :, lanes] = jnp.zeros((rest, LANES), jnp.float32)


def slab_kernel(k0_table, beta_table, temp, mat, ylow, yhigh, xlow, xhigh, t_ext, k0_ext, b_ext):
    width = temp.shape[1]
    inner = slice(HALO, HALO + TE)
    high = slice(HALO + TE, 2 * HALO + TE)
    rest = slice(2 * HALO + TE, SLABX)
    for which, (own, target) in enumerate(((temp, t_ext), (mat, b_ext))):
        target[:, 0:PAD] = ylow[which]
        target[:, PAD + width : 2 * PAD + width] = yhigh[which]
        target[:, 2 * PAD + width :] = jnp.zeros((SLABX, LANES), jnp.float32)
        target[rest, PAD : PAD + width] = jnp.zeros((SLABX - TE - 2 * HALO, width), jnp.float32)
        for at in range(width // LANES):
            lanes = slice(PAD + at * LANES, PAD + (at + 1) * LANES)
            first = LOW_ROWS + at * SUB + 4 * which
            target[0:HALO, lanes] = xlow[first : first + HALO, :]
            first = HIGH_ROWS + at * SUB + 4 * which
            target[high, lanes] = xhigh[first : first + HALO, :]
            target[inner, lanes] = own[:, at * LANES : (at + 1) * LANES].astype(jnp.float32)
    for at in range(t_ext.shape[1] // LANES):
        lanes = slice(at * LANES, (at + 1) * LANES)
        ids = b_ext[:, lanes]
        k0_ext[:, lanes] = lookup(k0_table, ids)
        b_ext[:, lanes] = lookup(beta_table, ids)


def fill_maps(chips, pos, cell_at, cell_of):
    width_gy = 2 * chips
    tiles = width_gy * TILES
    i = lax.axis_index("gx")
    j = lax.axis_index("gy")
    rows_gx = lax.axis_size("gx")
    for at in range(2 * (2 * width_gy + 2)):
        for which in range(3):
            cell_at[which, at] = tiles
    for which, by in enumerate((0, -1, 1)):
        row = i + by
        valid = (row >= 0) & (row < rows_gx)
        first = jnp.clip(row, 0, rows_gx - 1) * tiles
        for part in range(width_gy):
            dev = part_device(part, chips, j)
            for t in range(TILES):
                tile = first + dev * TILES + t
                cell = (pos[tile, 1] + 1) * 2 + pos[tile, 2]
                slot = part * TILES + t
                cell_of[which, slot] = cell
                cell_at[which, cell] = jnp.where(valid, slot, tiles)


def part_device(part, chips, j):
    mate = j + 1 - 2 * lax.rem(j, 2)
    base = j if part < chips else mate
    return lax.rem(base - 2 * (part % chips) + 2 * chips, 2 * chips)


def sweep_kernel(chips, pos, *refs):
    width_gy = 2 * chips
    tiles = width_gy * TILES
    none = tiles
    bodies = refs[:width_gy]
    halos = refs[width_gy : 2 * width_gy]
    pot, slope, cell_at, cell_of, pa, pb, la, lb, ua, ub, s_c, s_l, s_u = refs[2 * width_gy :]
    i = lax.axis_index("gx")
    j = lax.axis_index("gy")
    rows_gx = lax.axis_size("gx")
    fill_maps(chips, pos, cell_at, cell_of)

    zero = jnp.zeros((SUB, LANES), jnp.float32)

    def unpack(source, start, t, target, first, count):
        def plane(p, carry):
            at = pl.multiple_of(p * ROW, ROW)
            target[first + p] = source[pl.ds(start + at + t, SUB, stride=TILES), :]
            return carry

        lax.fori_loop(0, count, plane, 0, unroll=min(count, 8))

    for part in range(width_gy):
        for t in range(TILES):
            slot = part * TILES + t
            for which, target in enumerate((pa, s_c)):
                unpack(bodies[part], which * TE * ROW, t, target, slot * TE, TE)
            at = 0
            for which, target in enumerate((la, s_l)):
                unpack(halos[part], at, t, target, slot * LOW[which], LOW[which])
                at += LOW[which] * ROW
            at = LOW_ROWS
            for which, target in enumerate((ua, s_u)):
                unpack(halos[part], at, t, target, slot * HIGH[which], HIGH[which])
                at += HIGH[which] * ROW
    for ref, count in ((pa, TE), (pb, TE), (la, LOW[0]), (lb, LOW[0]), (ua, HIGH[0]), (ub, HIGH[0])):
        for p in range(count):
            ref[none * count + p] = zero

    lane = lax.broadcasted_iota(jnp.int32, (SUB, LANES), 1)
    sub = lax.broadcasted_iota(jnp.int32, (SUB, LANES), 0)
    depth = lane % TE
    first_y, last_y = lane < TE, lane >= LANES - TE
    first_sub, last_sub = sub == 0, sub == SUB - 1
    first_z, last_z = depth == 0, depth == TE - 1

    def y_plus(own, ghost):
        turned = roll(jnp.where(first_sub, ghost, own), -1, 0)
        return roll(jnp.where(first_y, turned, own), -TE, 1)

    def y_minus(own, ghost):
        turned = roll(jnp.where(last_sub, ghost, own), 1, 0)
        return roll(jnp.where(last_y, turned, own), TE, 1)

    def z_plus(own, ghost):
        return jnp.where(last_z, roll(ghost, TE - 1, 1), roll(own, -1, 1))

    def z_minus(own, ghost):
        return jnp.where(first_z, roll(ghost, 1 - TE, 1), roll(own, 1, 1))

    def around(which, slot):
        cell = cell_of[which, slot]
        upper = cell % 2
        y_m = cell_at[which, cell - 2]
        y_p = cell_at[which, cell + 2]
        z_m = jnp.where(upper == 1, cell_at[which, cell - upper], none)
        z_p = jnp.where(upper == 0, cell_at[which, cell + 1 - upper], none)
        return cell, y_m, y_p, z_m, z_p

    bufs = ((pa, la, ua), (pb, lb, ub))
    for k in range(SWEEPS):
        weight = cheb_weight(k, SWEEPS)
        keep, gain = 1.0 - weight, weight / (6.0 + EPS)
        (c_src, l_src, u_src), (c_dst, l_dst, u_dst) = bufs[k % 2], bufs[(k + 1) % 2]

        def relax(field, size, slots, p, x_m, x_p, s):
            slot, y_m, y_p, z_m, z_p = slots
            own = field[slot * size + p]
            total = (x_m + x_p) + s
            total = total + y_minus(own, field[y_m * size + p])
            total = total + y_plus(own, field[y_p * size + p])
            total = total + z_minus(own, field[z_m * size + p])
            total = total + z_plus(own, field[z_p * size + p])
            return keep * own + gain * total

        def sweep_tile(slot, carry):
            cell, *near = around(0, slot)
            slots = (slot, *near)
            below, above = cell_at[1, cell], cell_at[2, cell]
            for p in range(TE):
                x_m = c_src[slot * TE + p - 1] if p > 0 else l_src[below * LOW[0] + LOW[0] - 1]
                x_p = c_src[slot * TE + p + 1] if p < TE - 1 else u_src[above * HIGH[0]]
                c_dst[slot * TE + p] = relax(c_src, TE, slots, p, x_m, x_p, s_c[slot * TE + p])
            cell, *near = around(1, slot)
            slots = (slot, *near)
            centre = cell_at[0, cell]
            for p in range(k + 1, LOW[0]):
                x_m = l_src[slot * LOW[0] + p - 1]
                x_p = l_src[slot * LOW[0] + p + 1] if p < LOW[0] - 1 else c_src[centre * TE]
                s = s_l[slot * LOW[1] + p - (LOW[0] - LOW[1])]
                l_dst[slot * LOW[0] + p] = relax(l_src, LOW[0], slots, p, x_m, x_p, s)
            cell, *near = around(2, slot)
            slots = (slot, *near)
            centre = cell_at[0, cell]
            for p in range(HIGH[0] - 1 - k):
                x_m = u_src[slot * HIGH[0] + p - 1] if p > 0 else c_src[centre * TE + TE - 1]
                x_p = u_src[slot * HIGH[0] + p + 1]
                u_dst[slot * HIGH[0] + p] = relax(u_src, HIGH[0], slots, p, x_m, x_p, s_u[slot * HIGH[1] + p])
            return carry

        lax.fori_loop(0, tiles, sweep_tile, 0)

    field, f_l, f_u = bufs[SWEEPS % 2]
    for t in range(TILES):
        for p in range(TE):
            pot[pl.ds(p * ROW + t, SUB, stride=TILES), :] = field[t * TE + p]

    def clear(at, carry):
        slope[pl.ds(pl.multiple_of(at * SUB, SUB), SUB), :] = zero
        return carry

    lax.fori_loop(0, slope.shape[0] // SUB, clear, 0, unroll=8)

    def squares(ref, size, slots, p, x_p):
        slot, _, y_p, _, z_p = slots
        own = ref[slot * size + p]
        d_x = x_p - own
        d_y = y_plus(own, ref[y_p * size + p]) - own
        d_z = z_plus(own, ref[z_p * size + p]) - own
        return d_x * d_x + d_y * d_y + d_z * d_z

    def put(local, x, value):
        slope[pl.ds(pl.multiple_of((local * SLABX + x) * SUB, SUB), SUB), :] = value

    def slope_tile(slot, carry):
        for which in range(3):
            cell, *near = around(which, slot)
            slots = (slot, *near)
            local, inside = window(which, cell, i, j, rows_gx)

            @pl.when(inside)
            def _():
                if which == 0:
                    above = cell_at[2, cell]
                    for p in range(TE):
                        x_p = field[slot * TE + p + 1] if p < TE - 1 else f_u[above * HIGH[0]]
                        put(local, HALO + p, squares(field, TE, slots, p, x_p))
                elif which == 1:
                    centre = cell_at[0, cell]
                    for p in range(2):
                        q = LOW[0] - 2 + p
                        x_p = f_l[slot * LOW[0] + q + 1] if p < 1 else field[centre * TE]
                        put(local, HALO - 2 + p, squares(f_l, LOW[0], slots, q, x_p))
                else:
                    for p in range(2):
                        x_p = f_u[slot * HIGH[0] + p + 1]
                        put(local, HALO + TE + p, squares(f_u, HIGH[0], slots, p, x_p))

        return carry

    lax.fori_loop(0, tiles, slope_tile, 0)


def window(which, cell, i, j, rows_gx):
    local = cell - 4 * j
    inside = (local >= 0) & (local < 8)
    if which > 0:
        row = i - 1 if which == 1 else i + 1
        inside = inside & (row >= 0) & (row < rows_gx)
    return local, inside


def slab_steps_kernel(chips, pos, *refs):
    width_gy = 2 * chips
    tiles = width_gy * TILES
    sigmas = refs[:width_gy]
    halos = refs[width_gy : 2 * width_gy]
    slope, t_in, k0_ext, b_ext, temp_out = refs[2 * width_gy : 2 * width_gy + 5]
    sends = refs[2 * width_gy + 5 : 3 * width_gy + 5]
    heat, q_ext, t_ext, blocks = refs[3 * width_gy + 5 :]
    i = lax.axis_index("gx")
    j = lax.axis_index("gy")
    rows_gx = lax.axis_size("gx")
    lane = lax.broadcasted_iota(jnp.int32, (SUB, LANES), 1)
    zero = jnp.zeros((SUB, LANES), jnp.float32)

    def clear(at, carry):
        heat[pl.ds(pl.multiple_of(at * SUB, SUB), SUB), :] = zero
        return carry

    lax.fori_loop(0, heat.shape[0] // SUB, clear, 0, unroll=8)
    low_at, high_at = (LOW[0] + LOW[1]) * ROW, LOW_ROWS + (HIGH[0] + HIGH[1]) * ROW
    for part in range(width_gy):
        dev = part_device(part, chips, j)
        for t in range(TILES):
            for which, by in enumerate((0, -1, 1)):
                tile = jnp.clip(i + by, 0, rows_gx - 1) * tiles + dev * TILES + t
                cell = (pos[tile, 1] + 1) * 2 + pos[tile, 2]
                local, inside = window(which, cell, i, j, rows_gx)
                source, start, x, count = (
                    (sigmas[part], 0, HALO, TE),
                    (halos[part], low_at, HALO - 2, 2),
                    (halos[part], high_at, HALO + TE, 2),
                )[which]

                @pl.when(inside)
                def _():
                    for p in range(count):
                        rows = pl.ds(pl.multiple_of((local * SLABX + x + p) * SUB, SUB), SUB)
                        sigma = source[pl.ds(start + p * ROW + t, SUB, stride=TILES), :]
                        heat[rows, :] = sigma * slope[rows, :]

    quarter = [(lane >= q * TE) & (lane < (q + 1) * TE) for q in range(3)]

    def pick(parts):
        return jnp.where(
            quarter[0], parts[0], jnp.where(quarter[1], parts[1], jnp.where(quarter[2], parts[2], parts[3]))
        )

    quads = (t_in.shape[1] - LANES) // (2 * LANES)
    for m in range(quads):
        y0 = 4 * m - 4 + TE
        col, yq = y0 // TE, y0 % TE // 4
        for g in range(SLABX // SUB):
            a = heat[pl.ds((2 * col * SLABX + g * SUB) * SUB + yq, SUB, stride=SUB), :]
            b = heat[pl.ds(((2 * col + 1) * SLABX + g * SUB) * SUB + yq, SUB, stride=SUB), :]
            rows = slice(g * SUB, (g + 1) * SUB)
            q_ext[rows, 2 * m * LANES : (2 * m + 1) * LANES] = pick(
                (a, roll(b, TE, 1), roll(a, TE, 1), roll(b, 2 * TE, 1))
            )
            q_ext[rows, (2 * m + 1) * LANES : (2 * m + 2) * LANES] = pick(
                (roll(a, 2 * TE, 1), roll(b, -TE, 1), roll(a, -TE, 1), b)
            )

    wide = (SLABX, LANES)
    lane_w = lax.broadcasted_iota(jnp.int32, wide, 1)
    row_w = lax.broadcasted_iota(jnp.int32, wide, 0)
    half = lane_w < NZ
    no_z = lane_w % NZ == NZ - 1
    no_x = ((row_w == HALO - 1) & (i == 0)) | ((row_w == HALO + TE - 1) & (i == rows_gx - 1))
    nothing = jnp.zeros(wide, jnp.float32)
    count = 2 * quads
    low_block, high_block = PAD // LANES - 1, count - PAD // LANES - 1

    def load(ref, at):
        return ref[:, at * LANES : (at + 1) * LANES]

    for step in range(CSWEEPS):
        source = t_in if step == 0 else t_ext

        def fetch(at):
            temp = load(source, at)
            cond = load(k0_ext, at) / (1.0 + load(b_ext, at) * temp * temp)
            return temp, cond, roll(temp, NZ, 1), roll(cond, NZ, 1)

        ahead = fetch(0)
        flux_before = nothing
        for at in range(count):
            temp, cond, temp_r, cond_r = ahead
            ahead = fetch(at + 1)
            flux_y = (cond + jnp.where(half, cond_r, ahead[3])) * (jnp.where(half, temp_r, ahead[2]) - temp)
            if at == low_block:
                flux_y = jnp.where((lane_w >= NZ) & (j == 0), 0.0, flux_y)
            if at == high_block:
                flux_y = jnp.where((lane_w >= NZ) & (j == width_gy - 1), 0.0, flux_y)
            flux_yr = roll(flux_y, NZ, 1)
            div = flux_y - jnp.where(half, flux_before, flux_yr)
            flux_before = flux_yr
            flux_x = (cond + roll(cond, -1, 0)) * (roll(temp, -1, 0) - temp)
            flux_x = jnp.where(no_x, 0.0, flux_x)
            div = div + (flux_x - roll(flux_x, 1, 0))
            flux_z = (cond + roll(cond, -1, 1)) * (roll(temp, -1, 1) - temp)
            flux_z = jnp.where(no_z, 0.0, flux_z)
            div = div + (flux_z - roll(flux_z, 1, 1))
            t_ext[:, at * LANES : (at + 1) * LANES] = temp + DT * (0.5 * div + load(q_ext, at))
        t_ext[:, count * LANES :] = nothing

    temp_out[...] = t_ext[HALO : HALO + TE, PAD : PAD + temp_out.shape[1]]

    for m in range(quads - 2):
        col, yq = 4 * m // TE, 4 * m % TE // 4
        for g in range(TE // SUB):
            rows = slice(g * SUB, (g + 1) * SUB)
            v = temp_out[rows, 2 * m * LANES : (2 * m + 1) * LANES]
            w = temp_out[rows, (2 * m + 1) * LANES : (2 * m + 2) * LANES]
            a = pick((v, roll(v, -TE, 1), roll(w, 2 * TE, 1), roll(w, TE, 1)))
            b = pick((roll(v, -TE, 1), roll(v, 2 * TE, 1), roll(w, TE, 1), w))
            blocks[pl.ds((2 * col * TE + g * SUB) * SUB + yq, SUB, stride=SUB), :] = a
            blocks[pl.ds(((2 * col + 1) * TE + g * SUB) * SUB + yq, SUB, stride=SUB), :] = b
    for shift in range(width_gy):
        dev = lax.rem(j + shift, width_gy)
        for t in range(TILES):
            tile = i * tiles + dev * TILES + t
            col = pos[tile, 1] - 2 * j
            cell = jnp.clip(col, 0, 1) * 2 + pos[tile, 2]
            here = (col >= 0) & (col < 2)
            for p in range(TE):
                value = blocks[pl.ds(pl.multiple_of((cell * TE + p) * SUB, SUB), SUB), :]
                sends[shift][pl.ds(p * ROW + t, SUB, stride=TILES), :] = jnp.where(here, value, 0.0)


def shifted(value, axis, by, wrap=False):
    count = lax.axis_size(axis)
    pairs = [(d, (d + by) % count) for d in range(count) if wrap or 0 <= d + by < count]
    return lax.ppermute(value, axis, pairs)


def from_mate(value):
    return lax.ppermute(value, "gy", [(d, d ^ 1) for d in range(lax.axis_size("gy"))])


def to_rows(value):
    return value.reshape(TILES, -1, LANES).transpose(1, 0, 2).reshape(-1, LANES)


def from_rows(value):
    return value.reshape(-1, TILES, LANES).transpose(1, 0, 2).reshape(TILES, -1)


def everyone(value, chips):
    mine = [value] + [shifted(value, "gy", 2 * d, True) for d in range(1, chips)]
    return mine + [from_mate(part) for part in mine]


def everyone_direct(value, chips):
    mine = [value] + [shifted(value, "gy", 2 * d, True) for d in range(1, chips)]
    count = 2 * chips
    for d in range(chips):
        pairs = [(at, ((at ^ 1) + 2 * d) % count) for at in range(count)]
        mine.append(lax.ppermute(value, "gy", pairs))
    return mine


VMEM = pl.BlockSpec(memory_space=pltpu.VMEM)
SMEM = pl.BlockSpec(memory_space=pltpu.SMEM)
HBM = pl.BlockSpec(memory_space=pltpu.HBM)
PARAMS = pltpu.CompilerParams(vmem_limit_bytes=48 * 1024 * 1024)


def on_device(
    phi_init,
    source,
    tile_mat,
    tile_pos,
    neighbours,
    sigma_table,
    temp_init,
    slab_mat,
    k0_table,
    beta_table,
):
    f32 = jnp.float32
    width_gy = lax.axis_size("gy")
    chips = width_gy // 2
    tiles = width_gy * TILES
    size_x, width = temp_init.shape
    wide = width + 2 * PAD
    edge_rows = width // LANES * SUB

    def rows(count):
        return jax.ShapeDtypeStruct((count, LANES), f32)

    body, sigma, up, down = pl.pallas_call(
        prep_kernel,
        out_shape=(
            rows(2 * TE * ROW),
            rows(TE * ROW),
            rows(LOW_ROWS + edge_rows),
            rows(HIGH_ROWS + edge_rows),
        ),
        in_specs=[SMEM] + [HBM] * 5,
        out_specs=(VMEM,) * 4,
        scratch_shapes=[
            pltpu.VMEM((TE * ROW, LANES), f32),
            pltpu.VMEM((TE * ROW, LANES), jnp.int32),
            pltpu.VMEM((2, SUB, width), f32),
            pltpu.VMEM((2, SUB, width), jnp.int32),
            pltpu.SemaphoreType.DMA((7,)),
        ],
        compiler_params=PARAMS,
        name="prep",
    )(sigma_table, to_rows(phi_init), to_rows(source), to_rows(tile_mat), temp_init, slab_mat)
    bodies = everyone(body, chips)
    low, high = shifted(up, "gx", 1), shifted(down, "gx", -1)

    edge = jax.ShapeDtypeStruct((2, SLABX, PAD), f32)
    halo, edge_low, edge_high = pl.pallas_call(
        relay_kernel,
        out_shape=(rows(LOW_ROWS + HIGH_ROWS), edge, edge),
        in_specs=[VMEM] * 4,
        out_specs=(VMEM,) * 3,
        compiler_params=PARAMS,
        name="relay",
    )(low, high, temp_init, slab_mat)
    halos = everyone(halo, chips)
    ylow, yhigh = shifted(edge_high, "gy", 1), shifted(edge_low, "gy", -1)
    sigmas = everyone_direct(sigma, chips)

    ext = jax.ShapeDtypeStruct((SLABX, wide + LANES), f32)
    t_ext, k0_ext, b_ext = pl.pallas_call(
        slab_kernel,
        out_shape=(ext, ext, ext),
        in_specs=[SMEM, SMEM] + [VMEM] * 6,
        out_specs=(VMEM, VMEM, VMEM),
        compiler_params=PARAMS,
        name="slab_prep",
    )(k0_table, beta_table, temp_init, slab_mat, ylow, yhigh, low, high)

    def planes(count):
        return pltpu.VMEM(((tiles + 1) * count, SUB, LANES), f32)

    pot, slope = pl.pallas_call(
        functools.partial(sweep_kernel, chips),
        out_shape=(rows(TE * ROW), rows(8 * SLABX * SUB)),
        in_specs=[SMEM] + [VMEM] * (2 * width_gy),
        out_specs=(VMEM,) * 2,
        scratch_shapes=[
            pltpu.SMEM((3, 2 * (2 * width_gy + 2)), jnp.int32),
            pltpu.SMEM((3, tiles), jnp.int32),
            planes(TE), planes(TE), planes(LOW[0]), planes(LOW[0]), planes(HIGH[0]), planes(HIGH[0]),
            planes(TE), planes(LOW[1]), planes(HIGH[1]),
        ],
        compiler_params=PARAMS,
        name="sweeps",
    )(tile_pos, *bodies, *halos)

    temp, *sends = pl.pallas_call(
        functools.partial(slab_steps_kernel, chips),
        out_shape=(jax.ShapeDtypeStruct((size_x, width), f32),) + (rows(TE * ROW),) * width_gy,
        in_specs=[SMEM] + [VMEM] * (2 * width_gy + 4),
        out_specs=(VMEM,) * (1 + width_gy),
        scratch_shapes=[
            pltpu.VMEM((8 * SLABX * SUB, LANES), f32),
            pltpu.VMEM((SLABX, wide), f32),
            pltpu.VMEM((SLABX, wide + LANES), f32),
            pltpu.VMEM((4 * TE * SUB, LANES), f32),
        ],
        compiler_params=PARAMS,
        name="slab_steps",
    )(tile_pos, *sigmas, *halos, slope, t_ext, k0_ext, b_ext)
    tile_temps = sends[0]
    for by in range(1, width_gy):
        tile_temps = tile_temps + shifted(sends[by], "gy", by, True)
    return from_rows(pot), temp, from_rows(tile_temps)


def solution(mesh):
    placed = (
        P(("gx", "gy"), None),
        P(("gx", "gy"), None),
        P(("gx", "gy"), None),
        P(),
        P(("gx", "gy"), None),
        P(),
        P("gx", "gy"),
        P("gx", "gy"),
        P(),
        P(),
    )
    return jax.shard_map(
        on_device,
        mesh=mesh,
        in_specs=placed,
        out_specs=(P(("gx", "gy"), None), P("gx", "gy"), P(("gx", "gy"), None)),
        check_vma=False,
    )
```

```python
import functools
import math

import jax
import jax.numpy as jnp
from jax import lax
from jax.experimental import pallas as pl
from jax.experimental.pallas import tpu as pltpu
from jax.sharding import PartitionSpec as P

TE = 32
SWEEPS = 4
CSWEEPS = 3
NZ = 64
EPS = 2.0
DT = 0.15
LANES = 128
SUB = 8
TILES = 2
ROW = SUB * TILES

LOW = (SWEEPS + 2, SWEEPS + 1, 2)
HIGH = (SWEEPS + 3, SWEEPS + 2, 2)
LOW_ROWS = sum(LOW) * ROW
HIGH_ROWS = sum(HIGH) * ROW
SLABX = TE + SUB
HALO = CSWEEPS
HALF = TE
YBLOCKS = HALF + 2 * HALO
ROW0 = SUB
SLAB_ROWS = ROW0 + YBLOCKS * SLABX + SUB


def cheb_weight(step, count):
    return 1.0 / (1.0 + 0.75 * math.cos(math.pi * (2 * step + 1) / (2 * count)))


def lookup(table, ids):
    out = jnp.full(ids.shape, table[3], jnp.float32)
    for which in (2, 1, 0):
        out = jnp.where(ids == which, table[which], out)
    return out


def roll(value, by, axis):
    return pltpu.roll(value, by % value.shape[axis], axis)


def prep_kernel(table, phi, src, mat, temp, slab, body, sigma, up, down, src_v, mat_v, ends_t, ends_m, sems):
    rows = TE * ROW
    size_x, width = temp.shape
    moves = [(phi, body.at[0:rows]), (src, src_v), (mat, mat_v)]
    for which, first in enumerate((0, size_x - SUB)):
        moves.append((temp.at[first : first + SUB], ends_t.at[which]))
        moves.append((slab.at[first : first + SUB], ends_m.at[which]))
    moves = [pltpu.make_async_copy(*move, sems.at[at]) for at, move in enumerate(moves)]
    for move in moves:
        move.start()
    for move in moves:
        move.wait()
    sigma[...] = lookup(table, mat_v[...])
    body[rows : 2 * rows] = src_v[...] / sigma[...]
    at_up, at_down = 0, 0
    for ref, first in ((body, 0), (body, rows), (sigma, 0)):
        which = (first // rows) if ref is body else 2
        size = LOW[which] * ROW
        up[at_up : at_up + size] = ref[first + rows - size : first + rows]
        at_up += size
        size = HIGH[which] * ROW
        down[at_down : at_down + size] = ref[first : first + size]
        at_down += size
    sub = lax.broadcasted_iota(jnp.int32, (SUB, LANES), 0)
    for at in range(width // LANES):
        lanes = slice(at * LANES, (at + 1) * LANES)
        t_low, m_low = ends_t[0, :, lanes], ends_m[0, :, lanes].astype(jnp.float32)
        t_high, m_high = ends_t[1, :, lanes], ends_m[1, :, lanes].astype(jnp.float32)
        first = at * SUB
        up[LOW_ROWS + first : LOW_ROWS + first + SUB] = jnp.where(sub < 4, roll(t_high, HALO, 0), roll(m_high, -1, 0))
        down[HIGH_ROWS + first : HIGH_ROWS + first + SUB] = jnp.where(sub < 4, t_low, roll(m_low, 4, 0))


def relay_kernel(low, high, halo):
    halo[0:LOW_ROWS] = low[0:LOW_ROWS]
    halo[LOW_ROWS : LOW_ROWS + HIGH_ROWS] = high[0:HIGH_ROWS]


def loose(pos):
    return jnp.minimum(pos[0, 0], 0)


def slab_kernel(pos, k0_table, beta_table, temp, mat, low, high, t_ext, k0_ext, b_ext, edge_low, edge_high, native_t, native_m):
    start = loose(pos)
    blocks = temp.shape[1] // LANES
    half = lax.broadcasted_iota(jnp.int32, (SUB, LANES), 1) < NZ
    for which, (own, native) in enumerate(((temp, native_t), (mat, native_m))):
        for at in range(blocks):
            lanes = slice(at * LANES, (at + 1) * LANES)
            first = at * SLABX
            side = LOW_ROWS + at * SUB
            value = low[side : side + SUB, :]
            native[first : first + SUB, :] = roll(value, -4, 0) if which else value
            for g in range(TE // SUB):
                value = own[g * SUB : (g + 1) * SUB, lanes].astype(jnp.float32)
                native[pl.ds(start + first + HALO + g * SUB, SUB), :] = value
            side = HIGH_ROWS + at * SUB
            value = high[side : side + SUB, :]
            native[pl.ds(start + first + HALO + TE, SUB), :] = roll(value, -4, 0) if which else value
    for at in range(blocks // 2):
        for g in range(SLABX // SUB):
            halves = []
            for native in (native_t, native_m):
                lower = native[at * SLABX + g * SUB : at * SLABX + (g + 1) * SUB, :]
                upper_at = (blocks // 2 + at) * SLABX + g * SUB
                upper = native[upper_at : upper_at + SUB, :]
                lower_r, upper_r = roll(lower, NZ, 1), roll(upper, NZ, 1)
                halves.append((lower, lower_r, upper, upper_r))
            for odd in range(2):
                y = 2 * at + odd
                temps, mats = (jnp.where(half, v[odd], v[3 - odd]) for v in halves)
                places = [(y + HALO, temps, mats)]
                if y >= HALF - HALO:
                    places.append((y - HALF + HALO, halves[0][1 - odd], halves[1][1 - odd]))
                if y < HALO:
                    places.append((y + HALF + HALO, halves[0][2 + odd], halves[1][2 + odd]))
                for block, t, m in places:
                    rows = slice(ROW0 + block * SLABX + g * SUB, ROW0 + block * SLABX + (g + 1) * SUB)
                    t_ext[rows] = t
                    k0_ext[rows] = lookup(k0_table, m)
                    b_ext[rows] = lookup(beta_table, m)
                if y < HALO:
                    rows = slice(y * SLABX + g * SUB, y * SLABX + (g + 1) * SUB)
                    edge_low[rows] = jnp.where(half, halves[0][odd], halves[1][1 - odd])
                if y >= HALF - HALO:
                    first = (y - HALF + HALO) * SLABX + g * SUB
                    edge_high[first : first + SUB] = jnp.where(half, halves[0][2 + odd], halves[1][3 - odd])


def fill_maps(chips, pos, cell_at, cell_of):
    width_gy = 2 * chips
    tiles = width_gy * TILES
    i = lax.axis_index("gx")
    j = lax.axis_index("gy")
    rows_gx = lax.axis_size("gx")
    for at in range(2 * (2 * width_gy + 2)):
        for which in range(3):
            cell_at[which, at] = tiles
    for which, by in enumerate((0, -1, 1)):
        row = i + by
        valid = (row >= 0) & (row < rows_gx)
        first = jnp.clip(row, 0, rows_gx - 1) * tiles
        for part in range(width_gy):
            dev = part_device(part, chips, j)
            for t in range(TILES):
                tile = first + dev * TILES + t
                cell = (pos[tile, 1] + 1) * 2 + pos[tile, 2]
                slot = part * TILES + t
                cell_of[which, slot] = cell
                cell_at[which, cell] = jnp.where(valid, slot, tiles)


def part_device(part, chips, j):
    mate = j + 1 - 2 * lax.rem(j, 2)
    base = j if part < chips else mate
    return lax.rem(base - 2 * (part % chips) + 2 * chips, 2 * chips)


def sweep_kernel(chips, pos, *refs):
    width_gy = 2 * chips
    tiles = width_gy * TILES
    none = tiles
    bodies = refs[:width_gy]
    halos = refs[width_gy : 2 * width_gy]
    pot, slope, cell_at, cell_of, pa, pb, la, lb, ua, ub, s_c, s_l, s_u = refs[2 * width_gy :]
    i = lax.axis_index("gx")
    j = lax.axis_index("gy")
    rows_gx = lax.axis_size("gx")
    fill_maps(chips, pos, cell_at, cell_of)

    zero = jnp.zeros((SUB, LANES), jnp.float32)

    def plane_at(ref, at, shift=0):
        first = ROW0 + at * SUB
        return ref[pl.ds(pl.multiple_of(first, SUB) if shift == 0 else first + shift, SUB), :]

    def put_plane(ref, at, value):
        ref[pl.ds(pl.multiple_of(ROW0 + at * SUB, SUB), SUB), :] = value

    def unpack(source, start, t, target, first, count):
        def plane(p, carry):
            at = pl.multiple_of(p * ROW, ROW)
            value = source[pl.ds(start + at + t, SUB, stride=TILES), :]
            if len(target.shape) == 3:
                target[first + p] = value
            else:
                put_plane(target, first + p, value)
            return carry

        lax.fori_loop(0, count, plane, 0, unroll=min(count, 8))

    for part in range(width_gy):
        for t in range(TILES):
            slot = part * TILES + t
            for which, target in enumerate((pa, s_c)):
                unpack(bodies[part], which * TE * ROW, t, target, slot * TE, TE)
            at = 0
            for which, target in enumerate((la, s_l)):
                unpack(halos[part], at, t, target, slot * LOW[which], LOW[which])
                at += LOW[which] * ROW
            at = LOW_ROWS
            for which, target in enumerate((ua, s_u)):
                unpack(halos[part], at, t, target, slot * HIGH[which], HIGH[which])
                at += HIGH[which] * ROW
    for ref, count in ((pa, TE), (pb, TE), (la, LOW[0]), (lb, LOW[0]), (ua, HIGH[0]), (ub, HIGH[0])):
        for p in range(count):
            put_plane(ref, none * count + p, zero)

    lane = lax.broadcasted_iota(jnp.int32, (SUB, LANES), 1)
    sub = lax.broadcasted_iota(jnp.int32, (SUB, LANES), 0)
    depth = lane % TE
    first_y, last_y = lane < TE, lane >= LANES - TE
    first_sub, last_sub = sub == 0, sub == SUB - 1
    first_z, last_z = depth == 0, depth == TE - 1

    def y_plus(ref, own, at, ghost_at):
        turned = jnp.where(last_sub, plane_at(ref, ghost_at, 1 - SUB), plane_at(ref, at, 1))
        return roll(jnp.where(first_y, turned, own), -TE, 1)

    def y_minus(ref, own, at, ghost_at):
        turned = jnp.where(first_sub, plane_at(ref, ghost_at, SUB - 1), plane_at(ref, at, -1))
        return roll(jnp.where(last_y, turned, own), TE, 1)

    def around(which, slot):
        cell = cell_of[which, slot]
        upper = cell % 2
        y_m = cell_at[which, cell - 2]
        y_p = cell_at[which, cell + 2]
        z = cell_at[which, cell + 1 - 2 * upper]
        turn = jnp.where(upper == 1, LANES + 1 - TE, TE - 1)
        meets = jnp.where(upper == 1, 0, TE - 1) == depth
        return cell, (slot, y_m, y_p, z, turn, meets)

    bufs = ((pa, la, ua), (pb, lb, ub))
    for k in range(SWEEPS):
        weight = cheb_weight(k, SWEEPS)
        keep, gain = 1.0 - weight, weight / (6.0 + EPS)
        (c_src, l_src, u_src), (c_dst, l_dst, u_dst) = bufs[k % 2], bufs[(k + 1) % 2]

        def relax(field, size, slots, p, x_m, x_p, s):
            slot, y_m, y_p, z, turn, meets = slots
            at = slot * size + p
            own = plane_at(field, at)
            total = (x_m + x_p) + s
            total = total + y_minus(field, own, at, y_m * size + p)
            total = total + y_plus(field, own, at, y_p * size + p)
            total = total + jnp.where(last_z, 0.0, roll(own, -1, 1))
            total = total + jnp.where(first_z, 0.0, roll(own, 1, 1))
            total = total + jnp.where(meets, pltpu.roll(plane_at(field, z * size + p), turn, 1), 0.0)
            return keep * own + gain * total

        def sweep_tile(slot, carry):
            cell, slots = around(0, slot)
            below, above = cell_at[1, cell], cell_at[2, cell]
            for p in range(TE):
                x_m = plane_at(c_src, slot * TE + p - 1) if p > 0 else plane_at(l_src, below * LOW[0] + LOW[0] - 1)
                x_p = plane_at(c_src, slot * TE + p + 1) if p < TE - 1 else plane_at(u_src, above * HIGH[0])
                put_plane(c_dst, slot * TE + p, relax(c_src, TE, slots, p, x_m, x_p, s_c[slot * TE + p]))
            cell, slots = around(1, slot)
            centre = cell_at[0, cell]
            for p in range(k + 1, LOW[0]):
                x_m = plane_at(l_src, slot * LOW[0] + p - 1)
                x_p = plane_at(l_src, slot * LOW[0] + p + 1) if p < LOW[0] - 1 else plane_at(c_src, centre * TE)
                s = s_l[slot * LOW[1] + p - (LOW[0] - LOW[1])]
                put_plane(l_dst, slot * LOW[0] + p, relax(l_src, LOW[0], slots, p, x_m, x_p, s))
            cell, slots = around(2, slot)
            centre = cell_at[0, cell]
            for p in range(HIGH[0] - 1 - k):
                x_m = plane_at(u_src, slot * HIGH[0] + p - 1) if p > 0 else plane_at(c_src, centre * TE + TE - 1)
                x_p = plane_at(u_src, slot * HIGH[0] + p + 1)
                s = s_u[slot * HIGH[1] + p]
                put_plane(u_dst, slot * HIGH[0] + p, relax(u_src, HIGH[0], slots, p, x_m, x_p, s))
            return carry

        lax.fori_loop(0, tiles, sweep_tile, 0)

    field, f_l, f_u = bufs[SWEEPS % 2]
    for t in range(TILES):
        for p in range(TE):
            pot[pl.ds(p * ROW + t, SUB, stride=TILES), :] = plane_at(field, t * TE + p)

    def clear(at, carry):
        slope[pl.ds(pl.multiple_of(at * SUB, SUB), SUB), :] = zero
        return carry

    lax.fori_loop(0, slope.shape[0] // SUB, clear, 0, unroll=8)

    def squares(ref, size, slots, p, x_p):
        slot, _, y_p, z, turn, meets = slots
        at = slot * size + p
        own = plane_at(ref, at)
        d_x = x_p - own
        d_y = y_plus(ref, own, at, y_p * size + p) - own
        ghost = jnp.where(meets, pltpu.roll(plane_at(ref, z * size + p), turn, 1), 0.0)
        d_z = jnp.where(last_z, ghost, roll(own, -1, 1)) - own
        return d_x * d_x + d_y * d_y + d_z * d_z

    def put(local, x, value):
        slope[pl.ds(pl.multiple_of((local * SLABX + x) * SUB, SUB), SUB), :] = value

    def slope_tile(slot, carry):
        for which in range(3):
            cell, slots = around(which, slot)
            local, inside = window(which, cell, i, j, rows_gx)

            @pl.when(inside)
            def _():
                if which == 0:
                    above = cell_at[2, cell]
                    for p in range(TE):
                        x_p = plane_at(field, slot * TE + p + 1) if p < TE - 1 else plane_at(f_u, above * HIGH[0])
                        put(local, HALO + p, squares(field, TE, slots, p, x_p))
                elif which == 1:
                    centre = cell_at[0, cell]
                    for p in range(2):
                        q = LOW[0] - 2 + p
                        x_p = plane_at(f_l, slot * LOW[0] + q + 1) if p < 1 else plane_at(field, centre * TE)
                        put(local, HALO - 2 + p, squares(f_l, LOW[0], slots, q, x_p))
                else:
                    for p in range(2):
                        x_p = plane_at(f_u, slot * HIGH[0] + p + 1)
                        put(local, HALO + TE + p, squares(f_u, HIGH[0], slots, p, x_p))

        return carry

    lax.fori_loop(0, tiles, slope_tile, 0)


def window(which, cell, i, j, rows_gx):
    local = cell - 4 * j
    inside = (local >= 0) & (local < 8)
    if which > 0:
        row = i - 1 if which == 1 else i + 1
        inside = inside & (row >= 0) & (row < rows_gx)
    return local, inside


def slab_steps_kernel(chips, pos, k0_table, beta_table, *refs):
    width_gy = 2 * chips
    tiles = width_gy * TILES
    sigmas = refs[:width_gy]
    halos = refs[width_gy : 2 * width_gy]
    slope, t_in, k0_in, b_in, ylow, yhigh, temp_out = refs[2 * width_gy : 2 * width_gy + 7]
    sends = refs[2 * width_gy + 7 : 3 * width_gy + 7]
    heat, q_ext, temp_a, temp_b, cond_a, cond_b, k0_edge, b_edge, blocks = refs[3 * width_gy + 7 :]
    i = lax.axis_index("gx")
    j = lax.axis_index("gy")
    rows_gx = lax.axis_size("gx")
    lane = lax.broadcasted_iota(jnp.int32, (SUB, LANES), 1)
    zero = jnp.zeros((SUB, LANES), jnp.float32)

    def clear(at, carry):
        heat[pl.ds(pl.multiple_of(at * SUB, SUB), SUB), :] = zero
        return carry

    lax.fori_loop(0, heat.shape[0] // SUB, clear, 0, unroll=8)
    low_at, high_at = (LOW[0] + LOW[1]) * ROW, LOW_ROWS + (HIGH[0] + HIGH[1]) * ROW
    for part in range(width_gy):
        dev = part_device(part, chips, j)
        for t in range(TILES):
            for which, by in enumerate((0, -1, 1)):
                tile = jnp.clip(i + by, 0, rows_gx - 1) * tiles + dev * TILES + t
                cell = (pos[tile, 1] + 1) * 2 + pos[tile, 2]
                local, inside = window(which, cell, i, j, rows_gx)
                source, start, x, count = (
                    (sigmas[part], 0, HALO, TE),
                    (halos[part], low_at, HALO - 2, 2),
                    (halos[part], high_at, HALO + TE, 2),
                )[which]

                @pl.when(inside)
                def _():
                    for p in range(count):
                        rows = pl.ds(pl.multiple_of((local * SLABX + x + p) * SUB, SUB), SUB)
                        sigma = source[pl.ds(start + p * ROW + t, SUB, stride=TILES), :]
                        heat[rows, :] = sigma * slope[rows, :]

    quarter = [(lane >= q * TE) & (lane < (q + 1) * TE) for q in range(3)]

    def pick(parts):
        return jnp.where(
            quarter[0], parts[0], jnp.where(quarter[1], parts[1], jnp.where(quarter[2], parts[2], parts[3]))
        )

    def turned(value, by):
        return value if by % 4 == 0 else roll(value, by * TE, 1)

    def rows_of(block, g):
        first = ROW0 + block * SLABX + g * SUB
        return slice(first, first + SUB)

    groups = SLABX // SUB
    for first in range(-1, HALF // 4 + 1):
        col, yq = first * 4 // TE + 1, first * 4 % TE // 4
        for g in range(groups):
            cells = [
                heat[pl.ds(((2 * col + c) * SLABX + g * SUB) * SUB + yq, SUB, stride=SUB), :] for c in range(4)
            ]
            for r in range(4):
                block = 4 * first + r + HALO
                if 0 < block < YBLOCKS - 1:
                    q_ext[rows_of(block, g)] = pick([turned(cells[c], c - r) for c in range(4)])

    start = loose(pos)
    sub = lax.broadcasted_iota(jnp.int32, (SUB, LANES), 0)
    half = lane < NZ
    no_z = lane % NZ == NZ - 1
    low_x = (sub == HALO - 1) & (i == 0), (sub == HALO) & (i == 0)
    high_x = (sub == (HALO + TE - 1) % SUB) & (i == rows_gx - 1)
    low_y, high_y = half & (j == 0), (lane >= NZ) & (j == width_gy - 1)

    def beside(ref, block, g, by):
        return ref[pl.ds(start + (ROW0 + block * SLABX + g * SUB + by), SUB), :]

    edges = {}
    for e in range(HALO):
        edges[e] = (ylow, e)
        edges[YBLOCKS - HALO + e] = (yhigh, e)
    for block in range(YBLOCKS):
        for g in range(groups):
            rows = rows_of(block, g)
            temp, k0, beta = t_in[rows], k0_in[rows], b_in[rows]
            if block in edges:
                edge, e = edges[block]
                value = edge[e * SLABX + g * SUB : e * SLABX + (g + 1) * SUB]
                swapped = roll(value, NZ, 1)
                if edge is ylow:
                    temp = jnp.where(half, value, temp)
                    k0 = jnp.where(half, lookup(k0_table, swapped), k0)
                    beta = jnp.where(half, lookup(beta_table, swapped), beta)
                else:
                    temp = jnp.where(half, temp, swapped)
                    k0 = jnp.where(half, k0, lookup(k0_table, value))
                    beta = jnp.where(half, beta, lookup(beta_table, value))
                k0_edge[rows_of(list(edges).index(block), g)] = k0
                b_edge[rows_of(list(edges).index(block), g)] = beta
            temp_a[rows] = temp
            cond_a[rows] = k0 / (1.0 + beta * temp * temp)

    for step in range(CSWEEPS):
        (t_src, c_src), (t_dst, c_dst) = ((temp_a, cond_a), (temp_b, cond_b))[:: 1 if step % 2 == 0 else -1]
        for g in range(groups):
            now = t_src[rows_of(step, g)], c_src[rows_of(step, g)]
            ahead = t_src[rows_of(step + 1, g)], c_src[rows_of(step + 1, g)]
            flux_y = (now[1] + ahead[1]) * (ahead[0] - now[0])
            if step == HALO - 1:
                flux_y = jnp.where(low_y, 0.0, flux_y)
            for block in range(step + 1, YBLOCKS - 1 - step):
                (temp, cond), before = ahead, flux_y
                ahead = t_src[rows_of(block + 1, g)], c_src[rows_of(block + 1, g)]
                flux_y = (cond + ahead[1]) * (ahead[0] - temp)
                if block == HALO - 1:
                    flux_y = jnp.where(low_y, 0.0, flux_y)
                if block == HALO + HALF - 1:
                    flux_y = jnp.where(high_y, 0.0, flux_y)
                flux_p = (cond + beside(c_src, block, g, 1)) * (beside(t_src, block, g, 1) - temp)
                flux_m = (cond + beside(c_src, block, g, -1)) * (beside(t_src, block, g, -1) - temp)
                if g == 0:
                    flux_p = jnp.where(low_x[0], 0.0, flux_p)
                    flux_m = jnp.where(low_x[1], 0.0, flux_m)
                if g == groups - 1:
                    flux_p = jnp.where(high_x, 0.0, flux_p)
                flux_z = (cond + roll(cond, -1, 1)) * (roll(temp, -1, 1) - temp)
                flux_z = jnp.where(no_z, 0.0, flux_z)
                div = (flux_y - before) + (flux_p + flux_m) + (flux_z - roll(flux_z, 1, 1))
                rows = rows_of(block, g)
                new = temp + DT * (0.5 * div + q_ext[rows])
                t_dst[rows] = new
                if step < CSWEEPS - 1:
                    if block in edges:
                        at = list(edges).index(block)
                        k0, beta = k0_edge[rows_of(at, g)], b_edge[rows_of(at, g)]
                    else:
                        k0, beta = k0_in[rows], b_in[rows]
                    c_dst[rows] = k0 / (1.0 + beta * new * new)
    final = temp_b if CSWEEPS % 2 else temp_a

    for yq in range(HALF // 4):
        for g in range(TE // SUB):
            x = slice(g * SUB, (g + 1) * SUB)
            turns = []
            for r in range(4):
                value = beside(final, HALO + 4 * yq + r, g, HALO)
                turns.append([turned(value, by) for by in range(4)])
            for pair in range(2):
                even, odd = turns[2 * pair], turns[2 * pair + 1]
                lower = (2 * yq + pair) * LANES
                upper = lower + temp_out.shape[1] // 2
                temp_out[x, lower : lower + LANES] = jnp.where(half, even[0], odd[2])
                temp_out[x, upper : upper + LANES] = jnp.where(half, even[2], odd[0])
            for c in range(4):
                value = pick([turns[r][(r - c) % 4] for r in range(4)])
                blocks[pl.ds((c * TE + g * SUB) * SUB + yq, SUB, stride=SUB), :] = value
    for shift in range(width_gy):
        dev = lax.rem(j + shift, width_gy)
        for t in range(TILES):
            tile = i * tiles + dev * TILES + t
            col = pos[tile, 1] - 2 * j
            cell = jnp.clip(col, 0, 1) * 2 + pos[tile, 2]
            here = (col >= 0) & (col < 2)
            for p in range(TE):
                value = blocks[pl.ds(pl.multiple_of((cell * TE + p) * SUB, SUB), SUB), :]
                sends[shift][pl.ds(p * ROW + t, SUB, stride=TILES), :] = jnp.where(here, value, 0.0)


def shifted(value, axis, by, wrap=False):
    count = lax.axis_size(axis)
    pairs = [(d, (d + by) % count) for d in range(count) if wrap or 0 <= d + by < count]
    return lax.ppermute(value, axis, pairs)


def from_mate(value):
    return lax.ppermute(value, "gy", [(d, d ^ 1) for d in range(lax.axis_size("gy"))])


def to_rows(value):
    return value.reshape(TILES, -1, LANES).transpose(1, 0, 2).reshape(-1, LANES)


def from_rows(value):
    return value.reshape(-1, TILES, LANES).transpose(1, 0, 2).reshape(TILES, -1)


def everyone(value, chips):
    mine = [value] + [shifted(value, "gy", 2 * d, True) for d in range(1, chips)]
    return mine + [from_mate(part) for part in mine]


def everyone_direct(value, chips):
    mine = [value] + [shifted(value, "gy", 2 * d, True) for d in range(1, chips)]
    count = 2 * chips
    for d in range(chips):
        pairs = [(at, ((at ^ 1) + 2 * d) % count) for at in range(count)]
        mine.append(lax.ppermute(value, "gy", pairs))
    return mine


VMEM = pl.BlockSpec(memory_space=pltpu.VMEM)
SMEM = pl.BlockSpec(memory_space=pltpu.SMEM)
HBM = pl.BlockSpec(memory_space=pltpu.HBM)
PARAMS = pltpu.CompilerParams(vmem_limit_bytes=48 * 1024 * 1024)


def on_device(
    phi_init,
    source,
    tile_mat,
    tile_pos,
    neighbours,
    sigma_table,
    temp_init,
    slab_mat,
    k0_table,
    beta_table,
):
    f32 = jnp.float32
    width_gy = lax.axis_size("gy")
    chips = width_gy // 2
    tiles = width_gy * TILES
    size_x, width = temp_init.shape
    edge_rows = width // LANES * SUB

    def rows(count):
        return jax.ShapeDtypeStruct((count, LANES), f32)

    body, sigma, up, down = pl.pallas_call(
        prep_kernel,
        out_shape=(
            rows(2 * TE * ROW),
            rows(TE * ROW),
            rows(LOW_ROWS + edge_rows),
            rows(HIGH_ROWS + edge_rows),
        ),
        in_specs=[SMEM] + [HBM] * 5,
        out_specs=(VMEM,) * 4,
        scratch_shapes=[
            pltpu.VMEM((TE * ROW, LANES), f32),
            pltpu.VMEM((TE * ROW, LANES), jnp.int32),
            pltpu.VMEM((2, SUB, width), f32),
            pltpu.VMEM((2, SUB, width), jnp.int32),
            pltpu.SemaphoreType.DMA((7,)),
        ],
        compiler_params=pltpu.CompilerParams(vmem_limit_bytes=62 * 1024 * 1024),
        name="prep",
    )(sigma_table, to_rows(phi_init), to_rows(source), to_rows(tile_mat), temp_init, slab_mat)
    bodies = everyone(body, chips)
    low, high = shifted(up, "gx", 1), shifted(down, "gx", -1)

    halo = pl.pallas_call(
        relay_kernel,
        out_shape=rows(LOW_ROWS + HIGH_ROWS),
        in_specs=[VMEM] * 2,
        out_specs=VMEM,
        compiler_params=PARAMS,
        name="relay",
    )(low, high)
    halos = everyone(halo, chips)
    sigmas = everyone_direct(sigma, chips)

    native = pltpu.VMEM((width // LANES * SLABX + SUB, LANES), f32)
    t_ext, k0_ext, b_ext, edge_low, edge_high = pl.pallas_call(
        slab_kernel,
        out_shape=(rows(SLAB_ROWS),) * 3 + (rows(HALO * SLABX),) * 2,
        in_specs=[SMEM] * 3 + [VMEM] * 4,
        out_specs=(VMEM,) * 5,
        scratch_shapes=[native, native],
        compiler_params=PARAMS,
        name="slab_prep",
    )(tile_pos, k0_table, beta_table, temp_init, slab_mat, low, high)
    ylow, yhigh = shifted(edge_high, "gy", 1), shifted(edge_low, "gy", -1)

    def planes(count):
        return pltpu.VMEM(((tiles + 1) * count, SUB, LANES), f32)

    def fields(count):
        return pltpu.VMEM((2 * ROW0 + (tiles + 1) * count * SUB, LANES), f32)

    pot, slope = pl.pallas_call(
        functools.partial(sweep_kernel, chips),
        out_shape=(rows(TE * ROW), rows(8 * SLABX * SUB)),
        in_specs=[SMEM] + [VMEM] * (2 * width_gy),
        out_specs=(VMEM,) * 2,
        scratch_shapes=[
            pltpu.SMEM((3, 2 * (2 * width_gy + 2)), jnp.int32),
            pltpu.SMEM((3, tiles), jnp.int32),
            fields(TE), fields(TE), fields(LOW[0]), fields(LOW[0]), fields(HIGH[0]), fields(HIGH[0]),
            planes(TE), planes(LOW[1]), planes(HIGH[1]),
        ],
        compiler_params=PARAMS,
        name="sweeps",
    )(tile_pos, *bodies, *halos)

    temp, *sends = pl.pallas_call(
        functools.partial(slab_steps_kernel, chips),
        out_shape=(jax.ShapeDtypeStruct((size_x, width), f32),) + (rows(TE * ROW),) * width_gy,
        in_specs=[SMEM] * 3 + [VMEM] * (2 * width_gy + 6),
        out_specs=(VMEM,) * (1 + width_gy),
        scratch_shapes=[pltpu.VMEM((8 * SLABX * SUB, LANES), f32)]
        + [pltpu.VMEM((SLAB_ROWS, LANES), f32)] * 5
        + [pltpu.VMEM((ROW0 + 2 * HALO * SLABX, LANES), f32)] * 2
        + [pltpu.VMEM((4 * TE * SUB, LANES), f32)],
        compiler_params=PARAMS,
        name="slab_steps",
    )(tile_pos, k0_table, beta_table, *sigmas, *halos, slope, t_ext, k0_ext, b_ext, ylow, yhigh)
    tile_temps = sends[0]
    for by in range(1, width_gy):
        tile_temps = tile_temps + shifted(sends[by], "gy", by, True)
    return from_rows(pot), temp, from_rows(tile_temps)


def solution(mesh):
    placed = (
        P(("gx", "gy"), None),
        P(("gx", "gy"), None),
        P(("gx", "gy"), None),
        P(),
        P(("gx", "gy"), None),
        P(),
        P("gx", "gy"),
        P("gx", "gy"),
        P(),
        P(),
    )
    return jax.shard_map(
        on_device,
        mesh=mesh,
        in_specs=placed,
        out_specs=(P(("gx", "gy"), None), P("gx", "gy"), P(("gx", "gy"), None)),
        check_vma=False,
    )
```

```python
import functools
import math

import jax
import jax.numpy as jnp
from jax import lax
from jax.experimental import pallas as pl
from jax.experimental.pallas import tpu as pltpu
from jax.sharding import PartitionSpec as P

TE = 32
SWEEPS = 4
CSWEEPS = 3
NZ = 64
EPS = 2.0
DT = 0.15
LANES = 128
SUB = 8
TILES = 2
ROW = SUB * TILES

LOW = (SWEEPS + 2, SWEEPS + 1, 2)
HIGH = (SWEEPS + 3, SWEEPS + 2, 2)
LOW_ROWS = sum(LOW) * ROW
HIGH_ROWS = sum(HIGH) * ROW
SLABX = TE + SUB
HALO = CSWEEPS
HALF = TE
YBLOCKS = HALF + 2 * HALO
BATCH = 8
ROW0 = SUB
SLAB_ROWS = ROW0 + YBLOCKS * SLABX + SUB


def cheb_weight(step, count):
    return 1.0 / (1.0 + 0.75 * math.cos(math.pi * (2 * step + 1) / (2 * count)))


def lookup(table, ids):
    out = jnp.full(ids.shape, table[3], jnp.float32)
    for which in (2, 1, 0):
        out = jnp.where(ids == which, table[which], out)
    return out


def roll(value, by, axis):
    return pltpu.roll(value, by % value.shape[axis], axis)


def prep_kernel(table, phi, src, mat, temp, slab, body, sigma, up, down, up_t, down_t, src_v, mat_v, ends_t, ends_m, sems):
    rows = TE * ROW
    size_x, width = temp.shape
    moves = [(phi, body.at[0:rows]), (src, src_v), (mat, mat_v)]
    for which, first in enumerate((0, size_x - SUB)):
        moves.append((temp.at[first : first + SUB], ends_t.at[which]))
        moves.append((slab.at[first : first + SUB], ends_m.at[which]))
    moves = [pltpu.make_async_copy(*move, sems.at[at]) for at, move in enumerate(moves)]
    for move in moves:
        move.start()
    for move in moves:
        move.wait()
    sigma[...] = lookup(table, mat_v[...])
    body[rows : 2 * rows] = src_v[...] / sigma[...]
    at_up, at_down = 0, 0
    for ref, first in ((body, 0), (body, rows), (sigma, 0)):
        which = (first // rows) if ref is body else 2
        size = LOW[which] * ROW
        up[at_up : at_up + size] = ref[first + rows - size : first + rows]
        at_up += size
        size = HIGH[which] * ROW
        down[at_down : at_down + size] = ref[first : first + size]
        at_down += size
    sub = lax.broadcasted_iota(jnp.int32, (SUB, LANES), 0)
    for at in range(width // LANES):
        lanes = slice(at * LANES, (at + 1) * LANES)
        t_low, m_low = ends_t[0, :, lanes], ends_m[0, :, lanes].astype(jnp.float32)
        t_high, m_high = ends_t[1, :, lanes], ends_m[1, :, lanes].astype(jnp.float32)
        first = at * SUB
        up_t[first : first + SUB] = jnp.where(sub < 4, roll(t_high, HALO, 0), roll(m_high, -1, 0))
        down_t[first : first + SUB] = jnp.where(sub < 4, t_low, roll(m_low, 4, 0))


def relay_kernel(low, high, halo):
    halo[0:LOW_ROWS] = low[...]
    halo[LOW_ROWS:] = high[...]


def loose(pos):
    return jnp.minimum(pos[0, 0], 0)


def slab_kernel(pos, k0_table, beta_table, temp, mat, low, high, t_ext, k0_ext, b_ext, edge_low, edge_high, native_t, native_m):
    start = loose(pos)
    blocks = temp.shape[1] // LANES
    half = lax.broadcasted_iota(jnp.int32, (SUB, LANES), 1) < NZ
    for which, (own, native) in enumerate(((temp, native_t), (mat, native_m))):
        for at in range(blocks):
            lanes = slice(at * LANES, (at + 1) * LANES)
            first = at * SLABX
            side = at * SUB
            value = low[side : side + SUB, :]
            native[first : first + SUB, :] = roll(value, -4, 0) if which else value
            for g in range(TE // SUB):
                value = own[g * SUB : (g + 1) * SUB, lanes].astype(jnp.float32)
                native[pl.ds(start + first + HALO + g * SUB, SUB), :] = value
            side = at * SUB
            value = high[side : side + SUB, :]
            native[pl.ds(start + first + HALO + TE, SUB), :] = roll(value, -4, 0) if which else value
    for at in range(blocks // 2):
        for g in range(SLABX // SUB):
            halves = []
            for native in (native_t, native_m):
                lower = native[at * SLABX + g * SUB : at * SLABX + (g + 1) * SUB, :]
                upper_at = (blocks // 2 + at) * SLABX + g * SUB
                upper = native[upper_at : upper_at + SUB, :]
                lower_r, upper_r = roll(lower, NZ, 1), roll(upper, NZ, 1)
                halves.append((lower, lower_r, upper, upper_r))
            for odd in range(2):
                y = 2 * at + odd
                temps, mats = (jnp.where(half, v[odd], v[3 - odd]) for v in halves)
                places = [(y + HALO, temps, mats)]
                if y >= HALF - HALO:
                    places.append((y - HALF + HALO, halves[0][1 - odd], halves[1][1 - odd]))
                if y < HALO:
                    places.append((y + HALF + HALO, halves[0][2 + odd], halves[1][2 + odd]))
                for block, t, m in places:
                    rows = slice(ROW0 + block * SLABX + g * SUB, ROW0 + block * SLABX + (g + 1) * SUB)
                    t_ext[rows] = t
                    k0_ext[rows] = lookup(k0_table, m)
                    b_ext[rows] = lookup(beta_table, m)
                if y < HALO:
                    rows = slice(y * SLABX + g * SUB, y * SLABX + (g + 1) * SUB)
                    edge_low[rows] = jnp.where(half, halves[0][odd], halves[1][1 - odd])
                if y >= HALF - HALO:
                    first = (y - HALF + HALO) * SLABX + g * SUB
                    edge_high[first : first + SUB] = jnp.where(half, halves[0][2 + odd], halves[1][3 - odd])


def fill_maps(chips, pos, cell_at, cell_of):
    width_gy = 2 * chips
    tiles = width_gy * TILES
    i = lax.axis_index("gx")
    j = lax.axis_index("gy")
    rows_gx = lax.axis_size("gx")
    for at in range(2 * (2 * width_gy + 2)):
        for which in range(3):
            cell_at[which, at] = tiles
    for which, by in enumerate((0, -1, 1)):
        row = i + by
        valid = (row >= 0) & (row < rows_gx)
        first = jnp.clip(row, 0, rows_gx - 1) * tiles
        for part in range(width_gy):
            dev = part_device(part, chips, j)
            for t in range(TILES):
                tile = first + dev * TILES + t
                cell = (pos[tile, 1] + 1) * 2 + pos[tile, 2]
                slot = part * TILES + t
                cell_of[which, slot] = cell
                cell_at[which, cell] = jnp.where(valid, slot, tiles)


def part_device(part, chips, j):
    mate = j + 1 - 2 * lax.rem(j, 2)
    base = j if part < chips else mate
    return lax.rem(base - 2 * (part % chips) + 2 * chips, 2 * chips)


def sweep_kernel(chips, pos, *refs):
    width_gy = 2 * chips
    tiles = width_gy * TILES
    none = tiles
    bodies = refs[:width_gy]
    halos = refs[width_gy : 2 * width_gy]
    pot, slope, cell_at, cell_of, pa, pb, la, lb, ua, ub, s_c, s_l, s_u = refs[2 * width_gy :]
    i = lax.axis_index("gx")
    j = lax.axis_index("gy")
    rows_gx = lax.axis_size("gx")
    fill_maps(chips, pos, cell_at, cell_of)

    zero = jnp.zeros((SUB, LANES), jnp.float32)

    def plane_at(ref, at, shift=0):
        first = ROW0 + at * SUB
        return ref[pl.ds(pl.multiple_of(first, SUB) if shift == 0 else first + shift, SUB), :]

    def put_plane(ref, at, value):
        ref[pl.ds(pl.multiple_of(ROW0 + at * SUB, SUB), SUB), :] = value

    def unpack(source, start, t, target, first, count):
        def plane(p, carry):
            at = pl.multiple_of(p * ROW, ROW)
            value = source[pl.ds(start + at + t, SUB, stride=TILES), :]
            if len(target.shape) == 3:
                target[first + p] = value
            else:
                put_plane(target, first + p, value)
            return carry

        lax.fori_loop(0, count, plane, 0, unroll=min(count, 8))

    for part in range(width_gy):
        for t in range(TILES):
            slot = part * TILES + t
            for which, target in enumerate((pa, s_c)):
                unpack(bodies[part], which * TE * ROW, t, target, slot * TE, TE)
            at = 0
            for which, target in enumerate((la, s_l)):
                unpack(halos[part], at, t, target, slot * LOW[which], LOW[which])
                at += LOW[which] * ROW
            at = LOW_ROWS
            for which, target in enumerate((ua, s_u)):
                unpack(halos[part], at, t, target, slot * HIGH[which], HIGH[which])
                at += HIGH[which] * ROW
    for ref, count in ((pa, TE), (pb, TE), (la, LOW[0]), (lb, LOW[0]), (ua, HIGH[0]), (ub, HIGH[0])):
        for p in range(count):
            put_plane(ref, none * count + p, zero)

    lane = lax.broadcasted_iota(jnp.int32, (SUB, LANES), 1)
    sub = lax.broadcasted_iota(jnp.int32, (SUB, LANES), 0)
    depth = lane % TE
    first_y, last_y = lane < TE, lane >= LANES - TE
    first_sub, last_sub = sub == 0, sub == SUB - 1
    first_z, last_z = depth == 0, depth == TE - 1

    def y_plus(ref, own, at, ghost_at):
        turned = jnp.where(last_sub, plane_at(ref, ghost_at, 1 - SUB), plane_at(ref, at, 1))
        return roll(jnp.where(first_y, turned, own), -TE, 1)

    def y_minus(ref, own, at, ghost_at):
        turned = jnp.where(first_sub, plane_at(ref, ghost_at, SUB - 1), plane_at(ref, at, -1))
        return roll(jnp.where(last_y, turned, own), TE, 1)

    def around(which, slot):
        cell = cell_of[which, slot]
        upper = cell % 2
        y_m = cell_at[which, cell - 2]
        y_p = cell_at[which, cell + 2]
        z = cell_at[which, cell + 1 - 2 * upper]
        turn = jnp.where(upper == 1, LANES + 1 - TE, TE - 1)
        meets = jnp.where(upper == 1, 0, TE - 1) == depth
        return cell, (slot, y_m, y_p, z, turn, meets)

    bufs = ((pa, la, ua), (pb, lb, ub))
    for k in range(SWEEPS):
        weight = cheb_weight(k, SWEEPS)
        keep, gain = 1.0 - weight, weight / (6.0 + EPS)
        (c_src, l_src, u_src), (c_dst, l_dst, u_dst) = bufs[k % 2], bufs[(k + 1) % 2]

        def relax(field, size, slots, p, x_m, x_p, s):
            slot, y_m, y_p, z, turn, meets = slots
            at = slot * size + p
            own = plane_at(field, at)
            total = (x_m + x_p) + s
            total = total + y_minus(field, own, at, y_m * size + p)
            total = total + y_plus(field, own, at, y_p * size + p)
            total = total + jnp.where(last_z, 0.0, roll(own, -1, 1))
            total = total + jnp.where(first_z, 0.0, roll(own, 1, 1))
            total = total + jnp.where(meets, pltpu.roll(plane_at(field, z * size + p), turn, 1), 0.0)
            return keep * own + gain * total

        def sweep_tile(slot, carry):
            cell, slots = around(0, slot)
            below, above = cell_at[1, cell], cell_at[2, cell]
            for first in range(0, TE, BATCH):
                results = []
                for p in range(first, first + BATCH):
                    x_m = plane_at(c_src, slot * TE + p - 1) if p > 0 else plane_at(l_src, below * LOW[0] + LOW[0] - 1)
                    x_p = plane_at(c_src, slot * TE + p + 1) if p < TE - 1 else plane_at(u_src, above * HIGH[0])
                    results.append(relax(c_src, TE, slots, p, x_m, x_p, s_c[slot * TE + p]))
                for p in range(first, first + BATCH):
                    put_plane(c_dst, slot * TE + p, results[p - first])
            cell, slots = around(1, slot)
            centre = cell_at[0, cell]
            results = []
            for p in range(k + 1, LOW[0]):
                x_m = plane_at(l_src, slot * LOW[0] + p - 1)
                x_p = plane_at(l_src, slot * LOW[0] + p + 1) if p < LOW[0] - 1 else plane_at(c_src, centre * TE)
                s = s_l[slot * LOW[1] + p - (LOW[0] - LOW[1])]
                results.append(relax(l_src, LOW[0], slots, p, x_m, x_p, s))
            for p in range(k + 1, LOW[0]):
                put_plane(l_dst, slot * LOW[0] + p, results[p - k - 1])
            cell, slots = around(2, slot)
            centre = cell_at[0, cell]
            results = []
            for p in range(HIGH[0] - 1 - k):
                x_m = plane_at(u_src, slot * HIGH[0] + p - 1) if p > 0 else plane_at(c_src, centre * TE + TE - 1)
                x_p = plane_at(u_src, slot * HIGH[0] + p + 1)
                results.append(relax(u_src, HIGH[0], slots, p, x_m, x_p, s_u[slot * HIGH[1] + p]))
            for p in range(HIGH[0] - 1 - k):
                put_plane(u_dst, slot * HIGH[0] + p, results[p])
            return carry

        lax.fori_loop(0, tiles, sweep_tile, 0)

    field, f_l, f_u = bufs[SWEEPS % 2]
    for t in range(TILES):
        for p in range(TE):
            pot[pl.ds(p * ROW + t, SUB, stride=TILES), :] = plane_at(field, t * TE + p)

    def clear(at, carry):
        slope[pl.ds(pl.multiple_of(at * SUB, SUB), SUB), :] = zero
        return carry

    lax.fori_loop(0, slope.shape[0] // SUB, clear, 0, unroll=8)

    def squares(ref, size, slots, p, x_p):
        slot, _, y_p, z, turn, meets = slots
        at = slot * size + p
        own = plane_at(ref, at)
        d_x = x_p - own
        d_y = y_plus(ref, own, at, y_p * size + p) - own
        ghost = jnp.where(meets, pltpu.roll(plane_at(ref, z * size + p), turn, 1), 0.0)
        d_z = jnp.where(last_z, ghost, roll(own, -1, 1)) - own
        return d_x * d_x + d_y * d_y + d_z * d_z

    def put(local, x, value):
        slope[pl.ds(pl.multiple_of((local * SLABX + x) * SUB, SUB), SUB), :] = value

    def slope_tile(slot, carry):
        for which in range(3):
            cell, slots = around(which, slot)
            local, inside = window(which, cell, i, j, rows_gx)

            @pl.when(inside)
            def _():
                if which == 0:
                    above = cell_at[2, cell]
                    for p in range(TE):
                        x_p = plane_at(field, slot * TE + p + 1) if p < TE - 1 else plane_at(f_u, above * HIGH[0])
                        put(local, HALO + p, squares(field, TE, slots, p, x_p))
                elif which == 1:
                    centre = cell_at[0, cell]
                    for p in range(2):
                        q = LOW[0] - 2 + p
                        x_p = plane_at(f_l, slot * LOW[0] + q + 1) if p < 1 else plane_at(field, centre * TE)
                        put(local, HALO - 2 + p, squares(f_l, LOW[0], slots, q, x_p))
                else:
                    for p in range(2):
                        x_p = plane_at(f_u, slot * HIGH[0] + p + 1)
                        put(local, HALO + TE + p, squares(f_u, HIGH[0], slots, p, x_p))

        return carry

    lax.fori_loop(0, tiles, slope_tile, 0)


def window(which, cell, i, j, rows_gx):
    local = cell - 4 * j
    inside = (local >= 0) & (local < 8)
    if which > 0:
        row = i - 1 if which == 1 else i + 1
        inside = inside & (row >= 0) & (row < rows_gx)
    return local, inside


def slab_steps_kernel(chips, pos, k0_table, beta_table, *refs):
    width_gy = 2 * chips
    tiles = width_gy * TILES
    sigmas = refs[:width_gy]
    halos = refs[width_gy : 2 * width_gy]
    slope, t_in, k0_in, b_in, ylow, yhigh, temp_out = refs[2 * width_gy : 2 * width_gy + 7]
    sends = refs[2 * width_gy + 7 : 3 * width_gy + 7]
    heat, q_ext, temp_a, temp_b, cond_a, cond_b, k0_edge, b_edge, blocks = refs[3 * width_gy + 7 :]
    i = lax.axis_index("gx")
    j = lax.axis_index("gy")
    rows_gx = lax.axis_size("gx")
    lane = lax.broadcasted_iota(jnp.int32, (SUB, LANES), 1)
    zero = jnp.zeros((SUB, LANES), jnp.float32)

    def clear(at, carry):
        heat[pl.ds(pl.multiple_of(at * SUB, SUB), SUB), :] = zero
        return carry

    lax.fori_loop(0, heat.shape[0] // SUB, clear, 0, unroll=8)
    low_at, high_at = (LOW[0] + LOW[1]) * ROW, LOW_ROWS + (HIGH[0] + HIGH[1]) * ROW
    for part in range(width_gy):
        dev = part_device(part, chips, j)
        for t in range(TILES):
            for which, by in enumerate((0, -1, 1)):
                tile = jnp.clip(i + by, 0, rows_gx - 1) * tiles + dev * TILES + t
                cell = (pos[tile, 1] + 1) * 2 + pos[tile, 2]
                local, inside = window(which, cell, i, j, rows_gx)
                source, start, x, count = (
                    (sigmas[part], 0, HALO, TE),
                    (halos[part], low_at, HALO - 2, 2),
                    (halos[part], high_at, HALO + TE, 2),
                )[which]

                @pl.when(inside)
                def _():
                    for p in range(count):
                        rows = pl.ds(pl.multiple_of((local * SLABX + x + p) * SUB, SUB), SUB)
                        sigma = source[pl.ds(start + p * ROW + t, SUB, stride=TILES), :]
                        heat[rows, :] = sigma * slope[rows, :]

    quarter = [(lane >= q * TE) & (lane < (q + 1) * TE) for q in range(3)]

    def pick(parts):
        return jnp.where(
            quarter[0], parts[0], jnp.where(quarter[1], parts[1], jnp.where(quarter[2], parts[2], parts[3]))
        )

    def turned(value, by):
        return value if by % 4 == 0 else roll(value, by * TE, 1)

    def rows_of(block, g):
        first = ROW0 + block * SLABX + g * SUB
        return slice(first, first + SUB)

    groups = SLABX // SUB
    for first in range(-1, HALF // 4 + 1):
        col, yq = first * 4 // TE + 1, first * 4 % TE // 4
        for g in range(groups):
            cells = [
                heat[pl.ds(((2 * col + c) * SLABX + g * SUB) * SUB + yq, SUB, stride=SUB), :] for c in range(4)
            ]
            for r in range(4):
                block = 4 * first + r + HALO
                if 0 < block < YBLOCKS - 1:
                    q_ext[rows_of(block, g)] = pick([turned(cells[c], c - r) for c in range(4)])

    sub = lax.broadcasted_iota(jnp.int32, (SUB, LANES), 0)
    half = lane < NZ
    no_z = lane % NZ == NZ - 1
    low_x = (sub == HALO - 1) & (i == 0)
    high_x = (sub == (HALO + TE - 1) % SUB) & (i == rows_gx - 1)
    low_y, high_y = half & (j == 0), (lane >= NZ) & (j == width_gy - 1)

    first_sub, last_sub = sub == 0, sub == SUB - 1

    def inverse(value):
        near = pl.reciprocal(value, approx=True)
        near = near * (2.0 - value * near)
        return near * (2.0 - value * near)

    def load(ref, block):
        return [ref[rows_of(block, g)] for g in range(groups)]

    def next_x(values):
        up = [roll(v, -1, 0) for v in values]
        return [jnp.where(last_sub, up[min(g + 1, groups - 1)], up[g]) for g in range(groups)]

    def last_x(values):
        down = [roll(v, 1, 0) for v in values]
        return [jnp.where(first_sub, down[max(g - 1, 0)], down[g]) for g in range(groups)]

    edges = {}
    for e in range(HALO):
        edges[e] = (ylow, e)
        edges[YBLOCKS - HALO + e] = (yhigh, e)
    for block in range(YBLOCKS):
        for g in range(groups):
            rows = rows_of(block, g)
            temp, k0, beta = t_in[rows], k0_in[rows], b_in[rows]
            if block in edges:
                edge, e = edges[block]
                value = edge[e * SLABX + g * SUB : e * SLABX + (g + 1) * SUB]
                swapped = roll(value, NZ, 1)
                if edge is ylow:
                    temp = jnp.where(half, value, temp)
                    k0 = jnp.where(half, lookup(k0_table, swapped), k0)
                    beta = jnp.where(half, lookup(beta_table, swapped), beta)
                else:
                    temp = jnp.where(half, temp, swapped)
                    k0 = jnp.where(half, k0, lookup(k0_table, value))
                    beta = jnp.where(half, beta, lookup(beta_table, value))
                k0_edge[rows_of(list(edges).index(block), g)] = k0
                b_edge[rows_of(list(edges).index(block), g)] = beta
            temp_a[rows] = temp
            cond_a[rows] = k0 * inverse(1.0 + beta * temp * temp)

    for step in range(CSWEEPS):
        (t_src, c_src), (t_dst, c_dst) = ((temp_a, cond_a), (temp_b, cond_b))[:: 1 if step % 2 == 0 else -1]
        ahead, flux_y = None, None
        for block in range(step, YBLOCKS - 1 - step):
            temp, cond = ahead or (load(t_src, block), load(c_src, block))
            ahead = load(t_src, block + 1), load(c_src, block + 1)
            before = flux_y
            flux_y = [(cond[g] + ahead[1][g]) * (ahead[0][g] - temp[g]) for g in range(groups)]
            if block == HALO - 1:
                flux_y = [jnp.where(low_y, 0.0, f) for f in flux_y]
            if block == HALO + HALF - 1:
                flux_y = [jnp.where(high_y, 0.0, f) for f in flux_y]
            if before is None:
                continue
            temp_x, cond_x = next_x(temp), next_x(cond)
            flux_x = [(cond[g] + cond_x[g]) * (temp_x[g] - temp[g]) for g in range(groups)]
            flux_x[0] = jnp.where(low_x, 0.0, flux_x[0])
            flux_x[-1] = jnp.where(high_x, 0.0, flux_x[-1])
            back_x = last_x(flux_x)
            results = []
            for g in range(groups):
                flux_z = (cond[g] + roll(cond[g], -1, 1)) * (roll(temp[g], -1, 1) - temp[g])
                flux_z = jnp.where(no_z, 0.0, flux_z)
                div = (flux_y[g] - before[g]) + (flux_x[g] - back_x[g]) + (flux_z - roll(flux_z, 1, 1))
                rows = rows_of(block, g)
                new = temp[g] + DT * (0.5 * div + q_ext[rows])
                if step < CSWEEPS - 1:
                    if block in edges:
                        at = list(edges).index(block)
                        k0, beta = k0_edge[rows_of(at, g)], b_edge[rows_of(at, g)]
                    else:
                        k0, beta = k0_in[rows], b_in[rows]
                    results.append((new, k0 * inverse(1.0 + beta * new * new)))
                else:
                    results.append((new, None))
            for g in range(groups):
                t_dst[rows_of(block, g)] = results[g][0]
                if step < CSWEEPS - 1:
                    c_dst[rows_of(block, g)] = results[g][1]
    final = temp_b if CSWEEPS % 2 else temp_a

    for yq in range(HALF // 4):
        for g in range(TE // SUB):
            x = slice(g * SUB, (g + 1) * SUB)
            turns = []
            for r in range(4):
                here, after = (final[rows_of(HALO + 4 * yq + r, at)] for at in (g, g + 1))
                value = jnp.where(sub < SUB - HALO, roll(here, -HALO, 0), roll(after, -HALO, 0))
                turns.append([turned(value, by) for by in range(4)])
            for pair in range(2):
                even, odd = turns[2 * pair], turns[2 * pair + 1]
                lower = (2 * yq + pair) * LANES
                upper = lower + temp_out.shape[1] // 2
                temp_out[x, lower : lower + LANES] = jnp.where(half, even[0], odd[2])
                temp_out[x, upper : upper + LANES] = jnp.where(half, even[2], odd[0])
            for c in range(4):
                value = pick([turns[r][(r - c) % 4] for r in range(4)])
                blocks[pl.ds((c * TE + g * SUB) * SUB + yq, SUB, stride=SUB), :] = value
    for shift in range(width_gy):
        dev = lax.rem(j + shift, width_gy)
        for t in range(TILES):
            tile = i * tiles + dev * TILES + t
            col = pos[tile, 1] - 2 * j
            cell = jnp.clip(col, 0, 1) * 2 + pos[tile, 2]
            here = (col >= 0) & (col < 2)
            for p in range(TE):
                value = blocks[pl.ds(pl.multiple_of((cell * TE + p) * SUB, SUB), SUB), :]
                sends[shift][pl.ds(p * ROW + t, SUB, stride=TILES), :] = jnp.where(here, value, 0.0)


def shifted(value, axis, by, wrap=False):
    count = lax.axis_size(axis)
    pairs = [(d, (d + by) % count) for d in range(count) if wrap or 0 <= d + by < count]
    return lax.ppermute(value, axis, pairs)


def from_mate(value):
    return lax.ppermute(value, "gy", [(d, d ^ 1) for d in range(lax.axis_size("gy"))])


def to_rows(value):
    return value.reshape(TILES, -1, LANES).transpose(1, 0, 2).reshape(-1, LANES)


def from_rows(value):
    return value.reshape(-1, TILES, LANES).transpose(1, 0, 2).reshape(TILES, -1)


def everyone(value, chips):
    mine = [value] + [shifted(value, "gy", 2 * d, True) for d in range(1, chips)]
    return mine + [from_mate(part) for part in mine]


def everyone_direct(value, chips):
    mine = [value] + [shifted(value, "gy", 2 * d, True) for d in range(1, chips)]
    count = 2 * chips
    for d in range(chips):
        pairs = [(at, ((at ^ 1) + 2 * d) % count) for at in range(count)]
        mine.append(lax.ppermute(value, "gy", pairs))
    return mine


VMEM = pl.BlockSpec(memory_space=pltpu.VMEM)
SMEM = pl.BlockSpec(memory_space=pltpu.SMEM)
HBM = pl.BlockSpec(memory_space=pltpu.HBM)
PARAMS = pltpu.CompilerParams(vmem_limit_bytes=32 * 1024 * 1024)


def on_device(
    phi_init,
    source,
    tile_mat,
    tile_pos,
    neighbours,
    sigma_table,
    temp_init,
    slab_mat,
    k0_table,
    beta_table,
):
    f32 = jnp.float32
    width_gy = lax.axis_size("gy")
    chips = width_gy // 2
    tiles = width_gy * TILES
    size_x, width = temp_init.shape
    edge_rows = width // LANES * SUB

    def rows(count):
        return jax.ShapeDtypeStruct((count, LANES), f32)

    body, sigma, up, down, up_t, down_t = pl.pallas_call(
        prep_kernel,
        out_shape=(
            rows(2 * TE * ROW),
            rows(TE * ROW),
            rows(LOW_ROWS),
            rows(HIGH_ROWS),
            rows(edge_rows),
            rows(edge_rows),
        ),
        in_specs=[SMEM] + [HBM] * 5,
        out_specs=(VMEM,) * 6,
        scratch_shapes=[
            pltpu.VMEM((TE * ROW, LANES), f32),
            pltpu.VMEM((TE * ROW, LANES), jnp.int32),
            pltpu.VMEM((2, SUB, width), f32),
            pltpu.VMEM((2, SUB, width), jnp.int32),
            pltpu.SemaphoreType.DMA((7,)),
        ],
        compiler_params=pltpu.CompilerParams(vmem_limit_bytes=62 * 1024 * 1024),
        name="prep",
    )(sigma_table, to_rows(phi_init), to_rows(source), to_rows(tile_mat), temp_init, slab_mat)
    bodies = everyone(body, chips)
    low, high = shifted(up, "gx", 1), shifted(down, "gx", -1)
    low_t, high_t = shifted(up_t, "gx", 1), shifted(down_t, "gx", -1)

    halo = pl.pallas_call(
        relay_kernel,
        out_shape=rows(LOW_ROWS + HIGH_ROWS),
        in_specs=[VMEM] * 2,
        out_specs=VMEM,
        compiler_params=PARAMS,
        name="relay",
    )(low, high)
    halos = [halo] + [shifted(halo, "gy", 2 * d, True) for d in range(1, chips)]
    sigmas = everyone_direct(sigma, chips)

    native = pltpu.VMEM((width // LANES * SLABX + SUB, LANES), f32)
    t_ext, k0_ext, b_ext, edge_low, edge_high = pl.pallas_call(
        slab_kernel,
        out_shape=(rows(SLAB_ROWS),) * 3 + (rows(HALO * SLABX),) * 2,
        in_specs=[SMEM] * 3 + [VMEM] * 4,
        out_specs=(VMEM,) * 5,
        scratch_shapes=[native, native],
        compiler_params=PARAMS,
        name="slab_prep",
    )(tile_pos, k0_table, beta_table, temp_init, slab_mat, low_t, high_t)
    *halos[1:], edge_low, edge_high = lax.optimization_barrier((*halos[1:], edge_low, edge_high))
    halos = halos + [from_mate(part) for part in halos]
    ylow, yhigh = shifted(edge_high, "gy", 1), shifted(edge_low, "gy", -1)

    def planes(count):
        return pltpu.VMEM(((tiles + 1) * count, SUB, LANES), f32)

    def fields(count):
        return pltpu.VMEM((2 * ROW0 + (tiles + 1) * count * SUB, LANES), f32)

    pot, slope = pl.pallas_call(
        functools.partial(sweep_kernel, chips),
        out_shape=(rows(TE * ROW), rows(8 * SLABX * SUB)),
        in_specs=[SMEM] + [VMEM] * (2 * width_gy),
        out_specs=(VMEM,) * 2,
        scratch_shapes=[
            pltpu.SMEM((3, 2 * (2 * width_gy + 2)), jnp.int32),
            pltpu.SMEM((3, tiles), jnp.int32),
            fields(TE), fields(TE), fields(LOW[0]), fields(LOW[0]), fields(HIGH[0]), fields(HIGH[0]),
            planes(TE), planes(LOW[1]), planes(HIGH[1]),
        ],
        compiler_params=PARAMS,
        name="sweeps",
    )(tile_pos, *bodies, *halos)

    temp, *sends = pl.pallas_call(
        functools.partial(slab_steps_kernel, chips),
        out_shape=(jax.ShapeDtypeStruct((size_x, width), f32),) + (rows(TE * ROW),) * width_gy,
        in_specs=[SMEM] * 3 + [VMEM] * (2 * width_gy + 6),
        out_specs=(VMEM,) * (1 + width_gy),
        scratch_shapes=[pltpu.VMEM((8 * SLABX * SUB, LANES), f32)]
        + [pltpu.VMEM((SLAB_ROWS, LANES), f32)] * 5
        + [pltpu.VMEM((ROW0 + 2 * HALO * SLABX, LANES), f32)] * 2
        + [pltpu.VMEM((4 * TE * SUB, LANES), f32)],
        compiler_params=PARAMS,
        name="slab_steps",
    )(tile_pos, k0_table, beta_table, *sigmas, *halos, slope, t_ext, k0_ext, b_ext, ylow, yhigh)
    tile_temps = sends[0]
    for by in range(1, width_gy):
        tile_temps = tile_temps + shifted(sends[by], "gy", by, True)
    return from_rows(pot), temp, from_rows(tile_temps)


def solution(mesh):
    placed = (
        P(("gx", "gy"), None),
        P(("gx", "gy"), None),
        P(("gx", "gy"), None),
        P(),
        P(("gx", "gy"), None),
        P(),
        P("gx", "gy"),
        P("gx", "gy"),
        P(),
        P(),
    )
    return jax.shard_map(
        on_device,
        mesh=mesh,
        in_specs=placed,
        out_specs=(P(("gx", "gy"), None), P("gx", "gy"), P(("gx", "gy"), None)),
        check_vma=False,
    )
```

```python
import functools
import math

import jax
import jax.numpy as jnp
from jax import lax
from jax.experimental import pallas as pl
from jax.experimental.pallas import tpu as pltpu
from jax.sharding import PartitionSpec as P

TE = 32
SWEEPS = 4
CSWEEPS = 3
NZ = 64
EPS = 2.0
DT = 0.15
LANES = 128
SUB = 8
TILES = 2
ROW = SUB * TILES

LOW = (SWEEPS + 2, SWEEPS + 1, 2)
HIGH = (SWEEPS + 3, SWEEPS + 2, 2)
LOW_ROWS = sum(LOW) * ROW
HIGH_ROWS = sum(HIGH) * ROW
SLABX = TE + SUB
HALO = CSWEEPS
HALF = TE
YBLOCKS = HALF + 2 * HALO
BATCH = 8
C_SIZE, L_SIZE, U_SIZE = TE + 2, LOW[0] + 1, HIGH[0] + 1
ROW0 = SUB
SLAB_ROWS = ROW0 + YBLOCKS * SLABX + SUB


def cheb_weight(step, count):
    return 1.0 / (1.0 + 0.75 * math.cos(math.pi * (2 * step + 1) / (2 * count)))


def lookup(table, ids):
    out = jnp.full(ids.shape, table[3], jnp.float32)
    for which in (2, 1, 0):
        out = jnp.where(ids == which, table[which], out)
    return out


def roll(value, by, axis):
    return pltpu.roll(value, by % value.shape[axis], axis)


def prep_kernel(table, phi, src, mat, temp, slab, body, sigma, up, down, src_v, mat_v, ends_t, ends_m, sems):
    rows = TE * ROW
    size_x, width = temp.shape
    moves = [(phi, body.at[0:rows]), (src, src_v), (mat, mat_v)]
    for which, first in enumerate((0, size_x - SUB)):
        moves.append((temp.at[first : first + SUB], ends_t.at[which]))
        moves.append((slab.at[first : first + SUB], ends_m.at[which]))
    moves = [pltpu.make_async_copy(*move, sems.at[at]) for at, move in enumerate(moves)]
    for move in moves:
        move.start()
    for move in moves:
        move.wait()
    sigma[...] = lookup(table, mat_v[...])
    body[rows : 2 * rows] = src_v[...] / sigma[...]
    at_up, at_down = 0, 0
    for ref, first in ((body, 0), (body, rows), (sigma, 0)):
        which = (first // rows) if ref is body else 2
        size = LOW[which] * ROW
        up[at_up : at_up + size] = ref[first + rows - size : first + rows]
        at_up += size
        size = HIGH[which] * ROW
        down[at_down : at_down + size] = ref[first : first + size]
        at_down += size
    sub = lax.broadcasted_iota(jnp.int32, (SUB, LANES), 0)
    for at in range(width // LANES):
        lanes = slice(at * LANES, (at + 1) * LANES)
        t_low, m_low = ends_t[0, :, lanes], ends_m[0, :, lanes].astype(jnp.float32)
        t_high, m_high = ends_t[1, :, lanes], ends_m[1, :, lanes].astype(jnp.float32)
        first = at * SUB
        up[LOW_ROWS + first : LOW_ROWS + first + SUB] = jnp.where(sub < 4, roll(t_high, HALO, 0), roll(m_high, -1, 0))
        down[HIGH_ROWS + first : HIGH_ROWS + first + SUB] = jnp.where(sub < 4, t_low, roll(m_low, 4, 0))


def relay_kernel(low, high, halo):
    halo[0:LOW_ROWS] = low[0:LOW_ROWS]
    halo[LOW_ROWS:] = high[0:HIGH_ROWS]


def loose(pos):
    return jnp.minimum(pos[0, 0], 0)


def slab_kernel(pos, k0_table, beta_table, temp, mat, low, high, t_ext, k0_ext, b_ext, edge_low, edge_high, native_t, native_m):
    start = loose(pos)
    blocks = temp.shape[1] // LANES
    half = lax.broadcasted_iota(jnp.int32, (SUB, LANES), 1) < NZ
    for which, (own, native) in enumerate(((temp, native_t), (mat, native_m))):
        for at in range(blocks):
            lanes = slice(at * LANES, (at + 1) * LANES)
            first = at * SLABX
            side = LOW_ROWS + at * SUB
            value = low[side : side + SUB, :]
            native[first : first + SUB, :] = roll(value, -4, 0) if which else value
            for g in range(TE // SUB):
                value = own[g * SUB : (g + 1) * SUB, lanes].astype(jnp.float32)
                native[pl.ds(start + first + HALO + g * SUB, SUB), :] = value
            side = HIGH_ROWS + at * SUB
            value = high[side : side + SUB, :]
            native[pl.ds(start + first + HALO + TE, SUB), :] = roll(value, -4, 0) if which else value
    for at in range(blocks // 2):
        for g in range(SLABX // SUB):
            halves = []
            for native in (native_t, native_m):
                lower = native[at * SLABX + g * SUB : at * SLABX + (g + 1) * SUB, :]
                upper_at = (blocks // 2 + at) * SLABX + g * SUB
                upper = native[upper_at : upper_at + SUB, :]
                lower_r, upper_r = roll(lower, NZ, 1), roll(upper, NZ, 1)
                halves.append((lower, lower_r, upper, upper_r))
            for odd in range(2):
                y = 2 * at + odd
                temps, mats = (jnp.where(half, v[odd], v[3 - odd]) for v in halves)
                places = [(y + HALO, temps, mats)]
                if y >= HALF - HALO:
                    places.append((y - HALF + HALO, halves[0][1 - odd], halves[1][1 - odd]))
                if y < HALO:
                    places.append((y + HALF + HALO, halves[0][2 + odd], halves[1][2 + odd]))
                for block, t, m in places:
                    rows = slice(ROW0 + block * SLABX + g * SUB, ROW0 + block * SLABX + (g + 1) * SUB)
                    t_ext[rows] = t
                    k0_ext[rows] = lookup(k0_table, m)
                    b_ext[rows] = lookup(beta_table, m)
                if y < HALO:
                    rows = slice(y * SLABX + g * SUB, y * SLABX + (g + 1) * SUB)
                    edge_low[rows] = jnp.where(half, halves[0][odd], halves[1][1 - odd])
                if y >= HALF - HALO:
                    first = (y - HALF + HALO) * SLABX + g * SUB
                    edge_high[first : first + SUB] = jnp.where(half, halves[0][2 + odd], halves[1][3 - odd])


def fill_maps(chips, pos, cell_at, cell_of):
    width_gy = 2 * chips
    tiles = width_gy * TILES
    i = lax.axis_index("gx")
    j = lax.axis_index("gy")
    rows_gx = lax.axis_size("gx")
    for at in range(2 * (2 * width_gy + 2)):
        for which in range(3):
            cell_at[which, at] = tiles
    for which, by in enumerate((0, -1, 1)):
        row = i + by
        valid = (row >= 0) & (row < rows_gx)
        first = jnp.clip(row, 0, rows_gx - 1) * tiles
        for part in range(width_gy):
            dev = part_device(part, chips, j)
            for t in range(TILES):
                tile = first + dev * TILES + t
                cell = (pos[tile, 1] + 1) * 2 + pos[tile, 2]
                slot = part * TILES + t
                cell_of[which, slot] = cell
                cell_at[which, cell] = jnp.where(valid, slot, tiles)


def part_device(part, chips, j):
    mate = j + 1 - 2 * lax.rem(j, 2)
    base = j if part < chips else mate
    return lax.rem(base - 2 * (part % chips) + 2 * chips, 2 * chips)


def sweep_kernel(chips, pos, *refs):
    width_gy = 2 * chips
    tiles = width_gy * TILES
    none = tiles
    bodies = refs[:width_gy]
    halos = refs[width_gy : 2 * width_gy]
    pot, slope, cell_at, cell_of, pa, pb, la, lb, ua, ub, s_c, s_l, s_u = refs[2 * width_gy :]
    i = lax.axis_index("gx")
    j = lax.axis_index("gy")
    rows_gx = lax.axis_size("gx")
    fill_maps(chips, pos, cell_at, cell_of)

    zero = jnp.zeros((SUB, LANES), jnp.float32)

    def plane_at(ref, at, shift=0):
        first = ROW0 + at * SUB
        return ref[pl.ds(pl.multiple_of(first, SUB) if shift == 0 else first + shift, SUB), :]

    def put_plane(ref, at, value):
        ref[pl.ds(pl.multiple_of(ROW0 + at * SUB, SUB), SUB), :] = value

    def unpack(source, start, t, target, first, count):
        def plane(p, carry):
            at = pl.multiple_of(p * ROW, ROW)
            value = source[pl.ds(start + at + t, SUB, stride=TILES), :]
            if len(target.shape) == 3:
                target[first + p] = value
            else:
                put_plane(target, first + p, value)
            return carry

        lax.fori_loop(0, count, plane, 0, unroll=min(count, 8))

    for part in range(width_gy):
        for t in range(TILES):
            slot = part * TILES + t
            unpack(bodies[part], 0, t, pa, slot * C_SIZE + 1, TE)
            unpack(bodies[part], TE * ROW, t, s_c, slot * TE, TE)
            unpack(halos[part], 0, t, la, slot * L_SIZE, LOW[0])
            unpack(halos[part], LOW[0] * ROW, t, s_l, slot * LOW[1], LOW[1])
            unpack(halos[part], LOW_ROWS, t, ua, slot * U_SIZE + 1, HIGH[0])
            unpack(halos[part], LOW_ROWS + HIGH[0] * ROW, t, s_u, slot * HIGH[1], HIGH[1])
    for ref, count in ((pa, C_SIZE), (pb, C_SIZE), (la, L_SIZE), (lb, L_SIZE), (ua, U_SIZE), (ub, U_SIZE)):
        for p in range(count):
            put_plane(ref, none * count + p, zero)

    lane = lax.broadcasted_iota(jnp.int32, (SUB, LANES), 1)
    sub = lax.broadcasted_iota(jnp.int32, (SUB, LANES), 0)
    depth = lane % TE
    first_y, last_y = lane < TE, lane >= LANES - TE
    first_sub, last_sub = sub == 0, sub == SUB - 1
    first_z, last_z = depth == 0, depth == TE - 1

    def y_plus(ref, own, at, ghost_at):
        turned = jnp.where(last_sub, plane_at(ref, ghost_at, 1 - SUB), plane_at(ref, at, 1))
        return roll(jnp.where(first_y, turned, own), -TE, 1)

    def y_minus(ref, own, at, ghost_at):
        turned = jnp.where(first_sub, plane_at(ref, ghost_at, SUB - 1), plane_at(ref, at, -1))
        return roll(jnp.where(last_y, turned, own), TE, 1)

    def around(which, slot):
        cell = cell_of[which, slot]
        upper = cell % 2
        y_m = cell_at[which, cell - 2]
        y_p = cell_at[which, cell + 2]
        z = cell_at[which, cell + 1 - 2 * upper]
        turn = jnp.where(upper == 1, LANES + 1 - TE, TE - 1)
        meets = jnp.where(upper == 1, 0, TE - 1) == depth
        return cell, (slot, y_m, y_p, z, turn, meets)

    bufs = ((pa, la, ua), (pb, lb, ub))
    for k in range(SWEEPS):
        weight = cheb_weight(k, SWEEPS)
        keep, gain = 1.0 - weight, weight / (6.0 + EPS)
        (c_src, l_src, u_src), (c_dst, l_dst, u_dst) = bufs[k % 2], bufs[(k + 1) % 2]

        def ghosts(slot, carry):
            cell = cell_of[0, slot]
            below, above = cell_at[1, cell], cell_at[2, cell]
            put_plane(c_src, slot * C_SIZE, plane_at(l_src, below * L_SIZE + LOW[0] - 1))
            put_plane(c_src, slot * C_SIZE + TE + 1, plane_at(u_src, above * U_SIZE + 1))
            put_plane(l_src, slot * L_SIZE + LOW[0], plane_at(c_src, cell_at[0, cell_of[1, slot]] * C_SIZE + 1))
            put_plane(u_src, slot * U_SIZE, plane_at(c_src, cell_at[0, cell_of[2, slot]] * C_SIZE + TE))
            return carry

        lax.fori_loop(0, tiles, ghosts, 0)

        def relax(src, dst, size, slots, first, count, s_ref, s_at):
            slot, y_m, y_p, z, turn, meets = slots
            results = []
            for p in range(count):
                at = slot * size + first + p
                own = plane_at(src, at)
                total = (plane_at(src, at - 1) + plane_at(src, at + 1)) + s_ref[s_at + p]
                total = total + y_minus(src, own, at, y_m * size + first + p)
                total = total + y_plus(src, own, at, y_p * size + first + p)
                total = total + jnp.where(last_z, 0.0, roll(own, -1, 1))
                total = total + jnp.where(first_z, 0.0, roll(own, 1, 1))
                ghost = pltpu.roll(plane_at(src, z * size + first + p), turn, 1)
                results.append(keep * own + gain * (total + jnp.where(meets, ghost, 0.0)))
            for p in range(count):
                put_plane(dst, slot * size + first + p, results[p])

        def sweep_tile(slot, carry):
            _, slots = around(0, slot)

            def group(at, carry):
                first = at * BATCH
                relax(c_src, c_dst, C_SIZE, slots, first + 1, BATCH, s_c, slot * TE + first)
                return carry

            lax.fori_loop(0, TE // BATCH, group, 0)
            _, slots = around(1, slot)
            count = LOW[0] - 1 - k
            relax(l_src, l_dst, L_SIZE, slots, LOW[0] - count, count, s_l, (slot + 1) * LOW[1] - count)
            _, slots = around(2, slot)
            relax(u_src, u_dst, U_SIZE, slots, 1, HIGH[0] - 1 - k, s_u, slot * HIGH[1])
            return carry

        lax.fori_loop(0, tiles, sweep_tile, 0)

    field, f_l, f_u = bufs[SWEEPS % 2]
    for t in range(TILES):
        for p in range(TE):
            pot[pl.ds(p * ROW + t, SUB, stride=TILES), :] = plane_at(field, t * C_SIZE + 1 + p)

    def clear(at, carry):
        slope[pl.ds(pl.multiple_of(at * SUB, SUB), SUB), :] = zero
        return carry

    lax.fori_loop(0, slope.shape[0] // SUB, clear, 0, unroll=8)

    def squares(ref, size, slots, p, x_p):
        slot, _, y_p, z, turn, meets = slots
        at = slot * size + p
        own = plane_at(ref, at)
        d_x = (plane_at(ref, at + 1) if x_p is None else x_p) - own
        d_y = y_plus(ref, own, at, y_p * size + p) - own
        ghost = jnp.where(meets, pltpu.roll(plane_at(ref, z * size + p), turn, 1), 0.0)
        d_z = jnp.where(last_z, ghost, roll(own, -1, 1)) - own
        return d_x * d_x + d_y * d_y + d_z * d_z

    def put(local, x, value):
        slope[pl.ds(pl.multiple_of((local * SLABX + x) * SUB, SUB), SUB), :] = value

    def slope_tile(slot, carry):
        for which in range(3):
            cell, slots = around(which, slot)
            local, inside = window(which, cell, i, j, rows_gx)

            @pl.when(inside)
            def _():
                if which == 0:
                    put_plane(field, slot * C_SIZE + TE + 1, plane_at(f_u, cell_at[2, cell] * U_SIZE + 1))

                    def group(at, carry):
                        first = at * BATCH
                        values = [squares(field, C_SIZE, slots, 1 + first + p, None) for p in range(BATCH)]
                        for p in range(BATCH):
                            put(local, HALO + first + p, values[p])
                        return carry

                    lax.fori_loop(0, TE // BATCH, group, 0)
                elif which == 1:
                    centre = plane_at(field, cell_at[0, cell] * C_SIZE + 1)
                    put(local, HALO - 2, squares(f_l, L_SIZE, slots, LOW[0] - 2, None))
                    put(local, HALO - 1, squares(f_l, L_SIZE, slots, LOW[0] - 1, centre))
                else:
                    for p in range(2):
                        put(local, HALO + TE + p, squares(f_u, U_SIZE, slots, 1 + p, None))

        return carry

    lax.fori_loop(0, tiles, slope_tile, 0)


def window(which, cell, i, j, rows_gx):
    local = cell - 4 * j
    inside = (local >= 0) & (local < 8)
    if which > 0:
        row = i - 1 if which == 1 else i + 1
        inside = inside & (row >= 0) & (row < rows_gx)
    return local, inside


def slab_steps_kernel(chips, pos, k0_table, beta_table, *refs):
    width_gy = 2 * chips
    tiles = width_gy * TILES
    sigmas = refs[:width_gy]
    halos = refs[width_gy : 2 * width_gy]
    slope, t_in, k0_in, b_in, ylow, yhigh, temp_out = refs[2 * width_gy : 2 * width_gy + 7]
    sends = refs[2 * width_gy + 7 : 3 * width_gy + 7]
    heat, q_ext, temp_a, temp_b, cond_a, cond_b, k0_all, b_all, blocks = refs[3 * width_gy + 7 :]
    i = lax.axis_index("gx")
    j = lax.axis_index("gy")
    rows_gx = lax.axis_size("gx")
    lane = lax.broadcasted_iota(jnp.int32, (SUB, LANES), 1)
    zero = jnp.zeros((SUB, LANES), jnp.float32)

    def clear(at, carry):
        heat[pl.ds(pl.multiple_of(at * SUB, SUB), SUB), :] = zero
        return carry

    lax.fori_loop(0, heat.shape[0] // SUB, clear, 0, unroll=8)
    low_at, high_at = (LOW[0] + LOW[1]) * ROW, LOW_ROWS + (HIGH[0] + HIGH[1]) * ROW
    for part in range(width_gy):
        dev = part_device(part, chips, j)
        for t in range(TILES):
            for which, by in enumerate((0, -1, 1)):
                tile = jnp.clip(i + by, 0, rows_gx - 1) * tiles + dev * TILES + t
                cell = (pos[tile, 1] + 1) * 2 + pos[tile, 2]
                local, inside = window(which, cell, i, j, rows_gx)
                source, start, x, count = (
                    (sigmas[part], 0, HALO, TE),
                    (halos[part], low_at, HALO - 2, 2),
                    (halos[part], high_at, HALO + TE, 2),
                )[which]

                @pl.when(inside)
                def _():
                    def plane(p, carry):
                        rows = pl.ds(pl.multiple_of((local * SLABX + x + p) * SUB, SUB), SUB)
                        at = pl.multiple_of(start + p * ROW, SUB)
                        sigma = source[pl.ds(at + t, SUB, stride=TILES), :]
                        heat[rows, :] = sigma * slope[rows, :]
                        return carry

                    lax.fori_loop(0, count, plane, 0, unroll=min(count, 8))

    quarter = [(lane >= q * TE) & (lane < (q + 1) * TE) for q in range(3)]

    def pick(parts):
        return jnp.where(
            quarter[0], parts[0], jnp.where(quarter[1], parts[1], jnp.where(quarter[2], parts[2], parts[3]))
        )

    def turned(value, by):
        return value if by % 4 == 0 else roll(value, by * TE, 1)

    def rows_of(block, g):
        first = ROW0 + block * SLABX + g * SUB
        if not isinstance(first, int):
            first = pl.multiple_of(first, SUB)
        return pl.ds(first, SUB)

    groups = SLABX // SUB

    def place_heat(at, carry):
        first = at - 1
        col, yq = lax.div(first * 4 + TE, TE), lax.rem(first * 4 + TE, TE) // 4
        for g in range(groups):
            cells = [
                heat[pl.ds(pl.multiple_of(((2 * col + c) * SLABX + g * SUB) * SUB, SUB) + yq, SUB, stride=SUB), :]
                for c in range(4)
            ]
            for r in range(4):
                block = 4 * first + r + HALO + 1
                q_ext[rows_of(block, g)] = pick([turned(cells[c], c - r) for c in range(4)])
        return carry

    lax.fori_loop(0, HALF // 4 + 2, place_heat, 0)

    sub = lax.broadcasted_iota(jnp.int32, (SUB, LANES), 0)
    half = lane < NZ
    no_z = lane % NZ == NZ - 1
    low_x = (sub == HALO - 1) & (i == 0)
    high_x = (sub == (HALO + TE - 1) % SUB) & (i == rows_gx - 1)
    low_y, high_y = half & (j == 0), (lane >= NZ) & (j == width_gy - 1)

    first_sub, last_sub = sub == 0, sub == SUB - 1

    def inverse(value):
        near = pl.reciprocal(value, approx=True)
        near = near * (2.0 - value * near)
        return near * (2.0 - value * near)

    def load(ref, block):
        return [ref[rows_of(block, g)] for g in range(groups)]

    def next_x(values):
        up = [roll(v, -1, 0) for v in values]
        return [jnp.where(last_sub, up[min(g + 1, groups - 1)], up[g]) for g in range(groups)]

    def last_x(values):
        down = [roll(v, 1, 0) for v in values]
        return [jnp.where(first_sub, down[max(g - 1, 0)], down[g]) for g in range(groups)]

    def begin(block, edge, at):
        values = []
        for g in range(groups):
            rows = rows_of(block, g)
            temp, k0, beta = t_in[rows], k0_in[rows], b_in[rows]
            if edge is not None:
                value = edge[at * SLABX + g * SUB : at * SLABX + (g + 1) * SUB]
                swapped = roll(value, NZ, 1)
                if edge is ylow:
                    temp = jnp.where(half, value, temp)
                    k0 = jnp.where(half, lookup(k0_table, swapped), k0)
                    beta = jnp.where(half, lookup(beta_table, swapped), beta)
                else:
                    temp = jnp.where(half, temp, swapped)
                    k0 = jnp.where(half, k0, lookup(k0_table, value))
                    beta = jnp.where(half, beta, lookup(beta_table, value))
            values.append((rows, temp, k0, beta, k0 * inverse(1.0 + beta * temp * temp)))
        for rows, temp, k0, beta, cond in values:
            temp_a[rows], k0_all[rows], b_all[rows], cond_a[rows] = temp, k0, beta, cond

    for e in range(HALO):
        begin(e, ylow, e)
        begin(YBLOCKS - HALO + e, yhigh, e)

    def begin_inner(block, carry):
        begin(block, None, 0)
        return carry

    lax.fori_loop(HALO, YBLOCKS - HALO, begin_inner, 0, unroll=2)

    for step in range(CSWEEPS):
        (t_src, c_src), (t_dst, c_dst) = ((temp_a, cond_a), (temp_b, cond_b))[:: 1 if step % 2 == 0 else -1]

        def y_fluxes(block, temp, cond, temp_n, cond_n):
            closed = (low_y & (block == HALO - 1)) | (high_y & (block == HALO + HALF - 1))
            return [
                jnp.where(closed, 0.0, (cond[g] + cond_n[g]) * (temp_n[g] - temp[g])) for g in range(groups)
            ]

        def advance(block, carry):
            temp, cond, before = carry
            temp_n, cond_n = load(t_src, block + 1), load(c_src, block + 1)
            flux_y = y_fluxes(block, temp, cond, temp_n, cond_n)
            temp_x, cond_x = next_x(temp), next_x(cond)
            flux_x = [(cond[g] + cond_x[g]) * (temp_x[g] - temp[g]) for g in range(groups)]
            flux_x[0] = jnp.where(low_x, 0.0, flux_x[0])
            flux_x[-1] = jnp.where(high_x, 0.0, flux_x[-1])
            back_x = last_x(flux_x)
            results = []
            for g in range(groups):
                flux_z = (cond[g] + roll(cond[g], -1, 1)) * (roll(temp[g], -1, 1) - temp[g])
                flux_z = jnp.where(no_z, 0.0, flux_z)
                div = (flux_y[g] - before[g]) + (flux_x[g] - back_x[g]) + (flux_z - roll(flux_z, 1, 1))
                new = temp[g] + DT * (0.5 * div + q_ext[rows_of(block + 1, g)])
                if step < CSWEEPS - 1:
                    rows = rows_of(block, g)
                    results.append((new, k0_all[rows] * inverse(1.0 + b_all[rows] * new * new)))
                else:
                    results.append((new, None))
            for g in range(groups):
                t_dst[rows_of(block, g)] = results[g][0]
                if step < CSWEEPS - 1:
                    c_dst[rows_of(block, g)] = results[g][1]
            return temp_n, cond_n, flux_y

        first = (load(t_src, 0), load(c_src, 0))
        second = (load(t_src, 1), load(c_src, 1))
        lax.fori_loop(1, YBLOCKS - 1, advance, (*second, y_fluxes(0, *first, *second)), unroll=2)
    final = temp_b if CSWEEPS % 2 else temp_a

    def give_out(yq, carry):
        for g in range(TE // SUB):
            x = slice(g * SUB, (g + 1) * SUB)
            turns = []
            for r in range(4):
                here, after = (final[rows_of(HALO + 4 * yq + r, at)] for at in (g, g + 1))
                value = jnp.where(sub < SUB - HALO, roll(here, -HALO, 0), roll(after, -HALO, 0))
                turns.append([turned(value, by) for by in range(4)])
            for pair in range(2):
                even, odd = turns[2 * pair], turns[2 * pair + 1]
                lower = (2 * yq + pair) * LANES
                upper = lower + temp_out.shape[1] // 2
                temp_out[x, pl.ds(pl.multiple_of(lower, LANES), LANES)] = jnp.where(half, even[0], odd[2])
                temp_out[x, pl.ds(pl.multiple_of(upper, LANES), LANES)] = jnp.where(half, even[2], odd[0])
            for c in range(4):
                value = pick([turns[r][(r - c) % 4] for r in range(4)])
                blocks[pl.ds((c * TE + g * SUB) * SUB + yq, SUB, stride=SUB), :] = value
        return carry

    lax.fori_loop(0, HALF // 4, give_out, 0)
    places = []
    for shift in range(width_gy):
        dev = lax.rem(j + shift, width_gy)
        for t in range(TILES):
            tile = i * tiles + dev * TILES + t
            col = pos[tile, 1] - 2 * j
            cell = jnp.clip(col, 0, 1) * 2 + pos[tile, 2]
            places.append((sends[shift], t, cell, (col >= 0) & (col < 2)))

    def pack(p, carry):
        values = []
        for target, t, cell, here in places:
            value = blocks[pl.ds(pl.multiple_of((cell * TE + p) * SUB, SUB), SUB), :]
            values.append(jnp.where(here, value, 0.0))
        for (target, t, cell, here), value in zip(places, values):
            target[pl.ds(pl.multiple_of(p * ROW, ROW) + t, SUB, stride=TILES), :] = value
        return carry

    lax.fori_loop(0, TE, pack, 0, unroll=2)


def shifted(value, axis, by, wrap=False):
    count = lax.axis_size(axis)
    pairs = [(d, (d + by) % count) for d in range(count) if wrap or 0 <= d + by < count]
    return lax.ppermute(value, axis, pairs)


def from_mate(value):
    return lax.ppermute(value, "gy", [(d, d ^ 1) for d in range(lax.axis_size("gy"))])


def to_rows(value):
    return value.reshape(TILES, -1, LANES).transpose(1, 0, 2).reshape(-1, LANES)


def from_rows(value):
    return value.reshape(-1, TILES, LANES).transpose(1, 0, 2).reshape(TILES, -1)


def everyone(value, chips):
    mine = [value] + [shifted(value, "gy", 2 * d, True) for d in range(1, chips)]
    return mine + [from_mate(part) for part in mine]


def everyone_direct(value, chips):
    mine = [value] + [shifted(value, "gy", 2 * d, True) for d in range(1, chips)]
    count = 2 * chips
    for d in range(chips):
        pairs = [(at, ((at ^ 1) + 2 * d) % count) for at in range(count)]
        mine.append(lax.ppermute(value, "gy", pairs))
    return mine


VMEM = pl.BlockSpec(memory_space=pltpu.VMEM)
SMEM = pl.BlockSpec(memory_space=pltpu.SMEM)
HBM = pl.BlockSpec(memory_space=pltpu.HBM)
PARAMS = pltpu.CompilerParams(vmem_limit_bytes=32 * 1024 * 1024)


def on_device(
    phi_init,
    source,
    tile_mat,
    tile_pos,
    neighbours,
    sigma_table,
    temp_init,
    slab_mat,
    k0_table,
    beta_table,
):
    f32 = jnp.float32
    width_gy = lax.axis_size("gy")
    chips = width_gy // 2
    tiles = width_gy * TILES
    size_x, width = temp_init.shape
    edge_rows = width // LANES * SUB

    def rows(count):
        return jax.ShapeDtypeStruct((count, LANES), f32)

    body, sigma, up, down = pl.pallas_call(
        prep_kernel,
        out_shape=(
            rows(2 * TE * ROW),
            rows(TE * ROW),
            rows(LOW_ROWS + edge_rows),
            rows(HIGH_ROWS + edge_rows),
        ),
        in_specs=[SMEM] + [HBM] * 5,
        out_specs=(VMEM,) * 4,
        scratch_shapes=[
            pltpu.VMEM((TE * ROW, LANES), f32),
            pltpu.VMEM((TE * ROW, LANES), jnp.int32),
            pltpu.VMEM((2, SUB, width), f32),
            pltpu.VMEM((2, SUB, width), jnp.int32),
            pltpu.SemaphoreType.DMA((7,)),
        ],
        compiler_params=pltpu.CompilerParams(vmem_limit_bytes=62 * 1024 * 1024),
        name="prep",
    )(sigma_table, to_rows(phi_init), to_rows(source), to_rows(tile_mat), temp_init, slab_mat)
    bodies = everyone(body, chips)
    low, high = shifted(up, "gx", 1), shifted(down, "gx", -1)

    halo = pl.pallas_call(
        relay_kernel,
        out_shape=rows(LOW_ROWS + HIGH_ROWS),
        in_specs=[VMEM] * 2,
        out_specs=VMEM,
        compiler_params=PARAMS,
        name="relay",
    )(low, high)
    halos = [halo] + [shifted(halo, "gy", 2 * d, True) for d in range(1, chips)]
    sigmas = everyone_direct(sigma, chips)

    native = pltpu.VMEM((width // LANES * SLABX + SUB, LANES), f32)
    t_ext, k0_ext, b_ext, edge_low, edge_high = pl.pallas_call(
        slab_kernel,
        out_shape=(rows(SLAB_ROWS),) * 3 + (rows(HALO * SLABX),) * 2,
        in_specs=[SMEM] * 3 + [VMEM] * 4,
        out_specs=(VMEM,) * 5,
        scratch_shapes=[native, native],
        compiler_params=PARAMS,
        name="slab_prep",
    )(tile_pos, k0_table, beta_table, temp_init, slab_mat, low, high)
    *halos[1:], edge_low, edge_high = lax.optimization_barrier((*halos[1:], edge_low, edge_high))
    halos = halos + [from_mate(part) for part in halos]
    ylow, yhigh = shifted(edge_high, "gy", 1), shifted(edge_low, "gy", -1)

    def planes(count):
        return pltpu.VMEM(((tiles + 1) * count, SUB, LANES), f32)

    def fields(count):
        return pltpu.VMEM((2 * ROW0 + (tiles + 1) * count * SUB, LANES), f32)

    pot, slope = pl.pallas_call(
        functools.partial(sweep_kernel, chips),
        out_shape=(rows(TE * ROW), rows(8 * SLABX * SUB)),
        in_specs=[SMEM] + [VMEM] * (2 * width_gy),
        out_specs=(VMEM,) * 2,
        scratch_shapes=[
            pltpu.SMEM((3, 2 * (2 * width_gy + 2)), jnp.int32),
            pltpu.SMEM((3, tiles), jnp.int32),
            fields(C_SIZE), fields(C_SIZE), fields(L_SIZE), fields(L_SIZE), fields(U_SIZE), fields(U_SIZE),
            planes(TE), planes(LOW[1]), planes(HIGH[1]),
        ],
        compiler_params=PARAMS,
        name="sweeps",
    )(tile_pos, *bodies, *halos)

    temp, *sends = pl.pallas_call(
        functools.partial(slab_steps_kernel, chips),
        out_shape=(jax.ShapeDtypeStruct((size_x, width), f32),) + (rows(TE * ROW),) * width_gy,
        in_specs=[SMEM] * 3 + [VMEM] * (2 * width_gy + 6),
        out_specs=(VMEM,) * (1 + width_gy),
        scratch_shapes=[pltpu.VMEM((8 * SLABX * SUB, LANES), f32)]
        + [pltpu.VMEM((SLAB_ROWS + 3 * SLABX, LANES), f32)]
        + [pltpu.VMEM((SLAB_ROWS, LANES), f32)] * 6
        + [pltpu.VMEM((4 * TE * SUB, LANES), f32)],
        compiler_params=PARAMS,
        name="slab_steps",
    )(tile_pos, k0_table, beta_table, *sigmas, *halos, slope, t_ext, k0_ext, b_ext, ylow, yhigh)
    tile_temps = sends[0]
    for by in range(1, width_gy):
        tile_temps = tile_temps + shifted(sends[by], "gy", by, True)
    return from_rows(pot), temp, from_rows(tile_temps)


def solution(mesh):
    placed = (
        P(("gx", "gy"), None),
        P(("gx", "gy"), None),
        P(("gx", "gy"), None),
        P(),
        P(("gx", "gy"), None),
        P(),
        P("gx", "gy"),
        P("gx", "gy"),
        P(),
        P(),
    )
    return jax.shard_map(
        on_device,
        mesh=mesh,
        in_specs=placed,
        out_specs=(P(("gx", "gy"), None), P("gx", "gy"), P(("gx", "gy"), None)),
        check_vma=False,
    )
```

```python
import functools
import math

import jax
import jax.numpy as jnp
from jax import lax
from jax.experimental import pallas as pl
from jax.experimental.pallas import tpu as pltpu
from jax.sharding import PartitionSpec as P

TE = 32
SWEEPS = 4
CSWEEPS = 3
NZ = 64
EPS = 2.0
DT = 0.15
LANES = 128
SUB = 8
TILES = 2
ROW = SUB * TILES

LOW = (SWEEPS + 2, SWEEPS + 1, 2)
HIGH = (SWEEPS + 3, SWEEPS + 2, 2)
LOW_ROWS = sum(LOW) * ROW
HIGH_ROWS = sum(HIGH) * ROW
SIDE_ROWS = max(LOW_ROWS, HIGH_ROWS)
SLABX = TE + SUB
HALO = CSWEEPS
HALF = TE
YBLOCKS = HALF + 2 * HALO
C_SIZE, L_SIZE, U_SIZE = TE + 2, LOW[0] + 1, HIGH[0] + 1
ROW0 = SUB
SLAB_ROWS = ROW0 + YBLOCKS * SLABX + SUB


def cheb_weight(step, count):
    return 1.0 / (1.0 + 0.75 * math.cos(math.pi * (2 * step + 1) / (2 * count)))


def lookup(table, ids):
    out = jnp.full(ids.shape, table[3], jnp.float32)
    for which in (2, 1, 0):
        out = jnp.where(ids == which, table[which], out)
    return out


def roll(value, by, axis):
    return pltpu.roll(value, by % value.shape[axis], axis)


def prep_kernel(table, phi, src, mat, temp, slab, body, sigma, inner, outer, src_v, mat_v, ends_t, ends_m, sems):
    rows = TE * ROW
    size_x, width = temp.shape
    moves = [(phi, body.at[0:rows]), (src, src_v), (mat, mat_v)]
    for which, first in enumerate((0, size_x - SUB)):
        moves.append((temp.at[first : first + SUB], ends_t.at[which]))
        moves.append((slab.at[first : first + SUB], ends_m.at[which]))
    moves = [pltpu.make_async_copy(*move, sems.at[at]) for at, move in enumerate(moves)]
    for move in moves:
        move.start()
    for move in moves:
        move.wait()
    sigma[...] = lookup(table, mat_v[...])
    body[rows : 2 * rows] = src_v[...] / sigma[...]
    even = lax.rem(lax.axis_index("gx"), 2) == 0

    @pl.when(even)
    def _():
        fill_sides(body, sigma, ends_t, ends_m, inner, outer)

    @pl.when(jnp.logical_not(even))
    def _():
        fill_sides(body, sigma, ends_t, ends_m, outer, inner)


def fill_sides(body, sigma, ends_t, ends_m, up, down):
    rows = TE * ROW
    width = ends_t.shape[2]
    at_up, at_down = 0, 0
    for ref, first in ((body, 0), (body, rows), (sigma, 0)):
        which = (first // rows) if ref is body else 2
        size = LOW[which] * ROW
        up[at_up : at_up + size] = ref[first + rows - size : first + rows]
        at_up += size
        size = HIGH[which] * ROW
        down[at_down : at_down + size] = ref[first : first + size]
        at_down += size
    sub = lax.broadcasted_iota(jnp.int32, (SUB, LANES), 0)
    for at in range(width // LANES):
        lanes = slice(at * LANES, (at + 1) * LANES)
        t_low, m_low = ends_t[0, :, lanes], ends_m[0, :, lanes].astype(jnp.float32)
        t_high, m_high = ends_t[1, :, lanes], ends_m[1, :, lanes].astype(jnp.float32)
        first = at * SUB
        up[SIDE_ROWS + first : SIDE_ROWS + first + SUB] = jnp.where(sub < 4, roll(t_high, HALO, 0), roll(m_high, -1, 0))
        down[SIDE_ROWS + first : SIDE_ROWS + first + SUB] = jnp.where(sub < 4, t_low, roll(m_low, 4, 0))


def relay_kernel(inner, outer, halo):
    def join(low, high):
        halo[0:LOW_ROWS] = low[0:LOW_ROWS]
        halo[LOW_ROWS:] = high[0:HIGH_ROWS]

    even = lax.rem(lax.axis_index("gx"), 2) == 0
    pl.when(even)(lambda: join(outer, inner))
    pl.when(jnp.logical_not(even))(lambda: join(inner, outer))


def loose(pos):
    return jnp.minimum(pos[0, 0], 0)


def slab_kernel(pos, k0_table, beta_table, temp, mat, inner, outer, t_ext, k0_ext, b_ext, edge_low, edge_high, native_t, native_m):
    start = loose(pos)
    even = lax.rem(lax.axis_index("gx"), 2) == 0
    blocks = temp.shape[1] // LANES
    half = lax.broadcasted_iota(jnp.int32, (SUB, LANES), 1) < NZ
    for which, (own, native) in enumerate(((temp, native_t), (mat, native_m))):
        for at in range(blocks):
            lanes = slice(at * LANES, (at + 1) * LANES)
            first = at * SLABX
            side = slice(SIDE_ROWS + at * SUB, SIDE_ROWS + (at + 1) * SUB)
            value = jnp.where(even, outer[side, :], inner[side, :])
            native[first : first + SUB, :] = roll(value, -4, 0) if which else value
            for g in range(TE // SUB):
                value = own[g * SUB : (g + 1) * SUB, lanes].astype(jnp.float32)
                native[pl.ds(start + first + HALO + g * SUB, SUB), :] = value
            value = jnp.where(even, inner[side, :], outer[side, :])
            native[pl.ds(start + first + HALO + TE, SUB), :] = roll(value, -4, 0) if which else value
    for at in range(blocks // 2):
        for g in range(SLABX // SUB):
            halves = []
            for native in (native_t, native_m):
                lower = native[at * SLABX + g * SUB : at * SLABX + (g + 1) * SUB, :]
                upper_at = (blocks // 2 + at) * SLABX + g * SUB
                upper = native[upper_at : upper_at + SUB, :]
                lower_r, upper_r = roll(lower, NZ, 1), roll(upper, NZ, 1)
                halves.append((lower, lower_r, upper, upper_r))
            for odd in range(2):
                y = 2 * at + odd
                temps, mats = (jnp.where(half, v[odd], v[3 - odd]) for v in halves)
                places = [(y + HALO, temps, mats)]
                if y >= HALF - HALO:
                    places.append((y - HALF + HALO, halves[0][1 - odd], halves[1][1 - odd]))
                if y < HALO:
                    places.append((y + HALF + HALO, halves[0][2 + odd], halves[1][2 + odd]))
                for block, t, m in places:
                    rows = slice(ROW0 + block * SLABX + g * SUB, ROW0 + block * SLABX + (g + 1) * SUB)
                    t_ext[rows] = t
                    k0_ext[rows] = lookup(k0_table, m)
                    b_ext[rows] = lookup(beta_table, m)
                if y < HALO:
                    rows = slice(y * SLABX + g * SUB, y * SLABX + (g + 1) * SUB)
                    edge_low[rows] = jnp.where(half, halves[0][odd], halves[1][1 - odd])
                if y >= HALF - HALO:
                    first = (y - HALF + HALO) * SLABX + g * SUB
                    edge_high[first : first + SUB] = jnp.where(half, halves[0][2 + odd], halves[1][3 - odd])


def fill_maps(chips, pos, cell_at, cell_of):
    width_gy = 2 * chips
    tiles = width_gy * TILES
    i = lax.axis_index("gx")
    j = lax.axis_index("gy")
    rows_gx = lax.axis_size("gx")
    for at in range(2 * (2 * width_gy + 2)):
        for which in range(3):
            cell_at[which, at] = tiles
    for which, by in enumerate((0, -1, 1)):
        row = i + by
        valid = (row >= 0) & (row < rows_gx)
        first = jnp.clip(row, 0, rows_gx - 1) * tiles
        for part in range(width_gy):
            dev = part_device(part, chips, j)
            for t in range(TILES):
                tile = first + dev * TILES + t
                cell = (pos[tile, 1] + 1) * 2 + pos[tile, 2]
                slot = part * TILES + t
                cell_of[which, slot] = cell
                cell_at[which, cell] = jnp.where(valid, slot, tiles)


def part_device(part, chips, j):
    mate = j + 1 - 2 * lax.rem(j, 2)
    base = j if part < chips else mate
    return lax.rem(base - 2 * (part % chips) + 2 * chips, 2 * chips)


def sweep_kernel(chips, pos, *refs):
    width_gy = 2 * chips
    tiles = width_gy * TILES
    none = tiles
    bodies = refs[:width_gy]
    halos = refs[width_gy : 2 * width_gy]
    pot, slope, cell_at, cell_of, pa, pb, la, lb, ua, ub, s_c, s_l, s_u = refs[2 * width_gy :]
    i = lax.axis_index("gx")
    j = lax.axis_index("gy")
    rows_gx = lax.axis_size("gx")
    fill_maps(chips, pos, cell_at, cell_of)

    zero = jnp.zeros((SUB, LANES), jnp.float32)

    def plane_at(ref, at, shift=0):
        first = ROW0 + at * SUB
        return ref[pl.ds(pl.multiple_of(first, SUB) if shift == 0 else first + shift, SUB), :]

    def put_plane(ref, at, value):
        ref[pl.ds(pl.multiple_of(ROW0 + at * SUB, SUB), SUB), :] = value

    def unpack(source, start, t, target, first, count):
        def plane(p, carry):
            at = pl.multiple_of(p * ROW, ROW)
            value = source[pl.ds(start + at + t, SUB, stride=TILES), :]
            if len(target.shape) == 3:
                target[first + p] = value
            else:
                put_plane(target, first + p, value)
            return carry

        lax.fori_loop(0, count, plane, 0, unroll=min(count, 8))

    for part in range(width_gy):
        for t in range(TILES):
            slot = part * TILES + t
            unpack(bodies[part], 0, t, pa, slot * C_SIZE + 1, TE)
            unpack(bodies[part], TE * ROW, t, s_c, slot * TE, TE)
            unpack(halos[part], 0, t, la, slot * L_SIZE, LOW[0])
            unpack(halos[part], LOW[0] * ROW, t, s_l, slot * LOW[1], LOW[1])
            unpack(halos[part], LOW_ROWS, t, ua, slot * U_SIZE + 1, HIGH[0])
            unpack(halos[part], LOW_ROWS + HIGH[0] * ROW, t, s_u, slot * HIGH[1], HIGH[1])
    for ref, count in ((pa, C_SIZE), (pb, C_SIZE), (la, L_SIZE), (lb, L_SIZE), (ua, U_SIZE), (ub, U_SIZE)):
        for p in range(count):
            put_plane(ref, none * count + p, zero)

    lane = lax.broadcasted_iota(jnp.int32, (SUB, LANES), 1)
    sub = lax.broadcasted_iota(jnp.int32, (SUB, LANES), 0)
    depth = lane % TE
    first_y, last_y = lane < TE, lane >= LANES - TE
    first_sub, last_sub = sub == 0, sub == SUB - 1
    first_z, last_z = depth == 0, depth == TE - 1

    def y_plus(ref, own, at, ghost_at):
        turned = jnp.where(last_sub, plane_at(ref, ghost_at, 1 - SUB), plane_at(ref, at, 1))
        return roll(jnp.where(first_y, turned, own), -TE, 1)

    def y_minus(ref, own, at, ghost_at):
        turned = jnp.where(first_sub, plane_at(ref, ghost_at, SUB - 1), plane_at(ref, at, -1))
        return roll(jnp.where(last_y, turned, own), TE, 1)

    def around(which, slot):
        cell = cell_of[which, slot]
        upper = cell % 2
        y_m = cell_at[which, cell - 2]
        y_p = cell_at[which, cell + 2]
        z = cell_at[which, cell + 1 - 2 * upper]
        turn = jnp.where(upper == 1, LANES + 1 - TE, TE - 1)
        meets = jnp.where(upper == 1, 0, TE - 1) == depth
        return cell, (slot, y_m, y_p, z, turn, meets)

    bufs = ((pa, la, ua), (pb, lb, ub))
    for k in range(SWEEPS):
        weight = cheb_weight(k, SWEEPS)
        keep, gain = 1.0 - weight, weight / (6.0 + EPS)
        (c_src, l_src, u_src), (c_dst, l_dst, u_dst) = bufs[k % 2], bufs[(k + 1) % 2]

        def ghosts(slot, carry):
            cell = cell_of[0, slot]
            below, above = cell_at[1, cell], cell_at[2, cell]
            put_plane(c_src, slot * C_SIZE, plane_at(l_src, below * L_SIZE + LOW[0] - 1))
            put_plane(c_src, slot * C_SIZE + TE + 1, plane_at(u_src, above * U_SIZE + 1))
            put_plane(l_src, slot * L_SIZE + LOW[0], plane_at(c_src, cell_at[0, cell_of[1, slot]] * C_SIZE + 1))
            put_plane(u_src, slot * U_SIZE, plane_at(c_src, cell_at[0, cell_of[2, slot]] * C_SIZE + TE))
            return carry

        lax.fori_loop(0, tiles, ghosts, 0)

        def relax(src, dst, size, slots, first, count, s_ref, s_at):
            slot, y_m, y_p, z, turn, meets = slots
            at = slot * size + first
            before, own = plane_at(src, at - 1), plane_at(src, at)
            for p in range(count):
                after = plane_at(src, at + p + 1)
                total = (before + after) + s_ref[s_at + p]
                total = total + y_minus(src, own, at + p, y_m * size + first + p)
                total = total + y_plus(src, own, at + p, y_p * size + first + p)
                total = total + jnp.where(last_z, 0.0, roll(own, -1, 1))
                total = total + jnp.where(first_z, 0.0, roll(own, 1, 1))
                ghost = pltpu.roll(plane_at(src, z * size + first + p), turn, 1)
                put_plane(dst, at + p, keep * own + gain * (total + jnp.where(meets, ghost, 0.0)))
                before, own = own, after

        def sweep_tile(slot, carry):
            _, slots = around(0, slot)
            relax(c_src, c_dst, C_SIZE, slots, 1, TE, s_c, slot * TE)
            _, slots = around(1, slot)
            count = LOW[0] - 1 - k
            relax(l_src, l_dst, L_SIZE, slots, LOW[0] - count, count, s_l, (slot + 1) * LOW[1] - count)
            _, slots = around(2, slot)
            relax(u_src, u_dst, U_SIZE, slots, 1, HIGH[0] - 1 - k, s_u, slot * HIGH[1])
            return carry

        lax.fori_loop(0, tiles, sweep_tile, 0)

    field, f_l, f_u = bufs[SWEEPS % 2]
    for t in range(TILES):
        for p in range(TE):
            pot[pl.ds(p * ROW + t, SUB, stride=TILES), :] = plane_at(field, t * C_SIZE + 1 + p)

    def clear(at, carry):
        slope[pl.ds(pl.multiple_of(at * SUB, SUB), SUB), :] = zero
        return carry

    lax.fori_loop(0, slope.shape[0] // SUB, clear, 0, unroll=8)

    def squares(ref, size, slots, p, x_p):
        slot, _, y_p, z, turn, meets = slots
        at = slot * size + p
        own = plane_at(ref, at)
        d_x = (plane_at(ref, at + 1) if x_p is None else x_p) - own
        d_y = y_plus(ref, own, at, y_p * size + p) - own
        ghost = jnp.where(meets, pltpu.roll(plane_at(ref, z * size + p), turn, 1), 0.0)
        d_z = jnp.where(last_z, ghost, roll(own, -1, 1)) - own
        return d_x * d_x + d_y * d_y + d_z * d_z

    def put(local, x, value):
        slope[pl.ds(pl.multiple_of((local * SLABX + x) * SUB, SUB), SUB), :] = value

    def slope_tile(slot, carry):
        for which in range(3):
            cell, slots = around(which, slot)
            local, inside = window(which, cell, i, j, rows_gx)

            @pl.when(inside)
            def _():
                if which == 0:
                    put_plane(field, slot * C_SIZE + TE + 1, plane_at(f_u, cell_at[2, cell] * U_SIZE + 1))

                    for p in range(TE):
                        put(local, HALO + p, squares(field, C_SIZE, slots, 1 + p, None))
                elif which == 1:
                    centre = plane_at(field, cell_at[0, cell] * C_SIZE + 1)
                    put(local, HALO - 2, squares(f_l, L_SIZE, slots, LOW[0] - 2, None))
                    put(local, HALO - 1, squares(f_l, L_SIZE, slots, LOW[0] - 1, centre))
                else:
                    for p in range(2):
                        put(local, HALO + TE + p, squares(f_u, U_SIZE, slots, 1 + p, None))

        return carry

    lax.fori_loop(0, tiles, slope_tile, 0)


def window(which, cell, i, j, rows_gx):
    local = cell - 4 * j
    inside = (local >= 0) & (local < 8)
    if which > 0:
        row = i - 1 if which == 1 else i + 1
        inside = inside & (row >= 0) & (row < rows_gx)
    return local, inside


def slab_steps_kernel(chips, pos, k0_table, beta_table, *refs):
    width_gy = 2 * chips
    tiles = width_gy * TILES
    sigmas = refs[:width_gy]
    halos = refs[width_gy : 2 * width_gy]
    slope, t_in, k0_in, b_in, ylow, yhigh, temp_out = refs[2 * width_gy : 2 * width_gy + 7]
    sends = refs[2 * width_gy + 7 : 3 * width_gy + 7]
    heat, q_ext, temp_a, temp_b, cond_a, cond_b, k0_all, b_all, blocks = refs[3 * width_gy + 7 :]
    i = lax.axis_index("gx")
    j = lax.axis_index("gy")
    rows_gx = lax.axis_size("gx")
    lane = lax.broadcasted_iota(jnp.int32, (SUB, LANES), 1)
    zero = jnp.zeros((SUB, LANES), jnp.float32)

    def clear(at, carry):
        heat[pl.ds(pl.multiple_of(at * SUB, SUB), SUB), :] = zero
        return carry

    lax.fori_loop(0, heat.shape[0] // SUB, clear, 0, unroll=8)
    low_at, high_at = (LOW[0] + LOW[1]) * ROW, LOW_ROWS + (HIGH[0] + HIGH[1]) * ROW
    for part in range(width_gy):
        dev = part_device(part, chips, j)
        for t in range(TILES):
            for which, by in enumerate((0, -1, 1)):
                tile = jnp.clip(i + by, 0, rows_gx - 1) * tiles + dev * TILES + t
                cell = (pos[tile, 1] + 1) * 2 + pos[tile, 2]
                local, inside = window(which, cell, i, j, rows_gx)
                source, start, x, count = (
                    (sigmas[part], 0, HALO, TE),
                    (halos[part], low_at, HALO - 2, 2),
                    (halos[part], high_at, HALO + TE, 2),
                )[which]

                @pl.when(inside)
                def _():
                    def plane(p, carry):
                        rows = pl.ds(pl.multiple_of((local * SLABX + x + p) * SUB, SUB), SUB)
                        at = pl.multiple_of(start + p * ROW, SUB)
                        sigma = source[pl.ds(at + t, SUB, stride=TILES), :]
                        heat[rows, :] = sigma * slope[rows, :]
                        return carry

                    lax.fori_loop(0, count, plane, 0, unroll=count)

    quarter = [(lane >= q * TE) & (lane < (q + 1) * TE) for q in range(3)]

    def pick(parts):
        return jnp.where(
            quarter[0], parts[0], jnp.where(quarter[1], parts[1], jnp.where(quarter[2], parts[2], parts[3]))
        )

    def turned(value, by):
        return value if by % 4 == 0 else roll(value, by * TE, 1)

    def rows_of(block, g):
        first = ROW0 + block * SLABX + g * SUB
        if not isinstance(first, int):
            first = pl.multiple_of(first, SUB)
        return pl.ds(first, SUB)

    groups = SLABX // SUB

    def place_heat(at, carry):
        first = at - 1
        col, yq = lax.div(first * 4 + TE, TE), lax.rem(first * 4 + TE, TE) // 4
        for g in range(groups):
            cells = [
                heat[pl.ds(pl.multiple_of(((2 * col + c) * SLABX + g * SUB) * SUB, SUB) + yq, SUB, stride=SUB), :]
                for c in range(4)
            ]
            for r in range(4):
                block = 4 * first + r + HALO + 1
                q_ext[rows_of(block, g)] = pick([turned(cells[c], c - r) for c in range(4)])
        return carry

    lax.fori_loop(0, HALF // 4 + 2, place_heat, 0, unroll=2)

    sub = lax.broadcasted_iota(jnp.int32, (SUB, LANES), 0)
    half = lane < NZ
    no_z = lane % NZ == NZ - 1
    low_x = (sub == HALO - 1) & (i == 0)
    high_x = (sub == (HALO + TE - 1) % SUB) & (i == rows_gx - 1)
    low_y, high_y = half & (j == 0), (lane >= NZ) & (j == width_gy - 1)

    first_sub, last_sub = sub == 0, sub == SUB - 1

    def inverse(value):
        near = pl.reciprocal(value, approx=True)
        near = near * (2.0 - value * near)
        return near * (2.0 - value * near)

    def load(ref, block):
        return [ref[rows_of(block, g)] for g in range(groups)]

    def next_x(values):
        up = [roll(v, -1, 0) for v in values]
        return [jnp.where(last_sub, up[min(g + 1, groups - 1)], up[g]) for g in range(groups)]

    def last_x(values):
        down = [roll(v, 1, 0) for v in values]
        return [jnp.where(first_sub, down[max(g - 1, 0)], down[g]) for g in range(groups)]

    def begin(block, edge, at):
        values = []
        for g in range(groups):
            rows = rows_of(block, g)
            temp, k0, beta = t_in[rows], k0_in[rows], b_in[rows]
            if edge is not None:
                value = edge[at * SLABX + g * SUB : at * SLABX + (g + 1) * SUB]
                swapped = roll(value, NZ, 1)
                if edge is ylow:
                    temp = jnp.where(half, value, temp)
                    k0 = jnp.where(half, lookup(k0_table, swapped), k0)
                    beta = jnp.where(half, lookup(beta_table, swapped), beta)
                else:
                    temp = jnp.where(half, temp, swapped)
                    k0 = jnp.where(half, k0, lookup(k0_table, value))
                    beta = jnp.where(half, beta, lookup(beta_table, value))
            values.append((rows, temp, k0, beta, k0 * inverse(1.0 + beta * temp * temp)))
        for rows, temp, k0, beta, cond in values:
            temp_a[rows], k0_all[rows], b_all[rows], cond_a[rows] = temp, k0, beta, cond

    for e in range(HALO):
        begin(e, ylow, e)
        begin(YBLOCKS - HALO + e, yhigh, e)

    def begin_inner(block, carry):
        begin(block, None, 0)
        return carry

    lax.fori_loop(HALO, YBLOCKS - HALO, begin_inner, 0, unroll=4)

    for step in range(CSWEEPS):
        (t_src, c_src), (t_dst, c_dst) = ((temp_a, cond_a), (temp_b, cond_b))[:: 1 if step % 2 == 0 else -1]

        def y_fluxes(block, temp, cond, temp_n, cond_n):
            closed = (low_y & (block == HALO - 1)) | (high_y & (block == HALO + HALF - 1))
            return [
                jnp.where(closed, 0.0, (cond[g] + cond_n[g]) * (temp_n[g] - temp[g])) for g in range(groups)
            ]

        def advance(block, carry):
            temp, cond, before = carry
            temp_n, cond_n = load(t_src, block + 1), load(c_src, block + 1)
            flux_y = y_fluxes(block, temp, cond, temp_n, cond_n)
            temp_x, cond_x = next_x(temp), next_x(cond)
            flux_x = [(cond[g] + cond_x[g]) * (temp_x[g] - temp[g]) for g in range(groups)]
            flux_x[0] = jnp.where(low_x, 0.0, flux_x[0])
            flux_x[-1] = jnp.where(high_x, 0.0, flux_x[-1])
            back_x = last_x(flux_x)
            results = []
            for g in range(groups):
                flux_z = (cond[g] + roll(cond[g], -1, 1)) * (roll(temp[g], -1, 1) - temp[g])
                flux_z = jnp.where(no_z, 0.0, flux_z)
                div = (flux_y[g] - before[g]) + (flux_x[g] - back_x[g]) + (flux_z - roll(flux_z, 1, 1))
                new = temp[g] + DT * (0.5 * div + q_ext[rows_of(block + 1, g)])
                if step < CSWEEPS - 1:
                    rows = rows_of(block, g)
                    results.append((new, k0_all[rows] * inverse(1.0 + b_all[rows] * new * new)))
                else:
                    results.append((new, None))
            for g in range(groups):
                t_dst[rows_of(block, g)] = results[g][0]
                if step < CSWEEPS - 1:
                    c_dst[rows_of(block, g)] = results[g][1]
            return temp_n, cond_n, flux_y

        first = (load(t_src, 0), load(c_src, 0))
        second = (load(t_src, 1), load(c_src, 1))
        lax.fori_loop(1, YBLOCKS - 1, advance, (*second, y_fluxes(0, *first, *second)), unroll=6)
    final = temp_b if CSWEEPS % 2 else temp_a

    def give_out(yq, carry):
        for g in range(TE // SUB):
            x = slice(g * SUB, (g + 1) * SUB)
            turns = []
            for r in range(4):
                here, after = (final[rows_of(HALO + 4 * yq + r, at)] for at in (g, g + 1))
                value = jnp.where(sub < SUB - HALO, roll(here, -HALO, 0), roll(after, -HALO, 0))
                turns.append([turned(value, by) for by in range(4)])
            for pair in range(2):
                even, odd = turns[2 * pair], turns[2 * pair + 1]
                lower = (2 * yq + pair) * LANES
                upper = lower + temp_out.shape[1] // 2
                temp_out[x, pl.ds(pl.multiple_of(lower, LANES), LANES)] = jnp.where(half, even[0], odd[2])
                temp_out[x, pl.ds(pl.multiple_of(upper, LANES), LANES)] = jnp.where(half, even[2], odd[0])
            for c in range(4):
                value = pick([turns[r][(r - c) % 4] for r in range(4)])
                blocks[pl.ds((c * TE + g * SUB) * SUB + yq, SUB, stride=SUB), :] = value
        return carry

    lax.fori_loop(0, HALF // 4, give_out, 0, unroll=2)
    places = []
    for shift in range(width_gy):
        dev = lax.rem(j + shift, width_gy)
        for t in range(TILES):
            tile = i * tiles + dev * TILES + t
            col = pos[tile, 1] - 2 * j
            cell = jnp.clip(col, 0, 1) * 2 + pos[tile, 2]
            places.append((sends[shift], t, cell, (col >= 0) & (col < 2)))

    def pack(p, carry):
        values = []
        for target, t, cell, here in places:
            value = blocks[pl.ds(pl.multiple_of((cell * TE + p) * SUB, SUB), SUB), :]
            values.append(jnp.where(here, value, 0.0))
        for (target, t, cell, here), value in zip(places, values):
            target[pl.ds(pl.multiple_of(p * ROW, ROW) + t, SUB, stride=TILES), :] = value
        return carry

    lax.fori_loop(0, TE, pack, 0, unroll=4)


def shifted(value, axis, by, wrap=False):
    count = lax.axis_size(axis)
    pairs = [(d, (d + by) % count) for d in range(count) if wrap or 0 <= d + by < count]
    return lax.ppermute(value, axis, pairs)


def with_partner(value, axis, first):
    count = lax.axis_size(axis)
    pairs = [(d, d + 1) for d in range(first, count - 1, 2)]
    return lax.ppermute(value, axis, pairs + [(high, low) for low, high in pairs])


def from_mate(value):
    return lax.ppermute(value, "gy", [(d, d ^ 1) for d in range(lax.axis_size("gy"))])


def to_rows(value):
    return value.reshape(TILES, -1, LANES).transpose(1, 0, 2).reshape(-1, LANES)


def from_rows(value):
    return value.reshape(-1, TILES, LANES).transpose(1, 0, 2).reshape(TILES, -1)


def everyone(value, chips):
    mine = [value] + [shifted(value, "gy", 2 * d, True) for d in range(1, chips)]
    return mine + [from_mate(part) for part in mine]


def everyone_direct(value, chips):
    mine = [value] + [shifted(value, "gy", 2 * d, True) for d in range(1, chips)]
    count = 2 * chips
    for d in range(chips):
        pairs = [(at, ((at ^ 1) + 2 * d) % count) for at in range(count)]
        mine.append(lax.ppermute(value, "gy", pairs))
    return mine


VMEM = pl.BlockSpec(memory_space=pltpu.VMEM)
SMEM = pl.BlockSpec(memory_space=pltpu.SMEM)
HBM = pl.BlockSpec(memory_space=pltpu.HBM)
PARAMS = pltpu.CompilerParams(vmem_limit_bytes=32 * 1024 * 1024)


def on_device(
    phi_init,
    source,
    tile_mat,
    tile_pos,
    neighbours,
    sigma_table,
    temp_init,
    slab_mat,
    k0_table,
    beta_table,
):
    f32 = jnp.float32
    width_gy = lax.axis_size("gy")
    chips = width_gy // 2
    tiles = width_gy * TILES
    size_x, width = temp_init.shape
    edge_rows = width // LANES * SUB

    def rows(count):
        return jax.ShapeDtypeStruct((count, LANES), f32)

    body, sigma, inner, outer = pl.pallas_call(
        prep_kernel,
        out_shape=(
            rows(2 * TE * ROW),
            rows(TE * ROW),
            rows(SIDE_ROWS + edge_rows),
            rows(SIDE_ROWS + edge_rows),
        ),
        in_specs=[SMEM] + [HBM] * 5,
        out_specs=(VMEM,) * 4,
        scratch_shapes=[
            pltpu.VMEM((TE * ROW, LANES), f32),
            pltpu.VMEM((TE * ROW, LANES), jnp.int32),
            pltpu.VMEM((2, SUB, width), f32),
            pltpu.VMEM((2, SUB, width), jnp.int32),
            pltpu.SemaphoreType.DMA((7,)),
        ],
        compiler_params=pltpu.CompilerParams(vmem_limit_bytes=62 * 1024 * 1024),
        name="prep",
    )(sigma_table, to_rows(phi_init), to_rows(source), to_rows(tile_mat), temp_init, slab_mat)
    bodies = everyone(body, chips)
    inner, outer = with_partner(inner, "gx", 0), with_partner(outer, "gx", 1)

    halo = pl.pallas_call(
        relay_kernel,
        out_shape=rows(LOW_ROWS + HIGH_ROWS),
        in_specs=[VMEM] * 2,
        out_specs=VMEM,
        compiler_params=PARAMS,
        name="relay",
    )(inner, outer)
    halos = [halo] + [shifted(halo, "gy", 2 * d, True) for d in range(1, chips)]
    sigmas = everyone_direct(sigma, chips)

    native = pltpu.VMEM((width // LANES * SLABX + SUB, LANES), f32)
    t_ext, k0_ext, b_ext, edge_low, edge_high = pl.pallas_call(
        slab_kernel,
        out_shape=(rows(SLAB_ROWS),) * 3 + (rows(HALO * SLABX),) * 2,
        in_specs=[SMEM] * 3 + [VMEM] * 4,
        out_specs=(VMEM,) * 5,
        scratch_shapes=[native, native],
        compiler_params=PARAMS,
        name="slab_prep",
    )(tile_pos, k0_table, beta_table, temp_init, slab_mat, inner, outer)
    *halos[1:], edge_low, edge_high = lax.optimization_barrier((*halos[1:], edge_low, edge_high))
    halos = halos + [from_mate(part) for part in halos]
    ylow, yhigh = shifted(edge_high, "gy", 1), shifted(edge_low, "gy", -1)

    def planes(count):
        return pltpu.VMEM(((tiles + 1) * count, SUB, LANES), f32)

    def fields(count):
        return pltpu.VMEM((2 * ROW0 + (tiles + 1) * count * SUB, LANES), f32)

    pot, slope = pl.pallas_call(
        functools.partial(sweep_kernel, chips),
        out_shape=(rows(TE * ROW), rows(8 * SLABX * SUB)),
        in_specs=[SMEM] + [VMEM] * (2 * width_gy),
        out_specs=(VMEM,) * 2,
        scratch_shapes=[
            pltpu.SMEM((3, 2 * (2 * width_gy + 2)), jnp.int32),
            pltpu.SMEM((3, tiles), jnp.int32),
            fields(C_SIZE), fields(C_SIZE), fields(L_SIZE), fields(L_SIZE), fields(U_SIZE), fields(U_SIZE),
            planes(TE), planes(LOW[1]), planes(HIGH[1]),
        ],
        compiler_params=PARAMS,
        name="sweeps",
    )(tile_pos, *bodies, *halos)

    temp, *sends = pl.pallas_call(
        functools.partial(slab_steps_kernel, chips),
        out_shape=(jax.ShapeDtypeStruct((size_x, width), f32),) + (rows(TE * ROW),) * width_gy,
        in_specs=[SMEM] * 3 + [VMEM] * (2 * width_gy + 6),
        out_specs=(VMEM,) * (1 + width_gy),
        scratch_shapes=[pltpu.VMEM((8 * SLABX * SUB, LANES), f32)]
        + [pltpu.VMEM((SLAB_ROWS + 3 * SLABX, LANES), f32)]
        + [pltpu.VMEM((SLAB_ROWS, LANES), f32)] * 6
        + [pltpu.VMEM((4 * TE * SUB, LANES), f32)],
        compiler_params=PARAMS,
        name="slab_steps",
    )(tile_pos, k0_table, beta_table, *sigmas, *halos, slope, t_ext, k0_ext, b_ext, ylow, yhigh)
    tile_temps = sends[0]
    for by in range(1, width_gy):
        tile_temps = tile_temps + shifted(sends[by], "gy", by, True)
    return from_rows(pot), temp, from_rows(tile_temps)


def solution(mesh):
    placed = (
        P(("gx", "gy"), None),
        P(("gx", "gy"), None),
        P(("gx", "gy"), None),
        P(),
        P(("gx", "gy"), None),
        P(),
        P("gx", "gy"),
        P("gx", "gy"),
        P(),
        P(),
    )
    return jax.shard_map(
        on_device,
        mesh=mesh,
        in_specs=placed,
        out_specs=(P(("gx", "gy"), None), P("gx", "gy"), P(("gx", "gy"), None)),
        check_vma=False,
    )
```

```python
import functools
import math

import jax
import jax.numpy as jnp
from jax import lax
from jax.experimental import pallas as pl
from jax.experimental.pallas import tpu as pltpu
from jax.sharding import PartitionSpec as P

TE = 32
SWEEPS = 4
CSWEEPS = 3
NZ = 64
EPS = 2.0
DT = 0.15
LANES = 128
SUB = 8
TILES = 2
ROW = SUB * TILES

LOW = (SWEEPS + 2, SWEEPS + 1, 2)
HIGH = (SWEEPS + 3, SWEEPS + 2, 2)
LOW_ROWS = sum(LOW) * ROW
HIGH_ROWS = sum(HIGH) * ROW
SIDE_ROWS = max(LOW_ROWS, HIGH_ROWS)
SLABX = TE + SUB
HALO = CSWEEPS
HALF = TE
YBLOCKS = HALF + 2 * HALO
C_SIZE, L_SIZE, U_SIZE = TE + 2, LOW[0] + 1, HIGH[0] + 1
ROW0 = SUB
SLAB_ROWS = ROW0 + YBLOCKS * SLABX + SUB


def cheb_weight(step, count):
    return 1.0 / (1.0 + 0.75 * math.cos(math.pi * (2 * step + 1) / (2 * count)))


def lookup(table, ids):
    out = jnp.full(ids.shape, table[3], jnp.float32)
    for which in (2, 1, 0):
        out = jnp.where(ids == which, table[which], out)
    return out


def roll(value, by, axis):
    return pltpu.roll(value, by % value.shape[axis], axis)


def prep_kernel(table, phi, src, mat, temp, slab, body, sigma, inner, outer, src_v, mat_v, ends_t, ends_m, sems):
    rows = TE * ROW
    size_x, width = temp.shape
    moves = [(phi, body.at[0:rows]), (src, src_v), (mat, mat_v)]
    for which, first in enumerate((0, size_x - SUB)):
        moves.append((temp.at[first : first + SUB], ends_t.at[which]))
        moves.append((slab.at[first : first + SUB], ends_m.at[which]))
    moves = [pltpu.make_async_copy(*move, sems.at[at]) for at, move in enumerate(moves)]
    for move in moves:
        move.start()
    for move in moves:
        move.wait()
    sigma[...] = lookup(table, mat_v[...])
    body[rows : 2 * rows] = src_v[...] / sigma[...]
    even = lax.rem(lax.axis_index("gx"), 2) == 0

    @pl.when(even)
    def _():
        fill_sides(body, sigma, ends_t, ends_m, inner, outer)

    @pl.when(jnp.logical_not(even))
    def _():
        fill_sides(body, sigma, ends_t, ends_m, outer, inner)


def fill_sides(body, sigma, ends_t, ends_m, up, down):
    rows = TE * ROW
    width = ends_t.shape[2]
    at_up, at_down = 0, 0
    for ref, first in ((body, 0), (body, rows), (sigma, 0)):
        which = (first // rows) if ref is body else 2
        size = LOW[which] * ROW
        up[at_up : at_up + size] = ref[first + rows - size : first + rows]
        at_up += size
        size = HIGH[which] * ROW
        down[at_down : at_down + size] = ref[first : first + size]
        at_down += size
    sub = lax.broadcasted_iota(jnp.int32, (SUB, LANES), 0)
    for at in range(width // LANES):
        lanes = slice(at * LANES, (at + 1) * LANES)
        t_low, m_low = ends_t[0, :, lanes], ends_m[0, :, lanes].astype(jnp.float32)
        t_high, m_high = ends_t[1, :, lanes], ends_m[1, :, lanes].astype(jnp.float32)
        first = at * SUB
        up[SIDE_ROWS + first : SIDE_ROWS + first + SUB] = jnp.where(sub < 4, roll(t_high, HALO, 0), roll(m_high, -1, 0))
        down[SIDE_ROWS + first : SIDE_ROWS + first + SUB] = jnp.where(sub < 4, t_low, roll(m_low, 4, 0))


def relay_kernel(inner, outer, halo):
    def join(low, high):
        halo[0:LOW_ROWS] = low[0:LOW_ROWS]
        halo[LOW_ROWS:] = high[0:HIGH_ROWS]

    even = lax.rem(lax.axis_index("gx"), 2) == 0
    pl.when(even)(lambda: join(outer, inner))
    pl.when(jnp.logical_not(even))(lambda: join(inner, outer))


def loose(pos):
    return jnp.minimum(pos[0, 0], 0)


def slab_kernel(pos, k0_table, beta_table, temp, mat, inner, outer, t_ext, k0_ext, b_ext, edge_in, edge_out, native_t, native_m, edge_low, edge_high):
    start = loose(pos)
    even = lax.rem(lax.axis_index("gx"), 2) == 0
    blocks = temp.shape[1] // LANES
    half = lax.broadcasted_iota(jnp.int32, (SUB, LANES), 1) < NZ
    for which, (own, native) in enumerate(((temp, native_t), (mat, native_m))):
        for at in range(blocks):
            lanes = slice(at * LANES, (at + 1) * LANES)
            first = at * SLABX
            side = slice(SIDE_ROWS + at * SUB, SIDE_ROWS + (at + 1) * SUB)
            value = jnp.where(even, outer[side, :], inner[side, :])
            native[first : first + SUB, :] = roll(value, -4, 0) if which else value
            for g in range(TE // SUB):
                value = own[g * SUB : (g + 1) * SUB, lanes].astype(jnp.float32)
                native[pl.ds(start + first + HALO + g * SUB, SUB), :] = value
            value = jnp.where(even, inner[side, :], outer[side, :])
            native[pl.ds(start + first + HALO + TE, SUB), :] = roll(value, -4, 0) if which else value
    for at in range(blocks // 2):
        for g in range(SLABX // SUB):
            halves = []
            for native in (native_t, native_m):
                lower = native[at * SLABX + g * SUB : at * SLABX + (g + 1) * SUB, :]
                upper_at = (blocks // 2 + at) * SLABX + g * SUB
                upper = native[upper_at : upper_at + SUB, :]
                lower_r, upper_r = roll(lower, NZ, 1), roll(upper, NZ, 1)
                halves.append((lower, lower_r, upper, upper_r))
            for odd in range(2):
                y = 2 * at + odd
                temps, mats = (jnp.where(half, v[odd], v[3 - odd]) for v in halves)
                places = [(y + HALO, temps, mats)]
                if y >= HALF - HALO:
                    places.append((y - HALF + HALO, halves[0][1 - odd], halves[1][1 - odd]))
                if y < HALO:
                    places.append((y + HALF + HALO, halves[0][2 + odd], halves[1][2 + odd]))
                for block, t, m in places:
                    rows = slice(ROW0 + block * SLABX + g * SUB, ROW0 + block * SLABX + (g + 1) * SUB)
                    t_ext[rows] = t
                    k0_ext[rows] = lookup(k0_table, m)
                    b_ext[rows] = lookup(beta_table, m)
                if y < HALO:
                    rows = slice(y * SLABX + g * SUB, y * SLABX + (g + 1) * SUB)
                    edge_low[rows] = jnp.where(half, halves[0][odd], halves[1][1 - odd])
                if y >= HALF - HALO:
                    first = (y - HALF + HALO) * SLABX + g * SUB
                    edge_high[first : first + SUB] = jnp.where(half, halves[0][2 + odd], halves[1][3 - odd])
    even = lax.rem(lax.axis_index("gy"), 2) == 0
    edge_in[...] = jnp.where(even, edge_high[...], edge_low[...])
    edge_out[...] = jnp.where(even, edge_low[...], edge_high[...])


def fill_maps(chips, pos, cell_at, cell_of):
    width_gy = 2 * chips
    tiles = width_gy * TILES
    i = lax.axis_index("gx")
    j = lax.axis_index("gy")
    rows_gx = lax.axis_size("gx")
    for at in range(2 * (2 * width_gy + 2)):
        for which in range(3):
            cell_at[which, at] = tiles
    for which, by in enumerate((0, -1, 1)):
        row = i + by
        valid = (row >= 0) & (row < rows_gx)
        first = jnp.clip(row, 0, rows_gx - 1) * tiles
        for part in range(width_gy):
            dev = part_device(part, chips, j)
            for t in range(TILES):
                tile = first + dev * TILES + t
                cell = (pos[tile, 1] + 1) * 2 + pos[tile, 2]
                slot = part * TILES + t
                cell_of[which, slot] = cell
                cell_at[which, cell] = jnp.where(valid, slot, tiles)


def part_device(part, chips, j):
    mate = j + 1 - 2 * lax.rem(j, 2)
    base = j if part < chips else mate
    return lax.rem(base - 2 * (part % chips) + 2 * chips, 2 * chips)


def sweep_kernel(chips, pos, *refs):
    width_gy = 2 * chips
    tiles = width_gy * TILES
    none = tiles
    bodies = refs[:width_gy]
    halos = refs[width_gy : 2 * width_gy]
    pot, slope, cell_at, cell_of, pa, pb, la, lb, ua, ub, s_c, s_l, s_u = refs[2 * width_gy :]
    i = lax.axis_index("gx")
    j = lax.axis_index("gy")
    rows_gx = lax.axis_size("gx")
    fill_maps(chips, pos, cell_at, cell_of)

    zero = jnp.zeros((SUB, LANES), jnp.float32)

    def row_of(at):
        return ROW0 + at * SUB

    def plane_at(ref, row):
        return ref[pl.ds(pl.multiple_of(row, SUB), SUB), :]

    def loose_at(ref, row):
        return ref[pl.ds(row, SUB), :]

    def put_plane(ref, row, value):
        ref[pl.ds(pl.multiple_of(row, SUB), SUB), :] = value

    def unpack(source, start, t, target, first, count):
        def plane(p, carry):
            value = source[pl.ds(pl.multiple_of(p * ROW, ROW) + (start + t), SUB, stride=TILES), :]
            put_plane(target, p * SUB + row_of(first), value)
            return carry

        lax.fori_loop(0, count, plane, 0, unroll=min(count, 16))

    for part in range(width_gy):
        for t in range(TILES):
            slot = part * TILES + t
            unpack(bodies[part], 0, t, pa, slot * C_SIZE + 1, TE)
            unpack(bodies[part], TE * ROW, t, s_c, slot * TE, TE)
            unpack(halos[part], 0, t, la, slot * L_SIZE, LOW[0])
            unpack(halos[part], LOW[0] * ROW, t, s_l, slot * LOW[1], LOW[1])
            unpack(halos[part], LOW_ROWS, t, ua, slot * U_SIZE + 1, HIGH[0])
            unpack(halos[part], LOW_ROWS + HIGH[0] * ROW, t, s_u, slot * HIGH[1], HIGH[1])
    for ref, count in ((pa, C_SIZE), (pb, C_SIZE), (la, L_SIZE), (lb, L_SIZE), (ua, U_SIZE), (ub, U_SIZE)):
        for p in range(count):
            put_plane(ref, row_of(none * count + p), zero)

    lane = lax.broadcasted_iota(jnp.int32, (SUB, LANES), 1)
    sub = lax.broadcasted_iota(jnp.int32, (SUB, LANES), 0)
    depth = lane % TE
    first_y, last_y = lane < TE, lane >= LANES - TE
    first_sub, last_sub = sub == 0, sub == SUB - 1
    first_z, last_z = depth == 0, depth == TE - 1

    def y_plus(ref, own, row, ghost_row):
        turned = jnp.where(last_sub, loose_at(ref, ghost_row), loose_at(ref, row))
        return roll(jnp.where(first_y, turned, own), -TE, 1)

    def y_minus(ref, own, row, ghost_row):
        turned = jnp.where(first_sub, loose_at(ref, ghost_row), loose_at(ref, row))
        return roll(jnp.where(last_y, turned, own), TE, 1)

    def around(which, slot):
        cell = cell_of[which, slot]
        upper = cell % 2
        y_m = cell_at[which, cell - 2]
        y_p = cell_at[which, cell + 2]
        z = cell_at[which, cell + 1 - 2 * upper]
        turn = jnp.where(upper == 1, LANES + 1 - TE, TE - 1)
        meets = jnp.where(upper == 1, 0, TE - 1) == depth
        return cell, (slot, y_m, y_p, z, turn, meets)

    bufs = ((pa, la, ua), (pb, lb, ub))
    for k in range(SWEEPS):
        weight = cheb_weight(k, SWEEPS)
        keep, gain = 1.0 - weight, weight / (6.0 + EPS)
        (c_src, l_src, u_src), (c_dst, l_dst, u_dst) = bufs[k % 2], bufs[(k + 1) % 2]

        def ghosts(slot, carry):
            cell = cell_of[0, slot]
            below, above = cell_at[1, cell], cell_at[2, cell]
            own = slot * C_SIZE
            over, under = cell_at[0, cell_of[1, slot]], cell_at[0, cell_of[2, slot]]
            put_plane(c_src, row_of(own), plane_at(l_src, row_of(below * L_SIZE + LOW[0] - 1)))
            put_plane(c_src, row_of(own + TE + 1), plane_at(u_src, row_of(above * U_SIZE + 1)))
            put_plane(l_src, row_of(slot * L_SIZE + LOW[0]), plane_at(c_src, row_of(over * C_SIZE + 1)))
            put_plane(u_src, row_of(slot * U_SIZE), plane_at(c_src, row_of(under * C_SIZE + TE)))
            return carry

        lax.fori_loop(0, tiles, ghosts, 0)

        def relax(src, dst, size, slots, first, count, s_ref, s_at):
            slot, y_m, y_p, z, turn, meets = slots
            row, s_row = row_of(slot * size + first), row_of(s_at)
            up, down = row + 1, row - 1
            row_m, row_p = row_of(y_m * size + first) + (SUB - 1), row_of(y_p * size + first) - (SUB - 1)
            row_z = row_of(z * size + first)
            before, own = plane_at(src, row - SUB), plane_at(src, row)
            for step in range(0, count * SUB, SUB):
                after = plane_at(src, row + (step + SUB))
                total = (before + after) + plane_at(s_ref, s_row + step)
                total = total + y_minus(src, own, down + step, row_m + step)
                total = total + y_plus(src, own, up + step, row_p + step)
                total = total + jnp.where(last_z, 0.0, roll(own, -1, 1))
                total = total + jnp.where(first_z, 0.0, roll(own, 1, 1))
                ghost = pltpu.roll(plane_at(src, row_z + step), turn, 1)
                put_plane(dst, row + step, keep * own + gain * (total + jnp.where(meets, ghost, 0.0)))
                before, own = own, after

        def sweep_tile(slot, carry):
            _, slots = around(0, slot)
            relax(c_src, c_dst, C_SIZE, slots, 1, TE, s_c, slot * TE)
            _, slots = around(1, slot)
            count = LOW[0] - 1 - k
            relax(l_src, l_dst, L_SIZE, slots, LOW[0] - count, count, s_l, (slot + 1) * LOW[1] - count)
            _, slots = around(2, slot)
            relax(u_src, u_dst, U_SIZE, slots, 1, HIGH[0] - 1 - k, s_u, slot * HIGH[1])
            return carry

        lax.fori_loop(0, tiles, sweep_tile, 0)

    field, f_l, f_u = bufs[SWEEPS % 2]
    for t in range(TILES):
        for p in range(TE):
            pot[pl.ds(p * ROW + t, SUB, stride=TILES), :] = plane_at(field, row_of(t * C_SIZE + 1 + p))

    def clear(at, carry):
        slope[pl.ds(pl.multiple_of(at * SUB, SUB), SUB), :] = zero
        return carry

    lax.fori_loop(0, slope.shape[0] // SUB, clear, 0, unroll=8)

    def squares(ref, size, slots, local, x, first, count, x_last=None):
        slot, _, y_p, z, turn, meets = slots
        row = row_of(slot * size + first)
        up, row_p, row_z = row + 1, row_of(y_p * size + first) - (SUB - 1), row_of(z * size + first)
        target = (local * SLABX + x) * SUB
        own = plane_at(ref, row)
        for step in range(0, count * SUB, SUB):
            last = step == (count - 1) * SUB and x_last is not None
            after = x_last if last else plane_at(ref, row + (step + SUB))
            d_x = after - own
            d_y = y_plus(ref, own, up + step, row_p + step) - own
            ghost = jnp.where(meets, pltpu.roll(plane_at(ref, row_z + step), turn, 1), 0.0)
            d_z = jnp.where(last_z, ghost, roll(own, -1, 1)) - own
            put_plane(slope, target + step, d_x * d_x + d_y * d_y + d_z * d_z)
            own = after

    def slope_tile(slot, carry):
        for which in range(3):
            cell, slots = around(which, slot)
            local, inside = window(which, cell, i, j, rows_gx)

            @pl.when(inside)
            def _():
                if which == 0:
                    above = plane_at(f_u, row_of(cell_at[2, cell] * U_SIZE + 1))
                    squares(field, C_SIZE, slots, local, HALO, 1, TE, above)
                elif which == 1:
                    centre = plane_at(field, row_of(cell_at[0, cell] * C_SIZE + 1))
                    squares(f_l, L_SIZE, slots, local, HALO - 2, LOW[0] - 2, 2, centre)
                else:
                    squares(f_u, U_SIZE, slots, local, HALO + TE, 1, 2)

        return carry

    lax.fori_loop(0, tiles, slope_tile, 0)


def window(which, cell, i, j, rows_gx):
    local = cell - 4 * j
    inside = (local >= 0) & (local < 8)
    if which > 0:
        row = i - 1 if which == 1 else i + 1
        inside = inside & (row >= 0) & (row < rows_gx)
    return local, inside


def slab_steps_kernel(chips, pos, k0_table, beta_table, *refs):
    width_gy = 2 * chips
    tiles = width_gy * TILES
    sigmas = refs[:width_gy]
    halos = refs[width_gy : 2 * width_gy]
    slope, t_in, k0_in, b_in, y_in, y_out, temp_out = refs[2 * width_gy : 2 * width_gy + 7]
    sends = refs[2 * width_gy + 7 : 3 * width_gy + 7]
    heat, q_ext, temp_a, temp_b, cond_a, cond_b, k0_all, b_all, blocks = refs[3 * width_gy + 7 :]
    i = lax.axis_index("gx")
    j = lax.axis_index("gy")
    rows_gx = lax.axis_size("gx")
    lane = lax.broadcasted_iota(jnp.int32, (SUB, LANES), 1)
    zero = jnp.zeros((SUB, LANES), jnp.float32)

    def clear(at, carry):
        heat[pl.ds(pl.multiple_of(at * SUB, SUB), SUB), :] = zero
        return carry

    lax.fori_loop(0, heat.shape[0] // SUB, clear, 0, unroll=8)
    low_at, high_at = (LOW[0] + LOW[1]) * ROW, LOW_ROWS + (HIGH[0] + HIGH[1]) * ROW
    for part in range(width_gy):
        dev = part_device(part, chips, j)
        for t in range(TILES):
            for which, by in enumerate((0, -1, 1)):
                tile = jnp.clip(i + by, 0, rows_gx - 1) * tiles + dev * TILES + t
                cell = (pos[tile, 1] + 1) * 2 + pos[tile, 2]
                local, inside = window(which, cell, i, j, rows_gx)
                source, start, x, count = (
                    (sigmas[part], 0, HALO, TE),
                    (halos[part], low_at, HALO - 2, 2),
                    (halos[part], high_at, HALO + TE, 2),
                )[which]

                @pl.when(inside)
                def _():
                    def plane(p, carry):
                        rows = pl.ds(pl.multiple_of((local * SLABX + x + p) * SUB, SUB), SUB)
                        at = pl.multiple_of(start + p * ROW, SUB)
                        sigma = source[pl.ds(at + t, SUB, stride=TILES), :]
                        heat[rows, :] = sigma * slope[rows, :]
                        return carry

                    lax.fori_loop(0, count, plane, 0, unroll=count)

    quarter = [(lane >= q * TE) & (lane < (q + 1) * TE) for q in range(3)]

    def pick(parts):
        return jnp.where(
            quarter[0], parts[0], jnp.where(quarter[1], parts[1], jnp.where(quarter[2], parts[2], parts[3]))
        )

    def turned(value, by):
        return value if by % 4 == 0 else roll(value, by * TE, 1)

    def rows_of(block, g):
        first = ROW0 + block * SLABX + g * SUB
        if not isinstance(first, int):
            first = pl.multiple_of(first, SUB)
        return pl.ds(first, SUB)

    groups = SLABX // SUB

    def place_heat(at, carry):
        first = at - 1
        col, yq = lax.div(first * 4 + TE, TE), lax.rem(first * 4 + TE, TE) // 4
        for g in range(groups):
            cells = [
                heat[pl.ds(pl.multiple_of(((2 * col + c) * SLABX + g * SUB) * SUB, SUB) + yq, SUB, stride=SUB), :]
                for c in range(4)
            ]
            for r in range(4):
                block = 4 * first + r + HALO + 1
                q_ext[rows_of(block, g)] = pick([turned(cells[c], c - r) for c in range(4)])
        return carry

    lax.fori_loop(0, HALF // 4 + 2, place_heat, 0, unroll=2)

    sub = lax.broadcasted_iota(jnp.int32, (SUB, LANES), 0)
    half = lane < NZ
    no_z = lane % NZ == NZ - 1
    low_x = (sub == HALO - 1) & (i == 0)
    high_x = (sub == (HALO + TE - 1) % SUB) & (i == rows_gx - 1)
    low_y, high_y = half & (j == 0), (lane >= NZ) & (j == width_gy - 1)

    first_sub, last_sub = sub == 0, sub == SUB - 1

    def inverse(value):
        near = pl.reciprocal(value, approx=True)
        near = near * (2.0 - value * near)
        return near * (2.0 - value * near)

    def load(ref, block):
        return [ref[rows_of(block, g)] for g in range(groups)]

    def next_x(values):
        up = [roll(v, -1, 0) for v in values]
        return [jnp.where(last_sub, up[min(g + 1, groups - 1)], up[g]) for g in range(groups)]

    def last_x(values):
        down = [roll(v, 1, 0) for v in values]
        return [jnp.where(first_sub, down[max(g - 1, 0)], down[g]) for g in range(groups)]

    even = lax.rem(j, 2) == 0

    def begin(block, low, at):
        values = []
        for g in range(groups):
            rows = rows_of(block, g)
            temp, k0, beta = t_in[rows], k0_in[rows], b_in[rows]
            if low is not None:
                place = slice(at * SLABX + g * SUB, at * SLABX + (g + 1) * SUB)
                value = jnp.where(even, *((y_out[place], y_in[place])[:: 1 if low else -1]))
                swapped = roll(value, NZ, 1)
                if low:
                    temp = jnp.where(half, value, temp)
                    k0 = jnp.where(half, lookup(k0_table, swapped), k0)
                    beta = jnp.where(half, lookup(beta_table, swapped), beta)
                else:
                    temp = jnp.where(half, temp, swapped)
                    k0 = jnp.where(half, k0, lookup(k0_table, value))
                    beta = jnp.where(half, beta, lookup(beta_table, value))
            values.append((rows, temp, k0, beta, k0 * inverse(1.0 + beta * temp * temp)))
        for rows, temp, k0, beta, cond in values:
            temp_a[rows], k0_all[rows], b_all[rows], cond_a[rows] = temp, k0, beta, cond

    for e in range(HALO):
        begin(e, True, e)
        begin(YBLOCKS - HALO + e, False, e)

    def begin_inner(block, carry):
        begin(block, None, 0)
        return carry

    lax.fori_loop(HALO, YBLOCKS - HALO, begin_inner, 0, unroll=4)

    for step in range(CSWEEPS):
        (t_src, c_src), (t_dst, c_dst) = ((temp_a, cond_a), (temp_b, cond_b))[:: 1 if step % 2 == 0 else -1]

        def y_fluxes(block, temp, cond, temp_n, cond_n):
            closed = (low_y & (block == HALO - 1)) | (high_y & (block == HALO + HALF - 1))
            return [
                jnp.where(closed, 0.0, (cond[g] + cond_n[g]) * (temp_n[g] - temp[g])) for g in range(groups)
            ]

        def advance(block, carry):
            temp, cond, before = carry
            temp_n, cond_n = load(t_src, block + 1), load(c_src, block + 1)
            flux_y = y_fluxes(block, temp, cond, temp_n, cond_n)
            temp_x, cond_x = next_x(temp), next_x(cond)
            flux_x = [(cond[g] + cond_x[g]) * (temp_x[g] - temp[g]) for g in range(groups)]
            flux_x[0] = jnp.where(low_x, 0.0, flux_x[0])
            flux_x[-1] = jnp.where(high_x, 0.0, flux_x[-1])
            back_x = last_x(flux_x)
            results = []
            for g in range(groups):
                flux_z = (cond[g] + roll(cond[g], -1, 1)) * (roll(temp[g], -1, 1) - temp[g])
                flux_z = jnp.where(no_z, 0.0, flux_z)
                div = (flux_y[g] - before[g]) + (flux_x[g] - back_x[g]) + (flux_z - roll(flux_z, 1, 1))
                new = temp[g] + DT * (0.5 * div + q_ext[rows_of(block + 1, g)])
                if step < CSWEEPS - 1:
                    rows = rows_of(block, g)
                    results.append((new, k0_all[rows] * inverse(1.0 + b_all[rows] * new * new)))
                else:
                    results.append((new, None))
            for g in range(groups):
                t_dst[rows_of(block, g)] = results[g][0]
                if step < CSWEEPS - 1:
                    c_dst[rows_of(block, g)] = results[g][1]
            return temp_n, cond_n, flux_y

        first = (load(t_src, 0), load(c_src, 0))
        second = (load(t_src, 1), load(c_src, 1))
        lax.fori_loop(1, YBLOCKS - 1, advance, (*second, y_fluxes(0, *first, *second)), unroll=6)
    final = temp_b if CSWEEPS % 2 else temp_a

    def give_out(yq, carry):
        for g in range(TE // SUB):
            x = slice(g * SUB, (g + 1) * SUB)
            turns = []
            for r in range(4):
                here, after = (final[rows_of(HALO + 4 * yq + r, at)] for at in (g, g + 1))
                value = jnp.where(sub < SUB - HALO, roll(here, -HALO, 0), roll(after, -HALO, 0))
                turns.append([turned(value, by) for by in range(4)])
            for pair in range(2):
                even, odd = turns[2 * pair], turns[2 * pair + 1]
                lower = (2 * yq + pair) * LANES
                upper = lower + temp_out.shape[1] // 2
                temp_out[x, pl.ds(pl.multiple_of(lower, LANES), LANES)] = jnp.where(half, even[0], odd[2])
                temp_out[x, pl.ds(pl.multiple_of(upper, LANES), LANES)] = jnp.where(half, even[2], odd[0])
            for c in range(4):
                value = pick([turns[r][(r - c) % 4] for r in range(4)])
                blocks[pl.ds((c * TE + g * SUB) * SUB + yq, SUB, stride=SUB), :] = value
        return carry

    lax.fori_loop(0, HALF // 4, give_out, 0, unroll=2)
    places = []
    for shift in range(width_gy):
        dev = lax.rem(j + shift, width_gy)
        for t in range(TILES):
            tile = i * tiles + dev * TILES + t
            col = pos[tile, 1] - 2 * j
            cell = jnp.clip(col, 0, 1) * 2 + pos[tile, 2]
            places.append((sends[shift], t, cell, (col >= 0) & (col < 2)))

    def pack(p, carry):
        values = []
        for target, t, cell, here in places:
            value = blocks[pl.ds(pl.multiple_of((cell * TE + p) * SUB, SUB), SUB), :]
            values.append(jnp.where(here, value, 0.0))
        for (target, t, cell, here), value in zip(places, values):
            target[pl.ds(pl.multiple_of(p * ROW, ROW) + t, SUB, stride=TILES), :] = value
        return carry

    lax.fori_loop(0, TE, pack, 0, unroll=4)


def shifted(value, axis, by, wrap=False):
    count = lax.axis_size(axis)
    pairs = [(d, (d + by) % count) for d in range(count) if wrap or 0 <= d + by < count]
    return lax.ppermute(value, axis, pairs)


def with_partner(value, axis, first):
    count = lax.axis_size(axis)
    pairs = [(d, d + 1) for d in range(first, count - 1, 2)]
    return lax.ppermute(value, axis, pairs + [(high, low) for low, high in pairs])


def from_mate(value):
    return lax.ppermute(value, "gy", [(d, d ^ 1) for d in range(lax.axis_size("gy"))])


def to_rows(value):
    return value.reshape(TILES, -1, LANES).transpose(1, 0, 2).reshape(-1, LANES)


def from_rows(value):
    return value.reshape(-1, TILES, LANES).transpose(1, 0, 2).reshape(TILES, -1)


def everyone(value, chips):
    mine = [value] + [shifted(value, "gy", 2 * d, True) for d in range(1, chips)]
    return mine + [from_mate(part) for part in mine]


def everyone_direct(value, chips):
    mine = [value] + [shifted(value, "gy", 2 * d, True) for d in range(1, chips)]
    count = 2 * chips
    for d in range(chips):
        pairs = [(at, ((at ^ 1) + 2 * d) % count) for at in range(count)]
        mine.append(lax.ppermute(value, "gy", pairs))
    return mine


VMEM = pl.BlockSpec(memory_space=pltpu.VMEM)
SMEM = pl.BlockSpec(memory_space=pltpu.SMEM)
HBM = pl.BlockSpec(memory_space=pltpu.HBM)
PARAMS = pltpu.CompilerParams(vmem_limit_bytes=32 * 1024 * 1024)


def on_device(
    phi_init,
    source,
    tile_mat,
    tile_pos,
    neighbours,
    sigma_table,
    temp_init,
    slab_mat,
    k0_table,
    beta_table,
):
    f32 = jnp.float32
    width_gy = lax.axis_size("gy")
    chips = width_gy // 2
    tiles = width_gy * TILES
    size_x, width = temp_init.shape
    edge_rows = width // LANES * SUB

    def rows(count):
        return jax.ShapeDtypeStruct((count, LANES), f32)

    body, sigma, inner, outer = pl.pallas_call(
        prep_kernel,
        out_shape=(
            rows(2 * TE * ROW),
            rows(TE * ROW),
            rows(SIDE_ROWS + edge_rows),
            rows(SIDE_ROWS + edge_rows),
        ),
        in_specs=[SMEM] + [HBM] * 5,
        out_specs=(VMEM,) * 4,
        scratch_shapes=[
            pltpu.VMEM((TE * ROW, LANES), f32),
            pltpu.VMEM((TE * ROW, LANES), jnp.int32),
            pltpu.VMEM((2, SUB, width), f32),
            pltpu.VMEM((2, SUB, width), jnp.int32),
            pltpu.SemaphoreType.DMA((7,)),
        ],
        compiler_params=pltpu.CompilerParams(vmem_limit_bytes=62 * 1024 * 1024),
        name="prep",
    )(sigma_table, to_rows(phi_init), to_rows(source), to_rows(tile_mat), temp_init, slab_mat)
    bodies = everyone(body, chips)
    inner, outer = with_partner(inner, "gx", 0), with_partner(outer, "gx", 1)

    halo = pl.pallas_call(
        relay_kernel,
        out_shape=rows(LOW_ROWS + HIGH_ROWS),
        in_specs=[VMEM] * 2,
        out_specs=VMEM,
        compiler_params=PARAMS,
        name="relay",
    )(inner, outer)
    halos = [halo] + [shifted(halo, "gy", 2 * d, True) for d in range(1, chips)]
    sigmas = everyone_direct(sigma, chips)

    native = pltpu.VMEM((width // LANES * SLABX + SUB, LANES), f32)
    t_ext, k0_ext, b_ext, edge_in, edge_out = pl.pallas_call(
        slab_kernel,
        out_shape=(rows(SLAB_ROWS),) * 3 + (rows(HALO * SLABX),) * 2,
        in_specs=[SMEM] * 3 + [VMEM] * 4,
        out_specs=(VMEM,) * 5,
        scratch_shapes=[native, native] + [pltpu.VMEM((HALO * SLABX, LANES), f32)] * 2,
        compiler_params=PARAMS,
        name="slab_prep",
    )(tile_pos, k0_table, beta_table, temp_init, slab_mat, inner, outer)
    y_in, y_out = with_partner(edge_in, "gy", 0), with_partner(edge_out, "gy", 1)
    *halos[1:], y_in, y_out = lax.optimization_barrier((*halos[1:], y_in, y_out))
    halos = halos + [from_mate(part) for part in halos]

    def fields(count):
        return pltpu.VMEM((2 * ROW0 + (tiles + 1) * count * SUB, LANES), f32)

    pot, slope = pl.pallas_call(
        functools.partial(sweep_kernel, chips),
        out_shape=(rows(TE * ROW), rows(8 * SLABX * SUB)),
        in_specs=[SMEM] + [VMEM] * (2 * width_gy),
        out_specs=(VMEM,) * 2,
        scratch_shapes=[
            pltpu.SMEM((3, 2 * (2 * width_gy + 2)), jnp.int32),
            pltpu.SMEM((3, tiles), jnp.int32),
            fields(C_SIZE), fields(C_SIZE), fields(L_SIZE), fields(L_SIZE), fields(U_SIZE), fields(U_SIZE),
            fields(TE), fields(LOW[1]), fields(HIGH[1]),
        ],
        compiler_params=PARAMS,
        name="sweeps",
    )(tile_pos, *bodies, *halos)

    temp, *sends = pl.pallas_call(
        functools.partial(slab_steps_kernel, chips),
        out_shape=(jax.ShapeDtypeStruct((size_x, width), f32),) + (rows(TE * ROW),) * width_gy,
        in_specs=[SMEM] * 3 + [VMEM] * (2 * width_gy + 6),
        out_specs=(VMEM,) * (1 + width_gy),
        scratch_shapes=[pltpu.VMEM((8 * SLABX * SUB, LANES), f32)]
        + [pltpu.VMEM((SLAB_ROWS + 3 * SLABX, LANES), f32)]
        + [pltpu.VMEM((SLAB_ROWS, LANES), f32)] * 6
        + [pltpu.VMEM((4 * TE * SUB, LANES), f32)],
        compiler_params=PARAMS,
        name="slab_steps",
    )(tile_pos, k0_table, beta_table, *sigmas, *halos, slope, t_ext, k0_ext, b_ext, y_in, y_out)
    tile_temps = sends[0]
    for by in range(1, width_gy):
        tile_temps = tile_temps + shifted(sends[by], "gy", by, True)
    return from_rows(pot), temp, from_rows(tile_temps)


def solution(mesh):
    placed = (
        P(("gx", "gy"), None),
        P(("gx", "gy"), None),
        P(("gx", "gy"), None),
        P(),
        P(("gx", "gy"), None),
        P(),
        P("gx", "gy"),
        P("gx", "gy"),
        P(),
        P(),
    )
    return jax.shard_map(
        on_device,
        mesh=mesh,
        in_specs=placed,
        out_specs=(P(("gx", "gy"), None), P("gx", "gy"), P(("gx", "gy"), None)),
        check_vma=False,
    )
```

```python
import functools
import math

import jax
import jax.numpy as jnp
from jax import lax
from jax.experimental import pallas as pl
from jax.experimental.pallas import tpu as pltpu
from jax.sharding import PartitionSpec as P

TE = 32
SWEEPS = 4
CSWEEPS = 3
NZ = 64
EPS = 2.0
DT = 0.15
LANES = 128
SUB = 8
TILES = 2
ROW = SUB * TILES

LOW = (SWEEPS + 2, SWEEPS + 1, 2)
HIGH = (SWEEPS + 3, SWEEPS + 2, 2)
LOW_ROWS = sum(LOW) * ROW
HIGH_ROWS = sum(HIGH) * ROW
SIDE_ROWS = max(LOW_ROWS, HIGH_ROWS)
SLABX = TE + SUB
HALO = CSWEEPS
HALF = TE
YBLOCKS = HALF + 2 * HALO
C_SIZE, L_SIZE, U_SIZE = TE + 2, LOW[0] + 1, HIGH[0] + 1
ROW0 = ROW
SLAB_ROWS = ROW0 + YBLOCKS * SLABX + ROW0


def cheb_weight(step, count):
    return 1.0 / (1.0 + 0.75 * math.cos(math.pi * (2 * step + 1) / (2 * count)))


def lookup(table, ids):
    out = jnp.full(ids.shape, table[3], jnp.float32)
    for which in (2, 1, 0):
        out = jnp.where(ids == which, table[which], out)
    return out


def roll(value, by, axis):
    return pltpu.roll(value, by % value.shape[axis], axis)


def prep_kernel(table, phi, src, mat, temp, slab, body, sigma, inner, outer, src_v, mat_v, ends_t, ends_m, sems):
    rows = TE * ROW
    size_x, width = temp.shape
    moves = [(phi, body.at[0:rows]), (src, src_v), (mat, mat_v)]
    for which, first in enumerate((0, size_x - SUB)):
        moves.append((temp.at[first : first + SUB], ends_t.at[which]))
        moves.append((slab.at[first : first + SUB], ends_m.at[which]))
    moves = [pltpu.make_async_copy(*move, sems.at[at]) for at, move in enumerate(moves)]
    for move in moves:
        move.start()
    for move in moves:
        move.wait()
    sigma[...] = lookup(table, mat_v[...])
    body[rows : 2 * rows] = src_v[...] / sigma[...]
    even = lax.rem(lax.axis_index("gx"), 2) == 0

    @pl.when(even)
    def _():
        fill_sides(body, sigma, ends_t, ends_m, inner, outer)

    @pl.when(jnp.logical_not(even))
    def _():
        fill_sides(body, sigma, ends_t, ends_m, outer, inner)


def fill_sides(body, sigma, ends_t, ends_m, up, down):
    rows = TE * ROW
    width = ends_t.shape[2]
    at_up, at_down = 0, 0
    for ref, first in ((body, 0), (body, rows), (sigma, 0)):
        which = (first // rows) if ref is body else 2
        size = LOW[which] * ROW
        up[at_up : at_up + size] = ref[first + rows - size : first + rows]
        at_up += size
        size = HIGH[which] * ROW
        down[at_down : at_down + size] = ref[first : first + size]
        at_down += size
    sub = lax.broadcasted_iota(jnp.int32, (SUB, LANES), 0)
    for at in range(width // LANES):
        lanes = slice(at * LANES, (at + 1) * LANES)
        t_low, m_low = ends_t[0, :, lanes], ends_m[0, :, lanes].astype(jnp.float32)
        t_high, m_high = ends_t[1, :, lanes], ends_m[1, :, lanes].astype(jnp.float32)
        first = at * SUB
        up[SIDE_ROWS + first : SIDE_ROWS + first + SUB] = jnp.where(sub < 4, roll(t_high, HALO, 0), roll(m_high, -1, 0))
        down[SIDE_ROWS + first : SIDE_ROWS + first + SUB] = jnp.where(sub < 4, t_low, roll(m_low, 4, 0))


def relay_kernel(inner, outer, halo):
    def join(low, high):
        halo[0:LOW_ROWS] = low[0:LOW_ROWS]
        halo[LOW_ROWS:] = high[0:HIGH_ROWS]

    even = lax.rem(lax.axis_index("gx"), 2) == 0
    pl.when(even)(lambda: join(outer, inner))
    pl.when(jnp.logical_not(even))(lambda: join(inner, outer))


def loose(pos):
    return jnp.minimum(pos[0, 0], 0)


def slab_kernel(pos, k0_table, beta_table, temp, mat, inner, outer, t_ext, k0_ext, b_ext, edge_in, edge_out, native_t, native_m, edge_low, edge_high):
    start = loose(pos)
    even = lax.rem(lax.axis_index("gx"), 2) == 0
    blocks = temp.shape[1] // LANES
    half = lax.broadcasted_iota(jnp.int32, (SUB, LANES), 1) < NZ
    for which, (own, native) in enumerate(((temp, native_t), (mat, native_m))):
        for at in range(blocks):
            lanes = slice(at * LANES, (at + 1) * LANES)
            first = at * SLABX
            side = slice(SIDE_ROWS + at * SUB, SIDE_ROWS + (at + 1) * SUB)
            value = jnp.where(even, outer[side, :], inner[side, :])
            native[first : first + SUB, :] = roll(value, -4, 0) if which else value
            for g in range(TE // SUB):
                value = own[g * SUB : (g + 1) * SUB, lanes].astype(jnp.float32)
                native[pl.ds(start + first + HALO + g * SUB, SUB), :] = value
            value = jnp.where(even, inner[side, :], outer[side, :])
            native[pl.ds(start + first + HALO + TE, SUB), :] = roll(value, -4, 0) if which else value
    for at in range(blocks // 2):
        for g in range(SLABX // SUB):
            halves = []
            for native in (native_t, native_m):
                lower = native[at * SLABX + g * SUB : at * SLABX + (g + 1) * SUB, :]
                upper_at = (blocks // 2 + at) * SLABX + g * SUB
                upper = native[upper_at : upper_at + SUB, :]
                lower_r, upper_r = roll(lower, NZ, 1), roll(upper, NZ, 1)
                halves.append((lower, lower_r, upper, upper_r))
            for odd in range(2):
                y = 2 * at + odd
                temps, mats = (jnp.where(half, v[odd], v[3 - odd]) for v in halves)
                places = [(y + HALO, temps, mats)]
                if y >= HALF - HALO:
                    places.append((y - HALF + HALO, halves[0][1 - odd], halves[1][1 - odd]))
                if y < HALO:
                    places.append((y + HALF + HALO, halves[0][2 + odd], halves[1][2 + odd]))
                for block, t, m in places:
                    rows = slice(ROW0 + block * SLABX + g * SUB, ROW0 + block * SLABX + (g + 1) * SUB)
                    t_ext[rows] = t
                    k0_ext[rows] = lookup(k0_table, m)
                    b_ext[rows] = lookup(beta_table, m)
                if y < HALO:
                    rows = slice(y * SLABX + g * SUB, y * SLABX + (g + 1) * SUB)
                    edge_low[rows] = jnp.where(half, halves[0][odd], halves[1][1 - odd])
                if y >= HALF - HALO:
                    first = (y - HALF + HALO) * SLABX + g * SUB
                    edge_high[first : first + SUB] = jnp.where(half, halves[0][2 + odd], halves[1][3 - odd])
    even = lax.rem(lax.axis_index("gy"), 2) == 0
    edge_in[...] = jnp.where(even, edge_high[...], edge_low[...])
    edge_out[...] = jnp.where(even, edge_low[...], edge_high[...])


def fill_maps(chips, pos, cell_at, cell_of):
    width_gy = 2 * chips
    tiles = width_gy * TILES
    i = lax.axis_index("gx")
    j = lax.axis_index("gy")
    rows_gx = lax.axis_size("gx")
    for at in range(2 * (2 * width_gy + 2)):
        for which in range(3):
            cell_at[which, at] = tiles
    for which, by in enumerate((0, -1, 1)):
        row = i + by
        valid = (row >= 0) & (row < rows_gx)
        first = jnp.clip(row, 0, rows_gx - 1) * tiles
        for part in range(width_gy):
            dev = part_device(part, chips, j)
            for t in range(TILES):
                tile = first + dev * TILES + t
                cell = (pos[tile, 1] + 1) * 2 + pos[tile, 2]
                slot = part * TILES + t
                cell_of[which, slot] = cell
                cell_at[which, cell] = jnp.where(valid, slot, tiles)


def part_device(part, chips, j):
    mate = j + 1 - 2 * lax.rem(j, 2)
    base = j if part < chips else mate
    return lax.rem(base - 2 * (part % chips) + 2 * chips, 2 * chips)


def sweep_kernel(chips, pos, *refs):
    width_gy = 2 * chips
    tiles = width_gy * TILES
    none = tiles
    bodies = refs[:width_gy]
    halos = refs[width_gy : 2 * width_gy]
    pot, slope, cell_at, cell_of, pa, pb, la, lb, ua, ub, s_c, s_l, s_u, sems, pot_sem = refs[2 * width_gy :]
    i = lax.axis_index("gx")
    j = lax.axis_index("gy")
    rows_gx = lax.axis_size("gx")
    zero = jnp.zeros((SUB, LANES), jnp.float32)

    moves = []
    for part in range(width_gy):
        at = 0
        pieces = [(bodies[part], 0, pa, part * C_SIZE + 1, TE), (bodies[part], TE * ROW, s_c, part * TE, TE)]
        for target, first, count in (
            (la, part * L_SIZE, LOW[0]),
            (s_l, part * LOW[1], LOW[1]),
            (None, 0, LOW[2]),
            (ua, part * U_SIZE + 1, HIGH[0]),
            (s_u, part * HIGH[1], HIGH[1]),
        ):
            if target is not None:
                pieces.append((halos[part], at, target, first, count))
            at += count * ROW
        for source, start, target, first, count in pieces:
            move = pltpu.make_async_copy(
                source.at[start : start + count * ROW],
                target.at[ROW0 + first * ROW : ROW0 + (first + count) * ROW],
                sems.at[len(moves)],
            )
            move.start()
            moves.append(move)

    fill_maps(chips, pos, cell_at, cell_of)

    def row_of(slot, size, plane):
        return ROW0 + (lax.div(slot, TILES) * size + plane) * ROW + lax.rem(slot, TILES)

    def plane_at(ref, row):
        return ref[pl.ds(row, SUB, stride=TILES), :]

    def put_plane(ref, row, value):
        ref[pl.ds(row, SUB, stride=TILES), :] = value

    for ref, count in ((pa, C_SIZE), (pb, C_SIZE), (la, L_SIZE), (lb, L_SIZE), (ua, U_SIZE), (ub, U_SIZE)):
        first = ROW0 + width_gy * count * ROW
        for row in range(first, first + count * ROW, SUB):
            ref[row : row + SUB] = zero

    def clear(at, carry):
        slope[pl.ds(pl.multiple_of(at * SUB, SUB), SUB), :] = zero
        return carry

    lax.fori_loop(0, slope.shape[0] // SUB, clear, 0, unroll=8)
    for move in moves:
        move.wait()

    lane = lax.broadcasted_iota(jnp.int32, (SUB, LANES), 1)
    sub = lax.broadcasted_iota(jnp.int32, (SUB, LANES), 0)
    depth = lane % TE
    first_y, last_y = lane < TE, lane >= LANES - TE
    first_sub, last_sub = sub == 0, sub == SUB - 1
    first_z, last_z = depth == 0, depth == TE - 1

    def y_plus(ref, own, row, ghost_row):
        turned = jnp.where(last_sub, plane_at(ref, ghost_row), plane_at(ref, row))
        return roll(jnp.where(first_y, turned, own), -TE, 1)

    def y_minus(ref, own, row, ghost_row):
        turned = jnp.where(first_sub, plane_at(ref, ghost_row), plane_at(ref, row))
        return roll(jnp.where(last_y, turned, own), TE, 1)

    def around(which, slot):
        cell = cell_of[which, slot]
        upper = cell % 2
        y_m = cell_at[which, cell - 2]
        y_p = cell_at[which, cell + 2]
        z = cell_at[which, cell + 1 - 2 * upper]
        turn = jnp.where(upper == 1, LANES + 1 - TE, TE - 1)
        meets = jnp.where(upper == 1, 0, TE - 1) == depth
        return cell, (slot, y_m, y_p, z, turn, meets)

    bufs = ((pa, la, ua), (pb, lb, ub))
    for k in range(SWEEPS):
        weight = cheb_weight(k, SWEEPS)
        keep, gain = 1.0 - weight, weight / (6.0 + EPS)
        (c_src, l_src, u_src), (c_dst, l_dst, u_dst) = bufs[k % 2], bufs[(k + 1) % 2]

        def ghosts(slot, carry):
            cell = cell_of[0, slot]
            below, above = cell_at[1, cell], cell_at[2, cell]
            over, under = cell_at[0, cell_of[1, slot]], cell_at[0, cell_of[2, slot]]
            put_plane(c_src, row_of(slot, C_SIZE, 0), plane_at(l_src, row_of(below, L_SIZE, LOW[0] - 1)))
            put_plane(c_src, row_of(slot, C_SIZE, TE + 1), plane_at(u_src, row_of(above, U_SIZE, 1)))
            put_plane(l_src, row_of(slot, L_SIZE, LOW[0]), plane_at(c_src, row_of(over, C_SIZE, 1)))
            put_plane(u_src, row_of(slot, U_SIZE, 0), plane_at(c_src, row_of(under, C_SIZE, TE)))
            return carry

        lax.fori_loop(0, tiles, ghosts, 0)

        def relax(src, dst, size, slots, first, count, s_ref, s_size, s_first):
            slot, y_m, y_p, z, turn, meets = slots
            row, s_row = row_of(slot, size, first), row_of(slot, s_size, s_first)
            up, down = row + TILES, row - TILES
            row_m, row_p = row_of(y_m, size, first) + (ROW - TILES), row_of(y_p, size, first) - (ROW - TILES)
            row_z = row_of(z, size, first)
            before, own = plane_at(src, row - ROW), plane_at(src, row)
            for step in range(0, count * ROW, ROW):
                after = plane_at(src, row + (step + ROW))
                total = (before + after) + plane_at(s_ref, s_row + step)
                total = total + y_minus(src, own, down + step, row_m + step)
                total = total + y_plus(src, own, up + step, row_p + step)
                total = total + jnp.where(last_z, 0.0, roll(own, -1, 1))
                total = total + jnp.where(first_z, 0.0, roll(own, 1, 1))
                ghost = pltpu.roll(plane_at(src, row_z + step), turn, 1)
                put_plane(dst, row + step, keep * own + gain * (total + jnp.where(meets, ghost, 0.0)))
                before, own = own, after

        def sweep_tile(slot, carry):
            _, slots = around(0, slot)
            relax(c_src, c_dst, C_SIZE, slots, 1, TE, s_c, TE, 0)
            _, slots = around(1, slot)
            count = LOW[0] - 1 - k
            relax(l_src, l_dst, L_SIZE, slots, LOW[0] - count, count, s_l, LOW[1], LOW[1] - count)
            _, slots = around(2, slot)
            relax(u_src, u_dst, U_SIZE, slots, 1, HIGH[0] - 1 - k, s_u, HIGH[1], 0)
            return carry

        lax.fori_loop(0, tiles, sweep_tile, 0)

    field, f_l, f_u = bufs[SWEEPS % 2]
    pot_move = pltpu.make_async_copy(field.at[ROW0 + ROW : ROW0 + (TE + 1) * ROW], pot, pot_sem.at[0])
    pot_move.start()

    def squares(ref, size, slots, local, x, first, count, x_last=None):
        slot, _, y_p, z, turn, meets = slots
        row = row_of(slot, size, first)
        up, row_p, row_z = row + TILES, row_of(y_p, size, first) - (ROW - TILES), row_of(z, size, first)
        target = (local * SLABX + x) * SUB
        own = plane_at(ref, row)
        for p in range(count):
            last = p == count - 1 and x_last is not None
            after = x_last if last else plane_at(ref, row + (p + 1) * ROW)
            d_x = after - own
            d_y = y_plus(ref, own, up + p * ROW, row_p + p * ROW) - own
            ghost = jnp.where(meets, pltpu.roll(plane_at(ref, row_z + p * ROW), turn, 1), 0.0)
            d_z = jnp.where(last_z, ghost, roll(own, -1, 1)) - own
            rows = pl.ds(pl.multiple_of(target + p * SUB, SUB), SUB)
            slope[rows, :] = d_x * d_x + d_y * d_y + d_z * d_z
            own = after

    def slope_tile(slot, carry):
        for which in range(3):
            cell, slots = around(which, slot)
            local, inside = window(which, cell, i, j, rows_gx)

            @pl.when(inside)
            def _():
                if which == 0:
                    above = plane_at(f_u, row_of(cell_at[2, cell], U_SIZE, 1))
                    squares(field, C_SIZE, slots, local, HALO, 1, TE, above)
                elif which == 1:
                    centre = plane_at(field, row_of(cell_at[0, cell], C_SIZE, 1))
                    squares(f_l, L_SIZE, slots, local, HALO - 2, LOW[0] - 2, 2, centre)
                else:
                    squares(f_u, U_SIZE, slots, local, HALO + TE, 1, 2)

        return carry

    lax.fori_loop(0, tiles, slope_tile, 0)
    pot_move.wait()


def window(which, cell, i, j, rows_gx):
    local = cell - 4 * j
    inside = (local >= 0) & (local < 8)
    if which > 0:
        row = i - 1 if which == 1 else i + 1
        inside = inside & (row >= 0) & (row < rows_gx)
    return local, inside


def slab_steps_kernel(chips, pos, k0_table, beta_table, *refs):
    width_gy = 2 * chips
    tiles = width_gy * TILES
    sigmas = refs[:width_gy]
    halos = refs[width_gy : 2 * width_gy]
    slope, t_in, k0_in, b_in, y_in, y_out, temp_out = refs[2 * width_gy : 2 * width_gy + 7]
    sends = refs[2 * width_gy + 7 : 3 * width_gy + 7]
    heat, q_ext, temp_a, temp_b, cond_a, cond_b, k0_all, b_all, blocks = refs[3 * width_gy + 7 :]
    i = lax.axis_index("gx")
    j = lax.axis_index("gy")
    rows_gx = lax.axis_size("gx")
    lane = lax.broadcasted_iota(jnp.int32, (SUB, LANES), 1)
    zero = jnp.zeros((SUB, LANES), jnp.float32)

    def clear(at, carry):
        heat[pl.ds(pl.multiple_of(at * SUB, SUB), SUB), :] = zero
        return carry

    lax.fori_loop(0, heat.shape[0] // SUB, clear, 0, unroll=8)
    low_at, high_at = (LOW[0] + LOW[1]) * ROW, LOW_ROWS + (HIGH[0] + HIGH[1]) * ROW
    for part in range(width_gy):
        dev = part_device(part, chips, j)
        for t in range(TILES):
            for which, by in enumerate((0, -1, 1)):
                tile = jnp.clip(i + by, 0, rows_gx - 1) * tiles + dev * TILES + t
                cell = (pos[tile, 1] + 1) * 2 + pos[tile, 2]
                local, inside = window(which, cell, i, j, rows_gx)
                source, start, x, count = (
                    (sigmas[part], 0, HALO, TE),
                    (halos[part], low_at, HALO - 2, 2),
                    (halos[part], high_at, HALO + TE, 2),
                )[which]

                @pl.when(inside)
                def _():
                    def plane(p, carry):
                        rows = pl.ds(pl.multiple_of((local * SLABX + x + p) * SUB, SUB), SUB)
                        at = pl.multiple_of(start + p * ROW, SUB)
                        sigma = source[pl.ds(at + t, SUB, stride=TILES), :]
                        heat[rows, :] = sigma * slope[rows, :]
                        return carry

                    lax.fori_loop(0, count, plane, 0, unroll=count)

    quarter = [(lane >= q * TE) & (lane < (q + 1) * TE) for q in range(3)]

    def pick(parts):
        return jnp.where(
            quarter[0], parts[0], jnp.where(quarter[1], parts[1], jnp.where(quarter[2], parts[2], parts[3]))
        )

    def turned(value, by):
        return value if by % 4 == 0 else roll(value, by * TE, 1)

    def rows_of(block, g):
        first = ROW0 + block * SLABX + g * SUB
        if not isinstance(first, int):
            first = pl.multiple_of(first, SUB)
        return pl.ds(first, SUB)

    groups = SLABX // SUB

    def place_heat(at, carry):
        first = at - 1
        col, yq = lax.div(first * 4 + TE, TE), lax.rem(first * 4 + TE, TE) // 4
        for g in range(groups):
            cells = [
                heat[pl.ds(pl.multiple_of(((2 * col + c) * SLABX + g * SUB) * SUB, SUB) + yq, SUB, stride=SUB), :]
                for c in range(4)
            ]
            for r in range(4):
                block = 4 * first + r + HALO + 1
                q_ext[rows_of(block, g)] = pick([turned(cells[c], c - r) for c in range(4)])
        return carry

    lax.fori_loop(0, HALF // 4 + 2, place_heat, 0, unroll=2)

    sub = lax.broadcasted_iota(jnp.int32, (SUB, LANES), 0)
    half = lane < NZ
    no_z = lane % NZ == NZ - 1
    low_x = (sub == HALO - 1) & (i == 0)
    high_x = (sub == (HALO + TE - 1) % SUB) & (i == rows_gx - 1)
    low_y, high_y = half & (j == 0), (lane >= NZ) & (j == width_gy - 1)

    first_sub, last_sub = sub == 0, sub == SUB - 1

    def inverse(value):
        near = pl.reciprocal(value, approx=True)
        near = near * (2.0 - value * near)
        return near * (2.0 - value * near)

    def load(ref, block):
        return [ref[rows_of(block, g)] for g in range(groups)]

    def next_x(values):
        up = [roll(v, -1, 0) for v in values]
        return [jnp.where(last_sub, up[min(g + 1, groups - 1)], up[g]) for g in range(groups)]

    def last_x(values):
        down = [roll(v, 1, 0) for v in values]
        return [jnp.where(first_sub, down[max(g - 1, 0)], down[g]) for g in range(groups)]

    even = lax.rem(j, 2) == 0

    def begin(block, low, at):
        values = []
        for g in range(groups):
            rows = rows_of(block, g)
            temp, k0, beta = t_in[rows], k0_in[rows], b_in[rows]
            if low is not None:
                place = slice(at * SLABX + g * SUB, at * SLABX + (g + 1) * SUB)
                value = jnp.where(even, *((y_out[place], y_in[place])[:: 1 if low else -1]))
                swapped = roll(value, NZ, 1)
                if low:
                    temp = jnp.where(half, value, temp)
                    k0 = jnp.where(half, lookup(k0_table, swapped), k0)
                    beta = jnp.where(half, lookup(beta_table, swapped), beta)
                else:
                    temp = jnp.where(half, temp, swapped)
                    k0 = jnp.where(half, k0, lookup(k0_table, value))
                    beta = jnp.where(half, beta, lookup(beta_table, value))
            values.append((rows, temp, k0, beta, k0 * inverse(1.0 + beta * temp * temp)))
        for rows, temp, k0, beta, cond in values:
            temp_a[rows], k0_all[rows], b_all[rows], cond_a[rows] = temp, k0, beta, cond

    for e in range(HALO):
        begin(e, True, e)
        begin(YBLOCKS - HALO + e, False, e)

    def begin_inner(block, carry):
        begin(block, None, 0)
        return carry

    lax.fori_loop(HALO, YBLOCKS - HALO, begin_inner, 0, unroll=4)

    for step in range(CSWEEPS):
        (t_src, c_src), (t_dst, c_dst) = ((temp_a, cond_a), (temp_b, cond_b))[:: 1 if step % 2 == 0 else -1]

        def y_fluxes(block, temp, cond, temp_n, cond_n):
            closed = (low_y & (block == HALO - 1)) | (high_y & (block == HALO + HALF - 1))
            return [
                jnp.where(closed, 0.0, (cond[g] + cond_n[g]) * (temp_n[g] - temp[g])) for g in range(groups)
            ]

        def advance(block, carry):
            temp, cond, before = carry
            temp_n, cond_n = load(t_src, block + 1), load(c_src, block + 1)
            flux_y = y_fluxes(block, temp, cond, temp_n, cond_n)
            temp_x, cond_x = next_x(temp), next_x(cond)
            flux_x = [(cond[g] + cond_x[g]) * (temp_x[g] - temp[g]) for g in range(groups)]
            flux_x[0] = jnp.where(low_x, 0.0, flux_x[0])
            flux_x[-1] = jnp.where(high_x, 0.0, flux_x[-1])
            back_x = last_x(flux_x)
            results = []
            for g in range(groups):
                flux_z = (cond[g] + roll(cond[g], -1, 1)) * (roll(temp[g], -1, 1) - temp[g])
                flux_z = jnp.where(no_z, 0.0, flux_z)
                div = (flux_y[g] - before[g]) + (flux_x[g] - back_x[g]) + (flux_z - roll(flux_z, 1, 1))
                new = temp[g] + DT * (0.5 * div + q_ext[rows_of(block + 1, g)])
                if step < CSWEEPS - 1:
                    rows = rows_of(block, g)
                    results.append((new, k0_all[rows] * inverse(1.0 + b_all[rows] * new * new)))
                else:
                    results.append((new, None))
            for g in range(groups):
                t_dst[rows_of(block, g)] = results[g][0]
                if step < CSWEEPS - 1:
                    c_dst[rows_of(block, g)] = results[g][1]
            return temp_n, cond_n, flux_y

        first = (load(t_src, 0), load(c_src, 0))
        second = (load(t_src, 1), load(c_src, 1))
        lax.fori_loop(1, YBLOCKS - 1, advance, (*second, y_fluxes(0, *first, *second)), unroll=6)
    final = temp_b if CSWEEPS % 2 else temp_a

    def give_out(yq, carry):
        for g in range(TE // SUB):
            x = slice(g * SUB, (g + 1) * SUB)
            turns = []
            for r in range(4):
                here, after = (final[rows_of(HALO + 4 * yq + r, at)] for at in (g, g + 1))
                value = jnp.where(sub < SUB - HALO, roll(here, -HALO, 0), roll(after, -HALO, 0))
                turns.append([turned(value, by) for by in range(4)])
            for pair in range(2):
                even, odd = turns[2 * pair], turns[2 * pair + 1]
                lower = (2 * yq + pair) * LANES
                upper = lower + temp_out.shape[1] // 2
                temp_out[x, pl.ds(pl.multiple_of(lower, LANES), LANES)] = jnp.where(half, even[0], odd[2])
                temp_out[x, pl.ds(pl.multiple_of(upper, LANES), LANES)] = jnp.where(half, even[2], odd[0])
            for c in range(4):
                value = pick([turns[r][(r - c) % 4] for r in range(4)])
                blocks[pl.ds((c * TE + g * SUB) * SUB + yq, SUB, stride=SUB), :] = value
        return carry

    lax.fori_loop(0, HALF // 4, give_out, 0, unroll=2)
    places = []
    for shift in range(width_gy):
        dev = lax.rem(j + shift, width_gy)
        for t in range(TILES):
            tile = i * tiles + dev * TILES + t
            col = pos[tile, 1] - 2 * j
            cell = jnp.clip(col, 0, 1) * 2 + pos[tile, 2]
            places.append((sends[shift], t, cell, (col >= 0) & (col < 2)))

    def pack(p, carry):
        values = []
        for target, t, cell, here in places:
            value = blocks[pl.ds(pl.multiple_of((cell * TE + p) * SUB, SUB), SUB), :]
            values.append(jnp.where(here, value, 0.0))
        for (target, t, cell, here), value in zip(places, values):
            target[pl.ds(pl.multiple_of(p * ROW, ROW) + t, SUB, stride=TILES), :] = value
        return carry

    lax.fori_loop(0, TE, pack, 0, unroll=4)


def shifted(value, axis, by, wrap=False):
    count = lax.axis_size(axis)
    pairs = [(d, (d + by) % count) for d in range(count) if wrap or 0 <= d + by < count]
    return lax.ppermute(value, axis, pairs)


def with_partner(value, axis, first):
    count = lax.axis_size(axis)
    pairs = [(d, d + 1) for d in range(first, count - 1, 2)]
    return lax.ppermute(value, axis, pairs + [(high, low) for low, high in pairs])


def from_mate(value):
    return lax.ppermute(value, "gy", [(d, d ^ 1) for d in range(lax.axis_size("gy"))])


def to_rows(value):
    return value.reshape(TILES, -1, LANES).transpose(1, 0, 2).reshape(-1, LANES)


def from_rows(value):
    return value.reshape(-1, TILES, LANES).transpose(1, 0, 2).reshape(TILES, -1)


def everyone(value, chips):
    mine = [value] + [shifted(value, "gy", 2 * d, True) for d in range(1, chips)]
    return mine + [from_mate(part) for part in mine]


def everyone_direct(value, chips):
    mine = [value] + [shifted(value, "gy", 2 * d, True) for d in range(1, chips)]
    count = 2 * chips
    for d in range(chips):
        pairs = [(at, ((at ^ 1) + 2 * d) % count) for at in range(count)]
        mine.append(lax.ppermute(value, "gy", pairs))
    return mine


VMEM = pl.BlockSpec(memory_space=pltpu.VMEM)
SMEM = pl.BlockSpec(memory_space=pltpu.SMEM)
HBM = pl.BlockSpec(memory_space=pltpu.HBM)
ANY = pl.BlockSpec(memory_space=pl.ANY)
PARAMS = pltpu.CompilerParams(vmem_limit_bytes=32 * 1024 * 1024)


def on_device(
    phi_init,
    source,
    tile_mat,
    tile_pos,
    neighbours,
    sigma_table,
    temp_init,
    slab_mat,
    k0_table,
    beta_table,
):
    f32 = jnp.float32
    width_gy = lax.axis_size("gy")
    chips = width_gy // 2
    tiles = width_gy * TILES
    size_x, width = temp_init.shape
    edge_rows = width // LANES * SUB

    def rows(count):
        return jax.ShapeDtypeStruct((count, LANES), f32)

    body, sigma, inner, outer = pl.pallas_call(
        prep_kernel,
        out_shape=(
            rows(2 * TE * ROW),
            rows(TE * ROW),
            rows(SIDE_ROWS + edge_rows),
            rows(SIDE_ROWS + edge_rows),
        ),
        in_specs=[SMEM] + [HBM] * 5,
        out_specs=(VMEM,) * 4,
        scratch_shapes=[
            pltpu.VMEM((TE * ROW, LANES), f32),
            pltpu.VMEM((TE * ROW, LANES), jnp.int32),
            pltpu.VMEM((2, SUB, width), f32),
            pltpu.VMEM((2, SUB, width), jnp.int32),
            pltpu.SemaphoreType.DMA((7,)),
        ],
        compiler_params=pltpu.CompilerParams(vmem_limit_bytes=62 * 1024 * 1024),
        name="prep",
    )(sigma_table, to_rows(phi_init), to_rows(source), to_rows(tile_mat), temp_init, slab_mat)
    bodies = everyone(body, chips)
    inner, outer = with_partner(inner, "gx", 0), with_partner(outer, "gx", 1)

    halo = pl.pallas_call(
        relay_kernel,
        out_shape=rows(LOW_ROWS + HIGH_ROWS),
        in_specs=[VMEM] * 2,
        out_specs=VMEM,
        compiler_params=PARAMS,
        name="relay",
    )(inner, outer)
    halos = [halo] + [shifted(halo, "gy", 2 * d, True) for d in range(1, chips)]
    sigmas = everyone_direct(sigma, chips)

    native = pltpu.VMEM((width // LANES * SLABX + SUB, LANES), f32)
    t_ext, k0_ext, b_ext, edge_in, edge_out = pl.pallas_call(
        slab_kernel,
        out_shape=(rows(SLAB_ROWS),) * 3 + (rows(HALO * SLABX),) * 2,
        in_specs=[SMEM] * 3 + [VMEM] * 4,
        out_specs=(VMEM,) * 5,
        scratch_shapes=[native, native] + [pltpu.VMEM((HALO * SLABX, LANES), f32)] * 2,
        compiler_params=PARAMS,
        name="slab_prep",
    )(tile_pos, k0_table, beta_table, temp_init, slab_mat, inner, outer)
    y_in, y_out = with_partner(edge_in, "gy", 0), with_partner(edge_out, "gy", 1)
    *halos[1:], y_in, y_out = lax.optimization_barrier((*halos[1:], y_in, y_out))
    halos = halos + [from_mate(part) for part in halos]

    def fields(count):
        return pltpu.VMEM((2 * ROW0 + (width_gy + 1) * count * ROW, LANES), f32)

    pot, slope = pl.pallas_call(
        functools.partial(sweep_kernel, chips),
        out_shape=(rows(TE * ROW), rows(8 * SLABX * SUB)),
        in_specs=[SMEM] + [ANY] * (2 * width_gy),
        out_specs=(ANY, VMEM),
        scratch_shapes=[
            pltpu.SMEM((3, 2 * (2 * width_gy + 2)), jnp.int32),
            pltpu.SMEM((3, tiles), jnp.int32),
            fields(C_SIZE), fields(C_SIZE), fields(L_SIZE), fields(L_SIZE), fields(U_SIZE), fields(U_SIZE),
            fields(TE), fields(LOW[1]), fields(HIGH[1]),
            pltpu.SemaphoreType.DMA((6 * width_gy,)),
            pltpu.SemaphoreType.DMA((1,)),
        ],
        compiler_params=PARAMS,
        name="sweeps",
    )(tile_pos, *bodies, *halos)

    temp, *sends = pl.pallas_call(
        functools.partial(slab_steps_kernel, chips),
        out_shape=(jax.ShapeDtypeStruct((size_x, width), f32),) + (rows(TE * ROW),) * width_gy,
        in_specs=[SMEM] * 3 + [VMEM] * (2 * width_gy + 6),
        out_specs=(VMEM,) * (1 + width_gy),
        scratch_shapes=[pltpu.VMEM((8 * SLABX * SUB, LANES), f32)]
        + [pltpu.VMEM((SLAB_ROWS + 3 * SLABX, LANES), f32)]
        + [pltpu.VMEM((SLAB_ROWS, LANES), f32)] * 6
        + [pltpu.VMEM((4 * TE * SUB, LANES), f32)],
        compiler_params=PARAMS,
        name="slab_steps",
    )(tile_pos, k0_table, beta_table, *sigmas, *halos, slope, t_ext, k0_ext, b_ext, y_in, y_out)
    tile_temps = sends[0]
    for by in range(1, width_gy):
        tile_temps = tile_temps + shifted(sends[by], "gy", by, True)
    return from_rows(pot), temp, from_rows(tile_temps)


def solution(mesh):
    placed = (
        P(("gx", "gy"), None),
        P(("gx", "gy"), None),
        P(("gx", "gy"), None),
        P(),
        P(("gx", "gy"), None),
        P(),
        P("gx", "gy"),
        P("gx", "gy"),
        P(),
        P(),
    )
    return jax.shard_map(
        on_device,
        mesh=mesh,
        in_specs=placed,
        out_specs=(P(("gx", "gy"), None), P("gx", "gy"), P(("gx", "gy"), None)),
        check_vma=False,
    )
```

```python
import functools
import math

import jax
import jax.numpy as jnp
from jax import lax
from jax.experimental import pallas as pl
from jax.experimental.pallas import tpu as pltpu
from jax.sharding import PartitionSpec as P

TE = 32
SWEEPS = 4
CSWEEPS = 3
NZ = 64
EPS = 2.0
DT = 0.15
LANES = 128
SUB = 8
TILES = 2
ROW = SUB * TILES

LOW = (SWEEPS + 2, SWEEPS + 1, 2)
HIGH = (SWEEPS + 3, SWEEPS + 2, 2)
LOW_ROWS = sum(LOW) * ROW
HIGH_ROWS = sum(HIGH) * ROW
SIDE_ROWS = max(LOW_ROWS, HIGH_ROWS)
SLABX = TE + SUB
HALO = CSWEEPS
HALF = TE
YBLOCKS = HALF + 2 * HALO
C_SIZE, L_SIZE, U_SIZE = TE + 2, LOW[0] + 1, HIGH[0] + 1
ROW0 = ROW
SLAB_ROWS = ROW0 + YBLOCKS * SLABX + ROW0


def cheb_weight(step, count):
    return 1.0 / (1.0 + 0.75 * math.cos(math.pi * (2 * step + 1) / (2 * count)))


def lookup(table, ids):
    out = jnp.full(ids.shape, table[3], jnp.float32)
    for which in (2, 1, 0):
        out = jnp.where(ids == which, table[which], out)
    return out


def roll(value, by, axis):
    return pltpu.roll(value, by % value.shape[axis], axis)


def prep_kernel(table, phi, src, mat, temp, slab, body, s, sigma, inner, outer, src_v, mat_v, ends_t, ends_m, sems):
    rows = TE * ROW
    size_x, width = temp.shape
    moves = [(phi, body.at[0:rows]), (src, src_v), (mat, mat_v)]
    for which, first in enumerate((0, size_x - SUB)):
        moves.append((temp.at[first : first + SUB], ends_t.at[which]))
        moves.append((slab.at[first : first + SUB], ends_m.at[which]))
    moves = [pltpu.make_async_copy(*move, sems.at[at]) for at, move in enumerate(moves)]
    for move in moves:
        move.start()
    for move in moves:
        move.wait()
    sigma[...] = lookup(table, mat_v[...])
    s[...] = src_v[...] / sigma[...]
    body[rows : 2 * rows] = s[...]
    body[2 * rows : 3 * rows] = sigma[...]
    even = lax.rem(lax.axis_index("gx"), 2) == 0

    @pl.when(even)
    def _():
        fill_sides(body, sigma, ends_t, ends_m, inner, outer)

    @pl.when(jnp.logical_not(even))
    def _():
        fill_sides(body, sigma, ends_t, ends_m, outer, inner)


def fill_sides(body, sigma, ends_t, ends_m, up, down):
    rows = TE * ROW
    width = ends_t.shape[2]
    at_up, at_down = 0, 0
    for ref, first in ((body, 0), (body, rows), (sigma, 0)):
        which = (first // rows) if ref is body else 2
        size = LOW[which] * ROW
        up[at_up : at_up + size] = ref[first + rows - size : first + rows]
        at_up += size
        size = HIGH[which] * ROW
        down[at_down : at_down + size] = ref[first : first + size]
        at_down += size
    sub = lax.broadcasted_iota(jnp.int32, (SUB, LANES), 0)
    for at in range(width // LANES):
        lanes = slice(at * LANES, (at + 1) * LANES)
        t_low, m_low = ends_t[0, :, lanes], ends_m[0, :, lanes].astype(jnp.float32)
        t_high, m_high = ends_t[1, :, lanes], ends_m[1, :, lanes].astype(jnp.float32)
        first = at * SUB
        up[SIDE_ROWS + first : SIDE_ROWS + first + SUB] = jnp.where(sub < 4, roll(t_high, HALO, 0), roll(m_high, -1, 0))
        down[SIDE_ROWS + first : SIDE_ROWS + first + SUB] = jnp.where(sub < 4, t_low, roll(m_low, 4, 0))


def relay_kernel(inner, outer, halo):
    def join(low, high):
        halo[0:LOW_ROWS] = low[0:LOW_ROWS]
        halo[LOW_ROWS:] = high[0:HIGH_ROWS]

    even = lax.rem(lax.axis_index("gx"), 2) == 0
    pl.when(even)(lambda: join(outer, inner))
    pl.when(jnp.logical_not(even))(lambda: join(inner, outer))


def loose(pos):
    return jnp.minimum(pos[0, 0], 0)


def slab_kernel(pos, k0_table, beta_table, temp, mat, inner, outer, t_ext, k0_ext, b_ext, edge_in, edge_out, native_t, native_m, edge_low, edge_high):
    start = loose(pos)
    even = lax.rem(lax.axis_index("gx"), 2) == 0
    blocks = temp.shape[1] // LANES
    half = lax.broadcasted_iota(jnp.int32, (SUB, LANES), 1) < NZ
    for which, (own, native) in enumerate(((temp, native_t), (mat, native_m))):
        for at in range(blocks):
            lanes = slice(at * LANES, (at + 1) * LANES)
            first = at * SLABX
            side = slice(SIDE_ROWS + at * SUB, SIDE_ROWS + (at + 1) * SUB)
            value = jnp.where(even, outer[side, :], inner[side, :])
            native[first : first + SUB, :] = roll(value, -4, 0) if which else value
            for g in range(TE // SUB):
                value = own[g * SUB : (g + 1) * SUB, lanes].astype(jnp.float32)
                native[pl.ds(start + first + HALO + g * SUB, SUB), :] = value
            value = jnp.where(even, inner[side, :], outer[side, :])
            native[pl.ds(start + first + HALO + TE, SUB), :] = roll(value, -4, 0) if which else value
    for at in range(blocks // 2):
        for g in range(SLABX // SUB):
            halves = []
            for native in (native_t, native_m):
                lower = native[at * SLABX + g * SUB : at * SLABX + (g + 1) * SUB, :]
                upper_at = (blocks // 2 + at) * SLABX + g * SUB
                upper = native[upper_at : upper_at + SUB, :]
                lower_r, upper_r = roll(lower, NZ, 1), roll(upper, NZ, 1)
                halves.append((lower, lower_r, upper, upper_r))
            for odd in range(2):
                y = 2 * at + odd
                temps, mats = (jnp.where(half, v[odd], v[3 - odd]) for v in halves)
                places = [(y + HALO, temps, mats)]
                if y >= HALF - HALO:
                    places.append((y - HALF + HALO, halves[0][1 - odd], halves[1][1 - odd]))
                if y < HALO:
                    places.append((y + HALF + HALO, halves[0][2 + odd], halves[1][2 + odd]))
                for block, t, m in places:
                    rows = slice(ROW0 + block * SLABX + g * SUB, ROW0 + block * SLABX + (g + 1) * SUB)
                    t_ext[rows] = t
                    k0_ext[rows] = lookup(k0_table, m)
                    b_ext[rows] = lookup(beta_table, m)
                if y < HALO:
                    rows = slice(y * SLABX + g * SUB, y * SLABX + (g + 1) * SUB)
                    edge_low[rows] = jnp.where(half, halves[0][odd], halves[1][1 - odd])
                if y >= HALF - HALO:
                    first = (y - HALF + HALO) * SLABX + g * SUB
                    edge_high[first : first + SUB] = jnp.where(half, halves[0][2 + odd], halves[1][3 - odd])
    even = lax.rem(lax.axis_index("gy"), 2) == 0
    edge_in[...] = jnp.where(even, edge_high[...], edge_low[...])
    edge_out[...] = jnp.where(even, edge_low[...], edge_high[...])


def fill_maps(chips, pos, cell_at, cell_of):
    width_gy = 2 * chips
    tiles = width_gy * TILES
    i = lax.axis_index("gx")
    j = lax.axis_index("gy")
    rows_gx = lax.axis_size("gx")
    for at in range(2 * (2 * width_gy + 2)):
        for which in range(3):
            cell_at[which, at] = tiles
    for which, by in enumerate((0, -1, 1)):
        row = i + by
        valid = (row >= 0) & (row < rows_gx)
        first = jnp.clip(row, 0, rows_gx - 1) * tiles
        for part in range(width_gy):
            dev = part_device(part, chips, j)
            for t in range(TILES):
                tile = first + dev * TILES + t
                cell = (pos[tile, 1] + 1) * 2 + pos[tile, 2]
                slot = part * TILES + t
                cell_of[which, slot] = cell
                cell_at[which, cell] = jnp.where(valid, slot, tiles)


def part_device(part, chips, j):
    mate = j + 1 - 2 * lax.rem(j, 2)
    base = j if part < chips else mate
    return lax.rem(base - 2 * (part % chips) + 2 * chips, 2 * chips)


def sweep_kernel(chips, pos, *refs):
    width_gy = 2 * chips
    tiles = width_gy * TILES
    none = tiles
    half = 2 * chips - 1
    halos = refs[2 * half : 2 * half + width_gy]
    pot, slope, cell_at, cell_of, pa, pb, la, lb, ua, ub, s_c, s_l, s_u, sems, pot_sem = refs[2 * half + width_gy :]
    bodies = []
    for side in (refs[:half], refs[half : 2 * half]):
        bodies.append(((side[0], 0), (side[0], TE * ROW)))
        bodies += [((side[at], 0), (side[at + 1], 0)) for at in range(1, half, 2)]
    i = lax.axis_index("gx")
    j = lax.axis_index("gy")
    rows_gx = lax.axis_size("gx")
    zero = jnp.zeros((SUB, LANES), jnp.float32)

    moves = []
    for part in range(width_gy):
        at = 0
        pieces = [(*bodies[part][0], pa, part * C_SIZE + 1, TE), (*bodies[part][1], s_c, part * TE, TE)]
        for target, first, count in (
            (la, part * L_SIZE, LOW[0]),
            (s_l, part * LOW[1], LOW[1]),
            (None, 0, LOW[2]),
            (ua, part * U_SIZE + 1, HIGH[0]),
            (s_u, part * HIGH[1], HIGH[1]),
        ):
            if target is not None:
                pieces.append((halos[part], at, target, first, count))
            at += count * ROW
        for source, start, target, first, count in pieces:
            move = pltpu.make_async_copy(
                source.at[start : start + count * ROW],
                target.at[ROW0 + first * ROW : ROW0 + (first + count) * ROW],
                sems.at[len(moves)],
            )
            move.start()
            moves.append(move)

    fill_maps(chips, pos, cell_at, cell_of)

    def row_of(slot, size, plane):
        return ROW0 + (lax.div(slot, TILES) * size + plane) * ROW + lax.rem(slot, TILES)

    def plane_at(ref, row):
        return ref[pl.ds(row, SUB, stride=TILES), :]

    def put_plane(ref, row, value):
        ref[pl.ds(row, SUB, stride=TILES), :] = value

    for ref, count in ((pa, C_SIZE), (pb, C_SIZE), (la, L_SIZE), (lb, L_SIZE), (ua, U_SIZE), (ub, U_SIZE)):
        first = ROW0 + width_gy * count * ROW
        for row in range(first, first + count * ROW, SUB):
            ref[row : row + SUB] = zero

    def clear(at, carry):
        slope[pl.ds(pl.multiple_of(at * SUB, SUB), SUB), :] = zero
        return carry

    lax.fori_loop(0, slope.shape[0] // SUB, clear, 0, unroll=8)
    for move in moves:
        move.wait()

    lane = lax.broadcasted_iota(jnp.int32, (SUB, LANES), 1)
    sub = lax.broadcasted_iota(jnp.int32, (SUB, LANES), 0)
    depth = lane % TE
    first_y, last_y = lane < TE, lane >= LANES - TE
    first_sub, last_sub = sub == 0, sub == SUB - 1
    first_z, last_z = depth == 0, depth == TE - 1

    def y_plus(ref, own, row, ghost_row):
        turned = jnp.where(last_sub, plane_at(ref, ghost_row), plane_at(ref, row))
        return roll(jnp.where(first_y, turned, own), -TE, 1)

    def y_minus(ref, own, row, ghost_row):
        turned = jnp.where(first_sub, plane_at(ref, ghost_row), plane_at(ref, row))
        return roll(jnp.where(last_y, turned, own), TE, 1)

    def around(which, slot):
        cell = cell_of[which, slot]
        upper = cell % 2
        y_m = cell_at[which, cell - 2]
        y_p = cell_at[which, cell + 2]
        z = cell_at[which, cell + 1 - 2 * upper]
        turn = jnp.where(upper == 1, LANES + 1 - TE, TE - 1)
        meets = jnp.where(upper == 1, 0, TE - 1) == depth
        return cell, (slot, y_m, y_p, z, turn, meets)

    bufs = ((pa, la, ua), (pb, lb, ub))
    for k in range(SWEEPS):
        weight = cheb_weight(k, SWEEPS)
        keep, gain = 1.0 - weight, weight / (6.0 + EPS)
        (c_src, l_src, u_src), (c_dst, l_dst, u_dst) = bufs[k % 2], bufs[(k + 1) % 2]

        def ghosts(slot, carry):
            cell = cell_of[0, slot]
            below, above = cell_at[1, cell], cell_at[2, cell]
            over, under = cell_at[0, cell_of[1, slot]], cell_at[0, cell_of[2, slot]]
            put_plane(c_src, row_of(slot, C_SIZE, 0), plane_at(l_src, row_of(below, L_SIZE, LOW[0] - 1)))
            put_plane(c_src, row_of(slot, C_SIZE, TE + 1), plane_at(u_src, row_of(above, U_SIZE, 1)))
            put_plane(l_src, row_of(slot, L_SIZE, LOW[0]), plane_at(c_src, row_of(over, C_SIZE, 1)))
            put_plane(u_src, row_of(slot, U_SIZE, 0), plane_at(c_src, row_of(under, C_SIZE, TE)))
            return carry

        lax.fori_loop(0, tiles, ghosts, 0)

        def relax(src, dst, size, slots, first, count, s_ref, s_size, s_first):
            slot, y_m, y_p, z, turn, meets = slots
            row, s_row = row_of(slot, size, first), row_of(slot, s_size, s_first)
            up, down = row + TILES, row - TILES
            row_m, row_p = row_of(y_m, size, first) + (ROW - TILES), row_of(y_p, size, first) - (ROW - TILES)
            row_z = row_of(z, size, first)
            before, own = plane_at(src, row - ROW), plane_at(src, row)
            for step in range(0, count * ROW, ROW):
                after = plane_at(src, row + (step + ROW))
                total = (before + after) + plane_at(s_ref, s_row + step)
                total = total + y_minus(src, own, down + step, row_m + step)
                total = total + y_plus(src, own, up + step, row_p + step)
                total = total + jnp.where(last_z, 0.0, roll(own, -1, 1))
                total = total + jnp.where(first_z, 0.0, roll(own, 1, 1))
                ghost = pltpu.roll(plane_at(src, row_z + step), turn, 1)
                put_plane(dst, row + step, keep * own + gain * (total + jnp.where(meets, ghost, 0.0)))
                before, own = own, after

        def sweep_tile(slot, carry):
            _, slots = around(0, slot)
            relax(c_src, c_dst, C_SIZE, slots, 1, TE, s_c, TE, 0)
            _, slots = around(1, slot)
            count = LOW[0] - 1 - k
            relax(l_src, l_dst, L_SIZE, slots, LOW[0] - count, count, s_l, LOW[1], LOW[1] - count)
            _, slots = around(2, slot)
            relax(u_src, u_dst, U_SIZE, slots, 1, HIGH[0] - 1 - k, s_u, HIGH[1], 0)
            return carry

        lax.fori_loop(0, tiles, sweep_tile, 0)

    field, f_l, f_u = bufs[SWEEPS % 2]
    pot_move = pltpu.make_async_copy(field.at[ROW0 + ROW : ROW0 + (TE + 1) * ROW], pot, pot_sem.at[0])
    pot_move.start()

    def squares(ref, size, slots, local, x, first, count, x_last=None):
        slot, _, y_p, z, turn, meets = slots
        row = row_of(slot, size, first)
        up, row_p, row_z = row + TILES, row_of(y_p, size, first) - (ROW - TILES), row_of(z, size, first)
        target = (local * SLABX + x) * SUB
        own = plane_at(ref, row)
        for p in range(count):
            last = p == count - 1 and x_last is not None
            after = x_last if last else plane_at(ref, row + (p + 1) * ROW)
            d_x = after - own
            d_y = y_plus(ref, own, up + p * ROW, row_p + p * ROW) - own
            ghost = jnp.where(meets, pltpu.roll(plane_at(ref, row_z + p * ROW), turn, 1), 0.0)
            d_z = jnp.where(last_z, ghost, roll(own, -1, 1)) - own
            rows = pl.ds(pl.multiple_of(target + p * SUB, SUB), SUB)
            slope[rows, :] = d_x * d_x + d_y * d_y + d_z * d_z
            own = after

    def slope_tile(slot, carry):
        for which in range(3):
            cell, slots = around(which, slot)
            local, inside = window(which, cell, i, j, rows_gx)

            @pl.when(inside)
            def _():
                if which == 0:
                    above = plane_at(f_u, row_of(cell_at[2, cell], U_SIZE, 1))
                    squares(field, C_SIZE, slots, local, HALO, 1, TE, above)
                elif which == 1:
                    centre = plane_at(field, row_of(cell_at[0, cell], C_SIZE, 1))
                    squares(f_l, L_SIZE, slots, local, HALO - 2, LOW[0] - 2, 2, centre)
                else:
                    squares(f_u, U_SIZE, slots, local, HALO + TE, 1, 2)

        return carry

    lax.fori_loop(0, tiles, slope_tile, 0)
    pot_move.wait()


def window(which, cell, i, j, rows_gx):
    local = cell - 4 * j
    inside = (local >= 0) & (local < 8)
    if which > 0:
        row = i - 1 if which == 1 else i + 1
        inside = inside & (row >= 0) & (row < rows_gx)
    return local, inside


def slab_steps_kernel(chips, pos, k0_table, beta_table, *refs):
    width_gy = 2 * chips
    tiles = width_gy * TILES
    halos = refs[width_gy : 2 * width_gy]
    slope, t_in, k0_in, b_in, y_in, y_out, temp_out = refs[2 * width_gy : 2 * width_gy + 7]
    sends = refs[2 * width_gy + 7 : 3 * width_gy + 7]
    heat, q_ext, temp_a, temp_b, cond_a, cond_b, k0_all, b_all, blocks, sigmas, sems = refs[3 * width_gy + 7 :]
    moves = []
    for part in range(width_gy):
        start = 2 * TE * ROW if part % chips == 0 else 0
        source = refs[part].at[start : start + TE * ROW]
        moves.append(pltpu.make_async_copy(source, sigmas.at[part], sems.at[part]))
        moves[-1].start()
    i = lax.axis_index("gx")
    j = lax.axis_index("gy")
    rows_gx = lax.axis_size("gx")
    lane = lax.broadcasted_iota(jnp.int32, (SUB, LANES), 1)
    zero = jnp.zeros((SUB, LANES), jnp.float32)

    quarter = [(lane >= q * TE) & (lane < (q + 1) * TE) for q in range(3)]

    def pick(parts):
        return jnp.where(
            quarter[0], parts[0], jnp.where(quarter[1], parts[1], jnp.where(quarter[2], parts[2], parts[3]))
        )

    def turned(value, by):
        return value if by % 4 == 0 else roll(value, by * TE, 1)

    def rows_of(block, g):
        first = ROW0 + block * SLABX + g * SUB
        if not isinstance(first, int):
            first = pl.multiple_of(first, SUB)
        return pl.ds(first, SUB)

    groups = SLABX // SUB

    sub = lax.broadcasted_iota(jnp.int32, (SUB, LANES), 0)
    half = lane < NZ
    no_z = lane % NZ == NZ - 1
    low_x = (sub == HALO - 1) & (i == 0)
    high_x = (sub == (HALO + TE - 1) % SUB) & (i == rows_gx - 1)
    low_y, high_y = half & (j == 0), (lane >= NZ) & (j == width_gy - 1)

    first_sub, last_sub = sub == 0, sub == SUB - 1

    def inverse(value):
        near = pl.reciprocal(value, approx=True)
        near = near * (2.0 - value * near)
        return near * (2.0 - value * near)

    def load(ref, block):
        return [ref[rows_of(block, g)] for g in range(groups)]

    def next_x(values):
        up = [roll(v, -1, 0) for v in values]
        return [jnp.where(last_sub, up[min(g + 1, groups - 1)], up[g]) for g in range(groups)]

    def last_x(values):
        down = [roll(v, 1, 0) for v in values]
        return [jnp.where(first_sub, down[max(g - 1, 0)], down[g]) for g in range(groups)]

    even = lax.rem(j, 2) == 0

    def begin(block, low, at):
        values = []
        for g in range(groups):
            rows = rows_of(block, g)
            temp, k0, beta = t_in[rows], k0_in[rows], b_in[rows]
            if low is not None:
                place = slice(at * SLABX + g * SUB, at * SLABX + (g + 1) * SUB)
                value = jnp.where(even, *((y_out[place], y_in[place])[:: 1 if low else -1]))
                swapped = roll(value, NZ, 1)
                if low:
                    temp = jnp.where(half, value, temp)
                    k0 = jnp.where(half, lookup(k0_table, swapped), k0)
                    beta = jnp.where(half, lookup(beta_table, swapped), beta)
                else:
                    temp = jnp.where(half, temp, swapped)
                    k0 = jnp.where(half, k0, lookup(k0_table, value))
                    beta = jnp.where(half, beta, lookup(beta_table, value))
            values.append((rows, temp, k0, beta, k0 * inverse(1.0 + beta * temp * temp)))
        for rows, temp, k0, beta, cond in values:
            temp_a[rows], k0_all[rows], b_all[rows], cond_a[rows] = temp, k0, beta, cond

    for e in range(HALO):
        begin(e, True, e)
        begin(YBLOCKS - HALO + e, False, e)

    def begin_inner(block, carry):
        begin(block, None, 0)
        return carry

    lax.fori_loop(HALO, YBLOCKS - HALO, begin_inner, 0, unroll=4)

    def clear(at, carry):
        heat[pl.ds(pl.multiple_of(at * SUB, SUB), SUB), :] = zero
        return carry

    lax.fori_loop(0, heat.shape[0] // SUB, clear, 0, unroll=8)
    for move in moves:
        move.wait()
    low_at, high_at = (LOW[0] + LOW[1]) * ROW, LOW_ROWS + (HIGH[0] + HIGH[1]) * ROW
    for part in range(width_gy):
        dev = part_device(part, chips, j)
        for t in range(TILES):
            for which, by in enumerate((0, -1, 1)):
                tile = jnp.clip(i + by, 0, rows_gx - 1) * tiles + dev * TILES + t
                cell = (pos[tile, 1] + 1) * 2 + pos[tile, 2]
                local, inside = window(which, cell, i, j, rows_gx)
                source, start, x, count = (
                    (sigmas.at[part], 0, HALO, TE),
                    (halos[part], low_at, HALO - 2, 2),
                    (halos[part], high_at, HALO + TE, 2),
                )[which]

                @pl.when(inside)
                def _():
                    def plane(p, carry):
                        rows = pl.ds(pl.multiple_of((local * SLABX + x + p) * SUB, SUB), SUB)
                        at = pl.multiple_of(start + p * ROW, SUB)
                        sigma = source[pl.ds(at + t, SUB, stride=TILES), :]
                        heat[rows, :] = sigma * slope[rows, :]
                        return carry

                    lax.fori_loop(0, count, plane, 0, unroll=count)

    def place_heat(at, carry):
        first = at - 1
        col, yq = lax.div(first * 4 + TE, TE), lax.rem(first * 4 + TE, TE) // 4
        for g in range(groups):
            cells = [
                heat[pl.ds(pl.multiple_of(((2 * col + c) * SLABX + g * SUB) * SUB, SUB) + yq, SUB, stride=SUB), :]
                for c in range(4)
            ]
            for r in range(4):
                block = 4 * first + r + HALO + 1
                q_ext[rows_of(block, g)] = pick([turned(cells[c], c - r) for c in range(4)])
        return carry

    lax.fori_loop(0, HALF // 4 + 2, place_heat, 0, unroll=2)

    for step in range(CSWEEPS):
        (t_src, c_src), (t_dst, c_dst) = ((temp_a, cond_a), (temp_b, cond_b))[:: 1 if step % 2 == 0 else -1]

        def y_fluxes(block, temp, cond, temp_n, cond_n):
            closed = (low_y & (block == HALO - 1)) | (high_y & (block == HALO + HALF - 1))
            return [
                jnp.where(closed, 0.0, (cond[g] + cond_n[g]) * (temp_n[g] - temp[g])) for g in range(groups)
            ]

        def advance(block, carry):
            temp, cond, before = carry
            temp_n, cond_n = load(t_src, block + 1), load(c_src, block + 1)
            flux_y = y_fluxes(block, temp, cond, temp_n, cond_n)
            temp_x, cond_x = next_x(temp), next_x(cond)
            flux_x = [(cond[g] + cond_x[g]) * (temp_x[g] - temp[g]) for g in range(groups)]
            flux_x[0] = jnp.where(low_x, 0.0, flux_x[0])
            flux_x[-1] = jnp.where(high_x, 0.0, flux_x[-1])
            back_x = last_x(flux_x)
            results = []
            for g in range(groups):
                flux_z = (cond[g] + roll(cond[g], -1, 1)) * (roll(temp[g], -1, 1) - temp[g])
                flux_z = jnp.where(no_z, 0.0, flux_z)
                div = (flux_y[g] - before[g]) + (flux_x[g] - back_x[g]) + (flux_z - roll(flux_z, 1, 1))
                new = temp[g] + DT * (0.5 * div + q_ext[rows_of(block + 1, g)])
                if step < CSWEEPS - 1:
                    rows = rows_of(block, g)
                    results.append((new, k0_all[rows] * inverse(1.0 + b_all[rows] * new * new)))
                else:
                    results.append((new, None))
            for g in range(groups):
                t_dst[rows_of(block, g)] = results[g][0]
                if step < CSWEEPS - 1:
                    c_dst[rows_of(block, g)] = results[g][1]
            return temp_n, cond_n, flux_y

        first = (load(t_src, 0), load(c_src, 0))
        second = (load(t_src, 1), load(c_src, 1))
        lax.fori_loop(1, YBLOCKS - 1, advance, (*second, y_fluxes(0, *first, *second)), unroll=6)
    final = temp_b if CSWEEPS % 2 else temp_a

    def give_out(yq, carry):
        for g in range(TE // SUB):
            x = slice(g * SUB, (g + 1) * SUB)
            turns = []
            for r in range(4):
                here, after = (final[rows_of(HALO + 4 * yq + r, at)] for at in (g, g + 1))
                value = jnp.where(sub < SUB - HALO, roll(here, -HALO, 0), roll(after, -HALO, 0))
                turns.append([turned(value, by) for by in range(4)])
            for pair in range(2):
                even, odd = turns[2 * pair], turns[2 * pair + 1]
                lower = (2 * yq + pair) * LANES
                upper = lower + temp_out.shape[1] // 2
                temp_out[x, pl.ds(pl.multiple_of(lower, LANES), LANES)] = jnp.where(half, even[0], odd[2])
                temp_out[x, pl.ds(pl.multiple_of(upper, LANES), LANES)] = jnp.where(half, even[2], odd[0])
            for c in range(4):
                value = pick([turns[r][(r - c) % 4] for r in range(4)])
                blocks[pl.ds((c * TE + g * SUB) * SUB + yq, SUB, stride=SUB), :] = value
        return carry

    lax.fori_loop(0, HALF // 4, give_out, 0, unroll=2)
    places = []
    for shift in range(width_gy):
        dev = lax.rem(j + shift, width_gy)
        for t in range(TILES):
            tile = i * tiles + dev * TILES + t
            col = pos[tile, 1] - 2 * j
            cell = jnp.clip(col, 0, 1) * 2 + pos[tile, 2]
            places.append((sends[shift], t, cell, (col >= 0) & (col < 2)))

    def pack(p, carry):
        values = []
        for target, t, cell, here in places:
            value = blocks[pl.ds(pl.multiple_of((cell * TE + p) * SUB, SUB), SUB), :]
            values.append(jnp.where(here, value, 0.0))
        for (target, t, cell, here), value in zip(places, values):
            target[pl.ds(pl.multiple_of(p * ROW, ROW) + t, SUB, stride=TILES), :] = value
        return carry

    lax.fori_loop(0, TE, pack, 0, unroll=4)


def shifted(value, axis, by, wrap=False):
    count = lax.axis_size(axis)
    pairs = [(d, (d + by) % count) for d in range(count) if wrap or 0 <= d + by < count]
    return lax.ppermute(value, axis, pairs)


def with_partner(value, axis, first):
    count = lax.axis_size(axis)
    pairs = [(d, d + 1) for d in range(first, count - 1, 2)]
    return lax.ppermute(value, axis, pairs + [(high, low) for low, high in pairs])


def from_mate(value):
    return lax.ppermute(value, "gy", [(d, d ^ 1) for d in range(lax.axis_size("gy"))])


def to_rows(value):
    return value.reshape(TILES, -1, LANES).transpose(1, 0, 2).reshape(-1, LANES)


def from_rows(value):
    return value.reshape(-1, TILES, LANES).transpose(1, 0, 2).reshape(TILES, -1)


def to_other_core(value, by):
    count = lax.axis_size("gy")
    return lax.ppermute(value, "gy", [(at, ((at ^ 1) + 2 * by) % count) for at in range(count)])


VMEM = pl.BlockSpec(memory_space=pltpu.VMEM)
SMEM = pl.BlockSpec(memory_space=pltpu.SMEM)
HBM = pl.BlockSpec(memory_space=pltpu.HBM)
ANY = pl.BlockSpec(memory_space=pl.ANY)
PARAMS = pltpu.CompilerParams(vmem_limit_bytes=32 * 1024 * 1024)


def on_device(
    phi_init,
    source,
    tile_mat,
    tile_pos,
    neighbours,
    sigma_table,
    temp_init,
    slab_mat,
    k0_table,
    beta_table,
):
    f32 = jnp.float32
    width_gy = lax.axis_size("gy")
    chips = width_gy // 2
    tiles = width_gy * TILES
    size_x, width = temp_init.shape
    edge_rows = width // LANES * SUB

    def rows(count):
        return jax.ShapeDtypeStruct((count, LANES), f32)

    phi = to_rows(phi_init)
    phis = [shifted(phi, "gy", 2 * d, True) for d in range(1, chips)]
    body, s, sigma, inner, outer = pl.pallas_call(
        prep_kernel,
        out_shape=(
            rows(3 * TE * ROW),
            rows(TE * ROW),
            rows(TE * ROW),
            rows(SIDE_ROWS + edge_rows),
            rows(SIDE_ROWS + edge_rows),
        ),
        in_specs=[SMEM] + [HBM] * 5,
        out_specs=(VMEM,) * 5,
        scratch_shapes=[
            pltpu.VMEM((TE * ROW, LANES), f32),
            pltpu.VMEM((TE * ROW, LANES), jnp.int32),
            pltpu.VMEM((2, SUB, width), f32),
            pltpu.VMEM((2, SUB, width), jnp.int32),
            pltpu.SemaphoreType.DMA((7,)),
        ],
        compiler_params=pltpu.CompilerParams(vmem_limit_bytes=62 * 1024 * 1024),
        name="prep",
    )(sigma_table, phi, to_rows(source), to_rows(tile_mat), temp_init, slab_mat)
    bodies = [body]
    for there, d in zip(phis, range(1, chips)):
        bodies += [there, shifted(s, "gy", 2 * d, True)]
    bodies += [from_mate(part) for part in bodies]
    inner, outer = with_partner(inner, "gx", 0), with_partner(outer, "gx", 1)

    halo = pl.pallas_call(
        relay_kernel,
        out_shape=rows(LOW_ROWS + HIGH_ROWS),
        in_specs=[VMEM] * 2,
        out_specs=VMEM,
        compiler_params=PARAMS,
        name="relay",
    )(inner, outer)
    halos = [halo] + [shifted(halo, "gy", 2 * d, True) for d in range(1, chips)]
    sigmas = [bodies[0]] + [shifted(sigma, "gy", 2 * d, True) for d in range(1, chips)]
    sigmas += [bodies[2 * chips - 1]] + [to_other_core(sigma, d) for d in range(1, chips)]

    native = pltpu.VMEM((width // LANES * SLABX + SUB, LANES), f32)
    t_ext, k0_ext, b_ext, edge_in, edge_out = pl.pallas_call(
        slab_kernel,
        out_shape=(rows(SLAB_ROWS),) * 3 + (rows(HALO * SLABX),) * 2,
        in_specs=[SMEM] * 3 + [VMEM] * 4,
        out_specs=(VMEM,) * 5,
        scratch_shapes=[native, native] + [pltpu.VMEM((HALO * SLABX, LANES), f32)] * 2,
        compiler_params=PARAMS,
        name="slab_prep",
    )(tile_pos, k0_table, beta_table, temp_init, slab_mat, inner, outer)
    y_in, y_out = with_partner(edge_in, "gy", 0), with_partner(edge_out, "gy", 1)
    *halos[1:], y_in = lax.optimization_barrier((*halos[1:], y_in))
    halos = halos + [from_mate(part) for part in halos]

    def fields(count):
        return pltpu.VMEM((2 * ROW0 + (width_gy + 1) * count * ROW, LANES), f32)

    pot, slope = pl.pallas_call(
        functools.partial(sweep_kernel, chips),
        out_shape=(rows(TE * ROW), rows(8 * SLABX * SUB)),
        in_specs=[SMEM] + [ANY] * (len(bodies) + width_gy),
        out_specs=(ANY, VMEM),
        scratch_shapes=[
            pltpu.SMEM((3, 2 * (2 * width_gy + 2)), jnp.int32),
            pltpu.SMEM((3, tiles), jnp.int32),
            fields(C_SIZE), fields(C_SIZE), fields(L_SIZE), fields(L_SIZE), fields(U_SIZE), fields(U_SIZE),
            fields(TE), fields(LOW[1]), fields(HIGH[1]),
            pltpu.SemaphoreType.DMA((6 * width_gy,)),
            pltpu.SemaphoreType.DMA((1,)),
        ],
        compiler_params=PARAMS,
        name="sweeps",
    )(tile_pos, *bodies, *halos)

    temp, *sends = pl.pallas_call(
        functools.partial(slab_steps_kernel, chips),
        out_shape=(jax.ShapeDtypeStruct((size_x, width), f32),) + (rows(TE * ROW),) * width_gy,
        in_specs=[SMEM] * 3 + [ANY] * width_gy + [VMEM] * (width_gy + 6),
        out_specs=(VMEM,) * (1 + width_gy),
        scratch_shapes=[pltpu.VMEM((8 * SLABX * SUB, LANES), f32)]
        + [pltpu.VMEM((SLAB_ROWS + 3 * SLABX, LANES), f32)]
        + [pltpu.VMEM((SLAB_ROWS, LANES), f32)] * 6
        + [pltpu.VMEM((4 * TE * SUB, LANES), f32), pltpu.VMEM((width_gy, TE * ROW, LANES), f32)]
        + [pltpu.SemaphoreType.DMA((width_gy,))],
        compiler_params=PARAMS,
        name="slab_steps",
    )(tile_pos, k0_table, beta_table, *sigmas, *halos, slope, t_ext, k0_ext, b_ext, y_in, y_out)
    tile_temps = sends[0]
    for by in range(1, width_gy):
        tile_temps = tile_temps + shifted(sends[by], "gy", by, True)
    return from_rows(pot), temp, from_rows(tile_temps)


def solution(mesh):
    placed = (
        P(("gx", "gy"), None),
        P(("gx", "gy"), None),
        P(("gx", "gy"), None),
        P(),
        P(("gx", "gy"), None),
        P(),
        P("gx", "gy"),
        P("gx", "gy"),
        P(),
        P(),
    )
    return jax.shard_map(
        on_device,
        mesh=mesh,
        in_specs=placed,
        out_specs=(P(("gx", "gy"), None), P("gx", "gy"), P(("gx", "gy"), None)),
        check_vma=False,
    )
```

```python
import functools
import math

import jax
import jax.numpy as jnp
from jax import lax
from jax.experimental import pallas as pl
from jax.experimental.pallas import tpu as pltpu
from jax.sharding import PartitionSpec as P

TE = 32
SWEEPS = 4
CSWEEPS = 3
NZ = 64
EPS = 2.0
DT = 0.15
LANES = 128
SUB = 8
TILES = 2
ROW = SUB * TILES

LOW = (SWEEPS + 2, SWEEPS + 1, 2)
HIGH = (SWEEPS + 3, SWEEPS + 2, 2)
LOW_ROWS = sum(LOW) * ROW
HIGH_ROWS = sum(HIGH) * ROW
SIDE_ROWS = max(LOW_ROWS, HIGH_ROWS)
SLABX = TE + SUB
HALO = CSWEEPS
HALF = TE
YBLOCKS = HALF + 2 * HALO
C_SIZE, L_SIZE, U_SIZE = TE + 2, LOW[0] + 1, HIGH[0] + 1
ROW0 = ROW
SLAB_ROWS = ROW0 + YBLOCKS * SLABX + ROW0


def cheb_weight(step, count):
    return 1.0 / (1.0 + 0.75 * math.cos(math.pi * (2 * step + 1) / (2 * count)))


def lookup(table, ids):
    out = jnp.full(ids.shape, table[3], jnp.float32)
    for which in (2, 1, 0):
        out = jnp.where(ids == which, table[which], out)
    return out


def roll(value, by, axis):
    return pltpu.roll(value, by % value.shape[axis], axis)


def prep_kernel(table, phi, src, mat, temp, slab, body, s, sigma, inner, outer, src_v, mat_v, ends_t, ends_m, sems):
    rows = TE * ROW
    size_x, width = temp.shape
    moves = [(phi, body.at[0:rows]), (src, src_v), (mat, mat_v)]
    for which, first in enumerate((0, size_x - SUB)):
        moves.append((temp.at[first : first + SUB], ends_t.at[which]))
        moves.append((slab.at[first : first + SUB], ends_m.at[which]))
    moves = [pltpu.make_async_copy(*move, sems.at[at]) for at, move in enumerate(moves)]
    for move in moves:
        move.start()
    for move in moves:
        move.wait()
    sigma[...] = lookup(table, mat_v[...])
    s[...] = src_v[...] / sigma[...]
    body[rows : 2 * rows] = s[...]
    body[2 * rows : 3 * rows] = sigma[...]
    even = lax.rem(lax.axis_index("gx"), 2) == 0

    @pl.when(even)
    def _():
        fill_sides(body, sigma, ends_t, ends_m, inner, outer)

    @pl.when(jnp.logical_not(even))
    def _():
        fill_sides(body, sigma, ends_t, ends_m, outer, inner)


def fill_sides(body, sigma, ends_t, ends_m, up, down):
    rows = TE * ROW
    width = ends_t.shape[2]
    at_up, at_down = 0, 0
    for ref, first in ((body, 0), (body, rows), (sigma, 0)):
        which = (first // rows) if ref is body else 2
        size = LOW[which] * ROW
        up[at_up : at_up + size] = ref[first + rows - size : first + rows]
        at_up += size
        size = HIGH[which] * ROW
        down[at_down : at_down + size] = ref[first : first + size]
        at_down += size
    sub = lax.broadcasted_iota(jnp.int32, (SUB, LANES), 0)
    for at in range(width // LANES):
        lanes = slice(at * LANES, (at + 1) * LANES)
        t_low, m_low = ends_t[0, :, lanes], ends_m[0, :, lanes].astype(jnp.float32)
        t_high, m_high = ends_t[1, :, lanes], ends_m[1, :, lanes].astype(jnp.float32)
        first = at * SUB
        up[SIDE_ROWS + first : SIDE_ROWS + first + SUB] = jnp.where(sub < 4, roll(t_high, HALO, 0), roll(m_high, -1, 0))
        down[SIDE_ROWS + first : SIDE_ROWS + first + SUB] = jnp.where(sub < 4, t_low, roll(m_low, 4, 0))


def relay_kernel(inner, outer, halo):
    def join(low, high):
        halo[0:LOW_ROWS] = low[0:LOW_ROWS]
        halo[LOW_ROWS:] = high[0:HIGH_ROWS]

    even = lax.rem(lax.axis_index("gx"), 2) == 0
    pl.when(even)(lambda: join(outer, inner))
    pl.when(jnp.logical_not(even))(lambda: join(inner, outer))


def loose(pos):
    return jnp.minimum(pos[0, 0], 0)


def slab_kernel(pos, k0_table, beta_table, temp, mat, inner, outer, t_ext, k0_ext, b_ext, edge_in, edge_out, native_t, native_m, edge_low, edge_high):
    start = loose(pos)
    even = lax.rem(lax.axis_index("gx"), 2) == 0
    blocks = temp.shape[1] // LANES
    half = lax.broadcasted_iota(jnp.int32, (SUB, LANES), 1) < NZ
    for which, (own, native) in enumerate(((temp, native_t), (mat, native_m))):
        for at in range(blocks):
            lanes = slice(at * LANES, (at + 1) * LANES)
            first = at * SLABX
            side = slice(SIDE_ROWS + at * SUB, SIDE_ROWS + (at + 1) * SUB)
            value = jnp.where(even, outer[side, :], inner[side, :])
            native[first : first + SUB, :] = roll(value, -4, 0) if which else value
            for g in range(TE // SUB):
                value = own[g * SUB : (g + 1) * SUB, lanes].astype(jnp.float32)
                native[pl.ds(start + first + HALO + g * SUB, SUB), :] = value
            value = jnp.where(even, inner[side, :], outer[side, :])
            native[pl.ds(start + first + HALO + TE, SUB), :] = roll(value, -4, 0) if which else value
    for at in range(blocks // 2):
        for g in range(SLABX // SUB):
            halves = []
            for native in (native_t, native_m):
                lower = native[at * SLABX + g * SUB : at * SLABX + (g + 1) * SUB, :]
                upper_at = (blocks // 2 + at) * SLABX + g * SUB
                upper = native[upper_at : upper_at + SUB, :]
                lower_r, upper_r = roll(lower, NZ, 1), roll(upper, NZ, 1)
                halves.append((lower, lower_r, upper, upper_r))
            for odd in range(2):
                y = 2 * at + odd
                temps, mats = (jnp.where(half, v[odd], v[3 - odd]) for v in halves)
                places = [(y + HALO, temps, mats)]
                if y >= HALF - HALO:
                    places.append((y - HALF + HALO, halves[0][1 - odd], halves[1][1 - odd]))
                if y < HALO:
                    places.append((y + HALF + HALO, halves[0][2 + odd], halves[1][2 + odd]))
                for block, t, m in places:
                    rows = slice(ROW0 + block * SLABX + g * SUB, ROW0 + block * SLABX + (g + 1) * SUB)
                    t_ext[rows] = t
                    k0_ext[rows] = lookup(k0_table, m)
                    b_ext[rows] = lookup(beta_table, m)
                if y < HALO:
                    rows = slice(y * SLABX + g * SUB, y * SLABX + (g + 1) * SUB)
                    edge_low[rows] = jnp.where(half, halves[0][odd], halves[1][1 - odd])
                if y >= HALF - HALO:
                    first = (y - HALF + HALO) * SLABX + g * SUB
                    edge_high[first : first + SUB] = jnp.where(half, halves[0][2 + odd], halves[1][3 - odd])
    even = lax.rem(lax.axis_index("gy"), 2) == 0
    edge_in[...] = jnp.where(even, edge_high[...], edge_low[...])
    edge_out[...] = jnp.where(even, edge_low[...], edge_high[...])


def fill_maps(chips, pos, cell_at, cell_of):
    width_gy = 2 * chips
    tiles = width_gy * TILES
    i = lax.axis_index("gx")
    j = lax.axis_index("gy")
    rows_gx = lax.axis_size("gx")
    for at in range(2 * (2 * width_gy + 2)):
        for which in range(3):
            cell_at[which, at] = tiles
    for which, by in enumerate((0, -1, 1)):
        row = i + by
        valid = (row >= 0) & (row < rows_gx)
        first = jnp.clip(row, 0, rows_gx - 1) * tiles
        for part in range(width_gy):
            dev = part_device(part, chips, j)
            for t in range(TILES):
                tile = first + dev * TILES + t
                cell = (pos[tile, 1] + 1) * 2 + pos[tile, 2]
                slot = part * TILES + t
                cell_of[which, slot] = cell
                cell_at[which, cell] = jnp.where(valid, slot, tiles)


def part_device(part, chips, j):
    mate = j + 1 - 2 * lax.rem(j, 2)
    base = j if part < chips else mate
    return lax.rem(base - 2 * (part % chips) + 2 * chips, 2 * chips)


def sweep_kernel(chips, pos, *refs):
    width_gy = 2 * chips
    tiles = width_gy * TILES
    none = tiles
    half = 2 * chips - 1
    halos = refs[2 * half : 2 * half + width_gy]
    pot, slope, cell_at, cell_of, pa, pb, la, lb, ua, ub, s_c, s_l, s_u, sems, pot_sem = refs[2 * half + width_gy :]
    bodies = []
    for side in (refs[:half], refs[half : 2 * half]):
        bodies.append(((side[0], 0), (side[0], TE * ROW)))
        bodies += [((side[at], 0), (side[at + 1], 0)) for at in range(1, half, 2)]
    i = lax.axis_index("gx")
    j = lax.axis_index("gy")
    rows_gx = lax.axis_size("gx")
    zero = jnp.zeros((SUB, LANES), jnp.float32)

    moves = []
    for part in range(width_gy):
        at = 0
        pieces = [(*bodies[part][0], pa, part * C_SIZE + 1, TE), (*bodies[part][1], s_c, part * TE, TE)]
        for target, first, count in (
            (la, part * L_SIZE, LOW[0]),
            (s_l, part * LOW[1], LOW[1]),
            (None, 0, LOW[2]),
            (ua, part * U_SIZE + 1, HIGH[0]),
            (s_u, part * HIGH[1], HIGH[1]),
        ):
            if target is not None:
                pieces.append((halos[part], at, target, first, count))
            at += count * ROW
        for source, start, target, first, count in pieces:
            move = pltpu.make_async_copy(
                source.at[start : start + count * ROW],
                target.at[ROW0 + first * ROW : ROW0 + (first + count) * ROW],
                sems.at[len(moves)],
            )
            move.start()
            moves.append(move)

    fill_maps(chips, pos, cell_at, cell_of)

    def row_of(slot, size, plane):
        return ROW0 + (lax.div(slot, TILES) * size + plane) * ROW + lax.rem(slot, TILES)

    def plane_at(ref, row):
        return ref[pl.ds(row, SUB, stride=TILES), :]

    def put_plane(ref, row, value):
        ref[pl.ds(row, SUB, stride=TILES), :] = value

    for ref, count in ((pa, C_SIZE), (pb, C_SIZE), (la, L_SIZE), (lb, L_SIZE), (ua, U_SIZE), (ub, U_SIZE)):
        first = ROW0 + width_gy * count * ROW
        for row in range(first, first + count * ROW, SUB):
            ref[row : row + SUB] = zero

    def clear(at, carry):
        slope[pl.ds(pl.multiple_of(at * SUB, SUB), SUB), :] = zero
        return carry

    lax.fori_loop(0, slope.shape[0] // SUB, clear, 0, unroll=8)
    for move in moves:
        move.wait()

    lane = lax.broadcasted_iota(jnp.int32, (SUB, LANES), 1)
    sub = lax.broadcasted_iota(jnp.int32, (SUB, LANES), 0)
    depth = lane % TE
    first_y, last_y = lane < TE, lane >= LANES - TE
    first_sub, last_sub = sub == 0, sub == SUB - 1
    first_z, last_z = depth == 0, depth == TE - 1

    def y_plus(ref, own, row, ghost_row):
        turned = jnp.where(last_sub, plane_at(ref, ghost_row), plane_at(ref, row))
        return roll(jnp.where(first_y, turned, own), -TE, 1)

    def y_minus(ref, own, row, ghost_row):
        turned = jnp.where(first_sub, plane_at(ref, ghost_row), plane_at(ref, row))
        return roll(jnp.where(last_y, turned, own), TE, 1)

    def around(which, slot):
        cell = cell_of[which, slot]
        upper = cell % 2
        y_m = cell_at[which, cell - 2]
        y_p = cell_at[which, cell + 2]
        z = cell_at[which, cell + 1 - 2 * upper]
        turn = jnp.where(upper == 1, LANES + 1 - TE, TE - 1)
        meets = jnp.where(upper == 1, 0, TE - 1) == depth
        return cell, (slot, y_m, y_p, z, turn, meets)

    bufs = ((pa, la, ua), (pb, lb, ub))
    for k in range(SWEEPS):
        weight = cheb_weight(k, SWEEPS)
        keep, gain = 1.0 - weight, weight / (6.0 + EPS)
        (c_src, l_src, u_src), (c_dst, l_dst, u_dst) = bufs[k % 2], bufs[(k + 1) % 2]

        def ghosts(slot, carry):
            cell = cell_of[0, slot]
            below, above = cell_at[1, cell], cell_at[2, cell]
            over, under = cell_at[0, cell_of[1, slot]], cell_at[0, cell_of[2, slot]]
            put_plane(c_src, row_of(slot, C_SIZE, 0), plane_at(l_src, row_of(below, L_SIZE, LOW[0] - 1)))
            put_plane(c_src, row_of(slot, C_SIZE, TE + 1), plane_at(u_src, row_of(above, U_SIZE, 1)))
            put_plane(l_src, row_of(slot, L_SIZE, LOW[0]), plane_at(c_src, row_of(over, C_SIZE, 1)))
            put_plane(u_src, row_of(slot, U_SIZE, 0), plane_at(c_src, row_of(under, C_SIZE, TE)))
            return carry

        lax.fori_loop(0, tiles, ghosts, 0)

        def relax(src, dst, size, slots, first, count, s_ref, s_size, s_first):
            slot, y_m, y_p, z, turn, meets = slots
            row, s_row = row_of(slot, size, first), row_of(slot, s_size, s_first)
            up, down = row + TILES, row - TILES
            row_m, row_p = row_of(y_m, size, first) + (ROW - TILES), row_of(y_p, size, first) - (ROW - TILES)
            row_z = row_of(z, size, first)
            before, own = plane_at(src, row - ROW), plane_at(src, row)
            for step in range(0, count * ROW, ROW):
                after = plane_at(src, row + (step + ROW))
                total = (before + after) + plane_at(s_ref, s_row + step)
                total = total + y_minus(src, own, down + step, row_m + step)
                total = total + y_plus(src, own, up + step, row_p + step)
                total = total + jnp.where(last_z, 0.0, roll(own, -1, 1))
                total = total + jnp.where(first_z, 0.0, roll(own, 1, 1))
                ghost = pltpu.roll(plane_at(src, row_z + step), turn, 1)
                put_plane(dst, row + step, keep * own + gain * (total + jnp.where(meets, ghost, 0.0)))
                before, own = own, after

        def sweep_tile(slot, carry):
            _, slots = around(0, slot)
            relax(c_src, c_dst, C_SIZE, slots, 1, TE, s_c, TE, 0)
            _, slots = around(1, slot)
            count = LOW[0] - 1 - k
            relax(l_src, l_dst, L_SIZE, slots, LOW[0] - count, count, s_l, LOW[1], LOW[1] - count)
            _, slots = around(2, slot)
            relax(u_src, u_dst, U_SIZE, slots, 1, HIGH[0] - 1 - k, s_u, HIGH[1], 0)
            return carry

        lax.fori_loop(0, tiles, sweep_tile, 0)

    field, f_l, f_u = bufs[SWEEPS % 2]
    pot_move = pltpu.make_async_copy(field.at[ROW0 + ROW : ROW0 + (TE + 1) * ROW], pot, pot_sem.at[0])
    pot_move.start()

    def squares(ref, size, slots, local, x, first, count, x_last=None):
        slot, _, y_p, z, turn, meets = slots
        row = row_of(slot, size, first)
        up, row_p, row_z = row + TILES, row_of(y_p, size, first) - (ROW - TILES), row_of(z, size, first)
        target = (local * SLABX + x) * SUB
        own = plane_at(ref, row)
        for p in range(count):
            last = p == count - 1 and x_last is not None
            after = x_last if last else plane_at(ref, row + (p + 1) * ROW)
            d_x = after - own
            d_y = y_plus(ref, own, up + p * ROW, row_p + p * ROW) - own
            ghost = jnp.where(meets, pltpu.roll(plane_at(ref, row_z + p * ROW), turn, 1), 0.0)
            d_z = jnp.where(last_z, ghost, roll(own, -1, 1)) - own
            rows = pl.ds(pl.multiple_of(target + p * SUB, SUB), SUB)
            slope[rows, :] = d_x * d_x + d_y * d_y + d_z * d_z
            own = after

    def slope_tile(slot, carry):
        for which in range(3):
            cell, slots = around(which, slot)
            local, inside = window(which, cell, i, j, rows_gx)

            @pl.when(inside)
            def _():
                if which == 0:
                    above = plane_at(f_u, row_of(cell_at[2, cell], U_SIZE, 1))
                    squares(field, C_SIZE, slots, local, HALO, 1, TE, above)
                elif which == 1:
                    centre = plane_at(field, row_of(cell_at[0, cell], C_SIZE, 1))
                    squares(f_l, L_SIZE, slots, local, HALO - 2, LOW[0] - 2, 2, centre)
                else:
                    squares(f_u, U_SIZE, slots, local, HALO + TE, 1, 2)

        return carry

    lax.fori_loop(0, tiles, slope_tile, 0)
    pot_move.wait()


def window(which, cell, i, j, rows_gx):
    local = cell - 4 * j
    inside = (local >= 0) & (local < 8)
    if which > 0:
        row = i - 1 if which == 1 else i + 1
        inside = inside & (row >= 0) & (row < rows_gx)
    return local, inside


def slab_steps_kernel(chips, pos, k0_table, beta_table, *refs):
    width_gy = 2 * chips
    tiles = width_gy * TILES
    halos = refs[width_gy : 2 * width_gy]
    slope, t_in, k0_in, b_in, y_in, y_out, temp_out = refs[2 * width_gy : 2 * width_gy + 7]
    mine, bundle = refs[2 * width_gy + 7 : 2 * width_gy + 9]
    across = refs[2 * width_gy + 9 : 2 * width_gy + 8 + chips]
    heat, q_ext, state_a, state_b, k0_all, b_all, blocks, sigmas, sems = refs[2 * width_gy + 8 + chips :]
    moves = []
    for part in range(width_gy):
        start = 2 * TE * ROW if part % chips == 0 else 0
        source = refs[part].at[start : start + TE * ROW]
        moves.append(pltpu.make_async_copy(source, sigmas.at[part], sems.at[part]))
        moves[-1].start()
    i = lax.axis_index("gx")
    j = lax.axis_index("gy")
    rows_gx = lax.axis_size("gx")
    lane = lax.broadcasted_iota(jnp.int32, (SUB, LANES), 1)
    zero = jnp.zeros((SUB, LANES), jnp.float32)

    quarter = [(lane >= q * TE) & (lane < (q + 1) * TE) for q in range(3)]

    def pick(parts):
        return jnp.where(
            quarter[0], parts[0], jnp.where(quarter[1], parts[1], jnp.where(quarter[2], parts[2], parts[3]))
        )

    def turned(value, by):
        return value if by % 4 == 0 else roll(value, by * TE, 1)

    def rows_of(block, g):
        first = ROW0 + block * SLABX + g * SUB
        if not isinstance(first, int):
            first = pl.multiple_of(first, SUB)
        return pl.ds(first, SUB)

    groups = SLABX // SUB

    sub = lax.broadcasted_iota(jnp.int32, (SUB, LANES), 0)
    half = lane < NZ
    no_z = lane % NZ == NZ - 1
    low_x = (sub == HALO - 1) & (i == 0), (sub == HALO) & (i == 0)
    high_x = (sub == (HALO + TE - 1) % SUB) & (i == rows_gx - 1)
    low_y, high_y = half & (j == 0), (lane >= NZ) & (j == width_gy - 1)

    def inverse(value):
        near = pl.reciprocal(value, approx=True)
        near = near * (2.0 - value * near)
        return near * (2.0 - value * near)

    def both_of(block, g, by=0):
        first = 2 * (ROW0 + block * SLABX + g * SUB + by)
        return pl.ds(first, SUB, stride=2), pl.ds(first + 1, SUB, stride=2)

    def load(ref, block, by=0):
        places = [both_of(block, g, by) for g in range(groups)]
        return [ref[at, :] for at, _ in places], [ref[at, :] for _, at in places]

    def store(ref, block, g, temp, cond=None):
        first, second = both_of(block, g)
        ref[first, :] = temp
        if cond is not None:
            ref[second, :] = cond

    even = lax.rem(j, 2) == 0

    def begin(block, low, at):
        values = []
        for g in range(groups):
            rows = rows_of(block, g)
            temp, k0, beta = t_in[rows], k0_in[rows], b_in[rows]
            if low is not None:
                place = slice(at * SLABX + g * SUB, at * SLABX + (g + 1) * SUB)
                value = jnp.where(even, *((y_out[place], y_in[place])[:: 1 if low else -1]))
                swapped = roll(value, NZ, 1)
                if low:
                    temp = jnp.where(half, value, temp)
                    k0 = jnp.where(half, lookup(k0_table, swapped), k0)
                    beta = jnp.where(half, lookup(beta_table, swapped), beta)
                else:
                    temp = jnp.where(half, temp, swapped)
                    k0 = jnp.where(half, k0, lookup(k0_table, value))
                    beta = jnp.where(half, beta, lookup(beta_table, value))
            values.append((rows, temp, k0, beta, k0 * inverse(1.0 + beta * temp * temp)))
        for g, (rows, temp, k0, beta, cond) in enumerate(values):
            k0_all[rows], b_all[rows] = k0, beta
            store(state_a, block, g, temp, cond)

    for e in range(HALO):
        begin(e, True, e)
        begin(YBLOCKS - HALO + e, False, e)

    def begin_inner(block, carry):
        begin(block, None, 0)
        return carry

    lax.fori_loop(HALO, YBLOCKS - HALO, begin_inner, 0, unroll=4)

    def clear(at, carry):
        heat[pl.ds(pl.multiple_of(at * SUB, SUB), SUB), :] = zero
        return carry

    lax.fori_loop(0, heat.shape[0] // SUB, clear, 0, unroll=8)
    for move in moves:
        move.wait()
    low_at, high_at = (LOW[0] + LOW[1]) * ROW, LOW_ROWS + (HIGH[0] + HIGH[1]) * ROW
    for part in range(width_gy):
        dev = part_device(part, chips, j)
        for t in range(TILES):
            for which, by in enumerate((0, -1, 1)):
                tile = jnp.clip(i + by, 0, rows_gx - 1) * tiles + dev * TILES + t
                cell = (pos[tile, 1] + 1) * 2 + pos[tile, 2]
                local, inside = window(which, cell, i, j, rows_gx)
                source, start, x, count = (
                    (sigmas.at[part], 0, HALO, TE),
                    (halos[part], low_at, HALO - 2, 2),
                    (halos[part], high_at, HALO + TE, 2),
                )[which]

                @pl.when(inside)
                def _():
                    def plane(p, carry):
                        rows = pl.ds(pl.multiple_of((local * SLABX + x + p) * SUB, SUB), SUB)
                        at = pl.multiple_of(start + p * ROW, SUB)
                        sigma = source[pl.ds(at + t, SUB, stride=TILES), :]
                        heat[rows, :] = sigma * slope[rows, :]
                        return carry

                    lax.fori_loop(0, count, plane, 0, unroll=count)

    def place_heat(at, carry):
        first = at - 1
        col, yq = lax.div(first * 4 + TE, TE), lax.rem(first * 4 + TE, TE) // 4
        for g in range(groups):
            cells = [
                heat[pl.ds(pl.multiple_of(((2 * col + c) * SLABX + g * SUB) * SUB, SUB) + yq, SUB, stride=SUB), :]
                for c in range(4)
            ]
            for r in range(4):
                block = 4 * first + r + HALO + 1
                q_ext[rows_of(block, g)] = pick([turned(cells[c], c - r) for c in range(4)])
        return carry

    lax.fori_loop(0, HALF // 4 + 2, place_heat, 0, unroll=2)

    for step in range(CSWEEPS):
        src, dst = (state_a, state_b)[:: 1 if step % 2 == 0 else -1]

        def y_fluxes(block, now, ahead):
            closed = (low_y & (block == HALO - 1)) | (high_y & (block == HALO + HALF - 1))
            return [flux(now, ahead, g, closed) for g in range(groups)]

        def flux(now, other, g, closed=None):
            value = (now[1][g] + other[1][g]) * (other[0][g] - now[0][g])
            return value if closed is None else jnp.where(closed, 0.0, value)

        def advance(block, carry):
            now, before = carry
            ahead = load(src, block + 1)
            flux_y = y_fluxes(block, now, ahead)
            x_p, x_m = load(src, block, 1), load(src, block, -1)
            results = []
            for g in range(groups):
                temp, cond = now[0][g], now[1][g]
                up = flux(now, x_p, g, {0: low_x[0], groups - 1: high_x}.get(g))
                down = flux(now, x_m, g, {0: low_x[1]}.get(g))
                flux_z = (cond + roll(cond, -1, 1)) * (roll(temp, -1, 1) - temp)
                flux_z = jnp.where(no_z, 0.0, flux_z)
                div = (flux_y[g] - before[g]) + (up + down) + (flux_z - roll(flux_z, 1, 1))
                new = temp + DT * (0.5 * div + q_ext[rows_of(block + 1, g)])
                if step < CSWEEPS - 1:
                    rows = rows_of(block, g)
                    results.append((new, k0_all[rows] * inverse(1.0 + b_all[rows] * new * new)))
                else:
                    results.append((new,))
            for g in range(groups):
                store(dst, block, g, *results[g])
            return ahead, flux_y

        first, second = load(src, 0), load(src, 1)
        lax.fori_loop(1, YBLOCKS - 1, advance, (second, y_fluxes(0, first, second)), unroll=6)
    final = state_b if CSWEEPS % 2 else state_a

    def give_out(yq, carry):
        for g in range(TE // SUB):
            x = slice(g * SUB, (g + 1) * SUB)
            turns = []
            for r in range(4):
                value = final[both_of(HALO + 4 * yq + r, g, HALO)[0], :]
                turns.append([turned(value, by) for by in range(4)])
            for pair in range(2):
                even, odd = turns[2 * pair], turns[2 * pair + 1]
                lower = (2 * yq + pair) * LANES
                upper = lower + temp_out.shape[1] // 2
                temp_out[x, pl.ds(pl.multiple_of(lower, LANES), LANES)] = jnp.where(half, even[0], odd[2])
                temp_out[x, pl.ds(pl.multiple_of(upper, LANES), LANES)] = jnp.where(half, even[2], odd[0])
            for c in range(4):
                value = pick([turns[r][(r - c) % 4] for r in range(4)])
                blocks[pl.ds((c * TE + g * SUB) * SUB + yq, SUB, stride=SUB), :] = value
        return carry

    lax.fori_loop(0, HALF // 4, give_out, 0, unroll=2)
    places = []
    mate = j + 1 - 2 * lax.rem(j, 2)
    targets = [(mine, 0, j)] + [(across[d - 1], 0, j + 2 * d) for d in range(1, chips)]
    targets += [(bundle, d * TE * ROW, mate + 2 * d) for d in range(chips)]
    for target, first, to in targets:
        dev = lax.rem(to, width_gy)
        for t in range(TILES):
            tile = i * tiles + dev * TILES + t
            col = pos[tile, 1] - 2 * j
            cell = jnp.clip(col, 0, 1) * 2 + pos[tile, 2]
            places.append((target, first + t, cell, (col >= 0) & (col < 2)))

    def pack(p, carry):
        values = []
        for _, _, cell, here in places:
            value = blocks[pl.ds(pl.multiple_of((cell * TE + p) * SUB, SUB), SUB), :]
            values.append(jnp.where(here, value, 0.0))
        for (target, first, _, _), value in zip(places, values):
            target[pl.ds(pl.multiple_of(p * ROW, ROW) + first, SUB, stride=TILES), :] = value
        return carry

    lax.fori_loop(0, TE, pack, 0, unroll=4)


def shifted(value, axis, by, wrap=False):
    count = lax.axis_size(axis)
    pairs = [(d, (d + by) % count) for d in range(count) if wrap or 0 <= d + by < count]
    return lax.ppermute(value, axis, pairs)


def with_partner(value, axis, first):
    count = lax.axis_size(axis)
    pairs = [(d, d + 1) for d in range(first, count - 1, 2)]
    return lax.ppermute(value, axis, pairs + [(high, low) for low, high in pairs])


def from_mate(value):
    return lax.ppermute(value, "gy", [(d, d ^ 1) for d in range(lax.axis_size("gy"))])


def to_rows(value):
    return value.reshape(TILES, -1, LANES).transpose(1, 0, 2).reshape(-1, LANES)


def from_rows(value):
    return value.reshape(-1, TILES, LANES).transpose(1, 0, 2).reshape(TILES, -1)


def to_other_core(value, by):
    count = lax.axis_size("gy")
    return lax.ppermute(value, "gy", [(at, ((at ^ 1) + 2 * by) % count) for at in range(count)])


VMEM = pl.BlockSpec(memory_space=pltpu.VMEM)
SMEM = pl.BlockSpec(memory_space=pltpu.SMEM)
HBM = pl.BlockSpec(memory_space=pltpu.HBM)
ANY = pl.BlockSpec(memory_space=pl.ANY)
PARAMS = pltpu.CompilerParams(vmem_limit_bytes=32 * 1024 * 1024)


def on_device(
    phi_init,
    source,
    tile_mat,
    tile_pos,
    neighbours,
    sigma_table,
    temp_init,
    slab_mat,
    k0_table,
    beta_table,
):
    f32 = jnp.float32
    width_gy = lax.axis_size("gy")
    chips = width_gy // 2
    tiles = width_gy * TILES
    size_x, width = temp_init.shape
    edge_rows = width // LANES * SUB

    def rows(count):
        return jax.ShapeDtypeStruct((count, LANES), f32)

    phi = to_rows(phi_init)
    phis = [shifted(phi, "gy", 2 * d, True) for d in range(1, chips)]
    body, s, sigma, inner, outer = pl.pallas_call(
        prep_kernel,
        out_shape=(
            rows(3 * TE * ROW),
            rows(TE * ROW),
            rows(TE * ROW),
            rows(SIDE_ROWS + edge_rows),
            rows(SIDE_ROWS + edge_rows),
        ),
        in_specs=[SMEM] + [HBM] * 5,
        out_specs=(VMEM,) * 5,
        scratch_shapes=[
            pltpu.VMEM((TE * ROW, LANES), f32),
            pltpu.VMEM((TE * ROW, LANES), jnp.int32),
            pltpu.VMEM((2, SUB, width), f32),
            pltpu.VMEM((2, SUB, width), jnp.int32),
            pltpu.SemaphoreType.DMA((7,)),
        ],
        compiler_params=pltpu.CompilerParams(vmem_limit_bytes=62 * 1024 * 1024),
        name="prep",
    )(sigma_table, phi, to_rows(source), to_rows(tile_mat), temp_init, slab_mat)
    bodies = [body]
    for there, d in zip(phis, range(1, chips)):
        bodies += [there, shifted(s, "gy", 2 * d, True)]
    bodies += [from_mate(part) for part in bodies]
    inner, outer = with_partner(inner, "gx", 0), with_partner(outer, "gx", 1)

    halo = pl.pallas_call(
        relay_kernel,
        out_shape=rows(LOW_ROWS + HIGH_ROWS),
        in_specs=[VMEM] * 2,
        out_specs=VMEM,
        compiler_params=PARAMS,
        name="relay",
    )(inner, outer)
    halos = [halo] + [shifted(halo, "gy", 2 * d, True) for d in range(1, chips)]
    sigmas = [bodies[0]] + [shifted(sigma, "gy", 2 * d, True) for d in range(1, chips)]
    sigmas += [bodies[2 * chips - 1]] + [to_other_core(sigma, d) for d in range(1, chips)]

    native = pltpu.VMEM((width // LANES * SLABX + SUB, LANES), f32)
    t_ext, k0_ext, b_ext, edge_in, edge_out = pl.pallas_call(
        slab_kernel,
        out_shape=(rows(SLAB_ROWS),) * 3 + (rows(HALO * SLABX),) * 2,
        in_specs=[SMEM] * 3 + [VMEM] * 4,
        out_specs=(VMEM,) * 5,
        scratch_shapes=[native, native] + [pltpu.VMEM((HALO * SLABX, LANES), f32)] * 2,
        compiler_params=PARAMS,
        name="slab_prep",
    )(tile_pos, k0_table, beta_table, temp_init, slab_mat, inner, outer)
    y_in, y_out = with_partner(edge_in, "gy", 0), with_partner(edge_out, "gy", 1)
    *halos[1:], y_in = lax.optimization_barrier((*halos[1:], y_in))
    halos = halos + [from_mate(part) for part in halos]

    def fields(count):
        return pltpu.VMEM((2 * ROW0 + (width_gy + 1) * count * ROW, LANES), f32)

    pot, slope = pl.pallas_call(
        functools.partial(sweep_kernel, chips),
        out_shape=(rows(TE * ROW), rows(8 * SLABX * SUB)),
        in_specs=[SMEM] + [ANY] * (len(bodies) + width_gy),
        out_specs=(ANY, VMEM),
        scratch_shapes=[
            pltpu.SMEM((3, 2 * (2 * width_gy + 2)), jnp.int32),
            pltpu.SMEM((3, tiles), jnp.int32),
            fields(C_SIZE), fields(C_SIZE), fields(L_SIZE), fields(L_SIZE), fields(U_SIZE), fields(U_SIZE),
            fields(TE), fields(LOW[1]), fields(HIGH[1]),
            pltpu.SemaphoreType.DMA((6 * width_gy,)),
            pltpu.SemaphoreType.DMA((1,)),
        ],
        compiler_params=PARAMS,
        name="sweeps",
    )(tile_pos, *bodies, *halos)

    temp, mine, bundle, *across = pl.pallas_call(
        functools.partial(slab_steps_kernel, chips),
        out_shape=(jax.ShapeDtypeStruct((size_x, width), f32), rows(TE * ROW), rows(chips * TE * ROW))
        + (rows(TE * ROW),) * (chips - 1),
        in_specs=[SMEM] * 3 + [ANY] * width_gy + [VMEM] * (width_gy + 6),
        out_specs=(VMEM,) * (2 + chips),
        scratch_shapes=[pltpu.VMEM((8 * SLABX * SUB, LANES), f32)]
        + [pltpu.VMEM((SLAB_ROWS + 3 * SLABX, LANES), f32)]
        + [pltpu.VMEM((2 * SLAB_ROWS, LANES), f32)] * 2
        + [pltpu.VMEM((SLAB_ROWS, LANES), f32)] * 2
        + [pltpu.VMEM((4 * TE * SUB, LANES), f32), pltpu.VMEM((width_gy, TE * ROW, LANES), f32)]
        + [pltpu.SemaphoreType.DMA((width_gy,))],
        compiler_params=PARAMS,
        name="slab_steps",
    )(tile_pos, k0_table, beta_table, *sigmas, *halos, slope, t_ext, k0_ext, b_ext, y_in, y_out)
    got = from_mate(bundle).reshape(chips, TE * ROW, LANES)
    tile_temps = mine + got[0]
    for d in range(1, chips):
        tile_temps = tile_temps + shifted(across[d - 1] + got[d], "gy", 2 * d, True)
    return from_rows(pot), temp, from_rows(tile_temps)


def solution(mesh):
    placed = (
        P(("gx", "gy"), None),
        P(("gx", "gy"), None),
        P(("gx", "gy"), None),
        P(),
        P(("gx", "gy"), None),
        P(),
        P("gx", "gy"),
        P("gx", "gy"),
        P(),
        P(),
    )
    return jax.shard_map(
        on_device,
        mesh=mesh,
        in_specs=placed,
        out_specs=(P(("gx", "gy"), None), P("gx", "gy"), P(("gx", "gy"), None)),
        check_vma=False,
    )
```

```python
import functools
import math

import jax
import jax.numpy as jnp
from jax import lax
from jax.experimental import pallas as pl
from jax.experimental.pallas import tpu as pltpu
from jax.sharding import PartitionSpec as P

TE = 32
SWEEPS = 4
CSWEEPS = 3
NZ = 64
EPS = 2.0
DT = 0.15
LANES = 128
SUB = 8
TILES = 2
ROW = SUB * TILES

LOW = (SWEEPS + 2, SWEEPS + 1, 2)
HIGH = (SWEEPS + 3, SWEEPS + 2, 2)
LOW_ROWS = sum(LOW) * ROW
HIGH_ROWS = sum(HIGH) * ROW
SIDE_ROWS = max(LOW_ROWS, HIGH_ROWS)
SLABX = TE + SUB
HALO = CSWEEPS
HALF = TE
YBLOCKS = HALF + 2 * HALO
C_SIZE, L_SIZE, U_SIZE = TE + 2, LOW[0] + 1, HIGH[0] + 1
ROW0 = ROW
SLAB_ROWS = ROW0 + YBLOCKS * SLABX + ROW0


def cheb_weight(step, count):
    return 1.0 / (1.0 + 0.75 * math.cos(math.pi * (2 * step + 1) / (2 * count)))


def lookup(table, ids):
    out = jnp.full(ids.shape, table[3], jnp.float32)
    for which in (2, 1, 0):
        out = jnp.where(ids == which, table[which], out)
    return out


def roll(value, by, axis):
    return pltpu.roll(value, by % value.shape[axis], axis)


def prep_kernel(table, pos, phi, src, mat, temp, slab, body, ready, sigma, inner, outer, src_v, mat_v, ends_t, ends_m, sems):
    rows = TE * ROW
    size_x, width = temp.shape
    moves = [(phi, body.at[0:rows]), (src, src_v), (mat, mat_v)]
    for which, first in enumerate((0, size_x - SUB)):
        moves.append((temp.at[first : first + SUB], ends_t.at[which]))
        moves.append((slab.at[first : first + SUB], ends_m.at[which]))
    moves = [pltpu.make_async_copy(*move, sems.at[at]) for at, move in enumerate(moves)]
    for move in moves:
        move.start()
    for move in moves:
        move.wait()
    sigma[...] = lookup(table, mat_v[...])
    body[rows : 2 * rows] = src_v[...] / sigma[...]
    first = (lax.axis_index("gx") * lax.axis_size("gy") + lax.axis_index("gy")) * TILES
    for t in range(TILES):

        @pl.when(pos[2, first + t] == 1)
        def _():
            def plane(p, carry):
                for ref, start in ((body, 0), (body, rows), (sigma, 0)):
                    at = pl.ds(pl.multiple_of(p * ROW, ROW) + (start + t), SUB, stride=TILES)
                    ref[at, :] = roll(ref[at, :], TE, 1)
                return carry

            lax.fori_loop(0, TE, plane, 0, unroll=8)

    ready[...] = body[0 : 2 * rows]
    body[2 * rows : 3 * rows] = sigma[...]
    even = lax.rem(lax.axis_index("gx"), 2) == 0

    @pl.when(even)
    def _():
        fill_sides(body, sigma, ends_t, ends_m, inner, outer)

    @pl.when(jnp.logical_not(even))
    def _():
        fill_sides(body, sigma, ends_t, ends_m, outer, inner)


def fill_sides(body, sigma, ends_t, ends_m, up, down):
    rows = TE * ROW
    width = ends_t.shape[2]
    at_up, at_down = 0, 0
    for ref, first in ((body, 0), (body, rows), (sigma, 0)):
        which = (first // rows) if ref is body else 2
        size = LOW[which] * ROW
        up[at_up : at_up + size] = ref[first + rows - size : first + rows]
        at_up += size
        size = HIGH[which] * ROW
        down[at_down : at_down + size] = ref[first : first + size]
        at_down += size
    sub = lax.broadcasted_iota(jnp.int32, (SUB, LANES), 0)
    for at in range(width // LANES):
        lanes = slice(at * LANES, (at + 1) * LANES)
        t_low, m_low = ends_t[0, :, lanes], ends_m[0, :, lanes].astype(jnp.float32)
        t_high, m_high = ends_t[1, :, lanes], ends_m[1, :, lanes].astype(jnp.float32)
        first = at * SUB
        up[SIDE_ROWS + first : SIDE_ROWS + first + SUB] = jnp.where(sub < 4, roll(t_high, HALO, 0), roll(m_high, -1, 0))
        down[SIDE_ROWS + first : SIDE_ROWS + first + SUB] = jnp.where(sub < 4, t_low, roll(m_low, 4, 0))


def relay_kernel(inner, outer, halo):
    def join(low, high):
        halo[0:LOW_ROWS] = low[0:LOW_ROWS]
        halo[LOW_ROWS:] = high[0:HIGH_ROWS]

    even = lax.rem(lax.axis_index("gx"), 2) == 0
    pl.when(even)(lambda: join(outer, inner))
    pl.when(jnp.logical_not(even))(lambda: join(inner, outer))


def loose(pos):
    return jnp.minimum(pos[0, 0], 0)


def slab_kernel(pos, k0_table, beta_table, temp, mat, inner, outer, t_ext, k0_ext, b_ext, edge_in, edge_out, native_t, native_m, edge_low, edge_high):
    start = loose(pos)
    even = lax.rem(lax.axis_index("gx"), 2) == 0
    blocks = temp.shape[1] // LANES
    half = lax.broadcasted_iota(jnp.int32, (SUB, LANES), 1) < NZ
    for which, (own, native) in enumerate(((temp, native_t), (mat, native_m))):
        for at in range(blocks):
            lanes = slice(at * LANES, (at + 1) * LANES)
            first = at * SLABX
            side = slice(SIDE_ROWS + at * SUB, SIDE_ROWS + (at + 1) * SUB)
            value = jnp.where(even, outer[side, :], inner[side, :])
            native[first : first + SUB, :] = roll(value, -4, 0) if which else value
            for g in range(TE // SUB):
                value = own[g * SUB : (g + 1) * SUB, lanes].astype(jnp.float32)
                native[pl.ds(start + first + HALO + g * SUB, SUB), :] = value
            value = jnp.where(even, inner[side, :], outer[side, :])
            native[pl.ds(start + first + HALO + TE, SUB), :] = roll(value, -4, 0) if which else value
    for at in range(blocks // 2):
        for g in range(SLABX // SUB):
            halves = []
            for native in (native_t, native_m):
                lower = native[at * SLABX + g * SUB : at * SLABX + (g + 1) * SUB, :]
                upper_at = (blocks // 2 + at) * SLABX + g * SUB
                upper = native[upper_at : upper_at + SUB, :]
                lower_r, upper_r = roll(lower, NZ, 1), roll(upper, NZ, 1)
                halves.append((lower, lower_r, upper, upper_r))
            for odd in range(2):
                y = 2 * at + odd
                temps, mats = (jnp.where(half, v[odd], v[3 - odd]) for v in halves)
                places = [(y + HALO, temps, mats)]
                if y >= HALF - HALO:
                    places.append((y - HALF + HALO, halves[0][1 - odd], halves[1][1 - odd]))
                if y < HALO:
                    places.append((y + HALF + HALO, halves[0][2 + odd], halves[1][2 + odd]))
                for block, t, m in places:
                    rows = slice(ROW0 + block * SLABX + g * SUB, ROW0 + block * SLABX + (g + 1) * SUB)
                    t_ext[rows] = t
                    k0_ext[rows] = lookup(k0_table, m)
                    b_ext[rows] = lookup(beta_table, m)
                if y < HALO:
                    rows = slice(y * SLABX + g * SUB, y * SLABX + (g + 1) * SUB)
                    edge_low[rows] = jnp.where(half, halves[0][odd], halves[1][1 - odd])
                if y >= HALF - HALO:
                    first = (y - HALF + HALO) * SLABX + g * SUB
                    edge_high[first : first + SUB] = jnp.where(half, halves[0][2 + odd], halves[1][3 - odd])
    even = lax.rem(lax.axis_index("gy"), 2) == 0
    edge_in[...] = jnp.where(even, edge_high[...], edge_low[...])
    edge_out[...] = jnp.where(even, edge_low[...], edge_high[...])


def fill_maps(chips, pos, cell_at, cell_of):
    width_gy = 2 * chips
    tiles = width_gy * TILES
    i = lax.axis_index("gx")
    j = lax.axis_index("gy")
    rows_gx = lax.axis_size("gx")
    for at in range(2 * (2 * width_gy + 2)):
        for which in range(3):
            cell_at[which, at] = tiles
    for which, by in enumerate((0, -1, 1)):
        row = i + by
        valid = (row >= 0) & (row < rows_gx)
        first = jnp.clip(row, 0, rows_gx - 1) * tiles
        for part in range(width_gy):
            dev = part_device(part, chips, j)
            for t in range(TILES):
                tile = first + dev * TILES + t
                cell = (pos[1, tile] + 1) * 2 + pos[2, tile]
                slot = part * TILES + t
                cell_of[which, slot] = cell
                cell_at[which, cell] = jnp.where(valid, slot, tiles)


def part_device(part, chips, j):
    mate = j + 1 - 2 * lax.rem(j, 2)
    base = j if part < chips else mate
    return lax.rem(base - 2 * (part % chips) + 2 * chips, 2 * chips)


def sweep_kernel(chips, pos, *refs):
    width_gy = 2 * chips
    tiles = width_gy * TILES
    none = tiles
    bodies, halos = refs[:width_gy], refs[width_gy : 2 * width_gy]
    pot, slope, cell_at, cell_of, pa, pb, la, lb, ua, ub, s_c, s_l, s_u, sems = refs[2 * width_gy :]
    i = lax.axis_index("gx")
    j = lax.axis_index("gy")
    rows_gx = lax.axis_size("gx")
    zero = jnp.zeros((SUB, LANES), jnp.float32)

    moves = []
    for part in range(width_gy):
        at = 0
        pieces = [(bodies[part], 0, pa, part * C_SIZE + 1, TE), (bodies[part], TE * ROW, s_c, part * TE, TE)]
        for target, first, count in (
            (la, part * L_SIZE, LOW[0]),
            (s_l, part * LOW[1], LOW[1]),
            (None, 0, LOW[2]),
            (ua, part * U_SIZE + 1, HIGH[0]),
            (s_u, part * HIGH[1], HIGH[1]),
        ):
            if target is not None:
                pieces.append((halos[part], at, target, first, count))
            at += count * ROW
        for source, start, target, first, count in pieces:
            move = pltpu.make_async_copy(
                source.at[start : start + count * ROW],
                target.at[ROW0 + first * ROW : ROW0 + (first + count) * ROW],
                sems.at[len(moves)],
            )
            move.start()
            moves.append(move)

    fill_maps(chips, pos, cell_at, cell_of)

    def row_of(slot, size, plane):
        return ROW0 + (lax.div(slot, TILES) * size + plane) * ROW + lax.rem(slot, TILES)

    def plane_at(ref, row):
        return ref[pl.ds(row, SUB, stride=TILES), :]

    def put_plane(ref, row, value):
        ref[pl.ds(row, SUB, stride=TILES), :] = value

    for ref, count in ((pa, C_SIZE), (pb, C_SIZE), (la, L_SIZE), (lb, L_SIZE), (ua, U_SIZE), (ub, U_SIZE)):
        first = ROW0 + width_gy * count * ROW
        for row in range(first, first + count * ROW, SUB):
            ref[row : row + SUB] = zero

    def clear(at, carry):
        slope[pl.ds(pl.multiple_of(at * SUB, SUB), SUB), :] = zero
        return carry

    lax.fori_loop(0, slope.shape[0] // SUB, clear, 0, unroll=8)
    for move in moves:
        move.wait()

    lane = lax.broadcasted_iota(jnp.int32, (SUB, LANES), 1)
    sub = lax.broadcasted_iota(jnp.int32, (SUB, LANES), 0)
    depth = lane % TE
    first_sub, last_sub = sub == 0, sub == SUB - 1
    first_z, last_z = depth == 0, depth == TE - 1

    def y_plus(ref, own, first_y, row, ghost_row):
        turned = jnp.where(last_sub, plane_at(ref, ghost_row), plane_at(ref, row))
        return roll(jnp.where(first_y, turned, own), -TE, 1)

    def y_minus(ref, own, last_y, row, ghost_row):
        turned = jnp.where(first_sub, plane_at(ref, ghost_row), plane_at(ref, row))
        return roll(jnp.where(last_y, turned, own), TE, 1)

    def z_plus(ref, own, ghost_row):
        return roll(jnp.where(first_z, plane_at(ref, ghost_row), own), -1, 1)

    def z_minus(ref, own, ghost_row):
        return roll(jnp.where(last_z, plane_at(ref, ghost_row), own), 1, 1)

    def around(which, slot):
        cell = cell_of[which, slot]
        upper = cell % 2
        beside = cell_at[which, cell + 1 - 2 * upper]
        near = (cell_at[which, cell - 2], cell_at[which, cell + 2])
        near += (jnp.where(upper == 1, beside, none), jnp.where(upper == 1, none, beside))
        quarter = lane // TE
        return cell, (slot, *near, quarter == upper, quarter == lax.rem(upper + 3, 4))

    bufs = ((pa, la, ua), (pb, lb, ub))
    for k in range(SWEEPS):
        weight = cheb_weight(k, SWEEPS)
        keep, gain = 1.0 - weight, weight / (6.0 + EPS)
        (c_src, l_src, u_src), (c_dst, l_dst, u_dst) = bufs[k % 2], bufs[(k + 1) % 2]

        def ghosts(slot, carry):
            cell = cell_of[0, slot]
            below, above = cell_at[1, cell], cell_at[2, cell]
            over, under = cell_at[0, cell_of[1, slot]], cell_at[0, cell_of[2, slot]]
            put_plane(c_src, row_of(slot, C_SIZE, 0), plane_at(l_src, row_of(below, L_SIZE, LOW[0] - 1)))
            put_plane(c_src, row_of(slot, C_SIZE, TE + 1), plane_at(u_src, row_of(above, U_SIZE, 1)))
            put_plane(l_src, row_of(slot, L_SIZE, LOW[0]), plane_at(c_src, row_of(over, C_SIZE, 1)))
            put_plane(u_src, row_of(slot, U_SIZE, 0), plane_at(c_src, row_of(under, C_SIZE, TE)))
            return carry

        lax.fori_loop(0, tiles, ghosts, 0)

        def relax(src, dst, size, slots, first, count, s_ref, s_size, s_first):
            slot, y_m, y_p, z_m, z_p, first_y, last_y = slots
            row, s_row = row_of(slot, size, first), row_of(slot, s_size, s_first)
            up, down = row + TILES, row - TILES
            row_m, row_p = row_of(y_m, size, first) + (ROW - TILES), row_of(y_p, size, first) - (ROW - TILES)
            row_zm, row_zp = row_of(z_m, size, first), row_of(z_p, size, first)
            before, own = plane_at(src, row - ROW), plane_at(src, row)
            for step in range(0, count * ROW, ROW):
                after = plane_at(src, row + (step + ROW))
                total = (before + after) + plane_at(s_ref, s_row + step)
                along_y = y_minus(src, own, last_y, down + step, row_m + step)
                along_y = along_y + y_plus(src, own, first_y, up + step, row_p + step)
                along_z = z_minus(src, own, row_zm + step) + z_plus(src, own, row_zp + step)
                put_plane(dst, row + step, keep * own + gain * (total + (along_y + along_z)))
                before, own = own, after

        def sweep_tile(slot, carry):
            _, slots = around(0, slot)
            relax(c_src, c_dst, C_SIZE, slots, 1, TE, s_c, TE, 0)
            _, slots = around(1, slot)
            count = LOW[0] - 1 - k
            relax(l_src, l_dst, L_SIZE, slots, LOW[0] - count, count, s_l, LOW[1], LOW[1] - count)
            _, slots = around(2, slot)
            relax(u_src, u_dst, U_SIZE, slots, 1, HIGH[0] - 1 - k, s_u, HIGH[1], 0)
            return carry

        lax.fori_loop(0, tiles, sweep_tile, 0)

    field, f_l, f_u = bufs[SWEEPS % 2]
    for t in range(TILES):
        turn = jnp.where(cell_of[0, t] % 2 == 1, LANES - TE, 0)

        def turn_back(p, carry):
            value = plane_at(field, p * ROW + row_of(t, C_SIZE, 1))
            put_plane(pot, pl.multiple_of(p * ROW, ROW) + t, pltpu.roll(value, turn, 1))
            return carry

        lax.fori_loop(0, TE, turn_back, 0, unroll=8)

    def squares(ref, size, slots, local, x, first, count, x_last=None):
        slot, _, y_p, _, z_p, first_y, _ = slots
        row = row_of(slot, size, first)
        up, row_p, row_z = row + TILES, row_of(y_p, size, first) - (ROW - TILES), row_of(z_p, size, first)
        target = (local * SLABX + x) * SUB
        own = plane_at(ref, row)
        for p in range(count):
            last = p == count - 1 and x_last is not None
            after = x_last if last else plane_at(ref, row + (p + 1) * ROW)
            d_x = after - own
            d_y = y_plus(ref, own, first_y, up + p * ROW, row_p + p * ROW) - own
            d_z = z_plus(ref, own, row_z + p * ROW) - own
            rows = pl.ds(pl.multiple_of(target + p * SUB, SUB), SUB)
            slope[rows, :] = d_x * d_x + d_y * d_y + d_z * d_z
            own = after

    def slope_tile(slot, carry):
        for which in range(3):
            cell, slots = around(which, slot)
            local, inside = window(which, cell, i, j, rows_gx)

            @pl.when(inside)
            def _():
                if which == 0:
                    above = plane_at(f_u, row_of(cell_at[2, cell], U_SIZE, 1))
                    squares(field, C_SIZE, slots, local, HALO, 1, TE, above)
                elif which == 1:
                    centre = plane_at(field, row_of(cell_at[0, cell], C_SIZE, 1))
                    squares(f_l, L_SIZE, slots, local, HALO - 2, LOW[0] - 2, 2, centre)
                else:
                    squares(f_u, U_SIZE, slots, local, HALO + TE, 1, 2)

        return carry

    lax.fori_loop(0, tiles, slope_tile, 0)


def window(which, cell, i, j, rows_gx):
    local = cell - 4 * j
    inside = (local >= 0) & (local < 8)
    if which > 0:
        row = i - 1 if which == 1 else i + 1
        inside = inside & (row >= 0) & (row < rows_gx)
    return local, inside


def slab_steps_kernel(chips, pos, k0_table, beta_table, *refs):
    width_gy = 2 * chips
    tiles = width_gy * TILES
    halos = refs[width_gy : 2 * width_gy]
    slope, t_in, k0_in, b_in, y_in, y_out, temp_out = refs[2 * width_gy : 2 * width_gy + 7]
    mine, bundle = refs[2 * width_gy + 7 : 2 * width_gy + 9]
    across = refs[2 * width_gy + 9 : 2 * width_gy + 8 + chips]
    heat, q_ext, state_a, state_b, k0_all, b_all, blocks, sigmas, sems = refs[2 * width_gy + 8 + chips :]
    moves = []
    for part in range(width_gy):
        start = 2 * TE * ROW if part % chips == 0 else 0
        source = refs[part].at[start : start + TE * ROW]
        moves.append(pltpu.make_async_copy(source, sigmas.at[part], sems.at[part]))
        moves[-1].start()
    i = lax.axis_index("gx")
    j = lax.axis_index("gy")
    rows_gx = lax.axis_size("gx")
    lane = lax.broadcasted_iota(jnp.int32, (SUB, LANES), 1)
    zero = jnp.zeros((SUB, LANES), jnp.float32)

    quarter = [(lane >= q * TE) & (lane < (q + 1) * TE) for q in range(3)]

    def pick(parts):
        return jnp.where(
            quarter[0], parts[0], jnp.where(quarter[1], parts[1], jnp.where(quarter[2], parts[2], parts[3]))
        )

    def turned(value, by):
        return value if by % 4 == 0 else roll(value, by * TE, 1)

    def rows_of(block, g):
        first = ROW0 + block * SLABX + g * SUB
        if not isinstance(first, int):
            first = pl.multiple_of(first, SUB)
        return pl.ds(first, SUB)

    groups = SLABX // SUB

    sub = lax.broadcasted_iota(jnp.int32, (SUB, LANES), 0)
    half = lane < NZ
    no_z = lane % NZ == NZ - 1
    low_x = (sub == HALO - 1) & (i == 0), (sub == HALO) & (i == 0)
    high_x = (sub == (HALO + TE - 1) % SUB) & (i == rows_gx - 1)
    low_y, high_y = half & (j == 0), (lane >= NZ) & (j == width_gy - 1)

    def inverse(value):
        near = pl.reciprocal(value, approx=True)
        near = near * (2.0 - value * near)
        return near * (2.0 - value * near)

    def both_of(block, g, by=0):
        first = 2 * (ROW0 + block * SLABX + g * SUB + by)
        return pl.ds(first, SUB, stride=2), pl.ds(first + 1, SUB, stride=2)

    def load(ref, block, by=0):
        places = [both_of(block, g, by) for g in range(groups)]
        return [ref[at, :] for at, _ in places], [ref[at, :] for _, at in places]

    def store(ref, block, g, temp, cond=None):
        first, second = both_of(block, g)
        ref[first, :] = temp
        if cond is not None:
            ref[second, :] = cond

    even = lax.rem(j, 2) == 0

    def begin(block, low, at):
        values = []
        for g in range(groups):
            rows = rows_of(block, g)
            temp, k0, beta = t_in[rows], k0_in[rows], b_in[rows]
            if low is not None:
                place = slice(at * SLABX + g * SUB, at * SLABX + (g + 1) * SUB)
                value = jnp.where(even, *((y_out[place], y_in[place])[:: 1 if low else -1]))
                swapped = roll(value, NZ, 1)
                if low:
                    temp = jnp.where(half, value, temp)
                    k0 = jnp.where(half, lookup(k0_table, swapped), k0)
                    beta = jnp.where(half, lookup(beta_table, swapped), beta)
                else:
                    temp = jnp.where(half, temp, swapped)
                    k0 = jnp.where(half, k0, lookup(k0_table, value))
                    beta = jnp.where(half, beta, lookup(beta_table, value))
            values.append((rows, temp, k0, beta, k0 * inverse(1.0 + beta * temp * temp)))
        for g, (rows, temp, k0, beta, cond) in enumerate(values):
            k0_all[rows], b_all[rows] = k0, beta
            store(state_a, block, g, temp, cond)

    for e in range(HALO):
        begin(e, True, e)
        begin(YBLOCKS - HALO + e, False, e)

    def begin_inner(block, carry):
        begin(block, None, 0)
        return carry

    lax.fori_loop(HALO, YBLOCKS - HALO, begin_inner, 0, unroll=4)

    def clear(at, carry):
        heat[pl.ds(pl.multiple_of(at * SUB, SUB), SUB), :] = zero
        return carry

    lax.fori_loop(0, heat.shape[0] // SUB, clear, 0, unroll=8)
    for move in moves:
        move.wait()
    low_at, high_at = (LOW[0] + LOW[1]) * ROW, LOW_ROWS + (HIGH[0] + HIGH[1]) * ROW
    for part in range(width_gy):
        dev = part_device(part, chips, j)
        for t in range(TILES):
            for which, by in enumerate((0, -1, 1)):
                tile = jnp.clip(i + by, 0, rows_gx - 1) * tiles + dev * TILES + t
                cell = (pos[1, tile] + 1) * 2 + pos[2, tile]
                local, inside = window(which, cell, i, j, rows_gx)
                source, start, x, count = (
                    (sigmas.at[part], 0, HALO, TE),
                    (halos[part], low_at, HALO - 2, 2),
                    (halos[part], high_at, HALO + TE, 2),
                )[which]

                @pl.when(inside)
                def _():
                    def plane(p, carry):
                        rows = pl.ds(pl.multiple_of((local * SLABX + x + p) * SUB, SUB), SUB)
                        at = pl.multiple_of(start + p * ROW, SUB)
                        sigma = source[pl.ds(at + t, SUB, stride=TILES), :]
                        heat[rows, :] = sigma * slope[rows, :]
                        return carry

                    lax.fori_loop(0, count, plane, 0, unroll=count)

    def place_heat(at, carry):
        first = at - 1
        col, yq = lax.div(first * 4 + TE, TE), lax.rem(first * 4 + TE, TE) // 4
        for g in range(groups):
            cells = [
                heat[pl.ds(pl.multiple_of(((2 * col + c) * SLABX + g * SUB) * SUB, SUB) + yq, SUB, stride=SUB), :]
                for c in range(4)
            ]
            for r in range(4):
                block = 4 * first + r + HALO + 1
                q_ext[rows_of(block, g)] = pick([turned(cells[c], c - r - c % 2) for c in range(4)])
        return carry

    lax.fori_loop(0, HALF // 4 + 2, place_heat, 0, unroll=2)

    for step in range(CSWEEPS):
        src, dst = (state_a, state_b)[:: 1 if step % 2 == 0 else -1]

        def y_fluxes(block, now, ahead):
            closed = (low_y & (block == HALO - 1)) | (high_y & (block == HALO + HALF - 1))
            return [flux(now, ahead, g, closed) for g in range(groups)]

        def flux(now, other, g, closed=None):
            value = (now[1][g] + other[1][g]) * (other[0][g] - now[0][g])
            return value if closed is None else jnp.where(closed, 0.0, value)

        def advance(block, carry):
            now, before = carry
            ahead = load(src, block + 1)
            flux_y = y_fluxes(block, now, ahead)
            x_p, x_m = load(src, block, 1), load(src, block, -1)
            results = []
            for g in range(groups):
                temp, cond = now[0][g], now[1][g]
                up = flux(now, x_p, g, {0: low_x[0], groups - 1: high_x}.get(g))
                down = flux(now, x_m, g, {0: low_x[1]}.get(g))
                flux_z = (cond + roll(cond, -1, 1)) * (roll(temp, -1, 1) - temp)
                flux_z = jnp.where(no_z, 0.0, flux_z)
                div = (flux_y[g] - before[g]) + (up + down) + (flux_z - roll(flux_z, 1, 1))
                new = temp + DT * (0.5 * div + q_ext[rows_of(block + 1, g)])
                if step < CSWEEPS - 1:
                    rows = rows_of(block, g)
                    results.append((new, k0_all[rows] * inverse(1.0 + b_all[rows] * new * new)))
                else:
                    results.append((new,))
            for g in range(groups):
                store(dst, block, g, *results[g])
            return ahead, flux_y

        first, second = load(src, 0), load(src, 1)
        lax.fori_loop(1, YBLOCKS - 1, advance, (second, y_fluxes(0, first, second)), unroll=6)
    final = state_b if CSWEEPS % 2 else state_a

    def give_out(yq, carry):
        for g in range(TE // SUB):
            x = slice(g * SUB, (g + 1) * SUB)
            turns = []
            for r in range(4):
                value = final[both_of(HALO + 4 * yq + r, g, HALO)[0], :]
                turns.append([turned(value, by) for by in range(4)])
            for pair in range(2):
                even, odd = turns[2 * pair], turns[2 * pair + 1]
                lower = (2 * yq + pair) * LANES
                upper = lower + temp_out.shape[1] // 2
                temp_out[x, pl.ds(pl.multiple_of(lower, LANES), LANES)] = jnp.where(half, even[0], odd[2])
                temp_out[x, pl.ds(pl.multiple_of(upper, LANES), LANES)] = jnp.where(half, even[2], odd[0])
            for c in range(4):
                value = pick([turns[r][(r - c) % 4] for r in range(4)])
                blocks[pl.ds((c * TE + g * SUB) * SUB + yq, SUB, stride=SUB), :] = value
        return carry

    lax.fori_loop(0, HALF // 4, give_out, 0, unroll=2)
    places = []
    mate = j + 1 - 2 * lax.rem(j, 2)
    targets = [(mine, 0, j)] + [(across[d - 1], 0, j + 2 * d) for d in range(1, chips)]
    targets += [(bundle, d * TE * ROW, mate + 2 * d) for d in range(chips)]
    for target, first, to in targets:
        dev = lax.rem(to, width_gy)
        for t in range(TILES):
            tile = i * tiles + dev * TILES + t
            col = pos[1, tile] - 2 * j
            cell = jnp.clip(col, 0, 1) * 2 + pos[2, tile]
            places.append((target, first + t, cell, (col >= 0) & (col < 2)))

    def pack(p, carry):
        values = []
        for _, _, cell, here in places:
            value = blocks[pl.ds(pl.multiple_of((cell * TE + p) * SUB, SUB), SUB), :]
            values.append(jnp.where(here, value, 0.0))
        for (target, first, _, _), value in zip(places, values):
            target[pl.ds(pl.multiple_of(p * ROW, ROW) + first, SUB, stride=TILES), :] = value
        return carry

    lax.fori_loop(0, TE, pack, 0, unroll=4)


def shifted(value, axis, by, wrap=False):
    count = lax.axis_size(axis)
    pairs = [(d, (d + by) % count) for d in range(count) if wrap or 0 <= d + by < count]
    return lax.ppermute(value, axis, pairs)


def with_partner(value, axis, first):
    count = lax.axis_size(axis)
    pairs = [(d, d + 1) for d in range(first, count - 1, 2)]
    return lax.ppermute(value, axis, pairs + [(high, low) for low, high in pairs])


def from_mate(value):
    return lax.ppermute(value, "gy", [(d, d ^ 1) for d in range(lax.axis_size("gy"))])


def to_rows(value):
    return value.reshape(TILES, -1, LANES).transpose(1, 0, 2).reshape(-1, LANES)


def from_rows(value):
    return value.reshape(-1, TILES, LANES).transpose(1, 0, 2).reshape(TILES, -1)


def to_other_core(value, by):
    count = lax.axis_size("gy")
    return lax.ppermute(value, "gy", [(at, ((at ^ 1) + 2 * by) % count) for at in range(count)])


VMEM = pl.BlockSpec(memory_space=pltpu.VMEM)
SMEM = pl.BlockSpec(memory_space=pltpu.SMEM)
HBM = pl.BlockSpec(memory_space=pltpu.HBM)
ANY = pl.BlockSpec(memory_space=pl.ANY)
PARAMS = pltpu.CompilerParams(vmem_limit_bytes=32 * 1024 * 1024)


def on_device(
    phi_init,
    source,
    tile_mat,
    tile_pos,
    neighbours,
    sigma_table,
    temp_init,
    slab_mat,
    k0_table,
    beta_table,
):
    f32 = jnp.float32
    pos = tile_pos.T
    width_gy = lax.axis_size("gy")
    chips = width_gy // 2
    tiles = width_gy * TILES
    size_x, width = temp_init.shape
    edge_rows = width // LANES * SUB

    def rows(count):
        return jax.ShapeDtypeStruct((count, LANES), f32)

    body, ready, sigma, inner, outer = pl.pallas_call(
        prep_kernel,
        out_shape=(
            rows(3 * TE * ROW),
            rows(2 * TE * ROW),
            rows(TE * ROW),
            rows(SIDE_ROWS + edge_rows),
            rows(SIDE_ROWS + edge_rows),
        ),
        in_specs=[SMEM] * 2 + [HBM] * 5,
        out_specs=(VMEM,) * 5,
        scratch_shapes=[
            pltpu.VMEM((TE * ROW, LANES), f32),
            pltpu.VMEM((TE * ROW, LANES), jnp.int32),
            pltpu.VMEM((2, SUB, width), f32),
            pltpu.VMEM((2, SUB, width), jnp.int32),
            pltpu.SemaphoreType.DMA((7,)),
        ],
        compiler_params=pltpu.CompilerParams(vmem_limit_bytes=62 * 1024 * 1024),
        name="prep",
    )(sigma_table, pos, to_rows(phi_init), to_rows(source), to_rows(tile_mat), temp_init, slab_mat)
    bodies = [body] + [shifted(ready, "gy", 2 * d, True) for d in range(1, chips)]
    bodies += [from_mate(part) for part in bodies]
    inner, outer = with_partner(inner, "gx", 0), with_partner(outer, "gx", 1)

    halo = pl.pallas_call(
        relay_kernel,
        out_shape=rows(LOW_ROWS + HIGH_ROWS),
        in_specs=[VMEM] * 2,
        out_specs=VMEM,
        compiler_params=PARAMS,
        name="relay",
    )(inner, outer)
    halos = [halo] + [shifted(halo, "gy", 2 * d, True) for d in range(1, chips)]
    sigmas = [bodies[0]] + [shifted(sigma, "gy", 2 * d, True) for d in range(1, chips)]
    sigmas += [bodies[chips]] + [to_other_core(sigma, d) for d in range(1, chips)]

    native = pltpu.VMEM((width // LANES * SLABX + SUB, LANES), f32)
    t_ext, k0_ext, b_ext, edge_in, edge_out = pl.pallas_call(
        slab_kernel,
        out_shape=(rows(SLAB_ROWS),) * 3 + (rows(HALO * SLABX),) * 2,
        in_specs=[SMEM] * 3 + [VMEM] * 4,
        out_specs=(VMEM,) * 5,
        scratch_shapes=[native, native] + [pltpu.VMEM((HALO * SLABX, LANES), f32)] * 2,
        compiler_params=PARAMS,
        name="slab_prep",
    )(pos, k0_table, beta_table, temp_init, slab_mat, inner, outer)
    y_in, y_out = with_partner(edge_in, "gy", 0), with_partner(edge_out, "gy", 1)
    *halos[1:], y_in = lax.optimization_barrier((*halos[1:], y_in))
    halos = halos + [from_mate(part) for part in halos]

    def fields(count):
        return pltpu.VMEM((2 * ROW0 + (width_gy + 1) * count * ROW, LANES), f32)

    pot, slope = pl.pallas_call(
        functools.partial(sweep_kernel, chips),
        out_shape=(rows(TE * ROW), rows(8 * SLABX * SUB)),
        in_specs=[SMEM] + [ANY] * (2 * width_gy),
        out_specs=(VMEM, VMEM),
        scratch_shapes=[
            pltpu.SMEM((3, 2 * (2 * width_gy + 2)), jnp.int32),
            pltpu.SMEM((3, tiles), jnp.int32),
            fields(C_SIZE), fields(C_SIZE), fields(L_SIZE), fields(L_SIZE), fields(U_SIZE), fields(U_SIZE),
            fields(TE), fields(LOW[1]), fields(HIGH[1]),
            pltpu.SemaphoreType.DMA((6 * width_gy,)),
        ],
        compiler_params=PARAMS,
        name="sweeps",
    )(pos, *bodies, *halos)

    temp, mine, bundle, *across = pl.pallas_call(
        functools.partial(slab_steps_kernel, chips),
        out_shape=(jax.ShapeDtypeStruct((size_x, width), f32), rows(TE * ROW), rows(chips * TE * ROW))
        + (rows(TE * ROW),) * (chips - 1),
        in_specs=[SMEM] * 3 + [ANY] * width_gy + [VMEM] * (width_gy + 6),
        out_specs=(VMEM,) * (2 + chips),
        scratch_shapes=[pltpu.VMEM((8 * SLABX * SUB, LANES), f32)]
        + [pltpu.VMEM((SLAB_ROWS + 3 * SLABX, LANES), f32)]
        + [pltpu.VMEM((2 * SLAB_ROWS, LANES), f32)] * 2
        + [pltpu.VMEM((SLAB_ROWS, LANES), f32)] * 2
        + [pltpu.VMEM((4 * TE * SUB, LANES), f32), pltpu.VMEM((width_gy, TE * ROW, LANES), f32)]
        + [pltpu.SemaphoreType.DMA((width_gy,))],
        compiler_params=PARAMS,
        name="slab_steps",
    )(pos, k0_table, beta_table, *sigmas, *halos, slope, t_ext, k0_ext, b_ext, y_in, y_out)
    got = from_mate(bundle).reshape(chips, TE * ROW, LANES)
    tile_temps = mine + got[0]
    for d in range(1, chips):
        tile_temps = tile_temps + shifted(across[d - 1] + got[d], "gy", 2 * d, True)
    return from_rows(pot), temp, from_rows(tile_temps)


def solution(mesh):
    placed = (
        P(("gx", "gy"), None),
        P(("gx", "gy"), None),
        P(("gx", "gy"), None),
        P(),
        P(("gx", "gy"), None),
        P(),
        P("gx", "gy"),
        P("gx", "gy"),
        P(),
        P(),
    )
    return jax.shard_map(
        on_device,
        mesh=mesh,
        in_specs=placed,
        out_specs=(P(("gx", "gy"), None), P("gx", "gy"), P(("gx", "gy"), None)),
        check_vma=False,
    )
```

```python
import functools
import math

import jax
import jax.numpy as jnp
from jax import lax
from jax.experimental import pallas as pl
from jax.experimental.pallas import tpu as pltpu
from jax.sharding import PartitionSpec as P

TE = 32
SWEEPS = 4
CSWEEPS = 3
NZ = 64
EPS = 2.0
DT = 0.15
LANES = 128
SUB = 8
TILES = 2
ROW = SUB * TILES

LOW = (SWEEPS + 2, SWEEPS + 1, 2)
HIGH = (SWEEPS + 3, SWEEPS + 2, 2)
LOW_ROWS = sum(LOW) * ROW
HIGH_ROWS = sum(HIGH) * ROW
SIDE_ROWS = max(LOW_ROWS, HIGH_ROWS)
SLABX = TE + SUB
HALO = CSWEEPS
HALF = TE
YBLOCKS = HALF + 2 * HALO
CELLS = 9
ROW0 = ROW
SLAB_ROWS = ROW0 + YBLOCKS * SLABX + ROW0


def cheb_weight(step, count):
    return 1.0 / (1.0 + 0.75 * math.cos(math.pi * (2 * step + 1) / (2 * count)))


def lookup(table, ids):
    out = jnp.full(ids.shape, table[3], jnp.float32)
    for which in (2, 1, 0):
        out = jnp.where(ids == which, table[which], out)
    return out


def roll(value, by, axis):
    return pltpu.roll(value, by % value.shape[axis], axis)


def prep_kernel(table, pos, phi, src, mat, temp, slab, body, ready, sigma, inner, outer, src_v, mat_v, ends_t, ends_m, sems):
    rows = TE * ROW
    size_x, width = temp.shape
    moves = [(phi, body.at[0:rows]), (src, src_v), (mat, mat_v)]
    for which, first in enumerate((0, size_x - SUB)):
        moves.append((temp.at[first : first + SUB], ends_t.at[which]))
        moves.append((slab.at[first : first + SUB], ends_m.at[which]))
    moves = [pltpu.make_async_copy(*move, sems.at[at]) for at, move in enumerate(moves)]
    for move in moves:
        move.start()
    for move in moves:
        move.wait()
    sigma[...] = lookup(table, mat_v[...])
    body[rows : 2 * rows] = src_v[...] / sigma[...]
    first = (lax.axis_index("gx") * lax.axis_size("gy") + lax.axis_index("gy")) * TILES
    for t in range(TILES):

        @pl.when(pos[2, first + t] == 1)
        def _():
            def plane(p, carry):
                for ref, start in ((body, 0), (body, rows), (sigma, 0)):
                    at = pl.ds(pl.multiple_of(p * ROW, ROW) + (start + t), SUB, stride=TILES)
                    ref[at, :] = roll(ref[at, :], TE, 1)
                return carry

            lax.fori_loop(0, TE, plane, 0, unroll=8)

    ready[...] = body[0 : 2 * rows]
    body[2 * rows : 3 * rows] = sigma[...]
    even = lax.rem(lax.axis_index("gx"), 2) == 0

    @pl.when(even)
    def _():
        fill_sides(body, sigma, ends_t, ends_m, inner, outer)

    @pl.when(jnp.logical_not(even))
    def _():
        fill_sides(body, sigma, ends_t, ends_m, outer, inner)


def fill_sides(body, sigma, ends_t, ends_m, up, down):
    rows = TE * ROW
    width = ends_t.shape[2]
    at_up, at_down = 0, 0
    for ref, first in ((body, 0), (body, rows), (sigma, 0)):
        which = (first // rows) if ref is body else 2
        size = LOW[which] * ROW
        up[at_up : at_up + size] = ref[first + rows - size : first + rows]
        at_up += size
        size = HIGH[which] * ROW
        down[at_down : at_down + size] = ref[first : first + size]
        at_down += size
    sub = lax.broadcasted_iota(jnp.int32, (SUB, LANES), 0)
    for at in range(width // LANES):
        lanes = slice(at * LANES, (at + 1) * LANES)
        t_low, m_low = ends_t[0, :, lanes], ends_m[0, :, lanes].astype(jnp.float32)
        t_high, m_high = ends_t[1, :, lanes], ends_m[1, :, lanes].astype(jnp.float32)
        first = at * SUB
        up[SIDE_ROWS + first : SIDE_ROWS + first + SUB] = jnp.where(sub < 4, roll(t_high, HALO, 0), roll(m_high, -1, 0))
        down[SIDE_ROWS + first : SIDE_ROWS + first + SUB] = jnp.where(sub < 4, t_low, roll(m_low, 4, 0))


def relay_kernel(inner, outer, halo):
    def join(low, high):
        halo[0:LOW_ROWS] = low[0:LOW_ROWS]
        halo[LOW_ROWS:] = high[0:HIGH_ROWS]

    even = lax.rem(lax.axis_index("gx"), 2) == 0
    pl.when(even)(lambda: join(outer, inner))
    pl.when(jnp.logical_not(even))(lambda: join(inner, outer))


def loose(pos):
    return jnp.minimum(pos[0, 0], 0)


def slab_kernel(pos, k0_table, beta_table, temp, mat, inner, outer, t_ext, k0_ext, b_ext, edge_in, edge_out, native_t, native_m, edge_low, edge_high):
    start = loose(pos)
    even = lax.rem(lax.axis_index("gx"), 2) == 0
    blocks = temp.shape[1] // LANES
    half = lax.broadcasted_iota(jnp.int32, (SUB, LANES), 1) < NZ
    for which, (own, native) in enumerate(((temp, native_t), (mat, native_m))):
        for at in range(blocks):
            lanes = slice(at * LANES, (at + 1) * LANES)
            first = at * SLABX
            side = slice(SIDE_ROWS + at * SUB, SIDE_ROWS + (at + 1) * SUB)
            value = jnp.where(even, outer[side, :], inner[side, :])
            native[first : first + SUB, :] = roll(value, -4, 0) if which else value
            for g in range(TE // SUB):
                value = own[g * SUB : (g + 1) * SUB, lanes].astype(jnp.float32)
                native[pl.ds(start + first + HALO + g * SUB, SUB), :] = value
            value = jnp.where(even, inner[side, :], outer[side, :])
            native[pl.ds(start + first + HALO + TE, SUB), :] = roll(value, -4, 0) if which else value
    for at in range(blocks // 2):
        for g in range(SLABX // SUB):
            halves = []
            for native in (native_t, native_m):
                lower = native[at * SLABX + g * SUB : at * SLABX + (g + 1) * SUB, :]
                upper_at = (blocks // 2 + at) * SLABX + g * SUB
                upper = native[upper_at : upper_at + SUB, :]
                lower_r, upper_r = roll(lower, NZ, 1), roll(upper, NZ, 1)
                halves.append((lower, lower_r, upper, upper_r))
            for odd in range(2):
                y = 2 * at + odd
                temps, mats = (jnp.where(half, v[odd], v[3 - odd]) for v in halves)
                places = [(y + HALO, temps, mats)]
                if y >= HALF - HALO:
                    places.append((y - HALF + HALO, halves[0][1 - odd], halves[1][1 - odd]))
                if y < HALO:
                    places.append((y + HALF + HALO, halves[0][2 + odd], halves[1][2 + odd]))
                for block, t, m in places:
                    rows = slice(ROW0 + block * SLABX + g * SUB, ROW0 + block * SLABX + (g + 1) * SUB)
                    t_ext[rows] = t
                    k0_ext[rows] = lookup(k0_table, m)
                    b_ext[rows] = lookup(beta_table, m)
                if y < HALO:
                    rows = slice(y * SLABX + g * SUB, y * SLABX + (g + 1) * SUB)
                    edge_low[rows] = jnp.where(half, halves[0][odd], halves[1][1 - odd])
                if y >= HALF - HALO:
                    first = (y - HALF + HALO) * SLABX + g * SUB
                    edge_high[first : first + SUB] = jnp.where(half, halves[0][2 + odd], halves[1][3 - odd])
    even = lax.rem(lax.axis_index("gy"), 2) == 0
    edge_in[...] = jnp.where(even, edge_high[...], edge_low[...])
    edge_out[...] = jnp.where(even, edge_low[...], edge_high[...])


def fill_maps(chips, pos, cell_at, cell_of):
    width_gy = 2 * chips
    tiles = width_gy * TILES
    i = lax.axis_index("gx")
    j = lax.axis_index("gy")
    rows_gx = lax.axis_size("gx")
    for at in range(2 * (2 * width_gy + 2)):
        for which in range(3):
            cell_at[which, at] = tiles
    for which, by in enumerate((0, -1, 1)):
        row = i + by
        valid = (row >= 0) & (row < rows_gx)
        first = jnp.clip(row, 0, rows_gx - 1) * tiles
        for part in range(width_gy):
            dev = part_device(part, chips, j)
            for t in range(TILES):
                tile = first + dev * TILES + t
                cell = (pos[1, tile] + 1) * 2 + pos[2, tile]
                slot = part * TILES + t
                cell_of[which, slot] = cell
                cell_at[which, cell] = jnp.where(valid, slot, tiles)


def part_device(part, chips, j):
    mate = j + 1 - 2 * lax.rem(j, 2)
    base = j if part < chips else mate
    return lax.rem(base - 2 * (part % chips) + 2 * chips, 2 * chips)


def sweep_kernel(chips, pos, *refs):
    width_gy = 2 * chips
    tiles = width_gy * TILES
    none = tiles
    bodies, halos = refs[:width_gy], refs[width_gy : 2 * width_gy]
    pot, slope, cell_at, cell_of, table, pa, pb, la, lb, ua, ub, s_c, s_l, s_u, sems = refs[2 * width_gy :]
    i = lax.axis_index("gx")
    j = lax.axis_index("gy")
    rows_gx = lax.axis_size("gx")
    zero = jnp.zeros((SUB, LANES), jnp.float32)

    moves = []
    for part in range(width_gy):
        at = 0
        pieces = [(bodies[part], 0, pa, part * TE, TE), (bodies[part], TE * ROW, s_c, part * TE, TE)]
        for target, first, count in (
            (la, part * LOW[0], LOW[0]),
            (s_l, part * LOW[1], LOW[1]),
            (None, 0, LOW[2]),
            (ua, part * HIGH[0], HIGH[0]),
            (s_u, part * HIGH[1], HIGH[1]),
        ):
            if target is not None:
                pieces.append((halos[part], at, target, first, count))
            at += count * ROW
        for source, start, target, first, count in pieces:
            move = pltpu.make_async_copy(
                source.at[start : start + count * ROW],
                target.at[ROW0 + first * ROW : ROW0 + (first + count) * ROW],
                sems.at[len(moves)],
            )
            move.start()
            moves.append(move)

    fill_maps(chips, pos, cell_at, cell_of)

    def row_of(slot, size):
        pair, second = lax.shift_right_logical(slot, 1), lax.bitwise_and(slot, 1)
        return ROW0 + pair * (size * ROW) + second

    def enter(slot, carry):
        for which, size in enumerate((TE, LOW[0], HIGH[0])):
            cell = cell_of[which, slot]
            upper = lax.bitwise_and(cell, 1)
            beside = cell_at[which, cell + 1 - 2 * upper]
            here = [cell_at[at, cell] for at in range(3)]
            near = (slot, cell_at[which, cell - 2], cell_at[which, cell + 2])
            near += (jnp.where(upper == 1, beside, none), jnp.where(upper == 1, none, beside))
            rows = [row_of(at, size) for at in near]
            if which == 0:
                rows += [row_of(here[1], LOW[0]) + (LOW[0] - 1) * ROW, row_of(here[2], HIGH[0])]
            else:
                centre = row_of(here[0], TE)
                rows += [centre + (TE - 1) * ROW, centre]
            rows.append(upper)
            for at, row in enumerate(rows):
                table[(which * tiles + slot) * 8 + at] = row
        return carry

    lax.fori_loop(0, tiles, enter, 0)

    def entry(which, slot):
        return [table[(which * tiles + slot) * 8 + at] for at in range(8)]

    def plane_at(ref, row):
        return ref[pl.ds(row, SUB, stride=TILES), :]

    def put_plane(ref, row, value):
        ref[pl.ds(row, SUB, stride=TILES), :] = value

    for ref, count in ((pa, TE), (pb, TE), (la, LOW[0]), (lb, LOW[0]), (ua, HIGH[0]), (ub, HIGH[0])):
        first = ROW0 + width_gy * count * ROW
        for row in range(first, first + count * ROW, SUB):
            ref[row : row + SUB] = zero

    def clear(at, carry):
        slope[pl.ds(pl.multiple_of(at * SUB, SUB), SUB), :] = zero
        return carry

    lax.fori_loop(0, slope.shape[0] // SUB, clear, 0, unroll=8)
    for move in moves:
        move.wait()

    lane = lax.broadcasted_iota(jnp.int32, (SUB, LANES), 1)
    sub = lax.broadcasted_iota(jnp.int32, (SUB, LANES), 0)
    depth = lane % TE
    first_sub, last_sub = sub == 0, sub == SUB - 1
    first_z, last_z = depth == 0, depth == TE - 1

    def y_plus(ref, own, first_y, row, ghost_row):
        turned = jnp.where(last_sub, plane_at(ref, ghost_row), plane_at(ref, row))
        return roll(jnp.where(first_y, turned, own), -TE, 1)

    def y_minus(ref, own, last_y, row, ghost_row):
        turned = jnp.where(first_sub, plane_at(ref, ghost_row), plane_at(ref, row))
        return roll(jnp.where(last_y, turned, own), TE, 1)

    def z_plus(ref, own, ghost_row):
        return roll(jnp.where(first_z, plane_at(ref, ghost_row), own), -1, 1)

    def z_minus(ref, own, ghost_row):
        return roll(jnp.where(last_z, plane_at(ref, ghost_row), own), 1, 1)

    def y_ends(upper):
        quarter = lane // TE
        return quarter == upper, quarter == lax.bitwise_and(upper + 3, 3)

    bufs = ((pa, la, ua), (pb, lb, ub))
    for k in range(SWEEPS):
        weight = cheb_weight(k, SWEEPS)
        keep, gain = 1.0 - weight, weight / (6.0 + EPS)
        (c_src, l_src, u_src), (c_dst, l_dst, u_dst) = bufs[k % 2], bufs[(k + 1) % 2]

        def relax(src, dst, places, first, count, s_ref, s_row, before, beyond):
            row, row_m, row_p, row_zm, row_zp, _, _, upper = places
            first_y, last_y = y_ends(upper)
            own = plane_at(src, row + first * ROW)
            for p in range(count):
                step = (first + p) * ROW
                after = plane_at(src, row + (step + ROW)) if beyond is None or p < count - 1 else beyond
                total = (before + after) + plane_at(s_ref, s_row + p * ROW)
                along_y = y_minus(src, own, last_y, row + (step - TILES), row_m + (step + ROW - TILES))
                along_y = along_y + y_plus(src, own, first_y, row + (step + TILES), row_p + (step + TILES - ROW))
                along_z = z_minus(src, own, row_zm + step) + z_plus(src, own, row_zp + step)
                put_plane(dst, row + step, keep * own + gain * (total + (along_y + along_z)))
                before, own = own, after

        def sweep_tile(slot, carry):
            at = entry(0, slot)
            relax(c_src, c_dst, at, 0, TE, s_c, at[0], plane_at(l_src, at[5]), plane_at(u_src, at[6]))
            at = entry(1, slot)
            count = LOW[0] - 1 - k
            s_row = row_of(slot, LOW[1]) + (LOW[1] - count) * ROW
            before, beyond = plane_at(l_src, at[0] + k * ROW), plane_at(c_src, at[6])
            relax(l_src, l_dst, at, k + 1, count, s_l, s_row, before, beyond)
            at = entry(2, slot)
            relax(u_src, u_dst, at, 0, HIGH[0] - 1 - k, s_u, row_of(slot, HIGH[1]), plane_at(c_src, at[5]), None)
            return carry

        lax.fori_loop(0, tiles, sweep_tile, 0, unroll=2)

    field, f_l, f_u = bufs[SWEEPS % 2]
    for t in range(TILES):
        turn = jnp.where(table[t * 8 + 7] == 1, LANES - TE, 0)

        def turn_back(p, carry):
            value = plane_at(field, p * ROW + (ROW0 + t))
            put_plane(pot, pl.multiple_of(p * ROW, ROW) + t, pltpu.roll(value, turn, 1))
            return carry

        lax.fori_loop(0, TE, turn_back, 0, unroll=8)

    def squares(ref, places, local, x, first, count, beyond):
        row, _, row_p, _, row_z, _, _, upper = places
        first_y, _ = y_ends(upper)
        target = (local * SLABX + x) * SUB
        own = plane_at(ref, row + first * ROW)
        for p in range(count):
            step = (first + p) * ROW
            after = plane_at(ref, row + (step + ROW)) if beyond is None or p < count - 1 else beyond
            d_x = after - own
            d_y = y_plus(ref, own, first_y, row + (step + TILES), row_p + (step + TILES - ROW)) - own
            d_z = z_plus(ref, own, row_z + step) - own
            rows = pl.ds(pl.multiple_of(target + p * SUB, SUB), SUB)
            slope[rows, :] = d_x * d_x + d_y * d_y + d_z * d_z
            own = after

    def slope_tile(slot, carry):
        at, local = entry(0, slot), window(0, cell_of[0, slot], i, j, rows_gx)
        squares(field, at, local, HALO, 0, TE, plane_at(f_u, at[6]))
        at, local = entry(1, slot), window(1, cell_of[1, slot], i, j, rows_gx)
        squares(f_l, at, local, HALO - 2, LOW[0] - 2, 2, plane_at(field, at[6]))
        at, local = entry(2, slot), window(2, cell_of[2, slot], i, j, rows_gx)
        squares(f_u, at, local, HALO + TE, 0, 2, None)
        return carry

    lax.fori_loop(0, tiles, slope_tile, 0, unroll=2)


def window(which, cell, i, j, rows_gx):
    local = cell - 4 * j
    inside = (local >= 0) & (local < CELLS - 1)
    if which > 0:
        row = i - 1 if which == 1 else i + 1
        inside = inside & (row >= 0) & (row < rows_gx)
    return jnp.where(inside, local, CELLS - 1)


def slab_steps_kernel(chips, pos, k0_table, beta_table, *refs):
    width_gy = 2 * chips
    tiles = width_gy * TILES
    halos = refs[width_gy : 2 * width_gy]
    slope, t_in, k0_in, b_in, y_in, y_out, temp_out = refs[2 * width_gy : 2 * width_gy + 7]
    mine, bundle = refs[2 * width_gy + 7 : 2 * width_gy + 9]
    across = refs[2 * width_gy + 9 : 2 * width_gy + 8 + chips]
    heat, q_ext, state_a, state_b, k0_all, b_all, blocks, sigmas, sems = refs[2 * width_gy + 8 + chips :]
    moves = []
    for part in range(width_gy):
        start = 2 * TE * ROW if part % chips == 0 else 0
        source = refs[part].at[start : start + TE * ROW]
        moves.append(pltpu.make_async_copy(source, sigmas.at[part], sems.at[part]))
        moves[-1].start()
    i = lax.axis_index("gx")
    j = lax.axis_index("gy")
    rows_gx = lax.axis_size("gx")
    lane = lax.broadcasted_iota(jnp.int32, (SUB, LANES), 1)
    zero = jnp.zeros((SUB, LANES), jnp.float32)

    quarter = [(lane >= q * TE) & (lane < (q + 1) * TE) for q in range(3)]

    def pick(parts):
        return jnp.where(
            quarter[0], parts[0], jnp.where(quarter[1], parts[1], jnp.where(quarter[2], parts[2], parts[3]))
        )

    def turned(value, by):
        return value if by % 4 == 0 else roll(value, by * TE, 1)

    def rows_of(block, g):
        first = ROW0 + block * SLABX + g * SUB
        if not isinstance(first, int):
            first = pl.multiple_of(first, SUB)
        return pl.ds(first, SUB)

    groups = SLABX // SUB

    sub = lax.broadcasted_iota(jnp.int32, (SUB, LANES), 0)
    half = lane < NZ
    no_z = lane % NZ == NZ - 1
    low_x = (sub == HALO - 1) & (i == 0), (sub == HALO) & (i == 0)
    high_x = (sub == (HALO + TE - 1) % SUB) & (i == rows_gx - 1)
    low_y, high_y = half & (j == 0), (lane >= NZ) & (j == width_gy - 1)

    def inverse(value):
        near = pl.reciprocal(value, approx=True)
        near = near * (2.0 - value * near)
        return near * (2.0 - value * near)

    def both_of(block, g, by=0):
        first = 2 * (ROW0 + block * SLABX + g * SUB + by)
        return pl.ds(first, SUB, stride=2), pl.ds(first + 1, SUB, stride=2)

    def load(ref, block, by=0):
        places = [both_of(block, g, by) for g in range(groups)]
        return [ref[at, :] for at, _ in places], [ref[at, :] for _, at in places]

    def store(ref, block, g, temp, cond=None):
        first, second = both_of(block, g)
        ref[first, :] = temp
        if cond is not None:
            ref[second, :] = cond

    even = lax.rem(j, 2) == 0

    def begin(block, low, at):
        values = []
        for g in range(groups):
            rows = rows_of(block, g)
            temp, k0, beta = t_in[rows], k0_in[rows], b_in[rows]
            if low is not None:
                place = slice(at * SLABX + g * SUB, at * SLABX + (g + 1) * SUB)
                value = jnp.where(even, *((y_out[place], y_in[place])[:: 1 if low else -1]))
                swapped = roll(value, NZ, 1)
                if low:
                    temp = jnp.where(half, value, temp)
                    k0 = jnp.where(half, lookup(k0_table, swapped), k0)
                    beta = jnp.where(half, lookup(beta_table, swapped), beta)
                else:
                    temp = jnp.where(half, temp, swapped)
                    k0 = jnp.where(half, k0, lookup(k0_table, value))
                    beta = jnp.where(half, beta, lookup(beta_table, value))
            values.append((rows, temp, k0, beta, k0 * inverse(1.0 + beta * temp * temp)))
        for g, (rows, temp, k0, beta, cond) in enumerate(values):
            k0_all[rows], b_all[rows] = k0, beta
            store(state_a, block, g, temp, cond)

    for e in range(HALO):
        begin(e, True, e)
        begin(YBLOCKS - HALO + e, False, e)

    def begin_inner(block, carry):
        begin(block, None, 0)
        return carry

    lax.fori_loop(HALO, YBLOCKS - HALO, begin_inner, 0, unroll=4)

    def clear(at, carry):
        heat[pl.ds(pl.multiple_of(at * SUB, SUB), SUB), :] = zero
        return carry

    lax.fori_loop(0, heat.shape[0] // SUB, clear, 0, unroll=8)
    for move in moves:
        move.wait()
    low_at, high_at = (LOW[0] + LOW[1]) * ROW, LOW_ROWS + (HIGH[0] + HIGH[1]) * ROW
    for part in range(width_gy):
        dev = part_device(part, chips, j)
        for t in range(TILES):
            for which, by in enumerate((0, -1, 1)):
                tile = jnp.clip(i + by, 0, rows_gx - 1) * tiles + dev * TILES + t
                cell = (pos[1, tile] + 1) * 2 + pos[2, tile]
                local = window(which, cell, i, j, rows_gx)
                source, start, x, count = (
                    (sigmas.at[part], 0, HALO, TE),
                    (halos[part], low_at, HALO - 2, 2),
                    (halos[part], high_at, HALO + TE, 2),
                )[which]
                first = pl.multiple_of((local * SLABX + x) * SUB, SUB)
                for p in range(count):
                    rows = pl.ds(pl.multiple_of(first + p * SUB, SUB), SUB)
                    sigma = source[pl.ds(start + p * ROW + t, SUB, stride=TILES), :]
                    heat[rows, :] = sigma * slope[rows, :]

    def place_heat(at, carry):
        first = at - 1
        col, yq = lax.div(first * 4 + TE, TE), lax.rem(first * 4 + TE, TE) // 4
        for g in range(groups):
            cells = [
                heat[pl.ds(pl.multiple_of(((2 * col + c) * SLABX + g * SUB) * SUB, SUB) + yq, SUB, stride=SUB), :]
                for c in range(4)
            ]
            for r in range(4):
                block = 4 * first + r + HALO + 1
                q_ext[rows_of(block, g)] = pick([turned(cells[c], c - r - c % 2) for c in range(4)])
        return carry

    lax.fori_loop(0, HALF // 4 + 2, place_heat, 0, unroll=2)

    for step in range(CSWEEPS):
        src, dst = (state_a, state_b)[:: 1 if step % 2 == 0 else -1]

        def y_fluxes(block, now, ahead):
            closed = (low_y & (block == HALO - 1)) | (high_y & (block == HALO + HALF - 1))
            return [flux(now, ahead, g, closed) for g in range(groups)]

        def flux(now, other, g, closed=None):
            value = (now[1][g] + other[1][g]) * (other[0][g] - now[0][g])
            return value if closed is None else jnp.where(closed, 0.0, value)

        def advance(block, carry):
            now, before = carry
            ahead = load(src, block + 1)
            flux_y = y_fluxes(block, now, ahead)
            x_p, x_m = load(src, block, 1), load(src, block, -1)
            results = []
            for g in range(groups):
                temp, cond = now[0][g], now[1][g]
                up = flux(now, x_p, g, {0: low_x[0], groups - 1: high_x}.get(g))
                down = flux(now, x_m, g, {0: low_x[1]}.get(g))
                flux_z = (cond + roll(cond, -1, 1)) * (roll(temp, -1, 1) - temp)
                flux_z = jnp.where(no_z, 0.0, flux_z)
                div = (flux_y[g] - before[g]) + (up + down) + (flux_z - roll(flux_z, 1, 1))
                new = temp + DT * (0.5 * div + q_ext[rows_of(block + 1, g)])
                if step < CSWEEPS - 1:
                    rows = rows_of(block, g)
                    results.append((new, k0_all[rows] * inverse(1.0 + b_all[rows] * new * new)))
                else:
                    results.append((new,))
            for g in range(groups):
                store(dst, block, g, *results[g])
            return ahead, flux_y

        first, second = load(src, 0), load(src, 1)
        lax.fori_loop(1, YBLOCKS - 1, advance, (second, y_fluxes(0, first, second)), unroll=6)
    final = state_b if CSWEEPS % 2 else state_a

    def give_out(yq, carry):
        for g in range(TE // SUB):
            x = slice(g * SUB, (g + 1) * SUB)
            turns = []
            for r in range(4):
                value = final[both_of(HALO + 4 * yq + r, g, HALO)[0], :]
                turns.append([turned(value, by) for by in range(4)])
            for pair in range(2):
                even, odd = turns[2 * pair], turns[2 * pair + 1]
                lower = (2 * yq + pair) * LANES
                upper = lower + temp_out.shape[1] // 2
                temp_out[x, pl.ds(pl.multiple_of(lower, LANES), LANES)] = jnp.where(half, even[0], odd[2])
                temp_out[x, pl.ds(pl.multiple_of(upper, LANES), LANES)] = jnp.where(half, even[2], odd[0])
            for c in range(4):
                value = pick([turns[r][(r - c) % 4] for r in range(4)])
                blocks[pl.ds((c * TE + g * SUB) * SUB + yq, SUB, stride=SUB), :] = value
        return carry

    lax.fori_loop(0, HALF // 4, give_out, 0, unroll=2)
    places = []
    mate = j + 1 - 2 * lax.rem(j, 2)
    targets = [(mine, 0, j)] + [(across[d - 1], 0, j + 2 * d) for d in range(1, chips)]
    targets += [(bundle, d * TE * ROW, mate + 2 * d) for d in range(chips)]
    for target, first, to in targets:
        dev = lax.rem(to, width_gy)
        for t in range(TILES):
            tile = i * tiles + dev * TILES + t
            col = pos[1, tile] - 2 * j
            cell = jnp.clip(col, 0, 1) * 2 + pos[2, tile]
            places.append((target, first + t, cell, (col >= 0) & (col < 2)))

    def pack(p, carry):
        values = []
        for _, _, cell, here in places:
            value = blocks[pl.ds(pl.multiple_of((cell * TE + p) * SUB, SUB), SUB), :]
            values.append(jnp.where(here, value, 0.0))
        for (target, first, _, _), value in zip(places, values):
            target[pl.ds(pl.multiple_of(p * ROW, ROW) + first, SUB, stride=TILES), :] = value
        return carry

    lax.fori_loop(0, TE, pack, 0, unroll=4)


def shifted(value, axis, by, wrap=False):
    count = lax.axis_size(axis)
    pairs = [(d, (d + by) % count) for d in range(count) if wrap or 0 <= d + by < count]
    return lax.ppermute(value, axis, pairs)


def with_partner(value, axis, first):
    count = lax.axis_size(axis)
    pairs = [(d, d + 1) for d in range(first, count - 1, 2)]
    return lax.ppermute(value, axis, pairs + [(high, low) for low, high in pairs])


def from_mate(value):
    return lax.ppermute(value, "gy", [(d, d ^ 1) for d in range(lax.axis_size("gy"))])


def to_rows(value):
    return value.reshape(TILES, -1, LANES).transpose(1, 0, 2).reshape(-1, LANES)


def from_rows(value):
    return value.reshape(-1, TILES, LANES).transpose(1, 0, 2).reshape(TILES, -1)


def to_other_core(value, by):
    count = lax.axis_size("gy")
    return lax.ppermute(value, "gy", [(at, ((at ^ 1) + 2 * by) % count) for at in range(count)])


VMEM = pl.BlockSpec(memory_space=pltpu.VMEM)
SMEM = pl.BlockSpec(memory_space=pltpu.SMEM)
HBM = pl.BlockSpec(memory_space=pltpu.HBM)
ANY = pl.BlockSpec(memory_space=pl.ANY)
PARAMS = pltpu.CompilerParams(vmem_limit_bytes=32 * 1024 * 1024)


def on_device(
    phi_init,
    source,
    tile_mat,
    tile_pos,
    neighbours,
    sigma_table,
    temp_init,
    slab_mat,
    k0_table,
    beta_table,
):
    f32 = jnp.float32
    pos = tile_pos.T
    width_gy = lax.axis_size("gy")
    chips = width_gy // 2
    tiles = width_gy * TILES
    size_x, width = temp_init.shape
    edge_rows = width // LANES * SUB

    def rows(count):
        return jax.ShapeDtypeStruct((count, LANES), f32)

    body, ready, sigma, inner, outer = pl.pallas_call(
        prep_kernel,
        out_shape=(
            rows(3 * TE * ROW),
            rows(2 * TE * ROW),
            rows(TE * ROW),
            rows(SIDE_ROWS + edge_rows),
            rows(SIDE_ROWS + edge_rows),
        ),
        in_specs=[SMEM] * 2 + [HBM] * 5,
        out_specs=(VMEM,) * 5,
        scratch_shapes=[
            pltpu.VMEM((TE * ROW, LANES), f32),
            pltpu.VMEM((TE * ROW, LANES), jnp.int32),
            pltpu.VMEM((2, SUB, width), f32),
            pltpu.VMEM((2, SUB, width), jnp.int32),
            pltpu.SemaphoreType.DMA((7,)),
        ],
        compiler_params=pltpu.CompilerParams(vmem_limit_bytes=62 * 1024 * 1024),
        name="prep",
    )(sigma_table, pos, to_rows(phi_init), to_rows(source), to_rows(tile_mat), temp_init, slab_mat)
    bodies = [body] + [shifted(ready, "gy", 2 * d, True) for d in range(1, chips)]
    bodies += [from_mate(part) for part in bodies]
    inner, outer = with_partner(inner, "gx", 0), with_partner(outer, "gx", 1)

    halo = pl.pallas_call(
        relay_kernel,
        out_shape=rows(LOW_ROWS + HIGH_ROWS),
        in_specs=[VMEM] * 2,
        out_specs=VMEM,
        compiler_params=PARAMS,
        name="relay",
    )(inner, outer)
    halos = [halo] + [shifted(halo, "gy", 2 * d, True) for d in range(1, chips)]
    sigmas = [bodies[0]] + [shifted(sigma, "gy", 2 * d, True) for d in range(1, chips)]
    sigmas += [bodies[chips]] + [to_other_core(sigma, d) for d in range(1, chips)]

    native = pltpu.VMEM((width // LANES * SLABX + SUB, LANES), f32)
    t_ext, k0_ext, b_ext, edge_in, edge_out = pl.pallas_call(
        slab_kernel,
        out_shape=(rows(SLAB_ROWS),) * 3 + (rows(HALO * SLABX),) * 2,
        in_specs=[SMEM] * 3 + [VMEM] * 4,
        out_specs=(VMEM,) * 5,
        scratch_shapes=[native, native] + [pltpu.VMEM((HALO * SLABX, LANES), f32)] * 2,
        compiler_params=PARAMS,
        name="slab_prep",
    )(pos, k0_table, beta_table, temp_init, slab_mat, inner, outer)
    y_in, y_out = with_partner(edge_in, "gy", 0), with_partner(edge_out, "gy", 1)
    *halos[1:], y_in = lax.optimization_barrier((*halos[1:], y_in))
    halos = halos + [from_mate(part) for part in halos]

    def fields(count):
        return pltpu.VMEM((2 * ROW0 + (width_gy + 1) * count * ROW, LANES), f32)

    pot, slope = pl.pallas_call(
        functools.partial(sweep_kernel, chips),
        out_shape=(rows(TE * ROW), rows(CELLS * SLABX * SUB)),
        in_specs=[SMEM] + [ANY] * (2 * width_gy),
        out_specs=(VMEM, VMEM),
        scratch_shapes=[
            pltpu.SMEM((3, 2 * (2 * width_gy + 2)), jnp.int32),
            pltpu.SMEM((3, tiles), jnp.int32),
            pltpu.SMEM((3 * tiles * 8,), jnp.int32),
            fields(TE), fields(TE), fields(LOW[0]), fields(LOW[0]), fields(HIGH[0]), fields(HIGH[0]),
            fields(TE), fields(LOW[1]), fields(HIGH[1]),
            pltpu.SemaphoreType.DMA((6 * width_gy,)),
        ],
        compiler_params=PARAMS,
        name="sweeps",
    )(pos, *bodies, *halos)

    temp, mine, bundle, *across = pl.pallas_call(
        functools.partial(slab_steps_kernel, chips),
        out_shape=(jax.ShapeDtypeStruct((size_x, width), f32), rows(TE * ROW), rows(chips * TE * ROW))
        + (rows(TE * ROW),) * (chips - 1),
        in_specs=[SMEM] * 3 + [ANY] * width_gy + [VMEM] * (width_gy + 6),
        out_specs=(VMEM,) * (2 + chips),
        scratch_shapes=[pltpu.VMEM((CELLS * SLABX * SUB, LANES), f32)]
        + [pltpu.VMEM((SLAB_ROWS + 3 * SLABX, LANES), f32)]
        + [pltpu.VMEM((2 * SLAB_ROWS, LANES), f32)] * 2
        + [pltpu.VMEM((SLAB_ROWS, LANES), f32)] * 2
        + [pltpu.VMEM((4 * TE * SUB, LANES), f32), pltpu.VMEM((width_gy, TE * ROW, LANES), f32)]
        + [pltpu.SemaphoreType.DMA((width_gy,))],
        compiler_params=PARAMS,
        name="slab_steps",
    )(pos, k0_table, beta_table, *sigmas, *halos, slope, t_ext, k0_ext, b_ext, y_in, y_out)
    got = from_mate(bundle).reshape(chips, TE * ROW, LANES)
    tile_temps = mine + got[0]
    for d in range(1, chips):
        tile_temps = tile_temps + shifted(across[d - 1] + got[d], "gy", 2 * d, True)
    return from_rows(pot), temp, from_rows(tile_temps)


def solution(mesh):
    placed = (
        P(("gx", "gy"), None),
        P(("gx", "gy"), None),
        P(("gx", "gy"), None),
        P(),
        P(("gx", "gy"), None),
        P(),
        P("gx", "gy"),
        P("gx", "gy"),
        P(),
        P(),
    )
    return jax.shard_map(
        on_device,
        mesh=mesh,
        in_specs=placed,
        out_specs=(P(("gx", "gy"), None), P("gx", "gy"), P(("gx", "gy"), None)),
        check_vma=False,
    )
```

```python
import functools
import math

import jax
import jax.numpy as jnp
from jax import lax
from jax.experimental import pallas as pl
from jax.experimental.pallas import tpu as pltpu
from jax.sharding import PartitionSpec as P

TE = 32
SWEEPS = 4
CSWEEPS = 3
NZ = 64
EPS = 2.0
DT = 0.15
LANES = 128
SUB = 8
TILES = 2
ROW = SUB * TILES

LOW = (SWEEPS + 2, SWEEPS + 1, 2)
HIGH = (SWEEPS + 3, SWEEPS + 2, 2)
LOW_ROWS = sum(LOW) * ROW
HIGH_ROWS = sum(HIGH) * ROW
SIDE_ROWS = max(LOW_ROWS, HIGH_ROWS)
SLABX = TE + SUB
HALO = CSWEEPS
HALF = TE
YBLOCKS = HALF + 2 * HALO
CELLS = 9
ROW0 = ROW
SLAB_ROWS = ROW0 + YBLOCKS * SLABX + ROW0


def cheb_weight(step, count):
    return 1.0 / (1.0 + 0.75 * math.cos(math.pi * (2 * step + 1) / (2 * count)))


def lookup(table, ids):
    out = jnp.full(ids.shape, table[3], jnp.float32)
    for which in (2, 1, 0):
        out = jnp.where(ids == which, table[which], out)
    return out


def roll(value, by, axis):
    return pltpu.roll(value, by % value.shape[axis], axis)


def prep_kernel(table, pos, phi, src, mat, temp, slab, body, ready, sigma, inner, outer, src_v, mat_v, ends_t, ends_m, sems):
    rows = TE * ROW
    size_x, width = temp.shape
    moves = [(phi, body.at[0:rows]), (src, src_v), (mat, mat_v)]
    for which, first in enumerate((0, size_x - SUB)):
        moves.append((temp.at[first : first + SUB], ends_t.at[which]))
        moves.append((slab.at[first : first + SUB], ends_m.at[which]))
    moves = [pltpu.make_async_copy(*move, sems.at[at]) for at, move in enumerate(moves)]
    for move in moves:
        move.start()
    for move in moves:
        move.wait()
    sigma[...] = lookup(table, mat_v[...])
    body[rows : 2 * rows] = src_v[...] / sigma[...]
    first = (lax.axis_index("gx") * lax.axis_size("gy") + lax.axis_index("gy")) * TILES
    for t in range(TILES):

        @pl.when(pos[2, first + t] == 1)
        def _():
            def plane(p, carry):
                for ref, start in ((body, 0), (body, rows), (sigma, 0)):
                    at = pl.ds(pl.multiple_of(p * ROW, ROW) + (start + t), SUB, stride=TILES)
                    ref[at, :] = roll(ref[at, :], TE, 1)
                return carry

            lax.fori_loop(0, TE, plane, 0, unroll=8)

    ready[...] = body[0 : 2 * rows]
    body[2 * rows : 3 * rows] = sigma[...]
    even = lax.rem(lax.axis_index("gx"), 2) == 0

    @pl.when(even)
    def _():
        fill_sides(body, sigma, ends_t, ends_m, inner, outer)

    @pl.when(jnp.logical_not(even))
    def _():
        fill_sides(body, sigma, ends_t, ends_m, outer, inner)


def fill_sides(body, sigma, ends_t, ends_m, up, down):
    rows = TE * ROW
    width = ends_t.shape[2]
    at_up, at_down = 0, 0
    for ref, first in ((body, 0), (body, rows), (sigma, 0)):
        which = (first // rows) if ref is body else 2
        size = LOW[which] * ROW
        up[at_up : at_up + size] = ref[first + rows - size : first + rows]
        at_up += size
        size = HIGH[which] * ROW
        down[at_down : at_down + size] = ref[first : first + size]
        at_down += size
    sub = lax.broadcasted_iota(jnp.int32, (SUB, LANES), 0)
    for at in range(width // LANES):
        lanes = slice(at * LANES, (at + 1) * LANES)
        t_low, m_low = ends_t[0, :, lanes], ends_m[0, :, lanes].astype(jnp.float32)
        t_high, m_high = ends_t[1, :, lanes], ends_m[1, :, lanes].astype(jnp.float32)
        first = at * SUB
        up[SIDE_ROWS + first : SIDE_ROWS + first + SUB] = jnp.where(sub < 4, roll(t_high, HALO, 0), roll(m_high, -1, 0))
        down[SIDE_ROWS + first : SIDE_ROWS + first + SUB] = jnp.where(sub < 4, t_low, roll(m_low, 4, 0))


def relay_kernel(inner, outer, halo):
    def join(low, high):
        halo[0:LOW_ROWS] = low[0:LOW_ROWS]
        halo[LOW_ROWS:] = high[0:HIGH_ROWS]

    even = lax.rem(lax.axis_index("gx"), 2) == 0
    pl.when(even)(lambda: join(outer, inner))
    pl.when(jnp.logical_not(even))(lambda: join(inner, outer))


def loose(pos):
    return jnp.minimum(pos[0, 0], 0)


def slab_kernel(pos, k0_table, beta_table, temp, mat, inner, outer, sigma, t_ext, k0_ext, b_ext, edge_in, packet, native_t, native_m, edge_low, edge_high):
    start = loose(pos)
    even = lax.rem(lax.axis_index("gx"), 2) == 0
    blocks = temp.shape[1] // LANES
    half = lax.broadcasted_iota(jnp.int32, (SUB, LANES), 1) < NZ
    for which, (own, native) in enumerate(((temp, native_t), (mat, native_m))):
        for at in range(blocks):
            lanes = slice(at * LANES, (at + 1) * LANES)
            first = at * SLABX
            side = slice(SIDE_ROWS + at * SUB, SIDE_ROWS + (at + 1) * SUB)
            value = jnp.where(even, outer[side, :], inner[side, :])
            native[first : first + SUB, :] = roll(value, -4, 0) if which else value
            for g in range(TE // SUB):
                value = own[g * SUB : (g + 1) * SUB, lanes].astype(jnp.float32)
                native[pl.ds(start + first + HALO + g * SUB, SUB), :] = value
            value = jnp.where(even, inner[side, :], outer[side, :])
            native[pl.ds(start + first + HALO + TE, SUB), :] = roll(value, -4, 0) if which else value
    for at in range(blocks // 2):
        for g in range(SLABX // SUB):
            halves = []
            for native in (native_t, native_m):
                lower = native[at * SLABX + g * SUB : at * SLABX + (g + 1) * SUB, :]
                upper_at = (blocks // 2 + at) * SLABX + g * SUB
                upper = native[upper_at : upper_at + SUB, :]
                lower_r, upper_r = roll(lower, NZ, 1), roll(upper, NZ, 1)
                halves.append((lower, lower_r, upper, upper_r))
            for odd in range(2):
                y = 2 * at + odd
                temps, mats = (jnp.where(half, v[odd], v[3 - odd]) for v in halves)
                places = [(y + HALO, temps, mats)]
                if y >= HALF - HALO:
                    places.append((y - HALF + HALO, halves[0][1 - odd], halves[1][1 - odd]))
                if y < HALO:
                    places.append((y + HALF + HALO, halves[0][2 + odd], halves[1][2 + odd]))
                for block, t, m in places:
                    rows = slice(ROW0 + block * SLABX + g * SUB, ROW0 + block * SLABX + (g + 1) * SUB)
                    t_ext[rows] = t
                    k0_ext[rows] = lookup(k0_table, m)
                    b_ext[rows] = lookup(beta_table, m)
                if y < HALO:
                    rows = slice(y * SLABX + g * SUB, y * SLABX + (g + 1) * SUB)
                    edge_low[rows] = jnp.where(half, halves[0][odd], halves[1][1 - odd])
                if y >= HALF - HALO:
                    first = (y - HALF + HALO) * SLABX + g * SUB
                    edge_high[first : first + SUB] = jnp.where(half, halves[0][2 + odd], halves[1][3 - odd])
    even = lax.rem(lax.axis_index("gy"), 2) == 0
    edge_in[...] = jnp.where(even, edge_high[...], edge_low[...])
    packet[0 : TE * ROW] = sigma[...]
    packet[TE * ROW :] = jnp.where(even, edge_low[...], edge_high[...])


def fill_maps(chips, pos, cell_at, cell_of):
    width_gy = 2 * chips
    tiles = width_gy * TILES
    i = lax.axis_index("gx")
    j = lax.axis_index("gy")
    rows_gx = lax.axis_size("gx")
    for at in range(2 * (2 * width_gy + 2)):
        for which in range(3):
            cell_at[which, at] = tiles
    for which, by in enumerate((0, -1, 1)):
        row = i + by
        valid = (row >= 0) & (row < rows_gx)
        first = jnp.clip(row, 0, rows_gx - 1) * tiles
        for part in range(width_gy):
            dev = part_device(part, chips, j)
            for t in range(TILES):
                tile = first + dev * TILES + t
                cell = (pos[1, tile] + 1) * 2 + pos[2, tile]
                slot = part * TILES + t
                cell_of[which, slot] = cell
                cell_at[which, cell] = jnp.where(valid, slot, tiles)


def part_device(part, chips, j):
    mate = j + 1 - 2 * lax.rem(j, 2)
    base = j if part < chips else mate
    return lax.rem(base - 2 * (part % chips) + 2 * chips, 2 * chips)


def sweep_kernel(chips, pos, *refs):
    width_gy = 2 * chips
    tiles = width_gy * TILES
    none = tiles
    bodies, halos = refs[:width_gy], refs[width_gy : 2 * width_gy]
    pot, slope, cell_at, cell_of, table, pa, pb, la, lb, ua, ub, s_c, s_l, s_u, sems = refs[2 * width_gy :]
    i = lax.axis_index("gx")
    j = lax.axis_index("gy")
    rows_gx = lax.axis_size("gx")
    zero = jnp.zeros((SUB, LANES), jnp.float32)

    moves = []
    for part in range(width_gy):
        at = 0
        pieces = [(bodies[part], 0, pa, part * TE, TE), (bodies[part], TE * ROW, s_c, part * TE, TE)]
        for target, first, count in (
            (la, part * LOW[0], LOW[0]),
            (s_l, part * LOW[1], LOW[1]),
            (None, 0, LOW[2]),
            (ua, part * HIGH[0], HIGH[0]),
            (s_u, part * HIGH[1], HIGH[1]),
        ):
            if target is not None:
                pieces.append((halos[part], at, target, first, count))
            at += count * ROW
        for source, start, target, first, count in pieces:
            move = pltpu.make_async_copy(
                source.at[start : start + count * ROW],
                target.at[ROW0 + first * ROW : ROW0 + (first + count) * ROW],
                sems.at[len(moves)],
            )
            move.start()
            moves.append(move)

    fill_maps(chips, pos, cell_at, cell_of)

    def row_of(slot, size):
        pair, second = lax.shift_right_logical(slot, 1), lax.bitwise_and(slot, 1)
        return ROW0 + pair * (size * ROW) + second

    def enter(slot, carry):
        for which, size in enumerate((TE, LOW[0], HIGH[0])):
            cell = cell_of[which, slot]
            upper = lax.bitwise_and(cell, 1)
            beside = cell_at[which, cell + 1 - 2 * upper]
            here = [cell_at[at, cell] for at in range(3)]
            near = (slot, cell_at[which, cell - 2], cell_at[which, cell + 2])
            near += (jnp.where(upper == 1, beside, none), jnp.where(upper == 1, none, beside))
            rows = [row_of(at, size) for at in near]
            if which == 0:
                rows += [row_of(here[1], LOW[0]) + (LOW[0] - 1) * ROW, row_of(here[2], HIGH[0])]
            else:
                centre = row_of(here[0], TE)
                rows += [centre + (TE - 1) * ROW, centre]
            rows.append(upper)
            for at, row in enumerate(rows):
                table[(which * tiles + slot) * 8 + at] = row
        return carry

    lax.fori_loop(0, tiles, enter, 0)

    def entry(which, slot):
        return [table[(which * tiles + slot) * 8 + at] for at in range(8)]

    def plane_at(ref, row):
        return ref[pl.ds(row, SUB, stride=TILES), :]

    def put_plane(ref, row, value):
        ref[pl.ds(row, SUB, stride=TILES), :] = value

    for ref, count in ((pa, TE), (pb, TE), (la, LOW[0]), (lb, LOW[0]), (ua, HIGH[0]), (ub, HIGH[0])):
        first = ROW0 + width_gy * count * ROW
        for row in range(first, first + count * ROW, SUB):
            ref[row : row + SUB] = zero

    def clear(at, carry):
        slope[pl.ds(pl.multiple_of(at * SUB, SUB), SUB), :] = zero
        return carry

    lax.fori_loop(0, slope.shape[0] // SUB, clear, 0, unroll=8)
    for move in moves:
        move.wait()

    lane = lax.broadcasted_iota(jnp.int32, (SUB, LANES), 1)
    sub = lax.broadcasted_iota(jnp.int32, (SUB, LANES), 0)
    depth = lane % TE
    first_sub, last_sub = sub == 0, sub == SUB - 1
    first_z, last_z = depth == 0, depth == TE - 1

    def y_plus(ref, own, first_y, row, ghost_row):
        turned = jnp.where(last_sub, plane_at(ref, ghost_row), plane_at(ref, row))
        return roll(jnp.where(first_y, turned, own), -TE, 1)

    def y_minus(ref, own, last_y, row, ghost_row):
        turned = jnp.where(first_sub, plane_at(ref, ghost_row), plane_at(ref, row))
        return roll(jnp.where(last_y, turned, own), TE, 1)

    def z_plus(ref, own, ghost_row):
        return roll(jnp.where(first_z, plane_at(ref, ghost_row), own), -1, 1)

    def z_minus(ref, own, ghost_row):
        return roll(jnp.where(last_z, plane_at(ref, ghost_row), own), 1, 1)

    def y_ends(upper):
        quarter = lane // TE
        return quarter == upper, quarter == lax.bitwise_and(upper + 3, 3)

    bufs = ((pa, la, ua), (pb, lb, ub))
    for k in range(SWEEPS):
        weight = cheb_weight(k, SWEEPS)
        keep, gain = 1.0 - weight, weight / (6.0 + EPS)
        (c_src, l_src, u_src), (c_dst, l_dst, u_dst) = bufs[k % 2], bufs[(k + 1) % 2]

        def relax(src, dst, places, first, count, s_ref, s_row, before, beyond):
            row, row_m, row_p, row_zm, row_zp, _, _, upper = places
            first_y, last_y = y_ends(upper)
            own = plane_at(src, row + first * ROW)
            for p in range(count):
                step = (first + p) * ROW
                after = plane_at(src, row + (step + ROW)) if beyond is None or p < count - 1 else beyond
                total = (before + after) + plane_at(s_ref, s_row + p * ROW)
                along_y = y_minus(src, own, last_y, row + (step - TILES), row_m + (step + ROW - TILES))
                along_y = along_y + y_plus(src, own, first_y, row + (step + TILES), row_p + (step + TILES - ROW))
                along_z = z_minus(src, own, row_zm + step) + z_plus(src, own, row_zp + step)
                put_plane(dst, row + step, keep * own + gain * (total + (along_y + along_z)))
                before, own = own, after

        def sweep_tile(slot, carry):
            at = entry(0, slot)
            relax(c_src, c_dst, at, 0, TE, s_c, at[0], plane_at(l_src, at[5]), plane_at(u_src, at[6]))
            at = entry(1, slot)
            count = LOW[0] - 1 - k
            s_row = row_of(slot, LOW[1]) + (LOW[1] - count) * ROW
            before, beyond = plane_at(l_src, at[0] + k * ROW), plane_at(c_src, at[6])
            relax(l_src, l_dst, at, k + 1, count, s_l, s_row, before, beyond)
            at = entry(2, slot)
            relax(u_src, u_dst, at, 0, HIGH[0] - 1 - k, s_u, row_of(slot, HIGH[1]), plane_at(c_src, at[5]), None)
            return carry

        lax.fori_loop(0, tiles, sweep_tile, 0, unroll=4)

    field, f_l, f_u = bufs[SWEEPS % 2]
    for t in range(TILES):
        turn = jnp.where(table[t * 8 + 7] == 1, LANES - TE, 0)

        def turn_back(p, carry):
            value = plane_at(field, p * ROW + (ROW0 + t))
            put_plane(pot, pl.multiple_of(p * ROW, ROW) + t, pltpu.roll(value, turn, 1))
            return carry

        lax.fori_loop(0, TE, turn_back, 0, unroll=8)

    def squares(ref, places, local, x, first, count, beyond):
        row, _, row_p, _, row_z, _, _, upper = places
        first_y, _ = y_ends(upper)
        target = (local * SLABX + x) * SUB
        own = plane_at(ref, row + first * ROW)
        for p in range(count):
            step = (first + p) * ROW
            after = plane_at(ref, row + (step + ROW)) if beyond is None or p < count - 1 else beyond
            d_x = after - own
            d_y = y_plus(ref, own, first_y, row + (step + TILES), row_p + (step + TILES - ROW)) - own
            d_z = z_plus(ref, own, row_z + step) - own
            rows = pl.ds(pl.multiple_of(target + p * SUB, SUB), SUB)
            slope[rows, :] = d_x * d_x + d_y * d_y + d_z * d_z
            own = after

    def slope_tile(slot, carry):
        at, local = entry(0, slot), window(0, cell_of[0, slot], i, j, rows_gx)
        squares(field, at, local, HALO, 0, TE, plane_at(f_u, at[6]))
        at, local = entry(1, slot), window(1, cell_of[1, slot], i, j, rows_gx)
        squares(f_l, at, local, HALO - 2, LOW[0] - 2, 2, plane_at(field, at[6]))
        at, local = entry(2, slot), window(2, cell_of[2, slot], i, j, rows_gx)
        squares(f_u, at, local, HALO + TE, 0, 2, None)
        return carry

    lax.fori_loop(0, tiles, slope_tile, 0, unroll=2)


def window(which, cell, i, j, rows_gx):
    local = cell - 4 * j
    inside = (local >= 0) & (local < CELLS - 1)
    if which > 0:
        row = i - 1 if which == 1 else i + 1
        inside = inside & (row >= 0) & (row < rows_gx)
    return jnp.where(inside, local, CELLS - 1)


def slab_steps_kernel(chips, pos, k0_table, beta_table, *refs):
    width_gy = 2 * chips
    tiles = width_gy * TILES
    halos = refs[width_gy : 2 * width_gy]
    slope, t_in, k0_in, b_in, y_in, temp_out = refs[2 * width_gy : 2 * width_gy + 6]
    mine, bundle = refs[2 * width_gy + 6 : 2 * width_gy + 8]
    across = refs[2 * width_gy + 8 : 2 * width_gy + 7 + chips]
    heat, q_ext, state_a, state_b, k0_all, b_all, blocks, sigmas, y_out, sems = refs[2 * width_gy + 7 + chips :]
    moves = []
    for part in range(width_gy):
        start = 2 * TE * ROW if part % chips == 0 else 0
        source = refs[part].at[start : start + TE * ROW]
        moves.append(pltpu.make_async_copy(source, sigmas.at[part], sems.at[part]))
        moves[-1].start()
    edges = []
    for which, d in enumerate((1, chips - 1)):
        source = refs[chips + d].at[TE * ROW : TE * ROW + HALO * SLABX]
        edges.append(pltpu.make_async_copy(source, y_out.at[which], sems.at[width_gy + which]))
        edges[-1].start()
    i = lax.axis_index("gx")
    j = lax.axis_index("gy")
    rows_gx = lax.axis_size("gx")
    lane = lax.broadcasted_iota(jnp.int32, (SUB, LANES), 1)
    zero = jnp.zeros((SUB, LANES), jnp.float32)

    quarter = [(lane >= q * TE) & (lane < (q + 1) * TE) for q in range(3)]

    def pick(parts):
        return jnp.where(
            quarter[0], parts[0], jnp.where(quarter[1], parts[1], jnp.where(quarter[2], parts[2], parts[3]))
        )

    def turned(value, by):
        return value if by % 4 == 0 else roll(value, by * TE, 1)

    def rows_of(block, g):
        first = ROW0 + block * SLABX + g * SUB
        if not isinstance(first, int):
            first = pl.multiple_of(first, SUB)
        return pl.ds(first, SUB)

    groups = SLABX // SUB

    sub = lax.broadcasted_iota(jnp.int32, (SUB, LANES), 0)
    half = lane < NZ
    no_z = lane % NZ == NZ - 1
    low_x = (sub == HALO - 1) & (i == 0), (sub == HALO) & (i == 0)
    high_x = (sub == (HALO + TE - 1) % SUB) & (i == rows_gx - 1)
    low_y, high_y = half & (j == 0), (lane >= NZ) & (j == width_gy - 1)

    def inverse(value):
        near = pl.reciprocal(value, approx=True)
        near = near * (2.0 - value * near)
        return near * (2.0 - value * near)

    def both_of(block, g, by=0):
        first = 2 * (ROW0 + block * SLABX + g * SUB + by)
        return pl.ds(first, SUB, stride=2), pl.ds(first + 1, SUB, stride=2)

    def load(ref, block, by=0):
        places = [both_of(block, g, by) for g in range(groups)]
        return [ref[at, :] for at, _ in places], [ref[at, :] for _, at in places]

    def store(ref, block, g, temp, cond=None):
        first, second = both_of(block, g)
        ref[first, :] = temp
        if cond is not None:
            ref[second, :] = cond

    even = lax.rem(j, 2) == 0

    def begin(block, low, at):
        values = []
        for g in range(groups):
            rows = rows_of(block, g)
            temp, k0, beta = t_in[rows], k0_in[rows], b_in[rows]
            if low is not None:
                place = slice(at * SLABX + g * SUB, at * SLABX + (g + 1) * SUB)
                other = jnp.where(even, y_out[0, place], y_out[1, place])
                value = jnp.where(even, *((other, y_in[place])[:: 1 if low else -1]))
                swapped = roll(value, NZ, 1)
                if low:
                    temp = jnp.where(half, value, temp)
                    k0 = jnp.where(half, lookup(k0_table, swapped), k0)
                    beta = jnp.where(half, lookup(beta_table, swapped), beta)
                else:
                    temp = jnp.where(half, temp, swapped)
                    k0 = jnp.where(half, k0, lookup(k0_table, value))
                    beta = jnp.where(half, beta, lookup(beta_table, value))
            values.append((rows, temp, k0, beta, k0 * inverse(1.0 + beta * temp * temp)))
        for g, (rows, temp, k0, beta, cond) in enumerate(values):
            k0_all[rows], b_all[rows] = k0, beta
            store(state_a, block, g, temp, cond)

    def begin_inner(block, carry):
        begin(block, None, 0)
        return carry

    lax.fori_loop(HALO, YBLOCKS - HALO, begin_inner, 0, unroll=8)
    for move in edges:
        move.wait()
    for e in range(HALO):
        begin(e, True, e)
        begin(YBLOCKS - HALO + e, False, e)

    def clear(at, carry):
        heat[pl.ds(pl.multiple_of(at * SUB, SUB), SUB), :] = zero
        return carry

    lax.fori_loop(0, heat.shape[0] // SUB, clear, 0, unroll=8)
    for move in moves:
        move.wait()
    low_at, high_at = (LOW[0] + LOW[1]) * ROW, LOW_ROWS + (HIGH[0] + HIGH[1]) * ROW
    for part in range(width_gy):
        dev = part_device(part, chips, j)
        for t in range(TILES):
            for which, by in enumerate((0, -1, 1)):
                tile = jnp.clip(i + by, 0, rows_gx - 1) * tiles + dev * TILES + t
                cell = (pos[1, tile] + 1) * 2 + pos[2, tile]
                local = window(which, cell, i, j, rows_gx)
                source, start, x, count = (
                    (sigmas.at[part], 0, HALO, TE),
                    (halos[part], low_at, HALO - 2, 2),
                    (halos[part], high_at, HALO + TE, 2),
                )[which]
                first = pl.multiple_of((local * SLABX + x) * SUB, SUB)
                for p in range(count):
                    rows = pl.ds(pl.multiple_of(first + p * SUB, SUB), SUB)
                    sigma = source[pl.ds(start + p * ROW + t, SUB, stride=TILES), :]
                    heat[rows, :] = sigma * slope[rows, :]

    def place_heat(at, carry):
        first = at - 1
        col, yq = lax.div(first * 4 + TE, TE), lax.rem(first * 4 + TE, TE) // 4
        for g in range(groups):
            cells = [
                heat[pl.ds(pl.multiple_of(((2 * col + c) * SLABX + g * SUB) * SUB, SUB) + yq, SUB, stride=SUB), :]
                for c in range(4)
            ]
            for r in range(4):
                block = 4 * first + r + HALO + 1
                q_ext[rows_of(block, g)] = pick([turned(cells[c], c - r - c % 2) for c in range(4)])
        return carry

    lax.fori_loop(0, HALF // 4 + 2, place_heat, 0, unroll=5)

    for step in range(CSWEEPS):
        src, dst = (state_a, state_b)[:: 1 if step % 2 == 0 else -1]

        def y_fluxes(block, now, ahead):
            closed = (low_y & (block == HALO - 1)) | (high_y & (block == HALO + HALF - 1))
            return [flux(now, ahead, g, closed) for g in range(groups)]

        def flux(now, other, g, closed=None):
            value = (now[1][g] + other[1][g]) * (other[0][g] - now[0][g])
            return value if closed is None else jnp.where(closed, 0.0, value)

        def advance(block, carry):
            now, before = carry
            ahead = load(src, block + 1)
            flux_y = y_fluxes(block, now, ahead)
            x_p, x_m = load(src, block, 1), load(src, block, -1)
            results = []
            for g in range(groups):
                temp, cond = now[0][g], now[1][g]
                up = flux(now, x_p, g, {0: low_x[0], groups - 1: high_x}.get(g))
                down = flux(now, x_m, g, {0: low_x[1]}.get(g))
                flux_z = (cond + roll(cond, -1, 1)) * (roll(temp, -1, 1) - temp)
                flux_z = jnp.where(no_z, 0.0, flux_z)
                div = (flux_y[g] - before[g]) + (up + down) + (flux_z - roll(flux_z, 1, 1))
                new = temp + DT * (0.5 * div + q_ext[rows_of(block + 1, g)])
                if step < CSWEEPS - 1:
                    rows = rows_of(block, g)
                    results.append((new, k0_all[rows] * inverse(1.0 + b_all[rows] * new * new)))
                else:
                    results.append((new,))
            for g in range(groups):
                store(dst, block, g, *results[g])
            return ahead, flux_y

        first, second = load(src, 0), load(src, 1)
        lax.fori_loop(1, YBLOCKS - 1, advance, (second, y_fluxes(0, first, second)), unroll=12)
    final = state_b if CSWEEPS % 2 else state_a

    def give_out(yq, carry):
        for g in range(TE // SUB):
            x = slice(g * SUB, (g + 1) * SUB)
            turns = []
            for r in range(4):
                value = final[both_of(HALO + 4 * yq + r, g, HALO)[0], :]
                turns.append([turned(value, by) for by in range(4)])
            for pair in range(2):
                even, odd = turns[2 * pair], turns[2 * pair + 1]
                lower = (2 * yq + pair) * LANES
                upper = lower + temp_out.shape[1] // 2
                temp_out[x, pl.ds(pl.multiple_of(lower, LANES), LANES)] = jnp.where(half, even[0], odd[2])
                temp_out[x, pl.ds(pl.multiple_of(upper, LANES), LANES)] = jnp.where(half, even[2], odd[0])
            for c in range(4):
                value = pick([turns[r][(r - c) % 4] for r in range(4)])
                blocks[pl.ds((c * TE + g * SUB) * SUB + yq, SUB, stride=SUB), :] = value
        return carry

    lax.fori_loop(0, HALF // 4, give_out, 0, unroll=4)
    places = []
    mate = j + 1 - 2 * lax.rem(j, 2)
    targets = [(mine, 0, j)] + [(across[d - 1], 0, j + 2 * d) for d in range(1, chips)]
    targets += [(bundle, d * TE * ROW, mate + 2 * d) for d in range(chips)]
    for target, first, to in targets:
        dev = lax.rem(to, width_gy)
        for t in range(TILES):
            tile = i * tiles + dev * TILES + t
            col = pos[1, tile] - 2 * j
            cell = jnp.clip(col, 0, 1) * 2 + pos[2, tile]
            places.append((target, first + t, cell, (col >= 0) & (col < 2)))

    def pack(p, carry):
        values = []
        for _, _, cell, here in places:
            value = blocks[pl.ds(pl.multiple_of((cell * TE + p) * SUB, SUB), SUB), :]
            values.append(jnp.where(here, value, 0.0))
        for (target, first, _, _), value in zip(places, values):
            target[pl.ds(pl.multiple_of(p * ROW, ROW) + first, SUB, stride=TILES), :] = value
        return carry

    lax.fori_loop(0, TE, pack, 0, unroll=8)


def shifted(value, axis, by, wrap=False):
    count = lax.axis_size(axis)
    pairs = [(d, (d + by) % count) for d in range(count) if wrap or 0 <= d + by < count]
    return lax.ppermute(value, axis, pairs)


def with_partner(value, axis, first):
    count = lax.axis_size(axis)
    pairs = [(d, d + 1) for d in range(first, count - 1, 2)]
    return lax.ppermute(value, axis, pairs + [(high, low) for low, high in pairs])


def from_mate(value):
    return lax.ppermute(value, "gy", [(d, d ^ 1) for d in range(lax.axis_size("gy"))])


def to_rows(value):
    return value.reshape(TILES, -1, LANES).transpose(1, 0, 2).reshape(-1, LANES)


def from_rows(value):
    return value.reshape(-1, TILES, LANES).transpose(1, 0, 2).reshape(TILES, -1)


def to_other_core(value, by):
    count = lax.axis_size("gy")
    return lax.ppermute(value, "gy", [(at, ((at ^ 1) + 2 * by) % count) for at in range(count)])


VMEM = pl.BlockSpec(memory_space=pltpu.VMEM)
SMEM = pl.BlockSpec(memory_space=pltpu.SMEM)
HBM = pl.BlockSpec(memory_space=pltpu.HBM)
ANY = pl.BlockSpec(memory_space=pl.ANY)
PARAMS = pltpu.CompilerParams(vmem_limit_bytes=32 * 1024 * 1024)


def on_device(
    phi_init,
    source,
    tile_mat,
    tile_pos,
    neighbours,
    sigma_table,
    temp_init,
    slab_mat,
    k0_table,
    beta_table,
):
    f32 = jnp.float32
    pos = tile_pos.T
    width_gy = lax.axis_size("gy")
    chips = width_gy // 2
    tiles = width_gy * TILES
    size_x, width = temp_init.shape
    edge_rows = width // LANES * SUB

    def rows(count):
        return jax.ShapeDtypeStruct((count, LANES), f32)

    body, ready, sigma, inner, outer = pl.pallas_call(
        prep_kernel,
        out_shape=(
            rows(3 * TE * ROW),
            rows(2 * TE * ROW),
            rows(TE * ROW),
            rows(SIDE_ROWS + edge_rows),
            rows(SIDE_ROWS + edge_rows),
        ),
        in_specs=[SMEM] * 2 + [HBM] * 5,
        out_specs=(VMEM,) * 5,
        scratch_shapes=[
            pltpu.VMEM((TE * ROW, LANES), f32),
            pltpu.VMEM((TE * ROW, LANES), jnp.int32),
            pltpu.VMEM((2, SUB, width), f32),
            pltpu.VMEM((2, SUB, width), jnp.int32),
            pltpu.SemaphoreType.DMA((7,)),
        ],
        compiler_params=pltpu.CompilerParams(vmem_limit_bytes=62 * 1024 * 1024),
        name="prep",
    )(sigma_table, pos, to_rows(phi_init), to_rows(source), to_rows(tile_mat), temp_init, slab_mat)
    bodies = [body] + [shifted(ready, "gy", 2 * d, True) for d in range(1, chips)]
    bodies += [from_mate(part) for part in bodies]
    inner, outer = with_partner(inner, "gx", 0), with_partner(outer, "gx", 1)

    halo = pl.pallas_call(
        relay_kernel,
        out_shape=rows(LOW_ROWS + HIGH_ROWS),
        in_specs=[VMEM] * 2,
        out_specs=VMEM,
        compiler_params=PARAMS,
        name="relay",
    )(inner, outer)
    halos = [halo] + [shifted(halo, "gy", 2 * d, True) for d in range(1, chips)]
    native = pltpu.VMEM((width // LANES * SLABX + SUB, LANES), f32)
    t_ext, k0_ext, b_ext, edge_in, packet = pl.pallas_call(
        slab_kernel,
        out_shape=(rows(SLAB_ROWS),) * 3 + (rows(HALO * SLABX), rows(TE * ROW + HALO * SLABX)),
        in_specs=[SMEM] * 3 + [VMEM] * 5,
        out_specs=(VMEM,) * 5,
        scratch_shapes=[native, native] + [pltpu.VMEM((HALO * SLABX, LANES), f32)] * 2,
        compiler_params=PARAMS,
        name="slab_prep",
    )(pos, k0_table, beta_table, temp_init, slab_mat, inner, outer, sigma)
    y_in = with_partner(edge_in, "gy", 0)
    sigmas = [bodies[0]] + [shifted(sigma, "gy", 2 * d, True) for d in range(1, chips)]
    sigmas += [bodies[chips]] + [
        to_other_core(packet if d in (1, chips - 1) else sigma, d) for d in range(1, chips)
    ]
    *halos[1:], y_in = lax.optimization_barrier((*halos[1:], y_in))
    halos = halos + [from_mate(part) for part in halos]

    def fields(count):
        return pltpu.VMEM((2 * ROW0 + (width_gy + 1) * count * ROW, LANES), f32)

    pot, slope = pl.pallas_call(
        functools.partial(sweep_kernel, chips),
        out_shape=(rows(TE * ROW), rows(CELLS * SLABX * SUB)),
        in_specs=[SMEM] + [ANY] * (2 * width_gy),
        out_specs=(VMEM, VMEM),
        scratch_shapes=[
            pltpu.SMEM((3, 2 * (2 * width_gy + 2)), jnp.int32),
            pltpu.SMEM((3, tiles), jnp.int32),
            pltpu.SMEM((3 * tiles * 8,), jnp.int32),
            fields(TE), fields(TE), fields(LOW[0]), fields(LOW[0]), fields(HIGH[0]), fields(HIGH[0]),
            fields(TE), fields(LOW[1]), fields(HIGH[1]),
            pltpu.SemaphoreType.DMA((6 * width_gy,)),
        ],
        compiler_params=PARAMS,
        name="sweeps",
    )(pos, *bodies, *halos)

    temp, mine, bundle, *across = pl.pallas_call(
        functools.partial(slab_steps_kernel, chips),
        out_shape=(jax.ShapeDtypeStruct((size_x, width), f32), rows(TE * ROW), rows(chips * TE * ROW))
        + (rows(TE * ROW),) * (chips - 1),
        in_specs=[SMEM] * 3 + [ANY] * width_gy + [VMEM] * (width_gy + 5),
        out_specs=(VMEM,) * (2 + chips),
        scratch_shapes=[pltpu.VMEM((CELLS * SLABX * SUB, LANES), f32)]
        + [pltpu.VMEM((SLAB_ROWS + 3 * SLABX, LANES), f32)]
        + [pltpu.VMEM((2 * SLAB_ROWS, LANES), f32)] * 2
        + [pltpu.VMEM((SLAB_ROWS, LANES), f32)] * 2
        + [pltpu.VMEM((4 * TE * SUB, LANES), f32), pltpu.VMEM((width_gy, TE * ROW, LANES), f32)]
        + [pltpu.VMEM((2, HALO * SLABX, LANES), f32), pltpu.SemaphoreType.DMA((width_gy + 2,))],
        compiler_params=PARAMS,
        name="slab_steps",
    )(pos, k0_table, beta_table, *sigmas, *halos, slope, t_ext, k0_ext, b_ext, y_in)
    got = from_mate(bundle).reshape(chips, TE * ROW, LANES)
    tile_temps = mine + got[0]
    for d in range(1, chips):
        tile_temps = tile_temps + shifted(across[d - 1] + got[d], "gy", 2 * d, True)
    return from_rows(pot), temp, from_rows(tile_temps)


def solution(mesh):
    placed = (
        P(("gx", "gy"), None),
        P(("gx", "gy"), None),
        P(("gx", "gy"), None),
        P(),
        P(("gx", "gy"), None),
        P(),
        P("gx", "gy"),
        P("gx", "gy"),
        P(),
        P(),
    )
    return jax.shard_map(
        on_device,
        mesh=mesh,
        in_specs=placed,
        out_specs=(P(("gx", "gy"), None), P("gx", "gy"), P(("gx", "gy"), None)),
        check_vma=False,
    )
```

```python
import functools
import math

import jax
import jax.numpy as jnp
from jax import lax
from jax.experimental import pallas as pl
from jax.experimental.pallas import tpu as pltpu
from jax.sharding import PartitionSpec as P

TE = 32
SWEEPS = 4
CSWEEPS = 3
NZ = 64
EPS = 2.0
DT = 0.15
LANES = 128
SUB = 8
TILES = 2
ROW = SUB * TILES

LOW = (SWEEPS + 2, SWEEPS + 1, 2)
HIGH = (SWEEPS + 3, SWEEPS + 2, 2)
LOW_ROWS = sum(LOW) * ROW
HIGH_ROWS = sum(HIGH) * ROW
SIDE_ROWS = max(LOW_ROWS, HIGH_ROWS)
SLABX = TE + SUB
HALO = CSWEEPS
HALF = TE
YBLOCKS = HALF + 2 * HALO
CELLS = 9
ROW0 = ROW
SLAB_ROWS = ROW0 + YBLOCKS * SLABX + ROW0


def cheb_weight(step, count):
    return 1.0 / (1.0 + 0.75 * math.cos(math.pi * (2 * step + 1) / (2 * count)))


def lookup(table, ids):
    out = jnp.full(ids.shape, table[3], jnp.float32)
    for which in (2, 1, 0):
        out = jnp.where(ids == which, table[which], out)
    return out


def roll(value, by, axis):
    return pltpu.roll(value, by % value.shape[axis], axis)


def prep_kernel(table, pos, phi, src, mat, temp, slab, body, ready, sigma, inner, outer, src_v, mat_v, ends_t, ends_m, sems):
    rows = TE * ROW
    size_x, width = temp.shape
    moves = [(phi, body.at[0:rows]), (src, src_v), (mat, mat_v)]
    for which, first in enumerate((0, size_x - SUB)):
        moves.append((temp.at[first : first + SUB], ends_t.at[which]))
        moves.append((slab.at[first : first + SUB], ends_m.at[which]))
    moves = [pltpu.make_async_copy(*move, sems.at[at]) for at, move in enumerate(moves)]
    for move in moves:
        move.start()
    for move in moves:
        move.wait()
    sigma[...] = lookup(table, mat_v[...])
    body[rows : 2 * rows] = src_v[...] / sigma[...]
    first = (lax.axis_index("gx") * lax.axis_size("gy") + lax.axis_index("gy")) * TILES
    for t in range(TILES):

        @pl.when(pos[2, first + t] == 1)
        def _():
            def plane(p, carry):
                for ref, start in ((body, 0), (body, rows), (sigma, 0)):
                    at = pl.ds(pl.multiple_of(p * ROW, ROW) + (start + t), SUB, stride=TILES)
                    ref[at, :] = roll(ref[at, :], TE, 1)
                return carry

            lax.fori_loop(0, TE, plane, 0, unroll=8)

    ready[...] = body[0 : 2 * rows]
    body[2 * rows : 3 * rows] = sigma[...]
    even = lax.rem(lax.axis_index("gx"), 2) == 0

    @pl.when(even)
    def _():
        fill_sides(body, sigma, ends_t, ends_m, inner, outer)

    @pl.when(jnp.logical_not(even))
    def _():
        fill_sides(body, sigma, ends_t, ends_m, outer, inner)


def fill_sides(body, sigma, ends_t, ends_m, up, down):
    rows = TE * ROW
    width = ends_t.shape[2]
    at_up, at_down = 0, 0
    for ref, first in ((body, 0), (body, rows), (sigma, 0)):
        which = (first // rows) if ref is body else 2
        size = LOW[which] * ROW
        up[at_up : at_up + size] = ref[first + rows - size : first + rows]
        at_up += size
        size = HIGH[which] * ROW
        down[at_down : at_down + size] = ref[first : first + size]
        at_down += size
    sub = lax.broadcasted_iota(jnp.int32, (SUB, LANES), 0)
    for at in range(width // LANES):
        lanes = slice(at * LANES, (at + 1) * LANES)
        t_low, m_low = ends_t[0, :, lanes], ends_m[0, :, lanes].astype(jnp.float32)
        t_high, m_high = ends_t[1, :, lanes], ends_m[1, :, lanes].astype(jnp.float32)
        first = at * SUB
        up[SIDE_ROWS + first : SIDE_ROWS + first + SUB] = jnp.where(sub < 4, roll(t_high, HALO, 0), roll(m_high, -1, 0))
        down[SIDE_ROWS + first : SIDE_ROWS + first + SUB] = jnp.where(sub < 4, t_low, roll(m_low, 4, 0))


def relay_kernel(inner, outer, halo):
    def join(low, high):
        halo[0:LOW_ROWS] = low[0:LOW_ROWS]
        halo[LOW_ROWS:] = high[0:HIGH_ROWS]

    even = lax.rem(lax.axis_index("gx"), 2) == 0
    pl.when(even)(lambda: join(outer, inner))
    pl.when(jnp.logical_not(even))(lambda: join(inner, outer))


def loose(pos):
    return jnp.minimum(pos[0, 0], 0)


def slab_kernel(pos, k0_table, beta_table, temp, mat, inner, outer, sigma, t_ext, k0_ext, b_ext, edge_in, packet, native_t, native_m, edge_low, edge_high):
    start = loose(pos)
    even = lax.rem(lax.axis_index("gx"), 2) == 0
    blocks = temp.shape[1] // LANES
    half = lax.broadcasted_iota(jnp.int32, (SUB, LANES), 1) < NZ
    for which, (own, native) in enumerate(((temp, native_t), (mat, native_m))):
        for at in range(blocks):
            lanes = slice(at * LANES, (at + 1) * LANES)
            first = at * SLABX
            side = slice(SIDE_ROWS + at * SUB, SIDE_ROWS + (at + 1) * SUB)
            value = jnp.where(even, outer[side, :], inner[side, :])
            native[first : first + SUB, :] = roll(value, -4, 0) if which else value
            for g in range(TE // SUB):
                value = own[g * SUB : (g + 1) * SUB, lanes].astype(jnp.float32)
                native[pl.ds(start + first + HALO + g * SUB, SUB), :] = value
            value = jnp.where(even, inner[side, :], outer[side, :])
            native[pl.ds(start + first + HALO + TE, SUB), :] = roll(value, -4, 0) if which else value
    for at in range(blocks // 2):
        for g in range(SLABX // SUB):
            halves = []
            for native in (native_t, native_m):
                lower = native[at * SLABX + g * SUB : at * SLABX + (g + 1) * SUB, :]
                upper_at = (blocks // 2 + at) * SLABX + g * SUB
                upper = native[upper_at : upper_at + SUB, :]
                lower_r, upper_r = roll(lower, NZ, 1), roll(upper, NZ, 1)
                halves.append((lower, lower_r, upper, upper_r))
            for odd in range(2):
                y = 2 * at + odd
                temps, mats = (jnp.where(half, v[odd], v[3 - odd]) for v in halves)
                places = [(y + HALO, temps, mats)]
                if y >= HALF - HALO:
                    places.append((y - HALF + HALO, halves[0][1 - odd], halves[1][1 - odd]))
                if y < HALO:
                    places.append((y + HALF + HALO, halves[0][2 + odd], halves[1][2 + odd]))
                for block, t, m in places:
                    rows = slice(ROW0 + block * SLABX + g * SUB, ROW0 + block * SLABX + (g + 1) * SUB)
                    t_ext[rows] = t
                    k0_ext[rows] = lookup(k0_table, m)
                    b_ext[rows] = lookup(beta_table, m)
                if y < HALO:
                    rows = slice(y * SLABX + g * SUB, y * SLABX + (g + 1) * SUB)
                    edge_low[rows] = jnp.where(half, halves[0][odd], halves[1][1 - odd])
                if y >= HALF - HALO:
                    first = (y - HALF + HALO) * SLABX + g * SUB
                    edge_high[first : first + SUB] = jnp.where(half, halves[0][2 + odd], halves[1][3 - odd])
    even = lax.rem(lax.axis_index("gy"), 2) == 0
    edge_in[...] = jnp.where(even, edge_high[...], edge_low[...])
    packet[0 : TE * ROW] = sigma[...]
    packet[TE * ROW :] = jnp.where(even, edge_low[...], edge_high[...])


def fill_maps(chips, pos, cell_at, cell_of):
    width_gy = 2 * chips
    tiles = width_gy * TILES
    i = lax.axis_index("gx")
    j = lax.axis_index("gy")
    rows_gx = lax.axis_size("gx")
    for at in range(2 * (2 * width_gy + 2)):
        for which in range(3):
            cell_at[which, at] = tiles
    for which, by in enumerate((0, -1, 1)):
        row = i + by
        valid = (row >= 0) & (row < rows_gx)
        first = jnp.clip(row, 0, rows_gx - 1) * tiles
        for part in range(width_gy):
            dev = part_device(part, chips, j)
            for t in range(TILES):
                tile = first + dev * TILES + t
                cell = (pos[1, tile] + 1) * 2 + pos[2, tile]
                slot = part * TILES + t
                cell_of[which, slot] = cell
                cell_at[which, cell] = jnp.where(valid, slot, tiles)


def part_device(part, chips, j):
    mate = j + 1 - 2 * lax.rem(j, 2)
    if isinstance(part, int):
        base, back = (j, part) if part < chips else (mate, part - chips)
    else:
        base = jnp.where(part < chips, j, mate)
        back = lax.rem(part, chips)
    return lax.rem(base - 2 * back + 2 * chips, 2 * chips)


def sweep_kernel(chips, pos, *refs):
    width_gy = 2 * chips
    tiles = width_gy * TILES
    none = tiles
    bodies, halos = refs[:width_gy], refs[width_gy : 2 * width_gy]
    pot, slope, cell_at, cell_of, table, c_buf, l_buf, u_buf, s_c, s_l, s_u, sems = refs[2 * width_gy :]
    c_turn, l_turn, u_turn = (ref.shape[0] // 2 for ref in (c_buf, l_buf, u_buf))
    i = lax.axis_index("gx")
    j = lax.axis_index("gy")
    rows_gx = lax.axis_size("gx")
    zero = jnp.zeros((SUB, LANES), jnp.float32)

    moves = []
    for part in range(width_gy):
        at = 0
        pieces = [(bodies[part], 0, c_buf, part * TE, TE), (bodies[part], TE * ROW, s_c, part * TE, TE)]
        for target, first, count in (
            (l_buf, part * LOW[0], LOW[0]),
            (s_l, part * LOW[1], LOW[1]),
            (None, 0, LOW[2]),
            (u_buf, part * HIGH[0], HIGH[0]),
            (s_u, part * HIGH[1], HIGH[1]),
        ):
            if target is not None:
                pieces.append((halos[part], at, target, first, count))
            at += count * ROW
        for source, start, target, first, count in pieces:
            move = pltpu.make_async_copy(
                source.at[start : start + count * ROW],
                target.at[ROW0 + first * ROW : ROW0 + (first + count) * ROW],
                sems.at[len(moves)],
            )
            move.start()
            moves.append(move)

    fill_maps(chips, pos, cell_at, cell_of)

    def row_of(slot, size):
        pair, second = lax.shift_right_logical(slot, 1), lax.bitwise_and(slot, 1)
        return ROW0 + pair * (size * ROW) + second

    def enter(slot, carry):
        for which, size in enumerate((TE, LOW[0], HIGH[0])):
            cell = cell_of[which, slot]
            upper = lax.bitwise_and(cell, 1)
            beside = cell_at[which, cell + 1 - 2 * upper]
            here = [cell_at[at, cell] for at in range(3)]
            near = (slot, cell_at[which, cell - 2], cell_at[which, cell + 2])
            near += (jnp.where(upper == 1, beside, none), jnp.where(upper == 1, none, beside))
            rows = [row_of(at, size) for at in near]
            if which == 0:
                rows += [row_of(here[1], LOW[0]) + (LOW[0] - 1) * ROW, row_of(here[2], HIGH[0])]
            else:
                centre = row_of(here[0], TE)
                rows += [centre + (TE - 1) * ROW, centre]
            rows.append(upper)
            for at, row in enumerate(rows):
                table[(which * tiles + slot) * 8 + at] = row
        return carry

    lax.fori_loop(0, tiles, enter, 0)

    def entry(which, slot):
        return [table[(which * tiles + slot) * 8 + at] for at in range(8)]

    def plane_at(ref, row):
        return ref[pl.ds(row, SUB, stride=TILES), :]

    def put_plane(ref, row, value):
        ref[pl.ds(row, SUB, stride=TILES), :] = value

    for ref, count in ((c_buf, TE), (l_buf, LOW[0]), (u_buf, HIGH[0])):
        for first in (0, ref.shape[0] // 2):
            first = first + ROW0 + width_gy * count * ROW
            for row in range(first, first + count * ROW, SUB):
                ref[row : row + SUB] = zero

    def clear(at, carry):
        slope[pl.ds(pl.multiple_of(at * SUB, SUB), SUB), :] = zero
        return carry

    lax.fori_loop(0, slope.shape[0] // SUB, clear, 0, unroll=8)
    for move in moves:
        move.wait()

    lane = lax.broadcasted_iota(jnp.int32, (SUB, LANES), 1)
    sub = lax.broadcasted_iota(jnp.int32, (SUB, LANES), 0)
    depth = lane % TE
    first_sub, last_sub = sub == 0, sub == SUB - 1
    first_z, last_z = depth == 0, depth == TE - 1

    def y_plus(ref, own, first_y, row, ghost_row):
        turned = jnp.where(last_sub, plane_at(ref, ghost_row), plane_at(ref, row))
        return roll(jnp.where(first_y, turned, own), -TE, 1)

    def y_minus(ref, own, last_y, row, ghost_row):
        turned = jnp.where(first_sub, plane_at(ref, ghost_row), plane_at(ref, row))
        return roll(jnp.where(last_y, turned, own), TE, 1)

    def z_plus(ref, own, ghost_row):
        return roll(jnp.where(first_z, plane_at(ref, ghost_row), own), -1, 1)

    def z_minus(ref, own, ghost_row):
        return roll(jnp.where(last_z, plane_at(ref, ghost_row), own), 1, 1)

    def y_ends(upper):
        quarter = lane // TE
        return quarter == upper, quarter == lax.bitwise_and(upper + 3, 3)

    def relax(ref, places, now, after_turn, first, count, s_ref, s_row, before, beyond, keep, gain):
        row, row_m, row_p, row_zm, row_zp, _, _, upper = places
        target = row + after_turn
        row, row_m, row_p, row_zm, row_zp = (at + now for at in (row, row_m, row_p, row_zm, row_zp))
        first_y, last_y = y_ends(upper)
        own = plane_at(ref, row + first * ROW)
        results = []
        for p in range(count):
            step = (first + p) * ROW
            after = plane_at(ref, row + (step + ROW)) if p < count - 1 else beyond
            total = (before + after) + plane_at(s_ref, s_row + p * ROW)
            along_y = y_minus(ref, own, last_y, row + (step - TILES), row_m + (step + ROW - TILES))
            along_y = along_y + y_plus(ref, own, first_y, row + (step + TILES), row_p + (step + TILES - ROW))
            along_z = z_minus(ref, own, row_zm + step) + z_plus(ref, own, row_zp + step)
            results.append(keep * own + gain * (total + (along_y + along_z)))
            before, own = own, after
            if len(results) == 8 or p == count - 1:
                for at, value in enumerate(results, p + 1 - len(results)):
                    put_plane(ref, target + (first + at) * ROW, value)
                results = []

    def sweep(k, carry):
        parity = lax.bitwise_and(k, 1)
        c_now, l_now, u_now = parity * c_turn, parity * l_turn, parity * u_turn
        weights = [cheb_weight(at, SWEEPS) for at in range(SWEEPS)]
        keep, gain = jnp.float32(1.0 - weights[0]), jnp.float32(weights[0] / (6.0 + EPS))
        for at in range(1, SWEEPS):
            keep = jnp.where(k == at, jnp.float32(1.0 - weights[at]), keep)
            gain = jnp.where(k == at, jnp.float32(weights[at] / (6.0 + EPS)), gain)

        def sweep_tile(slot, carry):
            at = entry(0, slot)
            ends = plane_at(l_buf, at[5] + l_now), plane_at(u_buf, at[6] + u_now)
            relax(c_buf, at, c_now, c_turn - c_now, 0, TE, s_c, at[0], *ends, keep, gain)
            at = entry(1, slot)
            ends = plane_at(l_buf, at[0] + l_now), plane_at(c_buf, at[6] + c_now)
            relax(l_buf, at, l_now, l_turn - l_now, 1, LOW[0] - 1, s_l, row_of(slot, LOW[1]), *ends, keep, gain)
            at = entry(2, slot)
            ends = plane_at(c_buf, at[5] + c_now), plane_at(u_buf, at[0] + u_now + (HIGH[0] - 1) * ROW)
            relax(u_buf, at, u_now, u_turn - u_now, 0, HIGH[0] - 1, s_u, row_of(slot, HIGH[1]), *ends, keep, gain)
            return carry

        lax.fori_loop(0, tiles, sweep_tile, 0, unroll=2)
        return carry

    lax.fori_loop(0, SWEEPS, sweep, 0)

    assert SWEEPS % 2 == 0
    field, f_l, f_u = c_buf, l_buf, u_buf
    for t in range(TILES):
        turn = jnp.where(table[t * 8 + 7] == 1, LANES - TE, 0)

        def turn_back(p, carry):
            value = plane_at(field, p * ROW + (ROW0 + t))
            put_plane(pot, pl.multiple_of(p * ROW, ROW) + t, pltpu.roll(value, turn, 1))
            return carry

        lax.fori_loop(0, TE, turn_back, 0, unroll=8)

    def squares(ref, places, local, x, first, count, beyond):
        row, _, row_p, _, row_z, _, _, upper = places
        first_y, _ = y_ends(upper)
        target = (local * SLABX + x) * SUB
        own = plane_at(ref, row + first * ROW)
        for p in range(count):
            step = (first + p) * ROW
            after = plane_at(ref, row + (step + ROW)) if beyond is None or p < count - 1 else beyond
            d_x = after - own
            d_y = y_plus(ref, own, first_y, row + (step + TILES), row_p + (step + TILES - ROW)) - own
            d_z = z_plus(ref, own, row_z + step) - own
            rows = pl.ds(pl.multiple_of(target + p * SUB, SUB), SUB)
            slope[rows, :] = d_x * d_x + d_y * d_y + d_z * d_z
            own = after

    def slope_tile(slot, carry):
        at, local = entry(0, slot), window(0, cell_of[0, slot], i, j, rows_gx)
        squares(field, at, local, HALO, 0, TE, plane_at(f_u, at[6]))
        at, local = entry(1, slot), window(1, cell_of[1, slot], i, j, rows_gx)
        squares(f_l, at, local, HALO - 2, LOW[0] - 2, 2, plane_at(field, at[6]))
        at, local = entry(2, slot), window(2, cell_of[2, slot], i, j, rows_gx)
        squares(f_u, at, local, HALO + TE, 0, 2, None)
        return carry

    lax.fori_loop(0, tiles, slope_tile, 0)


def window(which, cell, i, j, rows_gx):
    local = cell - 4 * j
    inside = (local >= 0) & (local < CELLS - 1)
    if which > 0:
        row = i - 1 if which == 1 else i + 1
        inside = inside & (row >= 0) & (row < rows_gx)
    return jnp.where(inside, local, CELLS - 1)


def slab_steps_kernel(chips, pos, k0_table, beta_table, *refs):
    width_gy = 2 * chips
    tiles = width_gy * TILES
    halos = refs[width_gy : 2 * width_gy]
    slope, t_in, k0_in, b_in, y_in, temp_out = refs[2 * width_gy : 2 * width_gy + 6]
    mine, bundle = refs[2 * width_gy + 6 : 2 * width_gy + 8]
    across = refs[2 * width_gy + 8 : 2 * width_gy + 7 + chips]
    heat, q_ext, state, k0_all, b_all, blocks, sigmas, y_out, sems = refs[2 * width_gy + 7 + chips :]
    moves = []
    for part in range(width_gy):
        start = 2 * TE * ROW if part % chips == 0 else 0
        source = refs[part].at[start : start + TE * ROW]
        target = sigmas.at[part * TE * ROW : (part + 1) * TE * ROW]
        moves.append(pltpu.make_async_copy(source, target, sems.at[part]))
        moves[-1].start()
    edges = []
    for which, d in enumerate((1, chips - 1)):
        source = refs[chips + d].at[TE * ROW : TE * ROW + HALO * SLABX]
        edges.append(pltpu.make_async_copy(source, y_out.at[which], sems.at[width_gy + which]))
        edges[-1].start()
    i = lax.axis_index("gx")
    j = lax.axis_index("gy")
    rows_gx = lax.axis_size("gx")
    lane = lax.broadcasted_iota(jnp.int32, (SUB, LANES), 1)
    zero = jnp.zeros((SUB, LANES), jnp.float32)

    quarter = [(lane >= q * TE) & (lane < (q + 1) * TE) for q in range(3)]

    def pick(parts):
        return jnp.where(
            quarter[0], parts[0], jnp.where(quarter[1], parts[1], jnp.where(quarter[2], parts[2], parts[3]))
        )

    def turned(value, by):
        return value if by % 4 == 0 else roll(value, by * TE, 1)

    def rows_of(block, g):
        first = ROW0 + block * SLABX + g * SUB
        if not isinstance(first, int):
            first = pl.multiple_of(first, SUB)
        return pl.ds(first, SUB)

    groups = SLABX // SUB

    sub = lax.broadcasted_iota(jnp.int32, (SUB, LANES), 0)
    half = lane < NZ
    no_z = lane % NZ == NZ - 1
    low_x = (sub == HALO - 1) & (i == 0), (sub == HALO) & (i == 0)
    high_x = (sub == (HALO + TE - 1) % SUB) & (i == rows_gx - 1)
    low_y, high_y = half & (j == 0), (lane >= NZ) & (j == width_gy - 1)

    def inverse(value):
        near = pl.reciprocal(value, approx=True)
        near = near * (2.0 - value * near)
        return near * (2.0 - value * near)

    def both_of(base, g, by=0):
        first = base + 2 * (g * SUB + by)
        return pl.ds(first, SUB, stride=2), pl.ds(first + 1, SUB, stride=2)

    def base_of(block):
        return 2 * ROW0 + block * (2 * SLABX)

    def load(base, by=0):
        places = [both_of(base, g, by) for g in range(groups)]
        return [state[at, :] for at, _ in places], [state[at, :] for _, at in places]

    def store(base, g, temp, cond):
        first, second = both_of(base, g)
        state[first, :], state[second, :] = temp, cond

    even = lax.rem(j, 2) == 0

    def begin(block, low, at):
        values = []
        for g in range(groups):
            rows = rows_of(block, g)
            temp, k0, beta = t_in[rows], k0_in[rows], b_in[rows]
            if low is not None:
                place = slice(at * SLABX + g * SUB, at * SLABX + (g + 1) * SUB)
                other = jnp.where(even, y_out[0, place], y_out[1, place])
                value = jnp.where(even, *((other, y_in[place])[:: 1 if low else -1]))
                swapped = roll(value, NZ, 1)
                if low:
                    temp = jnp.where(half, value, temp)
                    k0 = jnp.where(half, lookup(k0_table, swapped), k0)
                    beta = jnp.where(half, lookup(beta_table, swapped), beta)
                else:
                    temp = jnp.where(half, temp, swapped)
                    k0 = jnp.where(half, k0, lookup(k0_table, value))
                    beta = jnp.where(half, beta, lookup(beta_table, value))
            values.append((rows, temp, k0, beta, k0 * inverse(1.0 + beta * temp * temp)))
        for g, (rows, temp, k0, beta, cond) in enumerate(values):
            k0_all[rows], b_all[rows] = k0, beta
            store(base_of(block), g, temp, cond)

    def begin_inner(block, carry):
        begin(block, None, 0)
        return carry

    lax.fori_loop(HALO, YBLOCKS - HALO, begin_inner, 0, unroll=4)
    for move in edges:
        move.wait()
    for e in range(HALO):
        begin(e, True, e)
        begin(YBLOCKS - HALO + e, False, e)

    def clear(at, carry):
        heat[pl.ds(pl.multiple_of(at * SUB, SUB), SUB), :] = zero
        return carry

    lax.fori_loop(0, heat.shape[0] // SUB, clear, 0, unroll=8)
    for move in moves:
        move.wait()
    low_at, high_at = (LOW[0] + LOW[1]) * ROW, LOW_ROWS + (HIGH[0] + HIGH[1]) * ROW
    def put_heat(which, by, dev, t, x, count, sigma_of):
        tile = jnp.clip(i + by, 0, rows_gx - 1) * tiles + dev * TILES + t
        cell = (pos[1, tile] + 1) * 2 + pos[2, tile]
        first = pl.multiple_of((window(which, cell, i, j, rows_gx) * SLABX + x) * SUB, SUB)
        for p in range(count):
            rows = pl.ds(pl.multiple_of(first + p * SUB, SUB), SUB)
            heat[rows, :] = sigma_of(p) * slope[rows, :]

    def own_heat(slot, carry):
        part, t = lax.div(slot, TILES), lax.rem(slot, TILES)
        row = part * (TE * ROW) + t
        dev = part_device(part, chips, j)
        put_heat(0, 0, dev, t, HALO, TE, lambda p: sigmas[pl.ds(row + p * ROW, SUB, stride=TILES), :])
        return carry

    lax.fori_loop(0, tiles, own_heat, 0)
    for part in range(width_gy):
        dev = part_device(part, chips, j)
        for t in range(TILES):
            for which, by, x, at in ((1, -1, HALO - 2, low_at), (2, 1, HALO + TE, high_at)):
                rows = lambda p: pl.ds(at + p * ROW + t, SUB, stride=TILES)
                put_heat(which, by, dev, t, x, 2, lambda p: halos[part][rows(p), :])

    def place_heat(at, carry):
        first = at - 1
        col, yq = lax.div(first * 4 + TE, TE), lax.rem(first * 4 + TE, TE) // 4
        for g in range(groups):
            cells = [
                heat[pl.ds(pl.multiple_of(((2 * col + c) * SLABX + g * SUB) * SUB, SUB) + yq, SUB, stride=SUB), :]
                for c in range(4)
            ]
            for r in range(4):
                block = 4 * first + r + HALO + 1
                q_ext[rows_of(block, g)] = pick([turned(cells[c], c - r - c % 2) for c in range(4)])
        return carry

    lax.fori_loop(0, HALF // 4 + 2, place_heat, 0, unroll=2)

    turn = state.shape[0] // 2

    def flux(now, other, g, closed=None):
        value = (now[1][g] + other[1][g]) * (other[0][g] - now[0][g])
        return value if closed is None else jnp.where(closed, 0.0, value)

    def y_fluxes(block, now, ahead):
        closed = (low_y & (block == HALO - 1)) | (high_y & (block == HALO + HALF - 1))
        return [flux(now, ahead, g, closed) for g in range(groups)]

    def conduct(step, carry):
        source = lax.bitwise_and(step, 1) * turn
        target = turn - source

        def advance(block, carry):
            now, before = carry
            base = source + base_of(block)
            ahead = load(base + 2 * SLABX)
            flux_y = y_fluxes(block, now, ahead)
            x_p, x_m = load(base, 1), load(base, -1)
            results = []
            for g in range(groups):
                temp, cond = now[0][g], now[1][g]
                up = flux(now, x_p, g, {0: low_x[0], groups - 1: high_x}.get(g))
                down = flux(now, x_m, g, {0: low_x[1]}.get(g))
                flux_z = (cond + roll(cond, -1, 1)) * (roll(temp, -1, 1) - temp)
                flux_z = jnp.where(no_z, 0.0, flux_z)
                div = (flux_y[g] - before[g]) + (up + down) + (flux_z - roll(flux_z, 1, 1))
                new = temp + DT * (0.5 * div + q_ext[rows_of(block + 1, g)])
                rows = rows_of(block, g)
                results.append((new, k0_all[rows] * inverse(1.0 + b_all[rows] * new * new)))
            for g in range(groups):
                store(target + base_of(block), g, *results[g])
            return ahead, flux_y

        first, second = load(source + base_of(0)), load(source + base_of(1))
        lax.fori_loop(1, YBLOCKS - 1, advance, (second, y_fluxes(0, first, second)), unroll=6)
        return carry

    lax.fori_loop(0, CSWEEPS, conduct, 0)
    final = (CSWEEPS % 2) * turn

    def give_out(yq, carry):
        for g in range(TE // SUB):
            x = slice(g * SUB, (g + 1) * SUB)
            turns = []
            for r in range(4):
                value = state[both_of(final + base_of(HALO + 4 * yq + r), g, HALO)[0], :]
                turns.append([turned(value, by) for by in range(4)])
            for pair in range(2):
                even, odd = turns[2 * pair], turns[2 * pair + 1]
                lower = (2 * yq + pair) * LANES
                upper = lower + temp_out.shape[1] // 2
                temp_out[x, pl.ds(pl.multiple_of(lower, LANES), LANES)] = jnp.where(half, even[0], odd[2])
                temp_out[x, pl.ds(pl.multiple_of(upper, LANES), LANES)] = jnp.where(half, even[2], odd[0])
            for c in range(4):
                value = pick([turns[r][(r - c) % 4] for r in range(4)])
                blocks[pl.ds((c * TE + g * SUB) * SUB + yq, SUB, stride=SUB), :] = value
        return carry

    lax.fori_loop(0, HALF // 4, give_out, 0, unroll=2)
    places = []
    mate = j + 1 - 2 * lax.rem(j, 2)
    targets = [(mine, 0, j)] + [(across[d - 1], 0, j + 2 * d) for d in range(1, chips)]
    targets += [(bundle, d * TE * ROW, mate + 2 * d) for d in range(chips)]
    for target, first, to in targets:
        dev = lax.rem(to, width_gy)
        for t in range(TILES):
            tile = i * tiles + dev * TILES + t
            col = pos[1, tile] - 2 * j
            cell = jnp.clip(col, 0, 1) * 2 + pos[2, tile]
            places.append((target, first + t, cell, (col >= 0) & (col < 2)))

    def pack(p, carry):
        values = []
        for _, _, cell, here in places:
            value = blocks[pl.ds(pl.multiple_of((cell * TE + p) * SUB, SUB), SUB), :]
            values.append(jnp.where(here, value, 0.0))
        for (target, first, _, _), value in zip(places, values):
            target[pl.ds(pl.multiple_of(p * ROW, ROW) + first, SUB, stride=TILES), :] = value
        return carry

    lax.fori_loop(0, TE, pack, 0, unroll=4)


def shifted(value, axis, by, wrap=False):
    count = lax.axis_size(axis)
    pairs = [(d, (d + by) % count) for d in range(count) if wrap or 0 <= d + by < count]
    return lax.ppermute(value, axis, pairs)


def with_partner(value, axis, first):
    count = lax.axis_size(axis)
    pairs = [(d, d + 1) for d in range(first, count - 1, 2)]
    return lax.ppermute(value, axis, pairs + [(high, low) for low, high in pairs])


def from_mate(value):
    return lax.ppermute(value, "gy", [(d, d ^ 1) for d in range(lax.axis_size("gy"))])


def to_rows(value):
    return value.reshape(TILES, -1, LANES).transpose(1, 0, 2).reshape(-1, LANES)


def from_rows(value):
    return value.reshape(-1, TILES, LANES).transpose(1, 0, 2).reshape(TILES, -1)


def to_other_core(value, by):
    count = lax.axis_size("gy")
    return lax.ppermute(value, "gy", [(at, ((at ^ 1) + 2 * by) % count) for at in range(count)])


VMEM = pl.BlockSpec(memory_space=pltpu.VMEM)
SMEM = pl.BlockSpec(memory_space=pltpu.SMEM)
HBM = pl.BlockSpec(memory_space=pltpu.HBM)
ANY = pl.BlockSpec(memory_space=pl.ANY)
PARAMS = pltpu.CompilerParams(vmem_limit_bytes=32 * 1024 * 1024)


def on_device(
    phi_init,
    source,
    tile_mat,
    tile_pos,
    neighbours,
    sigma_table,
    temp_init,
    slab_mat,
    k0_table,
    beta_table,
):
    f32 = jnp.float32
    pos = tile_pos.T
    width_gy = lax.axis_size("gy")
    chips = width_gy // 2
    tiles = width_gy * TILES
    size_x, width = temp_init.shape
    edge_rows = width // LANES * SUB

    def rows(count):
        return jax.ShapeDtypeStruct((count, LANES), f32)

    body, ready, sigma, inner, outer = pl.pallas_call(
        prep_kernel,
        out_shape=(
            rows(3 * TE * ROW),
            rows(2 * TE * ROW),
            rows(TE * ROW),
            rows(SIDE_ROWS + edge_rows),
            rows(SIDE_ROWS + edge_rows),
        ),
        in_specs=[SMEM] * 2 + [HBM] * 5,
        out_specs=(VMEM,) * 5,
        scratch_shapes=[
            pltpu.VMEM((TE * ROW, LANES), f32),
            pltpu.VMEM((TE * ROW, LANES), jnp.int32),
            pltpu.VMEM((2, SUB, width), f32),
            pltpu.VMEM((2, SUB, width), jnp.int32),
            pltpu.SemaphoreType.DMA((7,)),
        ],
        compiler_params=pltpu.CompilerParams(vmem_limit_bytes=62 * 1024 * 1024),
        name="prep",
    )(sigma_table, pos, to_rows(phi_init), to_rows(source), to_rows(tile_mat), temp_init, slab_mat)
    bodies = [body] + [shifted(ready, "gy", 2 * d, True) for d in range(1, chips)]
    bodies += [from_mate(part) for part in bodies]
    inner, outer = with_partner(inner, "gx", 0), with_partner(outer, "gx", 1)

    halo = pl.pallas_call(
        relay_kernel,
        out_shape=rows(LOW_ROWS + HIGH_ROWS),
        in_specs=[VMEM] * 2,
        out_specs=VMEM,
        compiler_params=PARAMS,
        name="relay",
    )(inner, outer)
    halos = [halo] + [shifted(halo, "gy", 2 * d, True) for d in range(1, chips)]
    native = pltpu.VMEM((width // LANES * SLABX + SUB, LANES), f32)
    t_ext, k0_ext, b_ext, edge_in, packet = pl.pallas_call(
        slab_kernel,
        out_shape=(rows(SLAB_ROWS),) * 3 + (rows(HALO * SLABX), rows(TE * ROW + HALO * SLABX)),
        in_specs=[SMEM] * 3 + [VMEM] * 5,
        out_specs=(VMEM,) * 5,
        scratch_shapes=[native, native] + [pltpu.VMEM((HALO * SLABX, LANES), f32)] * 2,
        compiler_params=PARAMS,
        name="slab_prep",
    )(pos, k0_table, beta_table, temp_init, slab_mat, inner, outer, sigma)
    y_in = with_partner(edge_in, "gy", 0)
    sigmas = [bodies[0]] + [shifted(sigma, "gy", 2 * d, True) for d in range(1, chips)]
    sigmas += [bodies[chips]] + [
        to_other_core(packet if d in (1, chips - 1) else sigma, d) for d in range(1, chips)
    ]
    *halos[1:], y_in = lax.optimization_barrier((*halos[1:], y_in))
    halos = halos + [from_mate(part) for part in halos]

    def fields(count, buffers=1):
        return pltpu.VMEM((buffers * (2 * ROW0 + (width_gy + 1) * count * ROW), LANES), f32)

    pot, slope = pl.pallas_call(
        functools.partial(sweep_kernel, chips),
        out_shape=(rows(TE * ROW), rows(CELLS * SLABX * SUB)),
        in_specs=[SMEM] + [ANY] * (2 * width_gy),
        out_specs=(VMEM, VMEM),
        scratch_shapes=[
            pltpu.SMEM((3, 2 * (2 * width_gy + 2)), jnp.int32),
            pltpu.SMEM((3, tiles), jnp.int32),
            pltpu.SMEM((3 * tiles * 8,), jnp.int32),
            fields(TE, 2), fields(LOW[0], 2), fields(HIGH[0], 2),
            fields(TE), fields(LOW[1]), fields(HIGH[1]),
            pltpu.SemaphoreType.DMA((6 * width_gy,)),
        ],
        compiler_params=PARAMS,
        name="sweeps",
    )(pos, *bodies, *halos)

    temp, mine, bundle, *across = pl.pallas_call(
        functools.partial(slab_steps_kernel, chips),
        out_shape=(jax.ShapeDtypeStruct((size_x, width), f32), rows(TE * ROW), rows(chips * TE * ROW))
        + (rows(TE * ROW),) * (chips - 1),
        in_specs=[SMEM] * 3 + [ANY] * width_gy + [VMEM] * (width_gy + 5),
        out_specs=(VMEM,) * (2 + chips),
        scratch_shapes=[pltpu.VMEM((CELLS * SLABX * SUB, LANES), f32)]
        + [pltpu.VMEM((SLAB_ROWS + 3 * SLABX, LANES), f32)]
        + [pltpu.VMEM((4 * SLAB_ROWS, LANES), f32)]
        + [pltpu.VMEM((SLAB_ROWS, LANES), f32)] * 2
        + [pltpu.VMEM((4 * TE * SUB, LANES), f32), pltpu.VMEM((width_gy * TE * ROW, LANES), f32)]
        + [pltpu.VMEM((2, HALO * SLABX, LANES), f32), pltpu.SemaphoreType.DMA((width_gy + 2,))],
        compiler_params=PARAMS,
        name="slab_steps",
    )(pos, k0_table, beta_table, *sigmas, *halos, slope, t_ext, k0_ext, b_ext, y_in)
    got = from_mate(bundle).reshape(chips, TE * ROW, LANES)
    tile_temps = mine + got[0]
    for d in range(1, chips):
        tile_temps = tile_temps + shifted(across[d - 1] + got[d], "gy", 2 * d, True)
    return from_rows(pot), temp, from_rows(tile_temps)


def solution(mesh):
    placed = (
        P(("gx", "gy"), None),
        P(("gx", "gy"), None),
        P(("gx", "gy"), None),
        P(),
        P(("gx", "gy"), None),
        P(),
        P("gx", "gy"),
        P("gx", "gy"),
        P(),
        P(),
    )
    return jax.shard_map(
        on_device,
        mesh=mesh,
        in_specs=placed,
        out_specs=(P(("gx", "gy"), None), P("gx", "gy"), P(("gx", "gy"), None)),
        check_vma=False,
    )
```

```python
import functools
import math

import jax
import jax.numpy as jnp
from jax import lax
from jax.experimental import pallas as pl
from jax.experimental.pallas import tpu as pltpu
from jax.sharding import PartitionSpec as P

TE = 32
SWEEPS = 4
CSWEEPS = 3
NZ = 64
EPS = 2.0
DT = 0.15
LANES = 128
SUB = 8
TILES = 2
ROW = SUB * TILES

LOW = (SWEEPS + 2, SWEEPS + 1, 2)
HIGH = (SWEEPS + 3, SWEEPS + 2, 2)
LOW_ROWS = sum(LOW) * ROW
HIGH_ROWS = sum(HIGH) * ROW
SIDE_ROWS = max(LOW_ROWS, HIGH_ROWS)
SLABX = TE + SUB
HALO = CSWEEPS
HALF = TE
YBLOCKS = HALF + 2 * HALO
CELLS = 9
ROW0 = ROW
SLAB_ROWS = ROW0 + YBLOCKS * SLABX + ROW0


def cheb_weight(step, count):
    return 1.0 / (1.0 + 0.75 * math.cos(math.pi * (2 * step + 1) / (2 * count)))


def lookup(table, ids):
    out = jnp.full(ids.shape, table[3], jnp.float32)
    for which in (2, 1, 0):
        out = jnp.where(ids == which, table[which], out)
    return out


def roll(value, by, axis):
    return pltpu.roll(value, by % value.shape[axis], axis)


def prep_kernel(table, pos, phi, src, mat, temp, slab, body, ready, sigma, inner, outer, src_v, mat_v, ends_t, ends_m, sems):
    rows = TE * ROW
    size_x, width = temp.shape
    moves = [(phi, body.at[0:rows]), (src, src_v), (mat, mat_v)]
    for which, first in enumerate((0, size_x - SUB)):
        moves.append((temp.at[first : first + SUB], ends_t.at[which]))
        moves.append((slab.at[first : first + SUB], ends_m.at[which]))
    moves = [pltpu.make_async_copy(*move, sems.at[at]) for at, move in enumerate(moves)]
    for move in moves:
        move.start()
    for move in moves:
        move.wait()
    sigma[...] = lookup(table, mat_v[...])
    body[rows : 2 * rows] = src_v[...] / sigma[...]
    first = (lax.axis_index("gx") * lax.axis_size("gy") + lax.axis_index("gy")) * TILES
    for t in range(TILES):

        @pl.when(pos[2, first + t] == 1)
        def _():
            def plane(p, carry):
                for ref, start in ((body, 0), (body, rows), (sigma, 0)):
                    at = pl.ds(pl.multiple_of(p * ROW, ROW) + (start + t), SUB, stride=TILES)
                    ref[at, :] = roll(ref[at, :], TE, 1)
                return carry

            lax.fori_loop(0, TE, plane, 0, unroll=8)

    ready[...] = body[0 : 2 * rows]
    body[2 * rows : 3 * rows] = sigma[...]
    even = lax.rem(lax.axis_index("gx"), 2) == 0

    @pl.when(even)
    def _():
        fill_sides(body, sigma, ends_t, ends_m, inner, outer)

    @pl.when(jnp.logical_not(even))
    def _():
        fill_sides(body, sigma, ends_t, ends_m, outer, inner)


def fill_sides(body, sigma, ends_t, ends_m, up, down):
    rows = TE * ROW
    width = ends_t.shape[2]
    at_up, at_down = 0, 0
    for ref, first in ((body, 0), (body, rows), (sigma, 0)):
        which = (first // rows) if ref is body else 2
        size = LOW[which] * ROW
        up[at_up : at_up + size] = ref[first + rows - size : first + rows]
        at_up += size
        size = HIGH[which] * ROW
        down[at_down : at_down + size] = ref[first : first + size]
        at_down += size
    sub = lax.broadcasted_iota(jnp.int32, (SUB, LANES), 0)
    for at in range(width // LANES):
        lanes = slice(at * LANES, (at + 1) * LANES)
        t_low, m_low = ends_t[0, :, lanes], ends_m[0, :, lanes].astype(jnp.float32)
        t_high, m_high = ends_t[1, :, lanes], ends_m[1, :, lanes].astype(jnp.float32)
        first = at * SUB
        up[SIDE_ROWS + first : SIDE_ROWS + first + SUB] = jnp.where(sub < 4, roll(t_high, HALO, 0), roll(m_high, -1, 0))
        down[SIDE_ROWS + first : SIDE_ROWS + first + SUB] = jnp.where(sub < 4, t_low, roll(m_low, 4, 0))


def relay_kernel(inner, outer, halo):
    def join(low, high):
        halo[0:LOW_ROWS] = low[0:LOW_ROWS]
        halo[LOW_ROWS:] = high[0:HIGH_ROWS]

    even = lax.rem(lax.axis_index("gx"), 2) == 0
    pl.when(even)(lambda: join(outer, inner))
    pl.when(jnp.logical_not(even))(lambda: join(inner, outer))


def loose(pos):
    return jnp.minimum(pos[0, 0], 0)


def slab_kernel(pos, k0_table, beta_table, temp, mat, inner, outer, t_ext, k0_ext, b_ext, edge_in, edge_out, native_t, native_m, edge_low, edge_high):
    start = loose(pos)
    even = lax.rem(lax.axis_index("gx"), 2) == 0
    blocks = temp.shape[1] // LANES
    half = lax.broadcasted_iota(jnp.int32, (SUB, LANES), 1) < NZ
    for which, (own, native) in enumerate(((temp, native_t), (mat, native_m))):
        for at in range(blocks):
            lanes = slice(at * LANES, (at + 1) * LANES)
            first = at * SLABX
            side = slice(SIDE_ROWS + at * SUB, SIDE_ROWS + (at + 1) * SUB)
            value = jnp.where(even, outer[side, :], inner[side, :])
            native[first : first + SUB, :] = roll(value, -4, 0) if which else value
            for g in range(TE // SUB):
                value = own[g * SUB : (g + 1) * SUB, lanes].astype(jnp.float32)
                native[pl.ds(start + first + HALO + g * SUB, SUB), :] = value
            value = jnp.where(even, inner[side, :], outer[side, :])
            native[pl.ds(start + first + HALO + TE, SUB), :] = roll(value, -4, 0) if which else value
    for at in range(blocks // 2):
        for g in range(SLABX // SUB):
            halves = []
            for native in (native_t, native_m):
                lower = native[at * SLABX + g * SUB : at * SLABX + (g + 1) * SUB, :]
                upper_at = (blocks // 2 + at) * SLABX + g * SUB
                upper = native[upper_at : upper_at + SUB, :]
                lower_r, upper_r = roll(lower, NZ, 1), roll(upper, NZ, 1)
                halves.append((lower, lower_r, upper, upper_r))
            for odd in range(2):
                y = 2 * at + odd
                temps, mats = (jnp.where(half, v[odd], v[3 - odd]) for v in halves)
                places = [(y + HALO, temps, mats)]
                if y >= HALF - HALO:
                    places.append((y - HALF + HALO, halves[0][1 - odd], halves[1][1 - odd]))
                if y < HALO:
                    places.append((y + HALF + HALO, halves[0][2 + odd], halves[1][2 + odd]))
                for block, t, m in places:
                    rows = slice(ROW0 + block * SLABX + g * SUB, ROW0 + block * SLABX + (g + 1) * SUB)
                    t_ext[rows] = t
                    k0_ext[rows] = lookup(k0_table, m)
                    b_ext[rows] = lookup(beta_table, m)
                if y < HALO:
                    rows = slice(y * SLABX + g * SUB, y * SLABX + (g + 1) * SUB)
                    edge_low[rows] = jnp.where(half, halves[0][odd], halves[1][1 - odd])
                if y >= HALF - HALO:
                    first = (y - HALF + HALO) * SLABX + g * SUB
                    edge_high[first : first + SUB] = jnp.where(half, halves[0][2 + odd], halves[1][3 - odd])
    even = lax.rem(lax.axis_index("gy"), 2) == 0
    edge_in[...] = jnp.where(even, edge_high[...], edge_low[...])
    edge_out[...] = jnp.where(even, edge_low[...], edge_high[...])


def fill_maps(chips, pos, cell_at, cell_of):
    width_gy = 2 * chips
    tiles = width_gy * TILES
    i = lax.axis_index("gx")
    j = lax.axis_index("gy")
    rows_gx = lax.axis_size("gx")
    for at in range(2 * (2 * width_gy + 2)):
        for which in range(3):
            cell_at[which, at] = tiles
    for which, by in enumerate((0, -1, 1)):
        row = i + by
        valid = (row >= 0) & (row < rows_gx)
        first = jnp.clip(row, 0, rows_gx - 1) * tiles
        for part in range(width_gy):
            dev = part_device(part, chips, j)
            for t in range(TILES):
                tile = first + dev * TILES + t
                cell = (pos[1, tile] + 1) * 2 + pos[2, tile]
                slot = part * TILES + t
                cell_of[which, slot] = cell
                cell_at[which, cell] = jnp.where(valid, slot, tiles)


def part_device(part, chips, j):
    mate = j + 1 - 2 * lax.rem(j, 2)
    if isinstance(part, int):
        base, back = (j, part) if part < chips else (mate, part - chips)
    else:
        base = jnp.where(part < chips, j, mate)
        back = lax.rem(part, chips)
    return lax.rem(base - 2 * back + 2 * chips, 2 * chips)


def sweep_kernel(chips, pos, *refs):
    width_gy = 2 * chips
    tiles = width_gy * TILES
    none = tiles
    bodies, halos = refs[:width_gy], refs[width_gy : 2 * width_gy]
    pot, slope, cell_at, cell_of, table, pa, pb, la, lb, ua, ub, s_c, s_l, s_u, sems = refs[2 * width_gy :]
    i = lax.axis_index("gx")
    j = lax.axis_index("gy")
    rows_gx = lax.axis_size("gx")
    zero = jnp.zeros((SUB, LANES), jnp.float32)

    moves = []
    for part in range(width_gy):
        at = 0
        pieces = [(bodies[part], 0, pa, part * TE, TE), (bodies[part], TE * ROW, s_c, part * TE, TE)]
        for target, first, count in (
            (la, part * LOW[0], LOW[0]),
            (s_l, part * LOW[1], LOW[1]),
            (None, 0, LOW[2]),
            (ua, part * HIGH[0], HIGH[0]),
            (s_u, part * HIGH[1], HIGH[1]),
        ):
            if target is not None:
                pieces.append((halos[part], at, target, first, count))
            at += count * ROW
        for source, start, target, first, count in pieces:
            move = pltpu.make_async_copy(
                source.at[start : start + count * ROW],
                target.at[ROW0 + first * ROW : ROW0 + (first + count) * ROW],
                sems.at[len(moves)],
            )
            move.start()
            moves.append(move)

    fill_maps(chips, pos, cell_at, cell_of)

    def row_of(slot, size):
        pair, second = lax.shift_right_logical(slot, 1), lax.bitwise_and(slot, 1)
        return ROW0 + pair * (size * ROW) + second

    def enter(slot, carry):
        for which, size in enumerate((TE, LOW[0], HIGH[0])):
            cell = cell_of[which, slot]
            upper = lax.bitwise_and(cell, 1)
            beside = cell_at[which, cell + 1 - 2 * upper]
            here = [cell_at[at, cell] for at in range(3)]
            near = (slot, cell_at[which, cell - 2], cell_at[which, cell + 2])
            near += (jnp.where(upper == 1, beside, none), jnp.where(upper == 1, none, beside))
            rows = [row_of(at, size) for at in near]
            if which == 0:
                rows += [row_of(here[1], LOW[0]) + (LOW[0] - 1) * ROW, row_of(here[2], HIGH[0])]
            else:
                centre = row_of(here[0], TE)
                rows += [centre + (TE - 1) * ROW, centre]
            rows.append(upper)
            for at, row in enumerate(rows):
                table[(which * tiles + slot) * 8 + at] = row
        return carry

    lax.fori_loop(0, tiles, enter, 0)

    def entry(which, slot):
        return [table[(which * tiles + slot) * 8 + at] for at in range(8)]

    def plane_at(ref, row):
        return ref[pl.ds(row, SUB, stride=TILES), :]

    def put_plane(ref, row, value):
        ref[pl.ds(row, SUB, stride=TILES), :] = value

    for ref, count in ((pa, TE), (pb, TE), (la, LOW[0]), (lb, LOW[0]), (ua, HIGH[0]), (ub, HIGH[0])):
        first = ROW0 + width_gy * count * ROW
        for row in range(first, first + count * ROW, SUB):
            ref[row : row + SUB] = zero

    def clear(at, carry):
        slope[pl.ds(pl.multiple_of(at * SUB, SUB), SUB), :] = zero
        return carry

    lax.fori_loop(0, slope.shape[0] // SUB, clear, 0, unroll=8)
    for move in moves:
        move.wait()

    lane = lax.broadcasted_iota(jnp.int32, (SUB, LANES), 1)
    sub = lax.broadcasted_iota(jnp.int32, (SUB, LANES), 0)
    depth = lane % TE
    first_sub, last_sub = sub == 0, sub == SUB - 1
    first_z, last_z = depth == 0, depth == TE - 1

    def y_plus(ref, own, first_y, row, ghost_row):
        turned = jnp.where(last_sub, plane_at(ref, ghost_row), plane_at(ref, row))
        return roll(jnp.where(first_y, turned, own), -TE, 1)

    def y_minus(ref, own, last_y, row, ghost_row):
        turned = jnp.where(first_sub, plane_at(ref, ghost_row), plane_at(ref, row))
        return roll(jnp.where(last_y, turned, own), TE, 1)

    def z_plus(ref, own, ghost_row):
        return roll(jnp.where(first_z, plane_at(ref, ghost_row), own), -1, 1)

    def z_minus(ref, own, ghost_row):
        return roll(jnp.where(last_z, plane_at(ref, ghost_row), own), 1, 1)

    def y_ends(upper):
        quarter = lane // TE
        return quarter == upper, quarter == lax.bitwise_and(upper + 3, 3)

    bufs = ((pa, la, ua), (pb, lb, ub))
    weights = [cheb_weight(k, SWEEPS) for k in range(SWEEPS)]

    def relax(src, dst, places, first, count, s_ref, s_row, before, beyond, keep, gain):
        row, row_m, row_p, row_zm, row_zp, _, _, upper = places
        first_y, last_y = y_ends(upper)
        own = plane_at(src, row + first * ROW)
        for p in range(count):
            step = (first + p) * ROW
            after = plane_at(src, row + (step + ROW)) if p < count - 1 else beyond
            total = (before + after) + plane_at(s_ref, s_row + p * ROW)
            along_y = y_minus(src, own, last_y, row + (step - TILES), row_m + (step + ROW - TILES))
            along_y = along_y + y_plus(src, own, first_y, row + (step + TILES), row_p + (step + TILES - ROW))
            along_z = z_minus(src, own, row_zm + step) + z_plus(src, own, row_zp + step)
            put_plane(dst, row + step, keep * own + gain * (total + (along_y + along_z)))
            before, own = own, after

    def sweep(src, dst, keep, gain):
        (c_src, l_src, u_src), (c_dst, l_dst, u_dst) = src, dst

        def sweep_tile(slot, carry):
            at = entry(0, slot)
            ends = plane_at(l_src, at[5]), plane_at(u_src, at[6])
            relax(c_src, c_dst, at, 0, TE, s_c, at[0], *ends, keep, gain)
            at = entry(1, slot)
            ends = plane_at(l_src, at[0]), plane_at(c_src, at[6])
            relax(l_src, l_dst, at, 1, LOW[0] - 1, s_l, row_of(slot, LOW[1]), *ends, keep, gain)
            at = entry(2, slot)
            ends = plane_at(c_src, at[5]), plane_at(u_src, at[0] + (HIGH[0] - 1) * ROW)
            relax(u_src, u_dst, at, 0, HIGH[0] - 1, s_u, row_of(slot, HIGH[1]), *ends, keep, gain)
            return carry

        lax.fori_loop(0, tiles, sweep_tile, 0, unroll=2)

    def two_sweeps(pair, carry):
        for half, (src, dst) in enumerate((bufs, bufs[::-1])):
            keep, gain = jnp.float32(0.0), jnp.float32(0.0)
            for at in range(SWEEPS // 2):
                weight = weights[2 * at + half]
                keep = jnp.where(pair == at, jnp.float32(1.0 - weight), keep)
                gain = jnp.where(pair == at, jnp.float32(weight / (6.0 + EPS)), gain)
            sweep(src, dst, keep, gain)
        return carry

    lax.fori_loop(0, SWEEPS // 2, two_sweeps, 0)
    field, f_l, f_u = bufs[SWEEPS % 2]
    for t in range(TILES):
        turn = jnp.where(table[t * 8 + 7] == 1, LANES - TE, 0)

        def turn_back(p, carry):
            value = plane_at(field, p * ROW + (ROW0 + t))
            put_plane(pot, pl.multiple_of(p * ROW, ROW) + t, pltpu.roll(value, turn, 1))
            return carry

        lax.fori_loop(0, TE, turn_back, 0, unroll=8)

    def squares(ref, places, local, x, first, count, beyond):
        row, _, row_p, _, row_z, _, _, upper = places
        first_y, _ = y_ends(upper)
        target = (local * SLABX + x) * SUB
        own = plane_at(ref, row + first * ROW)
        for p in range(count):
            step = (first + p) * ROW
            after = plane_at(ref, row + (step + ROW)) if beyond is None or p < count - 1 else beyond
            d_x = after - own
            d_y = y_plus(ref, own, first_y, row + (step + TILES), row_p + (step + TILES - ROW)) - own
            d_z = z_plus(ref, own, row_z + step) - own
            rows = pl.ds(pl.multiple_of(target + p * SUB, SUB), SUB)
            slope[rows, :] = d_x * d_x + d_y * d_y + d_z * d_z
            own = after

    def slope_tile(slot, carry):
        at, local = entry(0, slot), window(0, cell_of[0, slot], i, j, rows_gx)
        squares(field, at, local, HALO, 0, TE, plane_at(f_u, at[6]))
        at, local = entry(1, slot), window(1, cell_of[1, slot], i, j, rows_gx)
        squares(f_l, at, local, HALO - 2, LOW[0] - 2, 2, plane_at(field, at[6]))
        at, local = entry(2, slot), window(2, cell_of[2, slot], i, j, rows_gx)
        squares(f_u, at, local, HALO + TE, 0, 2, None)
        return carry

    lax.fori_loop(0, tiles, slope_tile, 0, unroll=2)


def window(which, cell, i, j, rows_gx):
    local = cell - 4 * j
    inside = (local >= 0) & (local < CELLS - 1)
    if which > 0:
        row = i - 1 if which == 1 else i + 1
        inside = inside & (row >= 0) & (row < rows_gx)
    return jnp.where(inside, local, CELLS - 1)


def slab_steps_kernel(chips, pos, k0_table, beta_table, *refs):
    width_gy = 2 * chips
    tiles = width_gy * TILES
    halos = refs[width_gy : 2 * width_gy]
    slope, t_in, k0_in, b_in, y_in, y_out, temp_out = refs[2 * width_gy : 2 * width_gy + 7]
    mine, bundle = refs[2 * width_gy + 7 : 2 * width_gy + 9]
    across = refs[2 * width_gy + 9 : 2 * width_gy + 8 + chips]
    heat, q_ext, state_a, state_b, k0_all, b_all, blocks, sigmas, sems = refs[2 * width_gy + 8 + chips :]
    moves = []
    for part in range(width_gy):
        start = 2 * TE * ROW if part % chips == 0 else 0
        source = refs[part].at[start : start + TE * ROW]
        target = sigmas.at[part * TE * ROW : (part + 1) * TE * ROW]
        moves.append(pltpu.make_async_copy(source, target, sems.at[part]))
        moves[-1].start()
    i = lax.axis_index("gx")
    j = lax.axis_index("gy")
    rows_gx = lax.axis_size("gx")
    lane = lax.broadcasted_iota(jnp.int32, (SUB, LANES), 1)
    zero = jnp.zeros((SUB, LANES), jnp.float32)

    quarter = [(lane >= q * TE) & (lane < (q + 1) * TE) for q in range(3)]

    def pick(parts):
        return jnp.where(
            quarter[0], parts[0], jnp.where(quarter[1], parts[1], jnp.where(quarter[2], parts[2], parts[3]))
        )

    def turned(value, by):
        return value if by % 4 == 0 else roll(value, by * TE, 1)

    def rows_of(block, g):
        first = ROW0 + block * SLABX + g * SUB
        if not isinstance(first, int):
            first = pl.multiple_of(first, SUB)
        return pl.ds(first, SUB)

    groups = SLABX // SUB

    sub = lax.broadcasted_iota(jnp.int32, (SUB, LANES), 0)
    half = lane < NZ
    no_z = lane % NZ == NZ - 1
    low_x = (sub == HALO - 1) & (i == 0), (sub == HALO) & (i == 0)
    high_x = (sub == (HALO + TE - 1) % SUB) & (i == rows_gx - 1)
    low_y, high_y = half & (j == 0), (lane >= NZ) & (j == width_gy - 1)

    def inverse(value):
        near = pl.reciprocal(value, approx=True)
        near = near * (2.0 - value * near)
        return near * (2.0 - value * near)

    def both_of(block, g, by=0):
        first = 2 * (ROW0 + block * SLABX + g * SUB + by)
        return pl.ds(first, SUB, stride=2), pl.ds(first + 1, SUB, stride=2)

    def load(ref, block, by=0):
        places = [both_of(block, g, by) for g in range(groups)]
        return [ref[at, :] for at, _ in places], [ref[at, :] for _, at in places]

    def store(ref, block, g, temp, cond=None):
        first, second = both_of(block, g)
        ref[first, :] = temp
        if cond is not None:
            ref[second, :] = cond

    even = lax.rem(j, 2) == 0

    def begin(block, low, at):
        values = []
        for g in range(groups):
            rows = rows_of(block, g)
            temp, k0, beta = t_in[rows], k0_in[rows], b_in[rows]
            if low is not None:
                place = slice(at * SLABX + g * SUB, at * SLABX + (g + 1) * SUB)
                value = jnp.where(even, *((y_out[place], y_in[place])[:: 1 if low else -1]))
                swapped = roll(value, NZ, 1)
                if low:
                    temp = jnp.where(half, value, temp)
                    k0 = jnp.where(half, lookup(k0_table, swapped), k0)
                    beta = jnp.where(half, lookup(beta_table, swapped), beta)
                else:
                    temp = jnp.where(half, temp, swapped)
                    k0 = jnp.where(half, k0, lookup(k0_table, value))
                    beta = jnp.where(half, beta, lookup(beta_table, value))
            values.append((rows, temp, k0, beta, k0 * inverse(1.0 + beta * temp * temp)))
        for g, (rows, temp, k0, beta, cond) in enumerate(values):
            k0_all[rows], b_all[rows] = k0, beta
            store(state_a, block, g, temp, cond)

    for e in range(HALO):
        begin(e, True, e)
        begin(YBLOCKS - HALO + e, False, e)

    def begin_inner(block, carry):
        begin(block, None, 0)
        return carry

    lax.fori_loop(HALO, YBLOCKS - HALO, begin_inner, 0, unroll=4)

    def clear(at, carry):
        heat[pl.ds(pl.multiple_of(at * SUB, SUB), SUB), :] = zero
        return carry

    lax.fori_loop(0, heat.shape[0] // SUB, clear, 0, unroll=8)
    for move in moves:
        move.wait()
    low_at, high_at = (LOW[0] + LOW[1]) * ROW, LOW_ROWS + (HIGH[0] + HIGH[1]) * ROW
    def put_heat(which, by, dev, t, x, count, sigma_of):
        tile = jnp.clip(i + by, 0, rows_gx - 1) * tiles + dev * TILES + t
        cell = (pos[1, tile] + 1) * 2 + pos[2, tile]
        first = pl.multiple_of((window(which, cell, i, j, rows_gx) * SLABX + x) * SUB, SUB)
        for p in range(count):
            rows = pl.ds(pl.multiple_of(first + p * SUB, SUB), SUB)
            heat[rows, :] = sigma_of(p) * slope[rows, :]

    def own_heat(slot, carry):
        part, t = lax.div(slot, TILES), lax.rem(slot, TILES)
        row = part * (TE * ROW) + t
        dev = part_device(part, chips, j)
        put_heat(0, 0, dev, t, HALO, TE, lambda p: sigmas[pl.ds(row + p * ROW, SUB, stride=TILES), :])
        return carry

    lax.fori_loop(0, tiles, own_heat, 0)
    for part in range(width_gy):
        dev = part_device(part, chips, j)
        for t in range(TILES):
            for which, by, x, at in ((1, -1, HALO - 2, low_at), (2, 1, HALO + TE, high_at)):
                rows = lambda p: pl.ds(at + p * ROW + t, SUB, stride=TILES)
                put_heat(which, by, dev, t, x, 2, lambda p: halos[part][rows(p), :])

    def place_heat(at, carry):
        first = at - 1
        col, yq = lax.div(first * 4 + TE, TE), lax.rem(first * 4 + TE, TE) // 4
        for g in range(groups):
            cells = [
                heat[pl.ds(pl.multiple_of(((2 * col + c) * SLABX + g * SUB) * SUB, SUB) + yq, SUB, stride=SUB), :]
                for c in range(4)
            ]
            for r in range(4):
                block = 4 * first + r + HALO + 1
                q_ext[rows_of(block, g)] = pick([turned(cells[c], c - r - c % 2) for c in range(4)])
        return carry

    lax.fori_loop(0, HALF // 4 + 2, place_heat, 0, unroll=2)

    for step in range(CSWEEPS):
        src, dst = (state_a, state_b)[:: 1 if step % 2 == 0 else -1]

        def y_fluxes(block, now, ahead):
            closed = (low_y & (block == HALO - 1)) | (high_y & (block == HALO + HALF - 1))
            return [flux(now, ahead, g, closed) for g in range(groups)]

        def flux(now, other, g, closed=None):
            value = (now[1][g] + other[1][g]) * (other[0][g] - now[0][g])
            return value if closed is None else jnp.where(closed, 0.0, value)

        def advance(block, carry):
            now, before = carry
            ahead = load(src, block + 1)
            flux_y = y_fluxes(block, now, ahead)
            x_p, x_m = load(src, block, 1), load(src, block, -1)
            results = []
            for g in range(groups):
                temp, cond = now[0][g], now[1][g]
                up = flux(now, x_p, g, {0: low_x[0], groups - 1: high_x}.get(g))
                down = flux(now, x_m, g, {0: low_x[1]}.get(g))
                flux_z = (cond + roll(cond, -1, 1)) * (roll(temp, -1, 1) - temp)
                flux_z = jnp.where(no_z, 0.0, flux_z)
                div = (flux_y[g] - before[g]) + (up + down) + (flux_z - roll(flux_z, 1, 1))
                new = temp + DT * (0.5 * div + q_ext[rows_of(block + 1, g)])
                if step < CSWEEPS - 1:
                    rows = rows_of(block, g)
                    results.append((new, k0_all[rows] * inverse(1.0 + b_all[rows] * new * new)))
                else:
                    results.append((new,))
            for g in range(groups):
                store(dst, block, g, *results[g])
            return ahead, flux_y

        first, second = load(src, 0), load(src, 1)
        lax.fori_loop(1, YBLOCKS - 1, advance, (second, y_fluxes(0, first, second)), unroll=3)
    final = state_b if CSWEEPS % 2 else state_a

    def give_out(yq, carry):
        for g in range(TE // SUB):
            x = slice(g * SUB, (g + 1) * SUB)
            turns = []
            for r in range(4):
                value = final[both_of(HALO + 4 * yq + r, g, HALO)[0], :]
                turns.append([turned(value, by) for by in range(4)])
            for pair in range(2):
                even, odd = turns[2 * pair], turns[2 * pair + 1]
                lower = (2 * yq + pair) * LANES
                upper = lower + temp_out.shape[1] // 2
                temp_out[x, pl.ds(pl.multiple_of(lower, LANES), LANES)] = jnp.where(half, even[0], odd[2])
                temp_out[x, pl.ds(pl.multiple_of(upper, LANES), LANES)] = jnp.where(half, even[2], odd[0])
            for c in range(4):
                value = pick([turns[r][(r - c) % 4] for r in range(4)])
                blocks[pl.ds((c * TE + g * SUB) * SUB + yq, SUB, stride=SUB), :] = value
        return carry

    lax.fori_loop(0, HALF // 4, give_out, 0, unroll=2)
    places = []
    mate = j + 1 - 2 * lax.rem(j, 2)
    targets = [(mine, 0, j)] + [(across[d - 1], 0, j + 2 * d) for d in range(1, chips)]
    targets += [(bundle, d * TE * ROW, mate + 2 * d) for d in range(chips)]
    for target, first, to in targets:
        dev = lax.rem(to, width_gy)
        for t in range(TILES):
            tile = i * tiles + dev * TILES + t
            col = pos[1, tile] - 2 * j
            cell = jnp.clip(col, 0, 1) * 2 + pos[2, tile]
            places.append((target, first + t, cell, (col >= 0) & (col < 2)))

    def pack(p, carry):
        values = []
        for _, _, cell, here in places:
            value = blocks[pl.ds(pl.multiple_of((cell * TE + p) * SUB, SUB), SUB), :]
            values.append(jnp.where(here, value, 0.0))
        for (target, first, _, _), value in zip(places, values):
            target[pl.ds(pl.multiple_of(p * ROW, ROW) + first, SUB, stride=TILES), :] = value
        return carry

    lax.fori_loop(0, TE, pack, 0, unroll=4)


def shifted(value, axis, by, wrap=False):
    count = lax.axis_size(axis)
    pairs = [(d, (d + by) % count) for d in range(count) if wrap or 0 <= d + by < count]
    return lax.ppermute(value, axis, pairs)


def with_partner(value, axis, first):
    count = lax.axis_size(axis)
    pairs = [(d, d + 1) for d in range(first, count - 1, 2)]
    return lax.ppermute(value, axis, pairs + [(high, low) for low, high in pairs])


def from_mate(value):
    return lax.ppermute(value, "gy", [(d, d ^ 1) for d in range(lax.axis_size("gy"))])


def to_rows(value):
    return value.reshape(TILES, -1, LANES).transpose(1, 0, 2).reshape(-1, LANES)


def from_rows(value):
    return value.reshape(-1, TILES, LANES).transpose(1, 0, 2).reshape(TILES, -1)


def to_other_core(value, by):
    count = lax.axis_size("gy")
    return lax.ppermute(value, "gy", [(at, ((at ^ 1) + 2 * by) % count) for at in range(count)])


VMEM = pl.BlockSpec(memory_space=pltpu.VMEM)
SMEM = pl.BlockSpec(memory_space=pltpu.SMEM)
HBM = pl.BlockSpec(memory_space=pltpu.HBM)
ANY = pl.BlockSpec(memory_space=pl.ANY)
PARAMS = pltpu.CompilerParams(vmem_limit_bytes=32 * 1024 * 1024)


def on_device(
    phi_init,
    source,
    tile_mat,
    tile_pos,
    neighbours,
    sigma_table,
    temp_init,
    slab_mat,
    k0_table,
    beta_table,
):
    f32 = jnp.float32
    pos = tile_pos.T
    width_gy = lax.axis_size("gy")
    chips = width_gy // 2
    tiles = width_gy * TILES
    size_x, width = temp_init.shape
    edge_rows = width // LANES * SUB

    def rows(count):
        return jax.ShapeDtypeStruct((count, LANES), f32)

    body, ready, sigma, inner, outer = pl.pallas_call(
        prep_kernel,
        out_shape=(
            rows(3 * TE * ROW),
            rows(2 * TE * ROW),
            rows(TE * ROW),
            rows(SIDE_ROWS + edge_rows),
            rows(SIDE_ROWS + edge_rows),
        ),
        in_specs=[SMEM] * 2 + [HBM] * 5,
        out_specs=(VMEM,) * 5,
        scratch_shapes=[
            pltpu.VMEM((TE * ROW, LANES), f32),
            pltpu.VMEM((TE * ROW, LANES), jnp.int32),
            pltpu.VMEM((2, SUB, width), f32),
            pltpu.VMEM((2, SUB, width), jnp.int32),
            pltpu.SemaphoreType.DMA((7,)),
        ],
        compiler_params=pltpu.CompilerParams(vmem_limit_bytes=62 * 1024 * 1024),
        name="prep",
    )(sigma_table, pos, to_rows(phi_init), to_rows(source), to_rows(tile_mat), temp_init, slab_mat)
    bodies = [body] + [shifted(ready, "gy", 2 * d, True) for d in range(1, chips)]
    inner, outer = with_partner(inner, "gx", 0), with_partner(outer, "gx", 1)

    halo = pl.pallas_call(
        relay_kernel,
        out_shape=rows(LOW_ROWS + HIGH_ROWS),
        in_specs=[VMEM] * 2,
        out_specs=VMEM,
        compiler_params=PARAMS,
        name="relay",
    )(inner, outer)
    halos = [halo] + [shifted(halo, "gy", 2 * d, True) for d in range(1, chips)]
    inner, halos[0] = lax.optimization_barrier((inner, halos[0]))
    native = pltpu.VMEM((width // LANES * SLABX + SUB, LANES), f32)
    t_ext, k0_ext, b_ext, edge_in, edge_out = pl.pallas_call(
        slab_kernel,
        out_shape=(rows(SLAB_ROWS),) * 3 + (rows(HALO * SLABX),) * 2,
        in_specs=[SMEM] * 3 + [VMEM] * 4,
        out_specs=(VMEM,) * 5,
        scratch_shapes=[native, native] + [pltpu.VMEM((HALO * SLABX, LANES), f32)] * 2,
        compiler_params=PARAMS,
        name="slab_prep",
    )(pos, k0_table, beta_table, temp_init, slab_mat, inner, outer)
    y_in, y_out = with_partner(edge_in, "gy", 0), with_partner(edge_out, "gy", 1)
    *bodies[1:], y_in = lax.optimization_barrier((*bodies[1:], y_in))
    bodies += [from_mate(part) for part in bodies]
    sigmas = [bodies[0]] + [shifted(sigma, "gy", 2 * d, True) for d in range(1, chips)]
    sigmas += [bodies[chips]] + [to_other_core(sigma, d) for d in range(1, chips)]
    *halos[1:], y_in = lax.optimization_barrier((*halos[1:], y_in))
    halos = halos + [from_mate(part) for part in halos]

    def fields(count):
        return pltpu.VMEM((2 * ROW0 + (width_gy + 1) * count * ROW, LANES), f32)

    pot, slope = pl.pallas_call(
        functools.partial(sweep_kernel, chips),
        out_shape=(rows(TE * ROW), rows(CELLS * SLABX * SUB)),
        in_specs=[SMEM] + [ANY] * (2 * width_gy),
        out_specs=(VMEM, VMEM),
        scratch_shapes=[
            pltpu.SMEM((3, 2 * (2 * width_gy + 2)), jnp.int32),
            pltpu.SMEM((3, tiles), jnp.int32),
            pltpu.SMEM((3 * tiles * 8,), jnp.int32),
            fields(TE), fields(TE), fields(LOW[0]), fields(LOW[0]), fields(HIGH[0]), fields(HIGH[0]),
            fields(TE), fields(LOW[1]), fields(HIGH[1]),
            pltpu.SemaphoreType.DMA((6 * width_gy,)),
        ],
        compiler_params=PARAMS,
        name="sweeps",
    )(pos, *bodies, *halos)

    temp, mine, bundle, *across = pl.pallas_call(
        functools.partial(slab_steps_kernel, chips),
        out_shape=(jax.ShapeDtypeStruct((size_x, width), f32), rows(TE * ROW), rows(chips * TE * ROW))
        + (rows(TE * ROW),) * (chips - 1),
        in_specs=[SMEM] * 3 + [ANY] * width_gy + [VMEM] * (width_gy + 6),
        out_specs=(VMEM,) * (2 + chips),
        scratch_shapes=[pltpu.VMEM((CELLS * SLABX * SUB, LANES), f32)]
        + [pltpu.VMEM((SLAB_ROWS + 3 * SLABX, LANES), f32)]
        + [pltpu.VMEM((2 * SLAB_ROWS, LANES), f32)] * 2
        + [pltpu.VMEM((SLAB_ROWS, LANES), f32)] * 2
        + [pltpu.VMEM((4 * TE * SUB, LANES), f32), pltpu.VMEM((width_gy * TE * ROW, LANES), f32)]
        + [pltpu.SemaphoreType.DMA((width_gy,))],
        compiler_params=PARAMS,
        name="slab_steps",
    )(pos, k0_table, beta_table, *sigmas, *halos, slope, t_ext, k0_ext, b_ext, y_in, y_out)
    got = from_mate(bundle).reshape(chips, TE * ROW, LANES)
    tile_temps = mine + got[0]
    for d in range(1, chips):
        tile_temps = tile_temps + shifted(across[d - 1] + got[d], "gy", 2 * d, True)
    return from_rows(pot), temp, from_rows(tile_temps)


def solution(mesh):
    placed = (
        P(("gx", "gy"), None),
        P(("gx", "gy"), None),
        P(("gx", "gy"), None),
        P(),
        P(("gx", "gy"), None),
        P(),
        P("gx", "gy"),
        P("gx", "gy"),
        P(),
        P(),
    )
    return jax.shard_map(
        on_device,
        mesh=mesh,
        in_specs=placed,
        out_specs=(P(("gx", "gy"), None), P("gx", "gy"), P(("gx", "gy"), None)),
        check_vma=False,
    )
```

```python
import functools
import math

import jax
import jax.numpy as jnp
from jax import lax
from jax.experimental import pallas as pl
from jax.experimental.pallas import tpu as pltpu
from jax.sharding import PartitionSpec as P

TE = 32
SWEEPS = 4
CSWEEPS = 3
NZ = 64
EPS = 2.0
DT = 0.15
LANES = 128
SUB = 8
TILES = 2
ROW = SUB * TILES

LOW = (SWEEPS + 2, SWEEPS + 1, 2)
HIGH = (SWEEPS + 3, SWEEPS + 2, 2)
LOW_ROWS = sum(LOW) * ROW
HIGH_ROWS = sum(HIGH) * ROW
SIDE_ROWS = max(LOW_ROWS, HIGH_ROWS)
SLABX = TE + SUB
HALO = CSWEEPS
HALF = TE
YBLOCKS = HALF + 2 * HALO
CELLS = 9
ROW0 = ROW
SLAB_ROWS = ROW0 + YBLOCKS * SLABX + ROW0


def cheb_weight(step, count):
    return 1.0 / (1.0 + 0.75 * math.cos(math.pi * (2 * step + 1) / (2 * count)))


def lookup(table, ids):
    out = jnp.full(ids.shape, table[3], jnp.float32)
    for which in (2, 1, 0):
        out = jnp.where(ids == which, table[which], out)
    return out


def roll(value, by, axis):
    return pltpu.roll(value, by % value.shape[axis], axis)


def prep_kernel(table, pos, phi, src, mat, temp, slab, ready, sigma, inner, outer, phi_v, src_v, mat_v, ends_t, ends_m, sems):
    rows = TE * ROW
    size_x, width = temp.shape
    moves = [(phi, phi_v), (src, src_v), (mat, mat_v)]
    for which, first in enumerate((0, size_x - SUB)):
        moves.append((temp.at[first : first + SUB], ends_t.at[which]))
        moves.append((slab.at[first : first + SUB], ends_m.at[which]))
    moves = [pltpu.make_async_copy(*move, sems.at[at]) for at, move in enumerate(moves)]
    for move in moves:
        move.start()
    for move in moves:
        move.wait()
    first = (lax.axis_index("gx") * lax.axis_size("gy") + lax.axis_index("gy")) * TILES
    upper = [pos[2, first + t] == 1 for t in range(TILES)]

    def plane(p, carry):
        values = []
        for t in range(TILES):
            row = pl.multiple_of(p * ROW, ROW) + t
            at = pl.ds(row, SUB, stride=TILES)
            conduct = lookup(table, mat_v[at, :])
            three = (phi_v[at, :], src_v[at, :] / conduct, conduct)
            values.append((row, [jnp.where(upper[t], roll(v, TE, 1), v) for v in three]))
        for row, (potential, s, conduct) in values:
            ready[pl.ds(row, SUB, stride=TILES), :] = potential
            ready[pl.ds(row + rows, SUB, stride=TILES), :] = s
            sigma[pl.ds(row, SUB, stride=TILES), :] = conduct
        return carry

    lax.fori_loop(0, TE, plane, 0, unroll=8)
    even = lax.rem(lax.axis_index("gx"), 2) == 0

    @pl.when(even)
    def _():
        fill_sides(ready, sigma, ends_t, ends_m, inner, outer)

    @pl.when(jnp.logical_not(even))
    def _():
        fill_sides(ready, sigma, ends_t, ends_m, outer, inner)


def fill_sides(body, sigma, ends_t, ends_m, up, down):
    rows = TE * ROW
    width = ends_t.shape[2]
    at_up, at_down = 0, 0
    for ref, first in ((body, 0), (body, rows), (sigma, 0)):
        which = (first // rows) if ref is body else 2
        size = LOW[which] * ROW
        up[at_up : at_up + size] = ref[first + rows - size : first + rows]
        at_up += size
        size = HIGH[which] * ROW
        down[at_down : at_down + size] = ref[first : first + size]
        at_down += size
    sub = lax.broadcasted_iota(jnp.int32, (SUB, LANES), 0)
    for at in range(width // LANES):
        lanes = slice(at * LANES, (at + 1) * LANES)
        t_low, m_low = ends_t[0, :, lanes], ends_m[0, :, lanes].astype(jnp.float32)
        t_high, m_high = ends_t[1, :, lanes], ends_m[1, :, lanes].astype(jnp.float32)
        first = at * SUB
        up[SIDE_ROWS + first : SIDE_ROWS + first + SUB] = jnp.where(sub < 4, roll(t_high, HALO, 0), roll(m_high, -1, 0))
        down[SIDE_ROWS + first : SIDE_ROWS + first + SUB] = jnp.where(sub < 4, t_low, roll(m_low, 4, 0))


def relay_kernel(inner, outer, halo):
    def join(low, high):
        halo[0:LOW_ROWS] = low[0:LOW_ROWS]
        halo[LOW_ROWS:] = high[0:HIGH_ROWS]

    even = lax.rem(lax.axis_index("gx"), 2) == 0
    pl.when(even)(lambda: join(outer, inner))
    pl.when(jnp.logical_not(even))(lambda: join(inner, outer))


def loose(pos):
    return jnp.minimum(pos[0, 0], 0)


def slab_kernel(pos, k0_table, beta_table, temp, mat, inner, outer, t_ext, k0_ext, b_ext, edge_in, edge_out, native_t, native_m, edge_low, edge_high):
    start = loose(pos)
    even = lax.rem(lax.axis_index("gx"), 2) == 0
    blocks = temp.shape[1] // LANES
    half = lax.broadcasted_iota(jnp.int32, (SUB, LANES), 1) < NZ
    for which, (own, native) in enumerate(((temp, native_t), (mat, native_m))):
        for at in range(blocks):
            lanes = slice(at * LANES, (at + 1) * LANES)
            first = at * SLABX
            side = slice(SIDE_ROWS + at * SUB, SIDE_ROWS + (at + 1) * SUB)
            value = jnp.where(even, outer[side, :], inner[side, :])
            native[first : first + SUB, :] = roll(value, -4, 0) if which else value
            for g in range(TE // SUB):
                value = own[g * SUB : (g + 1) * SUB, lanes].astype(jnp.float32)
                native[pl.ds(start + first + HALO + g * SUB, SUB), :] = value
            value = jnp.where(even, inner[side, :], outer[side, :])
            native[pl.ds(start + first + HALO + TE, SUB), :] = roll(value, -4, 0) if which else value
    for at in range(blocks // 2):
        for g in range(SLABX // SUB):
            halves = []
            for native in (native_t, native_m):
                lower = native[at * SLABX + g * SUB : at * SLABX + (g + 1) * SUB, :]
                upper_at = (blocks // 2 + at) * SLABX + g * SUB
                upper = native[upper_at : upper_at + SUB, :]
                lower_r, upper_r = roll(lower, NZ, 1), roll(upper, NZ, 1)
                halves.append((lower, lower_r, upper, upper_r))
            for odd in range(2):
                y = 2 * at + odd
                temps, mats = (jnp.where(half, v[odd], v[3 - odd]) for v in halves)
                places = [(y + HALO, temps, mats)]
                if y >= HALF - HALO:
                    places.append((y - HALF + HALO, halves[0][1 - odd], halves[1][1 - odd]))
                if y < HALO:
                    places.append((y + HALF + HALO, halves[0][2 + odd], halves[1][2 + odd]))
                for block, t, m in places:
                    rows = slice(ROW0 + block * SLABX + g * SUB, ROW0 + block * SLABX + (g + 1) * SUB)
                    t_ext[rows] = t
                    k0_ext[rows] = lookup(k0_table, m)
                    b_ext[rows] = lookup(beta_table, m)
                if y < HALO:
                    rows = slice(y * SLABX + g * SUB, y * SLABX + (g + 1) * SUB)
                    edge_low[rows] = jnp.where(half, halves[0][odd], halves[1][1 - odd])
                if y >= HALF - HALO:
                    first = (y - HALF + HALO) * SLABX + g * SUB
                    edge_high[first : first + SUB] = jnp.where(half, halves[0][2 + odd], halves[1][3 - odd])
    even = lax.rem(lax.axis_index("gy"), 2) == 0
    edge_in[...] = jnp.where(even, edge_high[...], edge_low[...])
    edge_out[...] = jnp.where(even, edge_low[...], edge_high[...])


def fill_maps(chips, pos, cell_at, cell_of):
    width_gy = 2 * chips
    tiles = width_gy * TILES
    i = lax.axis_index("gx")
    j = lax.axis_index("gy")
    rows_gx = lax.axis_size("gx")
    for at in range(2 * (2 * width_gy + 2)):
        for which in range(3):
            cell_at[which, at] = tiles
    for which, by in enumerate((0, -1, 1)):
        row = i + by
        valid = (row >= 0) & (row < rows_gx)
        first = jnp.clip(row, 0, rows_gx - 1) * tiles
        for part in range(width_gy):
            dev = part_device(part, chips, j)
            for t in range(TILES):
                tile = first + dev * TILES + t
                cell = (pos[1, tile] + 1) * 2 + pos[2, tile]
                slot = part * TILES + t
                cell_of[which, slot] = cell
                cell_at[which, cell] = jnp.where(valid, slot, tiles)


def part_device(part, chips, j):
    mate = j + 1 - 2 * lax.rem(j, 2)
    base = j if part < chips else mate
    return lax.rem(base - 2 * (part % chips) + 2 * chips, 2 * chips)


def sweep_kernel(chips, pos, *refs):
    width_gy = 2 * chips
    tiles = width_gy * TILES
    none = tiles
    bodies, halos = refs[:width_gy], refs[width_gy : 2 * width_gy]
    pot, slope, cell_at, cell_of, table, pa, pb, la, lb, ua, ub, s_c, s_l, s_u, sems = refs[2 * width_gy :]
    i = lax.axis_index("gx")
    j = lax.axis_index("gy")
    rows_gx = lax.axis_size("gx")
    zero = jnp.zeros((SUB, LANES), jnp.float32)

    moves = []
    for part in range(width_gy):
        at = 0
        pieces = [(bodies[part], 0, pa, part * TE, TE), (bodies[part], TE * ROW, s_c, part * TE, TE)]
        for target, first, count in (
            (la, part * LOW[0], LOW[0]),
            (s_l, part * LOW[1], LOW[1]),
            (None, 0, LOW[2]),
            (ua, part * HIGH[0], HIGH[0]),
            (s_u, part * HIGH[1], HIGH[1]),
        ):
            if target is not None:
                pieces.append((halos[part], at, target, first, count))
            at += count * ROW
        for source, start, target, first, count in pieces:
            move = pltpu.make_async_copy(
                source.at[start : start + count * ROW],
                target.at[ROW0 + first * ROW : ROW0 + (first + count) * ROW],
                sems.at[len(moves)],
            )
            move.start()
            moves.append(move)

    fill_maps(chips, pos, cell_at, cell_of)

    def row_of(slot, size):
        pair, second = lax.shift_right_logical(slot, 1), lax.bitwise_and(slot, 1)
        return ROW0 + pair * (size * ROW) + second

    def enter(slot, carry):
        for which, size in enumerate((TE, LOW[0], HIGH[0])):
            cell = cell_of[which, slot]
            upper = lax.bitwise_and(cell, 1)
            beside = cell_at[which, cell + 1 - 2 * upper]
            here = [cell_at[at, cell] for at in range(3)]
            near = (slot, cell_at[which, cell - 2], cell_at[which, cell + 2])
            near += (jnp.where(upper == 1, beside, none), jnp.where(upper == 1, none, beside))
            rows = [row_of(at, size) for at in near]
            if which == 0:
                rows += [row_of(here[1], LOW[0]) + (LOW[0] - 1) * ROW, row_of(here[2], HIGH[0])]
            else:
                centre = row_of(here[0], TE)
                rows += [centre + (TE - 1) * ROW, centre]
            rows.append(upper)
            for at, row in enumerate(rows):
                table[(which * tiles + slot) * 8 + at] = row
        return carry

    lax.fori_loop(0, tiles, enter, 0)

    def entry(which, slot):
        return [table[(which * tiles + slot) * 8 + at] for at in range(8)]

    def plane_at(ref, row):
        return ref[pl.ds(row, SUB, stride=TILES), :]

    def put_plane(ref, row, value):
        ref[pl.ds(row, SUB, stride=TILES), :] = value

    for ref, count in ((pa, TE), (pb, TE), (la, LOW[0]), (lb, LOW[0]), (ua, HIGH[0]), (ub, HIGH[0])):
        first = ROW0 + width_gy * count * ROW
        for row in range(first, first + count * ROW, SUB):
            ref[row : row + SUB] = zero

    def clear(at, carry):
        slope[pl.ds(pl.multiple_of(at * SUB, SUB), SUB), :] = zero
        return carry

    lax.fori_loop(0, slope.shape[0] // SUB, clear, 0, unroll=8)
    for move in moves:
        move.wait()

    lane = lax.broadcasted_iota(jnp.int32, (SUB, LANES), 1)
    sub = lax.broadcasted_iota(jnp.int32, (SUB, LANES), 0)
    depth = lane % TE
    first_sub, last_sub = sub == 0, sub == SUB - 1
    first_z, last_z = depth == 0, depth == TE - 1

    def y_plus(ref, own, first_y, row, ghost_row):
        turned = jnp.where(last_sub, plane_at(ref, ghost_row), plane_at(ref, row))
        return roll(jnp.where(first_y, turned, own), -TE, 1)

    def y_minus(ref, own, last_y, row, ghost_row):
        turned = jnp.where(first_sub, plane_at(ref, ghost_row), plane_at(ref, row))
        return roll(jnp.where(last_y, turned, own), TE, 1)

    def z_plus(ref, own, ghost_row):
        return roll(jnp.where(first_z, plane_at(ref, ghost_row), own), -1, 1)

    def z_minus(ref, own, ghost_row):
        return roll(jnp.where(last_z, plane_at(ref, ghost_row), own), 1, 1)

    def y_ends(upper):
        quarter = lane // TE
        return quarter == upper, quarter == lax.bitwise_and(upper + 3, 3)

    bufs = ((pa, la, ua), (pb, lb, ub))
    for k in range(SWEEPS):
        weight = cheb_weight(k, SWEEPS)
        keep, gain = 1.0 - weight, weight / (6.0 + EPS)
        (c_src, l_src, u_src), (c_dst, l_dst, u_dst) = bufs[k % 2], bufs[(k + 1) % 2]

        def relax(src, dst, places, first, count, s_ref, s_row, before, beyond):
            row, row_m, row_p, row_zm, row_zp, _, _, upper = places
            first_y, last_y = y_ends(upper)
            own = plane_at(src, row + first * ROW)
            for p in range(count):
                step = (first + p) * ROW
                after = plane_at(src, row + (step + ROW)) if beyond is None or p < count - 1 else beyond
                total = (before + after) + plane_at(s_ref, s_row + p * ROW)
                along_y = y_minus(src, own, last_y, row + (step - TILES), row_m + (step + ROW - TILES))
                along_y = along_y + y_plus(src, own, first_y, row + (step + TILES), row_p + (step + TILES - ROW))
                along_z = z_minus(src, own, row_zm + step) + z_plus(src, own, row_zp + step)
                put_plane(dst, row + step, keep * own + gain * (total + (along_y + along_z)))
                before, own = own, after

        def sweep_tile(slot, carry):
            at = entry(0, slot)
            relax(c_src, c_dst, at, 0, TE, s_c, at[0], plane_at(l_src, at[5]), plane_at(u_src, at[6]))
            at = entry(1, slot)
            count = LOW[0] - 1 - k
            s_row = row_of(slot, LOW[1]) + (LOW[1] - count) * ROW
            before, beyond = plane_at(l_src, at[0] + k * ROW), plane_at(c_src, at[6])
            relax(l_src, l_dst, at, k + 1, count, s_l, s_row, before, beyond)
            at = entry(2, slot)
            relax(u_src, u_dst, at, 0, HIGH[0] - 1 - k, s_u, row_of(slot, HIGH[1]), plane_at(c_src, at[5]), None)
            return carry

        lax.fori_loop(0, tiles, sweep_tile, 0, unroll=4)

    field, f_l, f_u = bufs[SWEEPS % 2]
    for t in range(TILES):
        turn = jnp.where(table[t * 8 + 7] == 1, LANES - TE, 0)

        def turn_back(p, carry):
            value = plane_at(field, p * ROW + (ROW0 + t))
            put_plane(pot, pl.multiple_of(p * ROW, ROW) + t, pltpu.roll(value, turn, 1))
            return carry

        lax.fori_loop(0, TE, turn_back, 0, unroll=8)

    def squares(ref, places, local, x, first, count, beyond):
        row, _, row_p, _, row_z, _, _, upper = places
        first_y, _ = y_ends(upper)
        target = (local * SLABX + x) * SUB
        own = plane_at(ref, row + first * ROW)
        for p in range(count):
            step = (first + p) * ROW
            after = plane_at(ref, row + (step + ROW)) if beyond is None or p < count - 1 else beyond
            d_x = after - own
            d_y = y_plus(ref, own, first_y, row + (step + TILES), row_p + (step + TILES - ROW)) - own
            d_z = z_plus(ref, own, row_z + step) - own
            rows = pl.ds(pl.multiple_of(target + p * SUB, SUB), SUB)
            slope[rows, :] = d_x * d_x + d_y * d_y + d_z * d_z
            own = after

    def slope_tile(slot, carry):
        at, local = entry(0, slot), window(0, cell_of[0, slot], i, j, rows_gx)
        squares(field, at, local, HALO, 0, TE, plane_at(f_u, at[6]))
        at, local = entry(1, slot), window(1, cell_of[1, slot], i, j, rows_gx)
        squares(f_l, at, local, HALO - 2, LOW[0] - 2, 2, plane_at(field, at[6]))
        at, local = entry(2, slot), window(2, cell_of[2, slot], i, j, rows_gx)
        squares(f_u, at, local, HALO + TE, 0, 2, None)
        return carry

    lax.fori_loop(0, tiles, slope_tile, 0, unroll=2)


def window(which, cell, i, j, rows_gx):
    local = cell - 4 * j
    inside = (local >= 0) & (local < CELLS - 1)
    if which > 0:
        row = i - 1 if which == 1 else i + 1
        inside = inside & (row >= 0) & (row < rows_gx)
    return jnp.where(inside, local, CELLS - 1)


def slab_steps_kernel(chips, pos, k0_table, beta_table, *refs):
    width_gy = 2 * chips
    tiles = width_gy * TILES
    halos = refs[width_gy : 2 * width_gy]
    slope, t_in, k0_in, b_in, y_in, y_out, temp_out = refs[2 * width_gy : 2 * width_gy + 7]
    mine, bundle = refs[2 * width_gy + 7 : 2 * width_gy + 9]
    across = refs[2 * width_gy + 9 : 2 * width_gy + 8 + chips]
    heat, q_ext, state_a, state_b, k0_all, b_all, blocks, sigmas, sems = refs[2 * width_gy + 8 + chips :]
    moves = []
    for part in range(width_gy):
        moves.append(pltpu.make_async_copy(refs[part], sigmas.at[part], sems.at[part]))
        moves[-1].start()
    i = lax.axis_index("gx")
    j = lax.axis_index("gy")
    rows_gx = lax.axis_size("gx")
    lane = lax.broadcasted_iota(jnp.int32, (SUB, LANES), 1)
    zero = jnp.zeros((SUB, LANES), jnp.float32)

    quarter = [(lane >= q * TE) & (lane < (q + 1) * TE) for q in range(3)]

    def pick(parts):
        return jnp.where(
            quarter[0], parts[0], jnp.where(quarter[1], parts[1], jnp.where(quarter[2], parts[2], parts[3]))
        )

    def turned(value, by):
        return value if by % 4 == 0 else roll(value, by * TE, 1)

    def rows_of(block, g):
        first = ROW0 + block * SLABX + g * SUB
        if not isinstance(first, int):
            first = pl.multiple_of(first, SUB)
        return pl.ds(first, SUB)

    groups = SLABX // SUB

    sub = lax.broadcasted_iota(jnp.int32, (SUB, LANES), 0)
    half = lane < NZ
    no_z = lane % NZ == NZ - 1
    low_x = (sub == HALO - 1) & (i == 0), (sub == HALO) & (i == 0)
    high_x = (sub == (HALO + TE - 1) % SUB) & (i == rows_gx - 1)
    low_y, high_y = half & (j == 0), (lane >= NZ) & (j == width_gy - 1)

    def inverse(value):
        near = pl.reciprocal(value, approx=True)
        near = near * (2.0 - value * near)
        return near * (2.0 - value * near)

    def both_of(block, g, by=0):
        first = 2 * (ROW0 + block * SLABX + g * SUB + by)
        return pl.ds(first, SUB, stride=2), pl.ds(first + 1, SUB, stride=2)

    def load(ref, block, by=0):
        places = [both_of(block, g, by) for g in range(groups)]
        return [ref[at, :] for at, _ in places], [ref[at, :] for _, at in places]

    def store(ref, block, g, temp, cond=None):
        first, second = both_of(block, g)
        ref[first, :] = temp
        if cond is not None:
            ref[second, :] = cond

    even = lax.rem(j, 2) == 0

    def begin(block, low, at):
        values = []
        for g in range(groups):
            rows = rows_of(block, g)
            temp, k0, beta = t_in[rows], k0_in[rows], b_in[rows]
            if low is not None:
                place = slice(at * SLABX + g * SUB, at * SLABX + (g + 1) * SUB)
                value = jnp.where(even, *((y_out[place], y_in[place])[:: 1 if low else -1]))
                swapped = roll(value, NZ, 1)
                if low:
                    temp = jnp.where(half, value, temp)
                    k0 = jnp.where(half, lookup(k0_table, swapped), k0)
                    beta = jnp.where(half, lookup(beta_table, swapped), beta)
                else:
                    temp = jnp.where(half, temp, swapped)
                    k0 = jnp.where(half, k0, lookup(k0_table, value))
                    beta = jnp.where(half, beta, lookup(beta_table, value))
            values.append((rows, temp, k0, beta, k0 * inverse(1.0 + beta * temp * temp)))
        for g, (rows, temp, k0, beta, cond) in enumerate(values):
            k0_all[rows], b_all[rows] = k0, beta
            store(state_a, block, g, temp, cond)

    for e in range(HALO):
        begin(e, True, e)
        begin(YBLOCKS - HALO + e, False, e)

    def begin_inner(block, carry):
        begin(block, None, 0)
        return carry

    lax.fori_loop(HALO, YBLOCKS - HALO, begin_inner, 0, unroll=4)

    def clear(at, carry):
        heat[pl.ds(pl.multiple_of(at * SUB, SUB), SUB), :] = zero
        return carry

    lax.fori_loop(0, heat.shape[0] // SUB, clear, 0, unroll=8)
    for move in moves:
        move.wait()
    low_at, high_at = (LOW[0] + LOW[1]) * ROW, LOW_ROWS + (HIGH[0] + HIGH[1]) * ROW
    for part in range(width_gy):
        dev = part_device(part, chips, j)
        for t in range(TILES):
            for which, by in enumerate((0, -1, 1)):
                tile = jnp.clip(i + by, 0, rows_gx - 1) * tiles + dev * TILES + t
                cell = (pos[1, tile] + 1) * 2 + pos[2, tile]
                local = window(which, cell, i, j, rows_gx)
                source, start, x, count = (
                    (sigmas.at[part], 0, HALO, TE),
                    (halos[part], low_at, HALO - 2, 2),
                    (halos[part], high_at, HALO + TE, 2),
                )[which]
                first = pl.multiple_of((local * SLABX + x) * SUB, SUB)
                for p in range(count):
                    rows = pl.ds(pl.multiple_of(first + p * SUB, SUB), SUB)
                    sigma = source[pl.ds(start + p * ROW + t, SUB, stride=TILES), :]
                    heat[rows, :] = sigma * slope[rows, :]

    def place_heat(at, carry):
        first = at - 1
        col, yq = lax.div(first * 4 + TE, TE), lax.rem(first * 4 + TE, TE) // 4
        for g in range(groups):
            cells = [
                heat[pl.ds(pl.multiple_of(((2 * col + c) * SLABX + g * SUB) * SUB, SUB) + yq, SUB, stride=SUB), :]
                for c in range(4)
            ]
            for r in range(4):
                block = 4 * first + r + HALO + 1
                q_ext[rows_of(block, g)] = pick([turned(cells[c], c - r - c % 2) for c in range(4)])
        return carry

    lax.fori_loop(0, HALF // 4 + 2, place_heat, 0, unroll=2)

    for step in range(CSWEEPS):
        src, dst = (state_a, state_b)[:: 1 if step % 2 == 0 else -1]

        def y_fluxes(block, now, ahead):
            closed = (low_y & (block == HALO - 1)) | (high_y & (block == HALO + HALF - 1))
            return [flux(now, ahead, g, closed) for g in range(groups)]

        def flux(now, other, g, closed=None):
            value = (now[1][g] + other[1][g]) * (other[0][g] - now[0][g])
            return value if closed is None else jnp.where(closed, 0.0, value)

        def advance(block, carry):
            now, before = carry
            ahead = load(src, block + 1)
            flux_y = y_fluxes(block, now, ahead)
            x_p, x_m = load(src, block, 1), load(src, block, -1)
            results = []
            for g in range(groups):
                temp, cond = now[0][g], now[1][g]
                up = flux(now, x_p, g, {0: low_x[0], groups - 1: high_x}.get(g))
                down = flux(now, x_m, g, {0: low_x[1]}.get(g))
                flux_z = (cond + roll(cond, -1, 1)) * (roll(temp, -1, 1) - temp)
                flux_z = jnp.where(no_z, 0.0, flux_z)
                div = (flux_y[g] - before[g]) + (up + down) + (flux_z - roll(flux_z, 1, 1))
                new = temp + DT * (0.5 * div + q_ext[rows_of(block + 1, g)])
                if step < CSWEEPS - 1:
                    rows = rows_of(block, g)
                    results.append((new, k0_all[rows] * inverse(1.0 + b_all[rows] * new * new)))
                else:
                    results.append((new,))
            for g in range(groups):
                store(dst, block, g, *results[g])
            return ahead, flux_y

        first, second = load(src, 0), load(src, 1)
        lax.fori_loop(1, YBLOCKS - 1, advance, (second, y_fluxes(0, first, second)), unroll=9)
    final = state_b if CSWEEPS % 2 else state_a

    def give_out(yq, carry):
        for g in range(TE // SUB):
            x = slice(g * SUB, (g + 1) * SUB)
            turns = []
            for r in range(4):
                value = final[both_of(HALO + 4 * yq + r, g, HALO)[0], :]
                turns.append([turned(value, by) for by in range(4)])
            for pair in range(2):
                even, odd = turns[2 * pair], turns[2 * pair + 1]
                lower = (2 * yq + pair) * LANES
                upper = lower + temp_out.shape[1] // 2
                temp_out[x, pl.ds(pl.multiple_of(lower, LANES), LANES)] = jnp.where(half, even[0], odd[2])
                temp_out[x, pl.ds(pl.multiple_of(upper, LANES), LANES)] = jnp.where(half, even[2], odd[0])
            for c in range(4):
                value = pick([turns[r][(r - c) % 4] for r in range(4)])
                blocks[pl.ds((c * TE + g * SUB) * SUB + yq, SUB, stride=SUB), :] = value
        return carry

    lax.fori_loop(0, HALF // 4, give_out, 0, unroll=2)
    places = []
    mate = j + 1 - 2 * lax.rem(j, 2)
    targets = [(mine, 0, j)] + [(across[d - 1], 0, j + 2 * d) for d in range(1, chips)]
    targets += [(bundle, d * TE * ROW, mate + 2 * d) for d in range(chips)]
    for target, first, to in targets:
        dev = lax.rem(to, width_gy)
        for t in range(TILES):
            tile = i * tiles + dev * TILES + t
            col = pos[1, tile] - 2 * j
            cell = jnp.clip(col, 0, 1) * 2 + pos[2, tile]
            places.append((target, first + t, cell, (col >= 0) & (col < 2)))

    def pack(p, carry):
        values = []
        for _, _, cell, here in places:
            value = blocks[pl.ds(pl.multiple_of((cell * TE + p) * SUB, SUB), SUB), :]
            values.append(jnp.where(here, value, 0.0))
        for (target, first, _, _), value in zip(places, values):
            target[pl.ds(pl.multiple_of(p * ROW, ROW) + first, SUB, stride=TILES), :] = value
        return carry

    lax.fori_loop(0, TE, pack, 0, unroll=4)


def shifted(value, axis, by, wrap=False):
    count = lax.axis_size(axis)
    pairs = [(d, (d + by) % count) for d in range(count) if wrap or 0 <= d + by < count]
    return lax.ppermute(value, axis, pairs)


def with_partner(value, axis, first):
    count = lax.axis_size(axis)
    pairs = [(d, d + 1) for d in range(first, count - 1, 2)]
    return lax.ppermute(value, axis, pairs + [(high, low) for low, high in pairs])


def from_mate(value):
    return lax.ppermute(value, "gy", [(d, d ^ 1) for d in range(lax.axis_size("gy"))])


def to_rows(value):
    return value.reshape(TILES, -1, LANES).transpose(1, 0, 2).reshape(-1, LANES)


def from_rows(value):
    return value.reshape(-1, TILES, LANES).transpose(1, 0, 2).reshape(TILES, -1)


def to_other_core(value, by):
    count = lax.axis_size("gy")
    return lax.ppermute(value, "gy", [(at, ((at ^ 1) + 2 * by) % count) for at in range(count)])


VMEM = pl.BlockSpec(memory_space=pltpu.VMEM)
SMEM = pl.BlockSpec(memory_space=pltpu.SMEM)
HBM = pl.BlockSpec(memory_space=pltpu.HBM)
ANY = pl.BlockSpec(memory_space=pl.ANY)
PARAMS = pltpu.CompilerParams(vmem_limit_bytes=32 * 1024 * 1024)


def on_device(
    phi_init,
    source,
    tile_mat,
    tile_pos,
    neighbours,
    sigma_table,
    temp_init,
    slab_mat,
    k0_table,
    beta_table,
):
    f32 = jnp.float32
    pos = tile_pos.T
    width_gy = lax.axis_size("gy")
    chips = width_gy // 2
    tiles = width_gy * TILES
    size_x, width = temp_init.shape
    edge_rows = width // LANES * SUB

    def rows(count):
        return jax.ShapeDtypeStruct((count, LANES), f32)

    ready, sigma, inner, outer = pl.pallas_call(
        prep_kernel,
        out_shape=(
            rows(2 * TE * ROW),
            rows(TE * ROW),
            rows(SIDE_ROWS + edge_rows),
            rows(SIDE_ROWS + edge_rows),
        ),
        in_specs=[SMEM] * 2 + [HBM] * 5,
        out_specs=(VMEM,) * 4,
        scratch_shapes=[
            pltpu.VMEM((TE * ROW, LANES), f32),
            pltpu.VMEM((TE * ROW, LANES), f32),
            pltpu.VMEM((TE * ROW, LANES), jnp.int32),
            pltpu.VMEM((2, SUB, width), f32),
            pltpu.VMEM((2, SUB, width), jnp.int32),
            pltpu.SemaphoreType.DMA((7,)),
        ],
        compiler_params=pltpu.CompilerParams(vmem_limit_bytes=62 * 1024 * 1024),
        name="prep",
    )(sigma_table, pos, to_rows(phi_init), to_rows(source), to_rows(tile_mat), temp_init, slab_mat)
    bodies = [ready] + [shifted(ready, "gy", 2 * d, True) for d in range(1, chips)]
    bodies += [from_mate(part) for part in bodies]
    inner, outer = with_partner(inner, "gx", 0), with_partner(outer, "gx", 1)

    halo = pl.pallas_call(
        relay_kernel,
        out_shape=rows(LOW_ROWS + HIGH_ROWS),
        in_specs=[VMEM] * 2,
        out_specs=VMEM,
        compiler_params=PARAMS,
        name="relay",
    )(inner, outer)
    halos = [halo] + [shifted(halo, "gy", 2 * d, True) for d in range(1, chips)]
    sigmas = [sigma] + [shifted(sigma, "gy", 2 * d, True) for d in range(1, chips)]
    sigmas += [from_mate(sigma)] + [to_other_core(sigma, d) for d in range(1, chips)]

    native = pltpu.VMEM((width // LANES * SLABX + SUB, LANES), f32)
    t_ext, k0_ext, b_ext, edge_in, edge_out = pl.pallas_call(
        slab_kernel,
        out_shape=(rows(SLAB_ROWS),) * 3 + (rows(HALO * SLABX),) * 2,
        in_specs=[SMEM] * 3 + [VMEM] * 4,
        out_specs=(VMEM,) * 5,
        scratch_shapes=[native, native] + [pltpu.VMEM((HALO * SLABX, LANES), f32)] * 2,
        compiler_params=PARAMS,
        name="slab_prep",
    )(pos, k0_table, beta_table, temp_init, slab_mat, inner, outer)
    y_in, y_out = with_partner(edge_in, "gy", 0), with_partner(edge_out, "gy", 1)
    *halos[1:], y_in = lax.optimization_barrier((*halos[1:], y_in))
    halos = halos + [from_mate(part) for part in halos]

    def fields(count):
        return pltpu.VMEM((2 * ROW0 + (width_gy + 1) * count * ROW, LANES), f32)

    pot, slope = pl.pallas_call(
        functools.partial(sweep_kernel, chips),
        out_shape=(rows(TE * ROW), rows(CELLS * SLABX * SUB)),
        in_specs=[SMEM] + [ANY] * (2 * width_gy),
        out_specs=(VMEM, VMEM),
        scratch_shapes=[
            pltpu.SMEM((3, 2 * (2 * width_gy + 2)), jnp.int32),
            pltpu.SMEM((3, tiles), jnp.int32),
            pltpu.SMEM((3 * tiles * 8,), jnp.int32),
            fields(TE), fields(TE), fields(LOW[0]), fields(LOW[0]), fields(HIGH[0]), fields(HIGH[0]),
            fields(TE), fields(LOW[1]), fields(HIGH[1]),
            pltpu.SemaphoreType.DMA((6 * width_gy,)),
        ],
        compiler_params=PARAMS,
        name="sweeps",
    )(pos, *bodies, *halos)

    temp, mine, bundle, *across = pl.pallas_call(
        functools.partial(slab_steps_kernel, chips),
        out_shape=(jax.ShapeDtypeStruct((size_x, width), f32), rows(TE * ROW), rows(chips * TE * ROW))
        + (rows(TE * ROW),) * (chips - 1),
        in_specs=[SMEM] * 3 + [ANY] * width_gy + [VMEM] * (width_gy + 6),
        out_specs=(VMEM,) * (2 + chips),
        scratch_shapes=[pltpu.VMEM((CELLS * SLABX * SUB, LANES), f32)]
        + [pltpu.VMEM((SLAB_ROWS + 3 * SLABX, LANES), f32)]
        + [pltpu.VMEM((2 * SLAB_ROWS, LANES), f32)] * 2
        + [pltpu.VMEM((SLAB_ROWS, LANES), f32)] * 2
        + [pltpu.VMEM((4 * TE * SUB, LANES), f32), pltpu.VMEM((width_gy, TE * ROW, LANES), f32)]
        + [pltpu.SemaphoreType.DMA((width_gy,))],
        compiler_params=PARAMS,
        name="slab_steps",
    )(pos, k0_table, beta_table, *sigmas, *halos, slope, t_ext, k0_ext, b_ext, y_in, y_out)
    got = from_mate(bundle).reshape(chips, TE * ROW, LANES)
    tile_temps = mine + got[0]
    for d in range(1, chips):
        tile_temps = tile_temps + shifted(across[d - 1] + got[d], "gy", 2 * d, True)
    return from_rows(pot), temp, from_rows(tile_temps)


def solution(mesh):
    placed = (
        P(("gx", "gy"), None),
        P(("gx", "gy"), None),
        P(("gx", "gy"), None),
        P(),
        P(("gx", "gy"), None),
        P(),
        P("gx", "gy"),
        P("gx", "gy"),
        P(),
        P(),
    )
    return jax.shard_map(
        on_device,
        mesh=mesh,
        in_specs=placed,
        out_specs=(P(("gx", "gy"), None), P("gx", "gy"), P(("gx", "gy"), None)),
        check_vma=False,
    )
```

```python
import functools
import math

import jax
import jax.numpy as jnp
from jax import lax
from jax.experimental import pallas as pl
from jax.experimental.pallas import tpu as pltpu
from jax.sharding import PartitionSpec as P

TE = 32
SWEEPS = 4
CSWEEPS = 3
NZ = 64
EPS = 2.0
DT = 0.15
LANES = 128
SUB = 8
TILES = 2
ROW = SUB * TILES

LOW = (SWEEPS + 2, SWEEPS + 1, 2)
HIGH = (SWEEPS + 3, SWEEPS + 2, 2)
LOW_ROWS = sum(LOW) * ROW
HIGH_ROWS = sum(HIGH) * ROW
SIDE_ROWS = max(LOW_ROWS, HIGH_ROWS)
SLABX = TE + SUB
HALO = CSWEEPS
HALF = TE
YBLOCKS = HALF + 2 * HALO
CELLS = 9
ROW0 = ROW
SLAB_ROWS = ROW0 + YBLOCKS * SLABX + ROW0


def cheb_weight(step, count):
    return 1.0 / (1.0 + 0.75 * math.cos(math.pi * (2 * step + 1) / (2 * count)))


def lookup(table, ids):
    out = jnp.full(ids.shape, table[3], jnp.float32)
    for which in (2, 1, 0):
        out = jnp.where(ids == which, table[which], out)
    return out


def roll(value, by, axis):
    return pltpu.roll(value, by % value.shape[axis], axis)


def prep_kernel(table, pos, phi, src, mat, temp, slab, ready, sigma, inner, outer, phi_v, src_v, mat_v, ends_t, ends_m, sems):
    rows = TE * ROW
    size_x, width = temp.shape
    moves = [(phi, phi_v), (src, src_v), (mat, mat_v)]
    for which, first in enumerate((0, size_x - SUB)):
        moves.append((temp.at[first : first + SUB], ends_t.at[which]))
        moves.append((slab.at[first : first + SUB], ends_m.at[which]))
    moves = [pltpu.make_async_copy(*move, sems.at[at]) for at, move in enumerate(moves)]
    for move in moves:
        move.start()
    for move in moves:
        move.wait()
    first = (lax.axis_index("gx") * lax.axis_size("gy") + lax.axis_index("gy")) * TILES
    upper = [pos[2, first + t] == 1 for t in range(TILES)]

    def plane(p, carry):
        values = []
        for t in range(TILES):
            row = pl.multiple_of(p * ROW, ROW) + t
            at = pl.ds(row, SUB, stride=TILES)
            conduct = lookup(table, mat_v[at, :])
            three = (phi_v[at, :], src_v[at, :] / conduct, conduct)
            values.append((row, [jnp.where(upper[t], roll(v, TE, 1), v) for v in three]))
        for row, (potential, s, conduct) in values:
            ready[pl.ds(row, SUB, stride=TILES), :] = potential
            ready[pl.ds(row + rows, SUB, stride=TILES), :] = s
            sigma[pl.ds(row, SUB, stride=TILES), :] = conduct
        return carry

    lax.fori_loop(0, TE, plane, 0, unroll=8)
    even = lax.rem(lax.axis_index("gx"), 2) == 0

    @pl.when(even)
    def _():
        fill_sides(ready, sigma, ends_t, ends_m, inner, outer)

    @pl.when(jnp.logical_not(even))
    def _():
        fill_sides(ready, sigma, ends_t, ends_m, outer, inner)


def fill_sides(body, sigma, ends_t, ends_m, up, down):
    rows = TE * ROW
    width = ends_t.shape[2]
    at_up, at_down = 0, 0
    for ref, first in ((body, 0), (body, rows), (sigma, 0)):
        which = (first // rows) if ref is body else 2
        size = LOW[which] * ROW
        up[at_up : at_up + size] = ref[first + rows - size : first + rows]
        at_up += size
        size = HIGH[which] * ROW
        down[at_down : at_down + size] = ref[first : first + size]
        at_down += size
    sub = lax.broadcasted_iota(jnp.int32, (SUB, LANES), 0)
    for at in range(width // LANES):
        lanes = slice(at * LANES, (at + 1) * LANES)
        t_low, m_low = ends_t[0, :, lanes], ends_m[0, :, lanes].astype(jnp.float32)
        t_high, m_high = ends_t[1, :, lanes], ends_m[1, :, lanes].astype(jnp.float32)
        first = at * SUB
        up[SIDE_ROWS + first : SIDE_ROWS + first + SUB] = jnp.where(sub < 4, roll(t_high, HALO, 0), roll(m_high, -1, 0))
        down[SIDE_ROWS + first : SIDE_ROWS + first + SUB] = jnp.where(sub < 4, t_low, roll(m_low, 4, 0))


def relay_kernel(inner, outer, halo):
    def join(low, high):
        halo[0:LOW_ROWS] = low[0:LOW_ROWS]
        halo[LOW_ROWS:] = high[0:HIGH_ROWS]

    even = lax.rem(lax.axis_index("gx"), 2) == 0
    pl.when(even)(lambda: join(outer, inner))
    pl.when(jnp.logical_not(even))(lambda: join(inner, outer))


def loose(pos):
    return jnp.minimum(pos[0, 0], 0)


def slab_kernel(pos, k0_table, beta_table, temp, mat, inner, outer, sigma, t_ext, k0_ext, b_ext, edge_in, packet, native_t, native_m, edge_low, edge_high):
    start = loose(pos)
    even = lax.rem(lax.axis_index("gx"), 2) == 0
    blocks = temp.shape[1] // LANES
    half = lax.broadcasted_iota(jnp.int32, (SUB, LANES), 1) < NZ
    for which, (own, native) in enumerate(((temp, native_t), (mat, native_m))):
        for at in range(blocks):
            lanes = slice(at * LANES, (at + 1) * LANES)
            first = at * SLABX
            side = slice(SIDE_ROWS + at * SUB, SIDE_ROWS + (at + 1) * SUB)
            value = jnp.where(even, outer[side, :], inner[side, :])
            native[first : first + SUB, :] = roll(value, -4, 0) if which else value
            for g in range(TE // SUB):
                value = own[g * SUB : (g + 1) * SUB, lanes].astype(jnp.float32)
                native[pl.ds(start + first + HALO + g * SUB, SUB), :] = value
            value = jnp.where(even, inner[side, :], outer[side, :])
            native[pl.ds(start + first + HALO + TE, SUB), :] = roll(value, -4, 0) if which else value
    for at in range(blocks // 2):
        for g in range(SLABX // SUB):
            halves = []
            for native in (native_t, native_m):
                lower = native[at * SLABX + g * SUB : at * SLABX + (g + 1) * SUB, :]
                upper_at = (blocks // 2 + at) * SLABX + g * SUB
                upper = native[upper_at : upper_at + SUB, :]
                lower_r, upper_r = roll(lower, NZ, 1), roll(upper, NZ, 1)
                halves.append((lower, lower_r, upper, upper_r))
            for odd in range(2):
                y = 2 * at + odd
                temps, mats = (jnp.where(half, v[odd], v[3 - odd]) for v in halves)
                places = [(y + HALO, temps, mats)]
                if y >= HALF - HALO:
                    places.append((y - HALF + HALO, halves[0][1 - odd], halves[1][1 - odd]))
                if y < HALO:
                    places.append((y + HALF + HALO, halves[0][2 + odd], halves[1][2 + odd]))
                for block, t, m in places:
                    rows = slice(ROW0 + block * SLABX + g * SUB, ROW0 + block * SLABX + (g + 1) * SUB)
                    t_ext[rows] = t
                    k0_ext[rows] = lookup(k0_table, m)
                    b_ext[rows] = lookup(beta_table, m)
                if y < HALO:
                    rows = slice(y * SLABX + g * SUB, y * SLABX + (g + 1) * SUB)
                    edge_low[rows] = jnp.where(half, halves[0][odd], halves[1][1 - odd])
                if y >= HALF - HALO:
                    first = (y - HALF + HALO) * SLABX + g * SUB
                    edge_high[first : first + SUB] = jnp.where(half, halves[0][2 + odd], halves[1][3 - odd])
    even = lax.rem(lax.axis_index("gy"), 2) == 0
    edge_in[...] = jnp.where(even, edge_high[...], edge_low[...])
    packet[0 : TE * ROW] = sigma[...]
    packet[TE * ROW :] = jnp.where(even, edge_low[...], edge_high[...])


def fill_maps(chips, pos, cell_at, cell_of):
    width_gy = 2 * chips
    tiles = width_gy * TILES
    i = lax.axis_index("gx")
    j = lax.axis_index("gy")
    rows_gx = lax.axis_size("gx")
    for at in range(2 * (2 * width_gy + 2)):
        for which in range(3):
            cell_at[which, at] = tiles
    for which, by in enumerate((0, -1, 1)):
        row = i + by
        valid = (row >= 0) & (row < rows_gx)
        first = jnp.clip(row, 0, rows_gx - 1) * tiles
        for part in range(width_gy):
            dev = part_device(part, chips, j)
            for t in range(TILES):
                tile = first + dev * TILES + t
                cell = (pos[1, tile] + 1) * 2 + pos[2, tile]
                slot = part * TILES + t
                cell_of[which, slot] = cell
                cell_at[which, cell] = jnp.where(valid, slot, tiles)


def part_device(part, chips, j):
    mate = j + 1 - 2 * lax.rem(j, 2)
    base = j if part < chips else mate
    return lax.rem(base - 2 * (part % chips) + 2 * chips, 2 * chips)


def sweep_kernel(chips, pos, *refs):
    width_gy = 2 * chips
    tiles = width_gy * TILES
    none = tiles
    bodies, halos = refs[:width_gy], refs[width_gy : 2 * width_gy]
    pot, slope, cell_at, cell_of, table, pa, pb, la, lb, ua, ub, s_c, s_l, s_u, sems = refs[2 * width_gy :]
    i = lax.axis_index("gx")
    j = lax.axis_index("gy")
    rows_gx = lax.axis_size("gx")
    zero = jnp.zeros((SUB, LANES), jnp.float32)

    moves = []
    for part in range(width_gy):
        at = 0
        pieces = [(bodies[part], 0, pa, part * TE, TE), (bodies[part], TE * ROW, s_c, part * TE, TE)]
        for target, first, count in (
            (la, part * LOW[0], LOW[0]),
            (s_l, part * LOW[1], LOW[1]),
            (None, 0, LOW[2]),
            (ua, part * HIGH[0], HIGH[0]),
            (s_u, part * HIGH[1], HIGH[1]),
        ):
            if target is not None:
                pieces.append((halos[part], at, target, first, count))
            at += count * ROW
        for source, start, target, first, count in pieces:
            move = pltpu.make_async_copy(
                source.at[start : start + count * ROW],
                target.at[ROW0 + first * ROW : ROW0 + (first + count) * ROW],
                sems.at[len(moves)],
            )
            move.start()
            moves.append(move)

    fill_maps(chips, pos, cell_at, cell_of)

    def row_of(slot, size):
        pair, second = lax.shift_right_logical(slot, 1), lax.bitwise_and(slot, 1)
        return ROW0 + pair * (size * ROW) + second

    def enter(slot, carry):
        for which, size in enumerate((TE, LOW[0], HIGH[0])):
            cell = cell_of[which, slot]
            upper = lax.bitwise_and(cell, 1)
            beside = cell_at[which, cell + 1 - 2 * upper]
            here = [cell_at[at, cell] for at in range(3)]
            near = (slot, cell_at[which, cell - 2], cell_at[which, cell + 2])
            near += (jnp.where(upper == 1, beside, none), jnp.where(upper == 1, none, beside))
            rows = [row_of(at, size) for at in near]
            if which == 0:
                rows += [row_of(here[1], LOW[0]) + (LOW[0] - 1) * ROW, row_of(here[2], HIGH[0])]
            else:
                centre = row_of(here[0], TE)
                rows += [centre + (TE - 1) * ROW, centre]
            rows.append(upper)
            for at, row in enumerate(rows):
                table[(which * tiles + slot) * 8 + at] = row
        return carry

    lax.fori_loop(0, tiles, enter, 0)

    def entry(which, slot):
        return [table[(which * tiles + slot) * 8 + at] for at in range(8)]

    def plane_at(ref, row):
        return ref[pl.ds(row, SUB, stride=TILES), :]

    def put_plane(ref, row, value):
        ref[pl.ds(row, SUB, stride=TILES), :] = value

    for ref, count in ((pa, TE), (pb, TE), (la, LOW[0]), (lb, LOW[0]), (ua, HIGH[0]), (ub, HIGH[0])):
        first = ROW0 + width_gy * count * ROW
        for row in range(first, first + count * ROW, SUB):
            ref[row : row + SUB] = zero

    def clear(at, carry):
        slope[pl.ds(pl.multiple_of(at * SUB, SUB), SUB), :] = zero
        return carry

    lax.fori_loop(0, slope.shape[0] // SUB, clear, 0, unroll=8)
    for move in moves:
        move.wait()

    lane = lax.broadcasted_iota(jnp.int32, (SUB, LANES), 1)
    sub = lax.broadcasted_iota(jnp.int32, (SUB, LANES), 0)
    depth = lane % TE
    first_sub, last_sub = sub == 0, sub == SUB - 1
    first_z, last_z = depth == 0, depth == TE - 1

    def y_plus(ref, own, first_y, row, ghost_row):
        turned = jnp.where(last_sub, plane_at(ref, ghost_row), plane_at(ref, row))
        return roll(jnp.where(first_y, turned, own), -TE, 1)

    def y_minus(ref, own, last_y, row, ghost_row):
        turned = jnp.where(first_sub, plane_at(ref, ghost_row), plane_at(ref, row))
        return roll(jnp.where(last_y, turned, own), TE, 1)

    def z_plus(ref, own, ghost_row):
        return roll(jnp.where(first_z, plane_at(ref, ghost_row), own), -1, 1)

    def z_minus(ref, own, ghost_row):
        return roll(jnp.where(last_z, plane_at(ref, ghost_row), own), 1, 1)

    def y_ends(upper):
        quarter = lane // TE
        return quarter == upper, quarter == lax.bitwise_and(upper + 3, 3)

    bufs = ((pa, la, ua), (pb, lb, ub))
    for k in range(SWEEPS):
        weight = cheb_weight(k, SWEEPS)
        keep, gain = 1.0 - weight, weight / (6.0 + EPS)
        (c_src, l_src, u_src), (c_dst, l_dst, u_dst) = bufs[k % 2], bufs[(k + 1) % 2]

        def relax(src, dst, places, first, count, s_ref, s_row, before, beyond):
            row, row_m, row_p, row_zm, row_zp, _, _, upper = places
            first_y, last_y = y_ends(upper)
            own = plane_at(src, row + first * ROW)
            for p in range(count):
                step = (first + p) * ROW
                after = plane_at(src, row + (step + ROW)) if beyond is None or p < count - 1 else beyond
                total = (before + after) + plane_at(s_ref, s_row + p * ROW)
                along_y = y_minus(src, own, last_y, row + (step - TILES), row_m + (step + ROW - TILES))
                along_y = along_y + y_plus(src, own, first_y, row + (step + TILES), row_p + (step + TILES - ROW))
                along_z = z_minus(src, own, row_zm + step) + z_plus(src, own, row_zp + step)
                put_plane(dst, row + step, keep * own + gain * (total + (along_y + along_z)))
                before, own = own, after

        def sweep_tile(slot, carry):
            at = entry(0, slot)
            relax(c_src, c_dst, at, 0, TE, s_c, at[0], plane_at(l_src, at[5]), plane_at(u_src, at[6]))
            at = entry(1, slot)
            count = LOW[0] - 1 - k
            s_row = row_of(slot, LOW[1]) + (LOW[1] - count) * ROW
            before, beyond = plane_at(l_src, at[0] + k * ROW), plane_at(c_src, at[6])
            relax(l_src, l_dst, at, k + 1, count, s_l, s_row, before, beyond)
            at = entry(2, slot)
            relax(u_src, u_dst, at, 0, HIGH[0] - 1 - k, s_u, row_of(slot, HIGH[1]), plane_at(c_src, at[5]), None)
            return carry

        lax.fori_loop(0, tiles, sweep_tile, 0, unroll=4)

    field, f_l, f_u = bufs[SWEEPS % 2]
    for t in range(TILES):
        turn = jnp.where(table[t * 8 + 7] == 1, LANES - TE, 0)

        def turn_back(p, carry):
            value = plane_at(field, p * ROW + (ROW0 + t))
            put_plane(pot, pl.multiple_of(p * ROW, ROW) + t, pltpu.roll(value, turn, 1))
            return carry

        lax.fori_loop(0, TE, turn_back, 0, unroll=8)

    def squares(ref, places, local, x, first, count, beyond):
        row, _, row_p, _, row_z, _, _, upper = places
        first_y, _ = y_ends(upper)
        target = (local * SLABX + x) * SUB
        own = plane_at(ref, row + first * ROW)
        for p in range(count):
            step = (first + p) * ROW
            after = plane_at(ref, row + (step + ROW)) if beyond is None or p < count - 1 else beyond
            d_x = after - own
            d_y = y_plus(ref, own, first_y, row + (step + TILES), row_p + (step + TILES - ROW)) - own
            d_z = z_plus(ref, own, row_z + step) - own
            rows = pl.ds(pl.multiple_of(target + p * SUB, SUB), SUB)
            slope[rows, :] = d_x * d_x + d_y * d_y + d_z * d_z
            own = after

    def slope_tile(slot, carry):
        at, local = entry(0, slot), window(0, cell_of[0, slot], i, j, rows_gx)
        squares(field, at, local, HALO, 0, TE, plane_at(f_u, at[6]))
        at, local = entry(1, slot), window(1, cell_of[1, slot], i, j, rows_gx)
        squares(f_l, at, local, HALO - 2, LOW[0] - 2, 2, plane_at(field, at[6]))
        at, local = entry(2, slot), window(2, cell_of[2, slot], i, j, rows_gx)
        squares(f_u, at, local, HALO + TE, 0, 2, None)
        return carry

    lax.fori_loop(0, tiles, slope_tile, 0, unroll=2)


def window(which, cell, i, j, rows_gx):
    local = cell - 4 * j
    inside = (local >= 0) & (local < CELLS - 1)
    if which > 0:
        row = i - 1 if which == 1 else i + 1
        inside = inside & (row >= 0) & (row < rows_gx)
    return jnp.where(inside, local, CELLS - 1)


def slab_steps_kernel(chips, pos, k0_table, beta_table, *refs):
    width_gy = 2 * chips
    tiles = width_gy * TILES
    halos = refs[width_gy : 2 * width_gy]
    slope, t_in, k0_in, b_in, y_in, temp_out = refs[2 * width_gy : 2 * width_gy + 6]
    mine, bundle = refs[2 * width_gy + 6 : 2 * width_gy + 8]
    across = refs[2 * width_gy + 8 : 2 * width_gy + 7 + chips]
    heat, q_ext, state_a, state_b, k0_all, b_all, blocks, sigmas, y_out, sems = refs[2 * width_gy + 7 + chips :]
    moves = []
    for part in range(width_gy):
        moves.append(pltpu.make_async_copy(refs[part].at[0 : TE * ROW], sigmas.at[part], sems.at[part]))
        moves[-1].start()
    edges = []
    for which, d in enumerate((1, chips - 1)):
        source = refs[chips + d].at[TE * ROW : TE * ROW + HALO * SLABX]
        edges.append(pltpu.make_async_copy(source, y_out.at[which], sems.at[width_gy + which]))
        edges[-1].start()
    i = lax.axis_index("gx")
    j = lax.axis_index("gy")
    rows_gx = lax.axis_size("gx")
    lane = lax.broadcasted_iota(jnp.int32, (SUB, LANES), 1)
    zero = jnp.zeros((SUB, LANES), jnp.float32)

    quarter = [(lane >= q * TE) & (lane < (q + 1) * TE) for q in range(3)]

    def pick(parts):
        return jnp.where(
            quarter[0], parts[0], jnp.where(quarter[1], parts[1], jnp.where(quarter[2], parts[2], parts[3]))
        )

    def turned(value, by):
        return value if by % 4 == 0 else roll(value, by * TE, 1)

    def rows_of(block, g):
        first = ROW0 + block * SLABX + g * SUB
        if not isinstance(first, int):
            first = pl.multiple_of(first, SUB)
        return pl.ds(first, SUB)

    groups = SLABX // SUB

    sub = lax.broadcasted_iota(jnp.int32, (SUB, LANES), 0)
    half = lane < NZ
    no_z = lane % NZ == NZ - 1
    low_x = (sub == HALO - 1) & (i == 0), (sub == HALO) & (i == 0)
    high_x = (sub == (HALO + TE - 1) % SUB) & (i == rows_gx - 1)
    low_y, high_y = half & (j == 0), (lane >= NZ) & (j == width_gy - 1)

    def inverse(value):
        near = pl.reciprocal(value, approx=True)
        near = near * (2.0 - value * near)
        return near * (2.0 - value * near)

    def both_of(block, g, by=0):
        first = 2 * (ROW0 + block * SLABX + g * SUB + by)
        return pl.ds(first, SUB, stride=2), pl.ds(first + 1, SUB, stride=2)

    def load(ref, block, by=0):
        places = [both_of(block, g, by) for g in range(groups)]
        return [ref[at, :] for at, _ in places], [ref[at, :] for _, at in places]

    def store(ref, block, g, temp, cond=None):
        first, second = both_of(block, g)
        ref[first, :] = temp
        if cond is not None:
            ref[second, :] = cond

    even = lax.rem(j, 2) == 0

    def begin(block, low, at):
        values = []
        for g in range(groups):
            rows = rows_of(block, g)
            temp, k0, beta = t_in[rows], k0_in[rows], b_in[rows]
            if low is not None:
                place = slice(at * SLABX + g * SUB, at * SLABX + (g + 1) * SUB)
                other = jnp.where(even, y_out[0, place], y_out[1, place])
                value = jnp.where(even, *((other, y_in[place])[:: 1 if low else -1]))
                swapped = roll(value, NZ, 1)
                if low:
                    temp = jnp.where(half, value, temp)
                    k0 = jnp.where(half, lookup(k0_table, swapped), k0)
                    beta = jnp.where(half, lookup(beta_table, swapped), beta)
                else:
                    temp = jnp.where(half, temp, swapped)
                    k0 = jnp.where(half, k0, lookup(k0_table, value))
                    beta = jnp.where(half, beta, lookup(beta_table, value))
            values.append((rows, temp, k0, beta, k0 * inverse(1.0 + beta * temp * temp)))
        for g, (rows, temp, k0, beta, cond) in enumerate(values):
            k0_all[rows], b_all[rows] = k0, beta
            store(state_a, block, g, temp, cond)

    def begin_inner(block, carry):
        begin(block, None, 0)
        return carry

    lax.fori_loop(HALO, YBLOCKS - HALO, begin_inner, 0, unroll=4)
    for move in edges:
        move.wait()
    for e in range(HALO):
        begin(e, True, e)
        begin(YBLOCKS - HALO + e, False, e)

    def clear(at, carry):
        heat[pl.ds(pl.multiple_of(at * SUB, SUB), SUB), :] = zero
        return carry

    lax.fori_loop(0, heat.shape[0] // SUB, clear, 0, unroll=8)
    for move in moves:
        move.wait()
    low_at, high_at = (LOW[0] + LOW[1]) * ROW, LOW_ROWS + (HIGH[0] + HIGH[1]) * ROW
    for part in range(width_gy):
        dev = part_device(part, chips, j)
        for t in range(TILES):
            for which, by in enumerate((0, -1, 1)):
                tile = jnp.clip(i + by, 0, rows_gx - 1) * tiles + dev * TILES + t
                cell = (pos[1, tile] + 1) * 2 + pos[2, tile]
                local = window(which, cell, i, j, rows_gx)
                source, start, x, count = (
                    (sigmas.at[part], 0, HALO, TE),
                    (halos[part], low_at, HALO - 2, 2),
                    (halos[part], high_at, HALO + TE, 2),
                )[which]
                first = pl.multiple_of((local * SLABX + x) * SUB, SUB)
                for p in range(count):
                    rows = pl.ds(pl.multiple_of(first + p * SUB, SUB), SUB)
                    sigma = source[pl.ds(start + p * ROW + t, SUB, stride=TILES), :]
                    heat[rows, :] = sigma * slope[rows, :]

    def place_heat(at, carry):
        first = at - 1
        col, yq = lax.div(first * 4 + TE, TE), lax.rem(first * 4 + TE, TE) // 4
        for g in range(groups):
            cells = [
                heat[pl.ds(pl.multiple_of(((2 * col + c) * SLABX + g * SUB) * SUB, SUB) + yq, SUB, stride=SUB), :]
                for c in range(4)
            ]
            for r in range(4):
                block = 4 * first + r + HALO + 1
                q_ext[rows_of(block, g)] = pick([turned(cells[c], c - r - c % 2) for c in range(4)])
        return carry

    lax.fori_loop(0, HALF // 4 + 2, place_heat, 0, unroll=2)

    for step in range(CSWEEPS):
        src, dst = (state_a, state_b)[:: 1 if step % 2 == 0 else -1]

        def y_fluxes(block, now, ahead):
            closed = (low_y & (block == HALO - 1)) | (high_y & (block == HALO + HALF - 1))
            return [flux(now, ahead, g, closed) for g in range(groups)]

        def flux(now, other, g, closed=None):
            value = (now[1][g] + other[1][g]) * (other[0][g] - now[0][g])
            return value if closed is None else jnp.where(closed, 0.0, value)

        def advance(block, carry):
            now, before = carry
            ahead = load(src, block + 1)
            flux_y = y_fluxes(block, now, ahead)
            x_p, x_m = load(src, block, 1), load(src, block, -1)
            results = []
            for g in range(groups):
                temp, cond = now[0][g], now[1][g]
                up = flux(now, x_p, g, {0: low_x[0], groups - 1: high_x}.get(g))
                down = flux(now, x_m, g, {0: low_x[1]}.get(g))
                flux_z = (cond + roll(cond, -1, 1)) * (roll(temp, -1, 1) - temp)
                flux_z = jnp.where(no_z, 0.0, flux_z)
                div = (flux_y[g] - before[g]) + (up + down) + (flux_z - roll(flux_z, 1, 1))
                new = temp + DT * (0.5 * div + q_ext[rows_of(block + 1, g)])
                if step < CSWEEPS - 1:
                    rows = rows_of(block, g)
                    results.append((new, k0_all[rows] * inverse(1.0 + b_all[rows] * new * new)))
                else:
                    results.append((new,))
            for g in range(groups):
                store(dst, block, g, *results[g])
            return ahead, flux_y

        first, second = load(src, 0), load(src, 1)
        lax.fori_loop(1, YBLOCKS - 1, advance, (second, y_fluxes(0, first, second)), unroll=9)
    final = state_b if CSWEEPS % 2 else state_a

    def give_out(yq, carry):
        for g in range(TE // SUB):
            x = slice(g * SUB, (g + 1) * SUB)
            turns = []
            for r in range(4):
                value = final[both_of(HALO + 4 * yq + r, g, HALO)[0], :]
                turns.append([turned(value, by) for by in range(4)])
            for pair in range(2):
                even, odd = turns[2 * pair], turns[2 * pair + 1]
                lower = (2 * yq + pair) * LANES
                upper = lower + temp_out.shape[1] // 2
                temp_out[x, pl.ds(pl.multiple_of(lower, LANES), LANES)] = jnp.where(half, even[0], odd[2])
                temp_out[x, pl.ds(pl.multiple_of(upper, LANES), LANES)] = jnp.where(half, even[2], odd[0])
            for c in range(4):
                value = pick([turns[r][(r - c) % 4] for r in range(4)])
                blocks[pl.ds((c * TE + g * SUB) * SUB + yq, SUB, stride=SUB), :] = value
        return carry

    lax.fori_loop(0, HALF // 4, give_out, 0, unroll=2)
    places = []
    mate = j + 1 - 2 * lax.rem(j, 2)
    targets = [(mine, 0, j)] + [(across[d - 1], 0, j + 2 * d) for d in range(1, chips)]
    targets += [(bundle, d * TE * ROW, mate + 2 * d) for d in range(chips)]
    for target, first, to in targets:
        dev = lax.rem(to, width_gy)
        for t in range(TILES):
            tile = i * tiles + dev * TILES + t
            col = pos[1, tile] - 2 * j
            cell = jnp.clip(col, 0, 1) * 2 + pos[2, tile]
            places.append((target, first + t, cell, (col >= 0) & (col < 2)))

    def pack(p, carry):
        values = []
        for _, _, cell, here in places:
            value = blocks[pl.ds(pl.multiple_of((cell * TE + p) * SUB, SUB), SUB), :]
            values.append(jnp.where(here, value, 0.0))
        for (target, first, _, _), value in zip(places, values):
            target[pl.ds(pl.multiple_of(p * ROW, ROW) + first, SUB, stride=TILES), :] = value
        return carry

    lax.fori_loop(0, TE, pack, 0, unroll=4)


def shifted(value, axis, by, wrap=False):
    count = lax.axis_size(axis)
    pairs = [(d, (d + by) % count) for d in range(count) if wrap or 0 <= d + by < count]
    return lax.ppermute(value, axis, pairs)


def with_partner(value, axis, first):
    count = lax.axis_size(axis)
    pairs = [(d, d + 1) for d in range(first, count - 1, 2)]
    return lax.ppermute(value, axis, pairs + [(high, low) for low, high in pairs])


def from_mate(value):
    return lax.ppermute(value, "gy", [(d, d ^ 1) for d in range(lax.axis_size("gy"))])


def to_rows(value):
    return value.reshape(TILES, -1, LANES).transpose(1, 0, 2).reshape(-1, LANES)


def from_rows(value):
    return value.reshape(-1, TILES, LANES).transpose(1, 0, 2).reshape(TILES, -1)


def to_other_core(value, by):
    count = lax.axis_size("gy")
    return lax.ppermute(value, "gy", [(at, ((at ^ 1) + 2 * by) % count) for at in range(count)])


VMEM = pl.BlockSpec(memory_space=pltpu.VMEM)
SMEM = pl.BlockSpec(memory_space=pltpu.SMEM)
HBM = pl.BlockSpec(memory_space=pltpu.HBM)
ANY = pl.BlockSpec(memory_space=pl.ANY)
PARAMS = pltpu.CompilerParams(vmem_limit_bytes=32 * 1024 * 1024)


def on_device(
    phi_init,
    source,
    tile_mat,
    tile_pos,
    neighbours,
    sigma_table,
    temp_init,
    slab_mat,
    k0_table,
    beta_table,
):
    f32 = jnp.float32
    pos = tile_pos.T
    width_gy = lax.axis_size("gy")
    chips = width_gy // 2
    tiles = width_gy * TILES
    size_x, width = temp_init.shape
    edge_rows = width // LANES * SUB

    def rows(count):
        return jax.ShapeDtypeStruct((count, LANES), f32)

    ready, sigma, inner, outer = pl.pallas_call(
        prep_kernel,
        out_shape=(
            rows(2 * TE * ROW),
            rows(TE * ROW),
            rows(SIDE_ROWS + edge_rows),
            rows(SIDE_ROWS + edge_rows),
        ),
        in_specs=[SMEM] * 2 + [HBM] * 5,
        out_specs=(VMEM,) * 4,
        scratch_shapes=[
            pltpu.VMEM((TE * ROW, LANES), f32),
            pltpu.VMEM((TE * ROW, LANES), f32),
            pltpu.VMEM((TE * ROW, LANES), jnp.int32),
            pltpu.VMEM((2, SUB, width), f32),
            pltpu.VMEM((2, SUB, width), jnp.int32),
            pltpu.SemaphoreType.DMA((7,)),
        ],
        compiler_params=pltpu.CompilerParams(vmem_limit_bytes=62 * 1024 * 1024),
        name="prep",
    )(sigma_table, pos, to_rows(phi_init), to_rows(source), to_rows(tile_mat), temp_init, slab_mat)
    bodies = [ready] + [shifted(ready, "gy", 2 * d, True) for d in range(1, chips)]
    bodies += [from_mate(part) for part in bodies]
    inner, outer = with_partner(inner, "gx", 0), with_partner(outer, "gx", 1)

    halo = pl.pallas_call(
        relay_kernel,
        out_shape=rows(LOW_ROWS + HIGH_ROWS),
        in_specs=[VMEM] * 2,
        out_specs=VMEM,
        compiler_params=PARAMS,
        name="relay",
    )(inner, outer)
    halos = [halo] + [shifted(halo, "gy", 2 * d, True) for d in range(1, chips)]
    native = pltpu.VMEM((width // LANES * SLABX + SUB, LANES), f32)
    t_ext, k0_ext, b_ext, edge_in, packet = pl.pallas_call(
        slab_kernel,
        out_shape=(rows(SLAB_ROWS),) * 3 + (rows(HALO * SLABX), rows(TE * ROW + HALO * SLABX)),
        in_specs=[SMEM] * 3 + [VMEM] * 5,
        out_specs=(VMEM,) * 5,
        scratch_shapes=[native, native] + [pltpu.VMEM((HALO * SLABX, LANES), f32)] * 2,
        compiler_params=PARAMS,
        name="slab_prep",
    )(pos, k0_table, beta_table, temp_init, slab_mat, inner, outer, sigma)
    y_in = with_partner(edge_in, "gy", 0)
    sigmas = [sigma] + [shifted(sigma, "gy", 2 * d, True) for d in range(1, chips)]
    sigmas += [from_mate(sigma)] + [
        to_other_core(packet if d in (1, chips - 1) else sigma, d) for d in range(1, chips)
    ]
    *halos[1:], y_in = lax.optimization_barrier((*halos[1:], y_in))
    halos = halos + [from_mate(part) for part in halos]

    def fields(count):
        return pltpu.VMEM((2 * ROW0 + (width_gy + 1) * count * ROW, LANES), f32)

    pot, slope = pl.pallas_call(
        functools.partial(sweep_kernel, chips),
        out_shape=(rows(TE * ROW), rows(CELLS * SLABX * SUB)),
        in_specs=[SMEM] + [ANY] * (2 * width_gy),
        out_specs=(VMEM, VMEM),
        scratch_shapes=[
            pltpu.SMEM((3, 2 * (2 * width_gy + 2)), jnp.int32),
            pltpu.SMEM((3, tiles), jnp.int32),
            pltpu.SMEM((3 * tiles * 8,), jnp.int32),
            fields(TE), fields(TE), fields(LOW[0]), fields(LOW[0]), fields(HIGH[0]), fields(HIGH[0]),
            fields(TE), fields(LOW[1]), fields(HIGH[1]),
            pltpu.SemaphoreType.DMA((6 * width_gy,)),
        ],
        compiler_params=PARAMS,
        name="sweeps",
    )(pos, *bodies, *halos)

    temp, mine, bundle, *across = pl.pallas_call(
        functools.partial(slab_steps_kernel, chips),
        out_shape=(jax.ShapeDtypeStruct((size_x, width), f32), rows(TE * ROW), rows(chips * TE * ROW))
        + (rows(TE * ROW),) * (chips - 1),
        in_specs=[SMEM] * 3 + [ANY] * width_gy + [VMEM] * (width_gy + 5),
        out_specs=(VMEM,) * (2 + chips),
        scratch_shapes=[pltpu.VMEM((CELLS * SLABX * SUB, LANES), f32)]
        + [pltpu.VMEM((SLAB_ROWS + 3 * SLABX, LANES), f32)]
        + [pltpu.VMEM((2 * SLAB_ROWS, LANES), f32)] * 2
        + [pltpu.VMEM((SLAB_ROWS, LANES), f32)] * 2
        + [pltpu.VMEM((4 * TE * SUB, LANES), f32), pltpu.VMEM((width_gy, TE * ROW, LANES), f32)]
        + [pltpu.VMEM((2, HALO * SLABX, LANES), f32), pltpu.SemaphoreType.DMA((width_gy + 2,))],
        compiler_params=PARAMS,
        name="slab_steps",
    )(pos, k0_table, beta_table, *sigmas, *halos, slope, t_ext, k0_ext, b_ext, y_in)
    got = from_mate(bundle).reshape(chips, TE * ROW, LANES)
    tile_temps = mine + got[0]
    for d in range(1, chips):
        tile_temps = tile_temps + shifted(across[d - 1] + got[d], "gy", 2 * d, True)
    return from_rows(pot), temp, from_rows(tile_temps)


def solution(mesh):
    placed = (
        P(("gx", "gy"), None),
        P(("gx", "gy"), None),
        P(("gx", "gy"), None),
        P(),
        P(("gx", "gy"), None),
        P(),
        P("gx", "gy"),
        P("gx", "gy"),
        P(),
        P(),
    )
    return jax.shard_map(
        on_device,
        mesh=mesh,
        in_specs=placed,
        out_specs=(P(("gx", "gy"), None), P("gx", "gy"), P(("gx", "gy"), None)),
        check_vma=False,
    )
```

```python
import functools
import math

import jax
import jax.numpy as jnp
from jax import lax
from jax.experimental import pallas as pl
from jax.experimental.pallas import tpu as pltpu
from jax.sharding import PartitionSpec as P

TE = 32
SWEEPS = 4
CSWEEPS = 3
NZ = 64
EPS = 2.0
DT = 0.15
LANES = 128
SUB = 8
TILES = 2
ROW = SUB * TILES

LOW = (SWEEPS + 2, SWEEPS + 1, 2)
HIGH = (SWEEPS + 3, SWEEPS + 2, 2)
LOW_ROWS = sum(LOW) * ROW
HIGH_ROWS = sum(HIGH) * ROW
SIDE_ROWS = max(LOW_ROWS, HIGH_ROWS)
SLABX = TE + SUB
HALO = CSWEEPS
HALF = TE
YBLOCKS = HALF + 2 * HALO
CELLS = 9
ROW0 = ROW
SLAB_ROWS = ROW0 + YBLOCKS * SLABX + ROW0


def cheb_weight(step, count):
    return 1.0 / (1.0 + 0.75 * math.cos(math.pi * (2 * step + 1) / (2 * count)))


def lookup(table, ids):
    out = jnp.full(ids.shape, table[3], jnp.float32)
    for which in (2, 1, 0):
        out = jnp.where(ids == which, table[which], out)
    return out


def roll(value, by, axis):
    return pltpu.roll(value, by % value.shape[axis], axis)


def prep_kernel(table, pos, phi, src, mat, temp, slab, ready, sigma, inner, outer, phi_v, src_v, mat_v, ends_t, ends_m, sems):
    rows = TE * ROW
    size_x, width = temp.shape
    moves = [(phi, phi_v), (src, src_v), (mat, mat_v)]
    for which, first in enumerate((0, size_x - SUB)):
        moves.append((temp.at[first : first + SUB], ends_t.at[which]))
        moves.append((slab.at[first : first + SUB], ends_m.at[which]))
    moves = [pltpu.make_async_copy(*move, sems.at[at]) for at, move in enumerate(moves)]
    for move in moves:
        move.start()
    for move in moves:
        move.wait()
    first = (lax.axis_index("gx") * lax.axis_size("gy") + lax.axis_index("gy")) * TILES
    upper = [pos[2, first + t] == 1 for t in range(TILES)]

    def plane(p, carry):
        values = []
        for t in range(TILES):
            row = pl.multiple_of(p * ROW, ROW) + t
            at = pl.ds(row, SUB, stride=TILES)
            conduct = lookup(table, mat_v[at, :])
            three = (phi_v[at, :], src_v[at, :] / conduct, conduct)
            values.append((row, [jnp.where(upper[t], roll(v, TE, 1), v) for v in three]))
        for row, (potential, s, conduct) in values:
            ready[pl.ds(row, SUB, stride=TILES), :] = potential
            ready[pl.ds(row + rows, SUB, stride=TILES), :] = s
            sigma[pl.ds(row, SUB, stride=TILES), :] = conduct
        return carry

    lax.fori_loop(0, TE, plane, 0, unroll=8)
    even = lax.rem(lax.axis_index("gx"), 2) == 0

    @pl.when(even)
    def _():
        fill_sides(ready, sigma, ends_t, ends_m, inner, outer)

    @pl.when(jnp.logical_not(even))
    def _():
        fill_sides(ready, sigma, ends_t, ends_m, outer, inner)


def fill_sides(body, sigma, ends_t, ends_m, up, down):
    rows = TE * ROW
    width = ends_t.shape[2]
    at_up, at_down = 0, 0
    for ref, first in ((body, 0), (body, rows), (sigma, 0)):
        which = (first // rows) if ref is body else 2
        size = LOW[which] * ROW
        up[at_up : at_up + size] = ref[first + rows - size : first + rows]
        at_up += size
        size = HIGH[which] * ROW
        down[at_down : at_down + size] = ref[first : first + size]
        at_down += size
    sub = lax.broadcasted_iota(jnp.int32, (SUB, LANES), 0)
    for at in range(width // LANES):
        lanes = slice(at * LANES, (at + 1) * LANES)
        t_low, m_low = ends_t[0, :, lanes], ends_m[0, :, lanes].astype(jnp.float32)
        t_high, m_high = ends_t[1, :, lanes], ends_m[1, :, lanes].astype(jnp.float32)
        first = at * SUB
        up[SIDE_ROWS + first : SIDE_ROWS + first + SUB] = jnp.where(sub < 4, roll(t_high, HALO, 0), roll(m_high, -1, 0))
        down[SIDE_ROWS + first : SIDE_ROWS + first + SUB] = jnp.where(sub < 4, t_low, roll(m_low, 4, 0))


def relay_kernel(inner, outer, halo):
    def join(low, high):
        halo[0:LOW_ROWS] = low[0:LOW_ROWS]
        halo[LOW_ROWS:] = high[0:HIGH_ROWS]

    even = lax.rem(lax.axis_index("gx"), 2) == 0
    pl.when(even)(lambda: join(outer, inner))
    pl.when(jnp.logical_not(even))(lambda: join(inner, outer))


def loose(pos):
    return jnp.minimum(pos[0, 0], 0)


def slab_kernel(pos, k0_table, beta_table, temp, mat, inner, outer, sigma, t_ext, k0_ext, b_ext, packet_in, packet, native_t, native_m, edge_low, edge_high):
    start = loose(pos)
    even = lax.rem(lax.axis_index("gx"), 2) == 0
    blocks = temp.shape[1] // LANES
    half = lax.broadcasted_iota(jnp.int32, (SUB, LANES), 1) < NZ
    for which, (own, native) in enumerate(((temp, native_t), (mat, native_m))):
        for at in range(blocks):
            lanes = slice(at * LANES, (at + 1) * LANES)
            first = at * SLABX
            side = slice(SIDE_ROWS + at * SUB, SIDE_ROWS + (at + 1) * SUB)
            value = jnp.where(even, outer[side, :], inner[side, :])
            native[first : first + SUB, :] = roll(value, -4, 0) if which else value
            for g in range(TE // SUB):
                value = own[g * SUB : (g + 1) * SUB, lanes].astype(jnp.float32)
                native[pl.ds(start + first + HALO + g * SUB, SUB), :] = value
            value = jnp.where(even, inner[side, :], outer[side, :])
            native[pl.ds(start + first + HALO + TE, SUB), :] = roll(value, -4, 0) if which else value
    for at in range(blocks // 2):
        for g in range(SLABX // SUB):
            halves = []
            for native in (native_t, native_m):
                lower = native[at * SLABX + g * SUB : at * SLABX + (g + 1) * SUB, :]
                upper_at = (blocks // 2 + at) * SLABX + g * SUB
                upper = native[upper_at : upper_at + SUB, :]
                lower_r, upper_r = roll(lower, NZ, 1), roll(upper, NZ, 1)
                halves.append((lower, lower_r, upper, upper_r))
            for odd in range(2):
                y = 2 * at + odd
                temps, mats = (jnp.where(half, v[odd], v[3 - odd]) for v in halves)
                places = [(y + HALO, temps, mats)]
                if y >= HALF - HALO:
                    places.append((y - HALF + HALO, halves[0][1 - odd], halves[1][1 - odd]))
                if y < HALO:
                    places.append((y + HALF + HALO, halves[0][2 + odd], halves[1][2 + odd]))
                for block, t, m in places:
                    rows = slice(ROW0 + block * SLABX + g * SUB, ROW0 + block * SLABX + (g + 1) * SUB)
                    t_ext[rows] = t
                    k0_ext[rows] = lookup(k0_table, m)
                    b_ext[rows] = lookup(beta_table, m)
                if y < HALO:
                    rows = slice(y * SLABX + g * SUB, y * SLABX + (g + 1) * SUB)
                    edge_low[rows] = jnp.where(half, halves[0][odd], halves[1][1 - odd])
                if y >= HALF - HALO:
                    first = (y - HALF + HALO) * SLABX + g * SUB
                    edge_high[first : first + SUB] = jnp.where(half, halves[0][2 + odd], halves[1][3 - odd])
    even = lax.rem(lax.axis_index("gy"), 2) == 0
    packet_in[0 : TE * ROW] = sigma[...]
    packet_in[TE * ROW :] = jnp.where(even, edge_high[...], edge_low[...])
    packet[0 : TE * ROW] = sigma[...]
    packet[TE * ROW :] = jnp.where(even, edge_low[...], edge_high[...])


def fill_maps(chips, pos, cell_at, cell_of):
    width_gy = 2 * chips
    tiles = width_gy * TILES
    i = lax.axis_index("gx")
    j = lax.axis_index("gy")
    rows_gx = lax.axis_size("gx")
    for at in range(2 * (2 * width_gy + 2)):
        for which in range(3):
            cell_at[which, at] = tiles
    for which, by in enumerate((0, -1, 1)):
        row = i + by
        valid = (row >= 0) & (row < rows_gx)
        first = jnp.clip(row, 0, rows_gx - 1) * tiles
        for part in range(width_gy):
            dev = part_device(part, chips, j)
            for t in range(TILES):
                tile = first + dev * TILES + t
                cell = (pos[1, tile] + 1) * 2 + pos[2, tile]
                slot = part * TILES + t
                cell_of[which, slot] = cell
                cell_at[which, cell] = jnp.where(valid, slot, tiles)


def part_device(part, chips, j):
    mate = j + 1 - 2 * lax.rem(j, 2)
    base = j if part < chips else mate
    return lax.rem(base - 2 * (part % chips) + 2 * chips, 2 * chips)


def sweep_kernel(chips, pos, *refs):
    width_gy = 2 * chips
    tiles = width_gy * TILES
    none = tiles
    bodies, halos = refs[:width_gy], refs[width_gy : 2 * width_gy]
    pot, slope, cell_at, cell_of, table, pa, pb, la, lb, ua, ub, s_c, s_l, s_u, sems = refs[2 * width_gy :]
    i = lax.axis_index("gx")
    j = lax.axis_index("gy")
    rows_gx = lax.axis_size("gx")
    zero = jnp.zeros((SUB, LANES), jnp.float32)

    moves = []
    for part in range(width_gy):
        at = 0
        pieces = [(bodies[part], 0, pa, part * TE, TE), (bodies[part], TE * ROW, s_c, part * TE, TE)]
        for target, first, count in (
            (la, part * LOW[0], LOW[0]),
            (s_l, part * LOW[1], LOW[1]),
            (None, 0, LOW[2]),
            (ua, part * HIGH[0], HIGH[0]),
            (s_u, part * HIGH[1], HIGH[1]),
        ):
            if target is not None:
                pieces.append((halos[part], at, target, first, count))
            at += count * ROW
        for source, start, target, first, count in pieces:
            move = pltpu.make_async_copy(
                source.at[start : start + count * ROW],
                target.at[ROW0 + first * ROW : ROW0 + (first + count) * ROW],
                sems.at[len(moves)],
            )
            move.start()
            moves.append(move)

    fill_maps(chips, pos, cell_at, cell_of)

    def row_of(slot, size):
        pair, second = lax.shift_right_logical(slot, 1), lax.bitwise_and(slot, 1)
        return ROW0 + pair * (size * ROW) + second

    def enter(slot, carry):
        for which, size in enumerate((TE, LOW[0], HIGH[0])):
            cell = cell_of[which, slot]
            upper = lax.bitwise_and(cell, 1)
            beside = cell_at[which, cell + 1 - 2 * upper]
            here = [cell_at[at, cell] for at in range(3)]
            near = (slot, cell_at[which, cell - 2], cell_at[which, cell + 2])
            near += (jnp.where(upper == 1, beside, none), jnp.where(upper == 1, none, beside))
            rows = [row_of(at, size) for at in near]
            if which == 0:
                rows += [row_of(here[1], LOW[0]) + (LOW[0] - 1) * ROW, row_of(here[2], HIGH[0])]
            else:
                centre = row_of(here[0], TE)
                rows += [centre + (TE - 1) * ROW, centre]
            rows.append(upper)
            for at, row in enumerate(rows):
                table[(which * tiles + slot) * 8 + at] = row
        return carry

    lax.fori_loop(0, tiles, enter, 0)

    def entry(which, slot):
        return [table[(which * tiles + slot) * 8 + at] for at in range(8)]

    def plane_at(ref, row):
        return ref[pl.ds(row, SUB, stride=TILES), :]

    def put_plane(ref, row, value):
        ref[pl.ds(row, SUB, stride=TILES), :] = value

    for ref, count in ((pa, TE), (pb, TE), (la, LOW[0]), (lb, LOW[0]), (ua, HIGH[0]), (ub, HIGH[0])):
        first = ROW0 + width_gy * count * ROW
        for row in range(first, first + count * ROW, SUB):
            ref[row : row + SUB] = zero

    def clear(at, carry):
        slope[pl.ds(pl.multiple_of(at * SUB, SUB), SUB), :] = zero
        return carry

    lax.fori_loop(0, slope.shape[0] // SUB, clear, 0, unroll=8)
    for move in moves:
        move.wait()

    lane = lax.broadcasted_iota(jnp.int32, (SUB, LANES), 1)
    sub = lax.broadcasted_iota(jnp.int32, (SUB, LANES), 0)
    depth = lane % TE
    first_sub, last_sub = sub == 0, sub == SUB - 1
    first_z, last_z = depth == 0, depth == TE - 1

    def y_plus(ref, own, first_y, row, ghost_row):
        turned = jnp.where(last_sub, plane_at(ref, ghost_row), plane_at(ref, row))
        return roll(jnp.where(first_y, turned, own), -TE, 1)

    def y_minus(ref, own, last_y, row, ghost_row):
        turned = jnp.where(first_sub, plane_at(ref, ghost_row), plane_at(ref, row))
        return roll(jnp.where(last_y, turned, own), TE, 1)

    def z_plus(ref, own, ghost_row):
        return roll(jnp.where(first_z, plane_at(ref, ghost_row), own), -1, 1)

    def z_minus(ref, own, ghost_row):
        return roll(jnp.where(last_z, plane_at(ref, ghost_row), own), 1, 1)

    def y_ends(upper):
        quarter = lane // TE
        return quarter == upper, quarter == lax.bitwise_and(upper + 3, 3)

    bufs = ((pa, la, ua), (pb, lb, ub))
    for k in range(SWEEPS):
        weight = cheb_weight(k, SWEEPS)
        keep, gain = 1.0 - weight, weight / (6.0 + EPS)
        (c_src, l_src, u_src), (c_dst, l_dst, u_dst) = bufs[k % 2], bufs[(k + 1) % 2]

        def relax(src, dst, places, first, count, s_ref, s_row, before, beyond):
            row, row_m, row_p, row_zm, row_zp, _, _, upper = places
            first_y, last_y = y_ends(upper)
            own = plane_at(src, row + first * ROW)
            for p in range(count):
                step = (first + p) * ROW
                after = plane_at(src, row + (step + ROW)) if beyond is None or p < count - 1 else beyond
                total = (before + after) + plane_at(s_ref, s_row + p * ROW)
                along_y = y_minus(src, own, last_y, row + (step - TILES), row_m + (step + ROW - TILES))
                along_y = along_y + y_plus(src, own, first_y, row + (step + TILES), row_p + (step + TILES - ROW))
                along_z = z_minus(src, own, row_zm + step) + z_plus(src, own, row_zp + step)
                put_plane(dst, row + step, keep * own + gain * (total + (along_y + along_z)))
                before, own = own, after

        def sweep_tile(slot, carry):
            at = entry(0, slot)
            relax(c_src, c_dst, at, 0, TE, s_c, at[0], plane_at(l_src, at[5]), plane_at(u_src, at[6]))
            at = entry(1, slot)
            count = LOW[0] - 1 - k
            s_row = row_of(slot, LOW[1]) + (LOW[1] - count) * ROW
            before, beyond = plane_at(l_src, at[0] + k * ROW), plane_at(c_src, at[6])
            relax(l_src, l_dst, at, k + 1, count, s_l, s_row, before, beyond)
            at = entry(2, slot)
            relax(u_src, u_dst, at, 0, HIGH[0] - 1 - k, s_u, row_of(slot, HIGH[1]), plane_at(c_src, at[5]), None)
            return carry

        lax.fori_loop(0, tiles, sweep_tile, 0, unroll=4)

    field, f_l, f_u = bufs[SWEEPS % 2]
    for t in range(TILES):
        turn = jnp.where(table[t * 8 + 7] == 1, LANES - TE, 0)

        def turn_back(p, carry):
            value = plane_at(field, p * ROW + (ROW0 + t))
            put_plane(pot, pl.multiple_of(p * ROW, ROW) + t, pltpu.roll(value, turn, 1))
            return carry

        lax.fori_loop(0, TE, turn_back, 0, unroll=8)

    def squares(ref, places, local, x, first, count, beyond):
        row, _, row_p, _, row_z, _, _, upper = places
        first_y, _ = y_ends(upper)
        target = (local * SLABX + x) * SUB
        own = plane_at(ref, row + first * ROW)
        for p in range(count):
            step = (first + p) * ROW
            after = plane_at(ref, row + (step + ROW)) if beyond is None or p < count - 1 else beyond
            d_x = after - own
            d_y = y_plus(ref, own, first_y, row + (step + TILES), row_p + (step + TILES - ROW)) - own
            d_z = z_plus(ref, own, row_z + step) - own
            rows = pl.ds(pl.multiple_of(target + p * SUB, SUB), SUB)
            slope[rows, :] = d_x * d_x + d_y * d_y + d_z * d_z
            own = after

    def slope_tile(slot, carry):
        at, local = entry(0, slot), window(0, cell_of[0, slot], i, j, rows_gx)
        squares(field, at, local, HALO, 0, TE, plane_at(f_u, at[6]))
        at, local = entry(1, slot), window(1, cell_of[1, slot], i, j, rows_gx)
        squares(f_l, at, local, HALO - 2, LOW[0] - 2, 2, plane_at(field, at[6]))
        at, local = entry(2, slot), window(2, cell_of[2, slot], i, j, rows_gx)
        squares(f_u, at, local, HALO + TE, 0, 2, None)
        return carry

    lax.fori_loop(0, tiles, slope_tile, 0, unroll=2)


def window(which, cell, i, j, rows_gx):
    local = cell - 4 * j
    inside = (local >= 0) & (local < CELLS - 1)
    if which > 0:
        row = i - 1 if which == 1 else i + 1
        inside = inside & (row >= 0) & (row < rows_gx)
    return jnp.where(inside, local, CELLS - 1)


def slab_steps_kernel(chips, pos, k0_table, beta_table, *refs):
    width_gy = 2 * chips
    tiles = width_gy * TILES
    halos = refs[width_gy : 2 * width_gy]
    slope, t_in, k0_in, b_in, temp_out = refs[2 * width_gy : 2 * width_gy + 5]
    mine, bundle = refs[2 * width_gy + 5 : 2 * width_gy + 7]
    across = refs[2 * width_gy + 7 : 2 * width_gy + 6 + chips]
    heat, q_ext, state_a, state_b, k0_all, b_all, blocks, sigmas, y_edges, sems = refs[2 * width_gy + 6 + chips :]
    moves = []
    for part in range(width_gy):
        moves.append(pltpu.make_async_copy(refs[part].at[0 : TE * ROW], sigmas.at[part], sems.at[part]))
        moves[-1].start()
    edges = []
    for which, d in enumerate((1, chips - 1, 0)):
        source = refs[chips + d].at[TE * ROW : TE * ROW + HALO * SLABX]
        edges.append(pltpu.make_async_copy(source, y_edges.at[which], sems.at[width_gy + which]))
        edges[-1].start()
    i = lax.axis_index("gx")
    j = lax.axis_index("gy")
    rows_gx = lax.axis_size("gx")
    lane = lax.broadcasted_iota(jnp.int32, (SUB, LANES), 1)
    zero = jnp.zeros((SUB, LANES), jnp.float32)

    quarter = [(lane >= q * TE) & (lane < (q + 1) * TE) for q in range(3)]

    def pick(parts):
        return jnp.where(
            quarter[0], parts[0], jnp.where(quarter[1], parts[1], jnp.where(quarter[2], parts[2], parts[3]))
        )

    def turned(value, by):
        return value if by % 4 == 0 else roll(value, by * TE, 1)

    def rows_of(block, g):
        first = ROW0 + block * SLABX + g * SUB
        if not isinstance(first, int):
            first = pl.multiple_of(first, SUB)
        return pl.ds(first, SUB)

    groups = SLABX // SUB

    sub = lax.broadcasted_iota(jnp.int32, (SUB, LANES), 0)
    half = lane < NZ
    no_z = lane % NZ == NZ - 1
    low_x = (sub == HALO - 1) & (i == 0), (sub == HALO) & (i == 0)
    high_x = (sub == (HALO + TE - 1) % SUB) & (i == rows_gx - 1)
    low_y, high_y = half & (j == 0), (lane >= NZ) & (j == width_gy - 1)

    def inverse(value):
        near = pl.reciprocal(value, approx=True)
        near = near * (2.0 - value * near)
        return near * (2.0 - value * near)

    def both_of(block, g, by=0):
        first = 2 * (ROW0 + block * SLABX + g * SUB + by)
        return pl.ds(first, SUB, stride=2), pl.ds(first + 1, SUB, stride=2)

    def load(ref, block, by=0):
        places = [both_of(block, g, by) for g in range(groups)]
        return [ref[at, :] for at, _ in places], [ref[at, :] for _, at in places]

    def store(ref, block, g, temp, cond=None):
        first, second = both_of(block, g)
        ref[first, :] = temp
        if cond is not None:
            ref[second, :] = cond

    even = lax.rem(j, 2) == 0

    def begin(block, low, at):
        values = []
        for g in range(groups):
            rows = rows_of(block, g)
            temp, k0, beta = t_in[rows], k0_in[rows], b_in[rows]
            if low is not None:
                place = slice(at * SLABX + g * SUB, at * SLABX + (g + 1) * SUB)
                other = jnp.where(even, y_edges[0, place], y_edges[1, place])
                value = jnp.where(even, *((other, y_edges[2, place])[:: 1 if low else -1]))
                swapped = roll(value, NZ, 1)
                if low:
                    temp = jnp.where(half, value, temp)
                    k0 = jnp.where(half, lookup(k0_table, swapped), k0)
                    beta = jnp.where(half, lookup(beta_table, swapped), beta)
                else:
                    temp = jnp.where(half, temp, swapped)
                    k0 = jnp.where(half, k0, lookup(k0_table, value))
                    beta = jnp.where(half, beta, lookup(beta_table, value))
            values.append((rows, temp, k0, beta, k0 * inverse(1.0 + beta * temp * temp)))
        for g, (rows, temp, k0, beta, cond) in enumerate(values):
            k0_all[rows], b_all[rows] = k0, beta
            store(state_a, block, g, temp, cond)

    def begin_inner(block, carry):
        begin(block, None, 0)
        return carry

    lax.fori_loop(HALO, YBLOCKS - HALO, begin_inner, 0, unroll=4)
    for move in edges:
        move.wait()
    for e in range(HALO):
        begin(e, True, e)
        begin(YBLOCKS - HALO + e, False, e)

    def clear(at, carry):
        heat[pl.ds(pl.multiple_of(at * SUB, SUB), SUB), :] = zero
        return carry

    lax.fori_loop(0, heat.shape[0] // SUB, clear, 0, unroll=8)
    for move in moves:
        move.wait()
    low_at, high_at = (LOW[0] + LOW[1]) * ROW, LOW_ROWS + (HIGH[0] + HIGH[1]) * ROW
    for part in range(width_gy):
        dev = part_device(part, chips, j)
        for t in range(TILES):
            for which, by in enumerate((0, -1, 1)):
                tile = jnp.clip(i + by, 0, rows_gx - 1) * tiles + dev * TILES + t
                cell = (pos[1, tile] + 1) * 2 + pos[2, tile]
                local = window(which, cell, i, j, rows_gx)
                source, start, x, count = (
                    (sigmas.at[part], 0, HALO, TE),
                    (halos[part], low_at, HALO - 2, 2),
                    (halos[part], high_at, HALO + TE, 2),
                )[which]
                first = pl.multiple_of((local * SLABX + x) * SUB, SUB)
                for p in range(count):
                    rows = pl.ds(pl.multiple_of(first + p * SUB, SUB), SUB)
                    sigma = source[pl.ds(start + p * ROW + t, SUB, stride=TILES), :]
                    heat[rows, :] = sigma * slope[rows, :]

    def place_heat(at, carry):
        first = at - 1
        col, yq = lax.div(first * 4 + TE, TE), lax.rem(first * 4 + TE, TE) // 4
        for g in range(groups):
            cells = [
                heat[pl.ds(pl.multiple_of(((2 * col + c) * SLABX + g * SUB) * SUB, SUB) + yq, SUB, stride=SUB), :]
                for c in range(4)
            ]
            for r in range(4):
                block = 4 * first + r + HALO + 1
                q_ext[rows_of(block, g)] = pick([turned(cells[c], c - r - c % 2) for c in range(4)])
        return carry

    lax.fori_loop(0, HALF // 4 + 2, place_heat, 0, unroll=2)

    for step in range(CSWEEPS):
        src, dst = (state_a, state_b)[:: 1 if step % 2 == 0 else -1]

        def y_fluxes(block, now, ahead):
            closed = (low_y & (block == HALO - 1)) | (high_y & (block == HALO + HALF - 1))
            return [flux(now, ahead, g, closed) for g in range(groups)]

        def flux(now, other, g, closed=None):
            value = (now[1][g] + other[1][g]) * (other[0][g] - now[0][g])
            return value if closed is None else jnp.where(closed, 0.0, value)

        def advance(block, carry):
            now, before = carry
            ahead = load(src, block + 1)
            flux_y = y_fluxes(block, now, ahead)
            x_p, x_m = load(src, block, 1), load(src, block, -1)
            results = []
            for g in range(groups):
                temp, cond = now[0][g], now[1][g]
                up = flux(now, x_p, g, {0: low_x[0], groups - 1: high_x}.get(g))
                down = flux(now, x_m, g, {0: low_x[1]}.get(g))
                flux_z = (cond + roll(cond, -1, 1)) * (roll(temp, -1, 1) - temp)
                flux_z = jnp.where(no_z, 0.0, flux_z)
                div = (flux_y[g] - before[g]) + (up + down) + (flux_z - roll(flux_z, 1, 1))
                new = temp + DT * (0.5 * div + q_ext[rows_of(block + 1, g)])
                if step < CSWEEPS - 1:
                    rows = rows_of(block, g)
                    results.append((new, k0_all[rows] * inverse(1.0 + b_all[rows] * new * new)))
                else:
                    results.append((new,))
            for g in range(groups):
                store(dst, block, g, *results[g])
            return ahead, flux_y

        first, second = load(src, 0), load(src, 1)
        lax.fori_loop(1, YBLOCKS - 1, advance, (second, y_fluxes(0, first, second)), unroll=9)
    final = state_b if CSWEEPS % 2 else state_a

    def give_out(yq, carry):
        for g in range(TE // SUB):
            x = slice(g * SUB, (g + 1) * SUB)
            turns = []
            for r in range(4):
                value = final[both_of(HALO + 4 * yq + r, g, HALO)[0], :]
                turns.append([turned(value, by) for by in range(4)])
            for pair in range(2):
                even, odd = turns[2 * pair], turns[2 * pair + 1]
                lower = (2 * yq + pair) * LANES
                upper = lower + temp_out.shape[1] // 2
                temp_out[x, pl.ds(pl.multiple_of(lower, LANES), LANES)] = jnp.where(half, even[0], odd[2])
                temp_out[x, pl.ds(pl.multiple_of(upper, LANES), LANES)] = jnp.where(half, even[2], odd[0])
            for c in range(4):
                value = pick([turns[r][(r - c) % 4] for r in range(4)])
                blocks[pl.ds((c * TE + g * SUB) * SUB + yq, SUB, stride=SUB), :] = value
        return carry

    lax.fori_loop(0, HALF // 4, give_out, 0, unroll=2)
    places = []
    mate = j + 1 - 2 * lax.rem(j, 2)
    targets = [(mine, 0, j)] + [(across[d - 1], 0, j + 2 * d) for d in range(1, chips)]
    targets += [(bundle, d * TE * ROW, mate + 2 * d) for d in range(chips)]
    for target, first, to in targets:
        dev = lax.rem(to, width_gy)
        for t in range(TILES):
            tile = i * tiles + dev * TILES + t
            col = pos[1, tile] - 2 * j
            cell = jnp.clip(col, 0, 1) * 2 + pos[2, tile]
            places.append((target, first + t, cell, (col >= 0) & (col < 2)))

    def pack(p, carry):
        values = []
        for _, _, cell, here in places:
            value = blocks[pl.ds(pl.multiple_of((cell * TE + p) * SUB, SUB), SUB), :]
            values.append(jnp.where(here, value, 0.0))
        for (target, first, _, _), value in zip(places, values):
            target[pl.ds(pl.multiple_of(p * ROW, ROW) + first, SUB, stride=TILES), :] = value
        return carry

    lax.fori_loop(0, TE, pack, 0, unroll=4)


def shifted(value, axis, by, wrap=False):
    count = lax.axis_size(axis)
    pairs = [(d, (d + by) % count) for d in range(count) if wrap or 0 <= d + by < count]
    return lax.ppermute(value, axis, pairs)


def with_partner(value, axis, first):
    count = lax.axis_size(axis)
    pairs = [(d, d + 1) for d in range(first, count - 1, 2)]
    return lax.ppermute(value, axis, pairs + [(high, low) for low, high in pairs])


def from_mate(value):
    return lax.ppermute(value, "gy", [(d, d ^ 1) for d in range(lax.axis_size("gy"))])


def to_rows(value):
    return value.reshape(TILES, -1, LANES).transpose(1, 0, 2).reshape(-1, LANES)


def from_rows(value):
    return value.reshape(-1, TILES, LANES).transpose(1, 0, 2).reshape(TILES, -1)


def to_other_core(value, by):
    count = lax.axis_size("gy")
    return lax.ppermute(value, "gy", [(at, ((at ^ 1) + 2 * by) % count) for at in range(count)])


VMEM = pl.BlockSpec(memory_space=pltpu.VMEM)
SMEM = pl.BlockSpec(memory_space=pltpu.SMEM)
HBM = pl.BlockSpec(memory_space=pltpu.HBM)
ANY = pl.BlockSpec(memory_space=pl.ANY)
PARAMS = pltpu.CompilerParams(vmem_limit_bytes=32 * 1024 * 1024)


def on_device(
    phi_init,
    source,
    tile_mat,
    tile_pos,
    neighbours,
    sigma_table,
    temp_init,
    slab_mat,
    k0_table,
    beta_table,
):
    f32 = jnp.float32
    pos = tile_pos.T
    width_gy = lax.axis_size("gy")
    chips = width_gy // 2
    tiles = width_gy * TILES
    size_x, width = temp_init.shape
    edge_rows = width // LANES * SUB

    def rows(count):
        return jax.ShapeDtypeStruct((count, LANES), f32)

    ready, sigma, inner, outer = pl.pallas_call(
        prep_kernel,
        out_shape=(
            rows(2 * TE * ROW),
            rows(TE * ROW),
            rows(SIDE_ROWS + edge_rows),
            rows(SIDE_ROWS + edge_rows),
        ),
        in_specs=[SMEM] * 2 + [HBM] * 5,
        out_specs=(VMEM,) * 4,
        scratch_shapes=[
            pltpu.VMEM((TE * ROW, LANES), f32),
            pltpu.VMEM((TE * ROW, LANES), f32),
            pltpu.VMEM((TE * ROW, LANES), jnp.int32),
            pltpu.VMEM((2, SUB, width), f32),
            pltpu.VMEM((2, SUB, width), jnp.int32),
            pltpu.SemaphoreType.DMA((7,)),
        ],
        compiler_params=pltpu.CompilerParams(vmem_limit_bytes=62 * 1024 * 1024),
        name="prep",
    )(sigma_table, pos, to_rows(phi_init), to_rows(source), to_rows(tile_mat), temp_init, slab_mat)
    bodies = [ready] + [shifted(ready, "gy", 2 * d, True) for d in range(1, chips)]
    bodies += [from_mate(part) for part in bodies]
    inner, outer = with_partner(inner, "gx", 0), with_partner(outer, "gx", 1)

    halo = pl.pallas_call(
        relay_kernel,
        out_shape=rows(LOW_ROWS + HIGH_ROWS),
        in_specs=[VMEM] * 2,
        out_specs=VMEM,
        compiler_params=PARAMS,
        name="relay",
    )(inner, outer)
    halos = [halo] + [shifted(halo, "gy", 2 * d, True) for d in range(1, chips)]
    native = pltpu.VMEM((width // LANES * SLABX + SUB, LANES), f32)
    t_ext, k0_ext, b_ext, packet_in, packet = pl.pallas_call(
        slab_kernel,
        out_shape=(rows(SLAB_ROWS),) * 3 + (rows(TE * ROW + HALO * SLABX),) * 2,
        in_specs=[SMEM] * 3 + [VMEM] * 5,
        out_specs=(VMEM,) * 5,
        scratch_shapes=[native, native] + [pltpu.VMEM((HALO * SLABX, LANES), f32)] * 2,
        compiler_params=PARAMS,
        name="slab_prep",
    )(pos, k0_table, beta_table, temp_init, slab_mat, inner, outer, sigma)
    y_in = from_mate(packet_in)
    *halos[1:], y_in = lax.optimization_barrier((*halos[1:], y_in))
    sigmas = [sigma] + [shifted(sigma, "gy", 2 * d, True) for d in range(1, chips)]
    sigmas += [y_in] + [
        to_other_core(packet if d in (1, chips - 1) else sigma, d) for d in range(1, chips)
    ]
    halos = halos + [from_mate(part) for part in halos]

    def fields(count):
        return pltpu.VMEM((2 * ROW0 + (width_gy + 1) * count * ROW, LANES), f32)

    pot, slope = pl.pallas_call(
        functools.partial(sweep_kernel, chips),
        out_shape=(rows(TE * ROW), rows(CELLS * SLABX * SUB)),
        in_specs=[SMEM] + [ANY] * (2 * width_gy),
        out_specs=(VMEM, VMEM),
        scratch_shapes=[
            pltpu.SMEM((3, 2 * (2 * width_gy + 2)), jnp.int32),
            pltpu.SMEM((3, tiles), jnp.int32),
            pltpu.SMEM((3 * tiles * 8,), jnp.int32),
            fields(TE), fields(TE), fields(LOW[0]), fields(LOW[0]), fields(HIGH[0]), fields(HIGH[0]),
            fields(TE), fields(LOW[1]), fields(HIGH[1]),
            pltpu.SemaphoreType.DMA((6 * width_gy,)),
        ],
        compiler_params=PARAMS,
        name="sweeps",
    )(pos, *bodies, *halos)

    temp, mine, bundle, *across = pl.pallas_call(
        functools.partial(slab_steps_kernel, chips),
        out_shape=(jax.ShapeDtypeStruct((size_x, width), f32), rows(TE * ROW), rows(chips * TE * ROW))
        + (rows(TE * ROW),) * (chips - 1),
        in_specs=[SMEM] * 3 + [ANY] * width_gy + [VMEM] * (width_gy + 4),
        out_specs=(VMEM,) * (2 + chips),
        scratch_shapes=[pltpu.VMEM((CELLS * SLABX * SUB, LANES), f32)]
        + [pltpu.VMEM((SLAB_ROWS + 3 * SLABX, LANES), f32)]
        + [pltpu.VMEM((2 * SLAB_ROWS, LANES), f32)] * 2
        + [pltpu.VMEM((SLAB_ROWS, LANES), f32)] * 2
        + [pltpu.VMEM((4 * TE * SUB, LANES), f32), pltpu.VMEM((width_gy, TE * ROW, LANES), f32)]
        + [pltpu.VMEM((3, HALO * SLABX, LANES), f32), pltpu.SemaphoreType.DMA((width_gy + 3,))],
        compiler_params=PARAMS,
        name="slab_steps",
    )(pos, k0_table, beta_table, *sigmas, *halos, slope, t_ext, k0_ext, b_ext)
    got = from_mate(bundle).reshape(chips, TE * ROW, LANES)
    tile_temps = mine + got[0]
    for d in range(1, chips):
        tile_temps = tile_temps + shifted(across[d - 1] + got[d], "gy", 2 * d, True)
    return from_rows(pot), temp, from_rows(tile_temps)


def solution(mesh):
    placed = (
        P(("gx", "gy"), None),
        P(("gx", "gy"), None),
        P(("gx", "gy"), None),
        P(),
        P(("gx", "gy"), None),
        P(),
        P("gx", "gy"),
        P("gx", "gy"),
        P(),
        P(),
    )
    return jax.shard_map(
        on_device,
        mesh=mesh,
        in_specs=placed,
        out_specs=(P(("gx", "gy"), None), P("gx", "gy"), P(("gx", "gy"), None)),
        check_vma=False,
    )
```

```python
import functools
import math

import jax
import jax.numpy as jnp
from jax import lax
from jax.experimental import pallas as pl
from jax.experimental.pallas import tpu as pltpu
from jax.sharding import PartitionSpec as P

TE = 32
SWEEPS = 4
CSWEEPS = 3
NZ = 64
EPS = 2.0
DT = 0.15
LANES = 128
SUB = 8
TILES = 2
ROW = SUB * TILES

LOW = (SWEEPS + 2, SWEEPS + 1, 2)
HIGH = (SWEEPS + 3, SWEEPS + 2, 2)
LOW_ROWS = sum(LOW) * ROW
HIGH_ROWS = sum(HIGH) * ROW
SIDE_ROWS = max(LOW_ROWS, HIGH_ROWS)
SLABX = TE + SUB
HALO = CSWEEPS
HALF = TE
YBLOCKS = HALF + 2 * HALO
CELLS = 9
ROW0 = ROW
SLAB_ROWS = ROW0 + YBLOCKS * SLABX + ROW0


def cheb_weight(step, count):
    return 1.0 / (1.0 + 0.75 * math.cos(math.pi * (2 * step + 1) / (2 * count)))


def lookup(table, ids):
    out = jnp.full(ids.shape, table[3], jnp.float32)
    for which in (2, 1, 0):
        out = jnp.where(ids == which, table[which], out)
    return out


def roll(value, by, axis):
    return pltpu.roll(value, by % value.shape[axis], axis)


def prep_kernel(table, pos, phi, src, mat, temp, slab, ready, sigma, inner, outer, phi_v, src_v, mat_v, ends_t, ends_m, sems):
    rows = TE * ROW
    size_x, width = temp.shape
    moves = [(phi, phi_v), (src, src_v), (mat, mat_v)]
    for which, first in enumerate((0, size_x - SUB)):
        moves.append((temp.at[first : first + SUB], ends_t.at[which]))
        moves.append((slab.at[first : first + SUB], ends_m.at[which]))
    moves = [pltpu.make_async_copy(*move, sems.at[at]) for at, move in enumerate(moves)]
    for move in moves:
        move.start()
    for move in moves:
        move.wait()
    first = (lax.axis_index("gx") * lax.axis_size("gy") + lax.axis_index("gy")) * TILES
    upper = [pos[2, first + t] == 1 for t in range(TILES)]

    def plane(p, carry):
        values = []
        for t in range(TILES):
            row = pl.multiple_of(p * ROW, ROW) + t
            at = pl.ds(row, SUB, stride=TILES)
            conduct = lookup(table, mat_v[at, :])
            three = (phi_v[at, :], src_v[at, :] / conduct, conduct)
            values.append((row, [jnp.where(upper[t], roll(v, TE, 1), v) for v in three]))
        for row, (potential, s, conduct) in values:
            ready[pl.ds(row, SUB, stride=TILES), :] = potential
            ready[pl.ds(row + rows, SUB, stride=TILES), :] = s
            sigma[pl.ds(row, SUB, stride=TILES), :] = conduct
        return carry

    lax.fori_loop(0, TE, plane, 0, unroll=8)
    even = lax.rem(lax.axis_index("gx"), 2) == 0

    @pl.when(even)
    def _():
        fill_sides(ready, sigma, ends_t, ends_m, inner, outer)

    @pl.when(jnp.logical_not(even))
    def _():
        fill_sides(ready, sigma, ends_t, ends_m, outer, inner)


def fill_sides(body, sigma, ends_t, ends_m, up, down):
    rows = TE * ROW
    width = ends_t.shape[2]
    at_up, at_down = 0, 0
    for ref, first in ((body, 0), (body, rows), (sigma, 0)):
        which = (first // rows) if ref is body else 2
        size = LOW[which] * ROW
        up[at_up : at_up + size] = ref[first + rows - size : first + rows]
        at_up += size
        size = HIGH[which] * ROW
        down[at_down : at_down + size] = ref[first : first + size]
        at_down += size
    sub = lax.broadcasted_iota(jnp.int32, (SUB, LANES), 0)
    for at in range(width // LANES):
        lanes = slice(at * LANES, (at + 1) * LANES)
        t_low, m_low = ends_t[0, :, lanes], ends_m[0, :, lanes].astype(jnp.float32)
        t_high, m_high = ends_t[1, :, lanes], ends_m[1, :, lanes].astype(jnp.float32)
        first = at * SUB
        up[SIDE_ROWS + first : SIDE_ROWS + first + SUB] = jnp.where(sub < 4, roll(t_high, HALO, 0), roll(m_high, -1, 0))
        down[SIDE_ROWS + first : SIDE_ROWS + first + SUB] = jnp.where(sub < 4, t_low, roll(m_low, 4, 0))


def relay_kernel(inner, outer, halo):
    def join(low, high):
        halo[0:LOW_ROWS] = low[0:LOW_ROWS]
        halo[LOW_ROWS:] = high[0:HIGH_ROWS]

    even = lax.rem(lax.axis_index("gx"), 2) == 0
    pl.when(even)(lambda: join(outer, inner))
    pl.when(jnp.logical_not(even))(lambda: join(inner, outer))


def loose(pos):
    return jnp.minimum(pos[0, 0], 0)


def slab_kernel(pos, k0_table, beta_table, temp, mat, inner, outer, sigma, t_ext, k0_ext, b_ext, edge_in, packet, native_t, native_m, edge_low, edge_high):
    start = loose(pos)
    even = lax.rem(lax.axis_index("gx"), 2) == 0
    blocks = temp.shape[1] // LANES
    half = lax.broadcasted_iota(jnp.int32, (SUB, LANES), 1) < NZ
    for which, (own, native) in enumerate(((temp, native_t), (mat, native_m))):
        for at in range(blocks):
            lanes = slice(at * LANES, (at + 1) * LANES)
            first = at * SLABX
            side = slice(SIDE_ROWS + at * SUB, SIDE_ROWS + (at + 1) * SUB)
            value = jnp.where(even, outer[side, :], inner[side, :])
            native[first : first + SUB, :] = roll(value, -4, 0) if which else value
            for g in range(TE // SUB):
                value = own[g * SUB : (g + 1) * SUB, lanes].astype(jnp.float32)
                native[pl.ds(start + first + HALO + g * SUB, SUB), :] = value
            value = jnp.where(even, inner[side, :], outer[side, :])
            native[pl.ds(start + first + HALO + TE, SUB), :] = roll(value, -4, 0) if which else value
    for at in range(blocks // 2):
        for g in range(SLABX // SUB):
            halves = []
            for native in (native_t, native_m):
                lower = native[at * SLABX + g * SUB : at * SLABX + (g + 1) * SUB, :]
                upper_at = (blocks // 2 + at) * SLABX + g * SUB
                upper = native[upper_at : upper_at + SUB, :]
                lower_r, upper_r = roll(lower, NZ, 1), roll(upper, NZ, 1)
                halves.append((lower, lower_r, upper, upper_r))
            for odd in range(2):
                y = 2 * at + odd
                temps, mats = (jnp.where(half, v[odd], v[3 - odd]) for v in halves)
                places = [(y + HALO, temps, mats)]
                if y >= HALF - HALO:
                    places.append((y - HALF + HALO, halves[0][1 - odd], halves[1][1 - odd]))
                if y < HALO:
                    places.append((y + HALF + HALO, halves[0][2 + odd], halves[1][2 + odd]))
                for block, t, m in places:
                    rows = slice(ROW0 + block * SLABX + g * SUB, ROW0 + block * SLABX + (g + 1) * SUB)
                    t_ext[rows] = t
                    k0_ext[rows] = lookup(k0_table, m)
                    b_ext[rows] = lookup(beta_table, m)
                if y < HALO:
                    rows = slice(y * SLABX + g * SUB, y * SLABX + (g + 1) * SUB)
                    edge_low[rows] = jnp.where(half, halves[0][odd], halves[1][1 - odd])
                if y >= HALF - HALO:
                    first = (y - HALF + HALO) * SLABX + g * SUB
                    edge_high[first : first + SUB] = jnp.where(half, halves[0][2 + odd], halves[1][3 - odd])
    even = lax.rem(lax.axis_index("gy"), 2) == 0
    edge_in[...] = jnp.where(even, edge_high[...], edge_low[...])
    packet[0 : TE * ROW] = sigma[...]
    packet[TE * ROW :] = jnp.where(even, edge_low[...], edge_high[...])


def fill_maps(chips, pos, cell_at, cell_of):
    width_gy = 2 * chips
    tiles = width_gy * TILES
    i = lax.axis_index("gx")
    j = lax.axis_index("gy")
    rows_gx = lax.axis_size("gx")
    for at in range(2 * (2 * width_gy + 2)):
        for which in range(3):
            cell_at[which, at] = tiles
    for which, by in enumerate((0, -1, 1)):
        row = i + by
        valid = (row >= 0) & (row < rows_gx)
        first = jnp.clip(row, 0, rows_gx - 1) * tiles
        for part in range(width_gy):
            dev = part_device(part, chips, j)
            for t in range(TILES):
                tile = first + dev * TILES + t
                cell = (pos[1, tile] + 1) * 2 + pos[2, tile]
                slot = part * TILES + t
                cell_of[which, slot] = cell
                cell_at[which, cell] = jnp.where(valid, slot, tiles)


def part_device(part, chips, j):
    mate = j + 1 - 2 * lax.rem(j, 2)
    base = j if part < chips else mate
    return lax.rem(base - 2 * (part % chips) + 2 * chips, 2 * chips)


def sweep_kernel(chips, pos, *refs):
    width_gy = 2 * chips
    tiles = width_gy * TILES
    none = tiles
    bodies, halos = refs[:width_gy], refs[width_gy : 2 * width_gy]
    pot, slope, cell_at, cell_of, table, pa, pb, la, lb, ua, ub, s_c, s_l, s_u, sems = refs[2 * width_gy :]
    i = lax.axis_index("gx")
    j = lax.axis_index("gy")
    rows_gx = lax.axis_size("gx")
    zero = jnp.zeros((SUB, LANES), jnp.float32)

    moves = []
    for part in range(width_gy):
        at = 0
        pieces = [(bodies[part], 0, pa, part * TE, TE), (bodies[part], TE * ROW, s_c, part * TE, TE)]
        for target, first, count in (
            (la, part * LOW[0], LOW[0]),
            (s_l, part * LOW[1], LOW[1]),
            (None, 0, LOW[2]),
            (ua, part * HIGH[0], HIGH[0]),
            (s_u, part * HIGH[1], HIGH[1]),
        ):
            if target is not None:
                pieces.append((halos[part], at, target, first, count))
            at += count * ROW
        for source, start, target, first, count in pieces:
            move = pltpu.make_async_copy(
                source.at[start : start + count * ROW],
                target.at[ROW0 + first * ROW : ROW0 + (first + count) * ROW],
                sems.at[len(moves)],
            )
            move.start()
            moves.append(move)

    fill_maps(chips, pos, cell_at, cell_of)

    def row_of(slot, size):
        pair, second = lax.shift_right_logical(slot, 1), lax.bitwise_and(slot, 1)
        return ROW0 + pair * (size * ROW) + second

    def enter(slot, carry):
        for which, size in enumerate((TE, LOW[0], HIGH[0])):
            cell = cell_of[which, slot]
            upper = lax.bitwise_and(cell, 1)
            beside = cell_at[which, cell + 1 - 2 * upper]
            here = [cell_at[at, cell] for at in range(3)]
            near = (slot, cell_at[which, cell - 2], cell_at[which, cell + 2])
            near += (jnp.where(upper == 1, beside, none), jnp.where(upper == 1, none, beside))
            rows = [row_of(at, size) for at in near]
            if which == 0:
                rows += [row_of(here[1], LOW[0]) + (LOW[0] - 1) * ROW, row_of(here[2], HIGH[0])]
            else:
                centre = row_of(here[0], TE)
                rows += [centre + (TE - 1) * ROW, centre]
            rows.append(upper)
            for at, row in enumerate(rows):
                table[(which * tiles + slot) * 8 + at] = row
        return carry

    lax.fori_loop(0, tiles, enter, 0)

    def entry(which, slot):
        return [table[(which * tiles + slot) * 8 + at] for at in range(8)]

    def plane_at(ref, row):
        return ref[pl.ds(row, SUB, stride=TILES), :]

    def put_plane(ref, row, value):
        ref[pl.ds(row, SUB, stride=TILES), :] = value

    for ref, count in ((pa, TE), (pb, TE), (la, LOW[0]), (lb, LOW[0]), (ua, HIGH[0]), (ub, HIGH[0])):
        first = ROW0 + width_gy * count * ROW
        for row in range(first, first + count * ROW, SUB):
            ref[row : row + SUB] = zero

    def clear(at, carry):
        slope[pl.ds(pl.multiple_of(at * SUB, SUB), SUB), :] = zero
        return carry

    lax.fori_loop(0, slope.shape[0] // SUB, clear, 0, unroll=8)
    for move in moves:
        move.wait()

    lane = lax.broadcasted_iota(jnp.int32, (SUB, LANES), 1)
    sub = lax.broadcasted_iota(jnp.int32, (SUB, LANES), 0)
    depth = lane % TE
    first_sub, last_sub = sub == 0, sub == SUB - 1
    first_z, last_z = depth == 0, depth == TE - 1

    def y_plus(ref, own, first_y, row, ghost_row):
        turned = jnp.where(last_sub, plane_at(ref, ghost_row), plane_at(ref, row))
        return roll(jnp.where(first_y, turned, own), -TE, 1)

    def y_minus(ref, own, last_y, row, ghost_row):
        turned = jnp.where(first_sub, plane_at(ref, ghost_row), plane_at(ref, row))
        return roll(jnp.where(last_y, turned, own), TE, 1)

    def z_plus(ref, own, ghost_row):
        return roll(jnp.where(first_z, plane_at(ref, ghost_row), own), -1, 1)

    def z_minus(ref, own, ghost_row):
        return roll(jnp.where(last_z, plane_at(ref, ghost_row), own), 1, 1)

    def y_ends(upper):
        quarter = lane // TE
        return quarter == upper, quarter == lax.bitwise_and(upper + 3, 3)

    bufs = ((pa, la, ua), (pb, lb, ub))
    for k in range(SWEEPS):
        weight = cheb_weight(k, SWEEPS)
        keep, gain = 1.0 - weight, weight / (6.0 + EPS)
        (c_src, l_src, u_src), (c_dst, l_dst, u_dst) = bufs[k % 2], bufs[(k + 1) % 2]

        def relax(src, dst, places, first, count, s_ref, s_row, before, beyond):
            row, row_m, row_p, row_zm, row_zp, _, _, upper = places
            first_y, last_y = y_ends(upper)
            own = plane_at(src, row + first * ROW)
            for p in range(count):
                step = (first + p) * ROW
                after = plane_at(src, row + (step + ROW)) if beyond is None or p < count - 1 else beyond
                total = (before + after) + plane_at(s_ref, s_row + p * ROW)
                along_y = y_minus(src, own, last_y, row + (step - TILES), row_m + (step + ROW - TILES))
                along_y = along_y + y_plus(src, own, first_y, row + (step + TILES), row_p + (step + TILES - ROW))
                along_z = z_minus(src, own, row_zm + step) + z_plus(src, own, row_zp + step)
                put_plane(dst, row + step, keep * own + gain * (total + (along_y + along_z)))
                before, own = own, after

        def sweep_tile(slot, carry):
            at = entry(0, slot)
            relax(c_src, c_dst, at, 0, TE, s_c, at[0], plane_at(l_src, at[5]), plane_at(u_src, at[6]))
            at = entry(1, slot)
            count = LOW[0] - 1 - k
            s_row = row_of(slot, LOW[1]) + (LOW[1] - count) * ROW
            before, beyond = plane_at(l_src, at[0] + k * ROW), plane_at(c_src, at[6])
            relax(l_src, l_dst, at, k + 1, count, s_l, s_row, before, beyond)
            at = entry(2, slot)
            relax(u_src, u_dst, at, 0, HIGH[0] - 1 - k, s_u, row_of(slot, HIGH[1]), plane_at(c_src, at[5]), None)
            return carry

        lax.fori_loop(0, tiles, sweep_tile, 0, unroll=4)

    field, f_l, f_u = bufs[SWEEPS % 2]
    for t in range(TILES):
        turn = jnp.where(table[t * 8 + 7] == 1, LANES - TE, 0)

        def turn_back(p, carry):
            value = plane_at(field, p * ROW + (ROW0 + t))
            put_plane(pot, pl.multiple_of(p * ROW, ROW) + t, pltpu.roll(value, turn, 1))
            return carry

        lax.fori_loop(0, TE, turn_back, 0, unroll=16)

    def squares(ref, places, local, x, first, count, beyond):
        row, _, row_p, _, row_z, _, _, upper = places
        first_y, _ = y_ends(upper)
        target = (local * SLABX + x) * SUB
        own = plane_at(ref, row + first * ROW)
        for p in range(count):
            step = (first + p) * ROW
            after = plane_at(ref, row + (step + ROW)) if beyond is None or p < count - 1 else beyond
            d_x = after - own
            d_y = y_plus(ref, own, first_y, row + (step + TILES), row_p + (step + TILES - ROW)) - own
            d_z = z_plus(ref, own, row_z + step) - own
            rows = pl.ds(pl.multiple_of(target + p * SUB, SUB), SUB)
            slope[rows, :] = d_x * d_x + d_y * d_y + d_z * d_z
            own = after

    def slope_tile(slot, carry):
        at, local = entry(0, slot), window(0, cell_of[0, slot], i, j, rows_gx)
        squares(field, at, local, HALO, 0, TE, plane_at(f_u, at[6]))
        at, local = entry(1, slot), window(1, cell_of[1, slot], i, j, rows_gx)
        squares(f_l, at, local, HALO - 2, LOW[0] - 2, 2, plane_at(field, at[6]))
        at, local = entry(2, slot), window(2, cell_of[2, slot], i, j, rows_gx)
        squares(f_u, at, local, HALO + TE, 0, 2, None)
        return carry

    lax.fori_loop(0, tiles, slope_tile, 0, unroll=4)


def window(which, cell, i, j, rows_gx):
    local = cell - 4 * j
    inside = (local >= 0) & (local < CELLS - 1)
    if which > 0:
        row = i - 1 if which == 1 else i + 1
        inside = inside & (row >= 0) & (row < rows_gx)
    return jnp.where(inside, local, CELLS - 1)


def slab_steps_kernel(chips, pos, k0_table, beta_table, *refs):
    width_gy = 2 * chips
    tiles = width_gy * TILES
    halos = refs[width_gy : 2 * width_gy]
    slope, t_in, k0_in, b_in, y_in, temp_out = refs[2 * width_gy : 2 * width_gy + 6]
    mine, bundle = refs[2 * width_gy + 6 : 2 * width_gy + 8]
    across = refs[2 * width_gy + 8 : 2 * width_gy + 7 + chips]
    heat, q_ext, state_a, state_b, k0_all, b_all, blocks, sigmas, y_out, sems = refs[2 * width_gy + 7 + chips :]
    moves = []
    for part in range(width_gy):
        moves.append(pltpu.make_async_copy(refs[part].at[0 : TE * ROW], sigmas.at[part], sems.at[part]))
        moves[-1].start()
    edges = []
    for which, d in enumerate((1, chips - 1)):
        source = refs[chips + d].at[TE * ROW : TE * ROW + HALO * SLABX]
        edges.append(pltpu.make_async_copy(source, y_out.at[which], sems.at[width_gy + which]))
        edges[-1].start()
    i = lax.axis_index("gx")
    j = lax.axis_index("gy")
    rows_gx = lax.axis_size("gx")
    lane = lax.broadcasted_iota(jnp.int32, (SUB, LANES), 1)
    zero = jnp.zeros((SUB, LANES), jnp.float32)

    quarter = [(lane >= q * TE) & (lane < (q + 1) * TE) for q in range(3)]

    def pick(parts):
        return jnp.where(
            quarter[0], parts[0], jnp.where(quarter[1], parts[1], jnp.where(quarter[2], parts[2], parts[3]))
        )

    def turned(value, by):
        return value if by % 4 == 0 else roll(value, by * TE, 1)

    def rows_of(block, g):
        first = ROW0 + block * SLABX + g * SUB
        if not isinstance(first, int):
            first = pl.multiple_of(first, SUB)
        return pl.ds(first, SUB)

    groups = SLABX // SUB

    sub = lax.broadcasted_iota(jnp.int32, (SUB, LANES), 0)
    half = lane < NZ
    no_z = lane % NZ == NZ - 1
    low_x = (sub == HALO - 1) & (i == 0), (sub == HALO) & (i == 0)
    high_x = (sub == (HALO + TE - 1) % SUB) & (i == rows_gx - 1)
    low_y, high_y = half & (j == 0), (lane >= NZ) & (j == width_gy - 1)

    def inverse(value):
        near = pl.reciprocal(value, approx=True)
        near = near * (2.0 - value * near)
        return near * (2.0 - value * near)

    def both_of(block, g, by=0):
        first = 2 * (ROW0 + block * SLABX + g * SUB + by)
        return pl.ds(first, SUB, stride=2), pl.ds(first + 1, SUB, stride=2)

    def load(ref, block, by=0):
        places = [both_of(block, g, by) for g in range(groups)]
        return [ref[at, :] for at, _ in places], [ref[at, :] for _, at in places]

    def store(ref, block, g, temp, cond=None):
        first, second = both_of(block, g)
        ref[first, :] = temp
        if cond is not None:
            ref[second, :] = cond

    even = lax.rem(j, 2) == 0

    def begin(block, low, at):
        values = []
        for g in range(groups):
            rows = rows_of(block, g)
            temp, k0, beta = t_in[rows], k0_in[rows], b_in[rows]
            if low is not None:
                place = slice(at * SLABX + g * SUB, at * SLABX + (g + 1) * SUB)
                other = jnp.where(even, y_out[0, place], y_out[1, place])
                value = jnp.where(even, *((other, y_in[place])[:: 1 if low else -1]))
                swapped = roll(value, NZ, 1)
                if low:
                    temp = jnp.where(half, value, temp)
                    k0 = jnp.where(half, lookup(k0_table, swapped), k0)
                    beta = jnp.where(half, lookup(beta_table, swapped), beta)
                else:
                    temp = jnp.where(half, temp, swapped)
                    k0 = jnp.where(half, k0, lookup(k0_table, value))
                    beta = jnp.where(half, beta, lookup(beta_table, value))
            values.append((rows, temp, k0, beta, k0 * inverse(1.0 + beta * temp * temp)))
        for g, (rows, temp, k0, beta, cond) in enumerate(values):
            k0_all[rows], b_all[rows] = k0, beta
            store(state_a, block, g, temp, cond)

    def begin_inner(block, carry):
        begin(block, None, 0)
        return carry

    lax.fori_loop(HALO, YBLOCKS - HALO, begin_inner, 0, unroll=4)
    for move in edges:
        move.wait()
    for e in range(HALO):
        begin(e, True, e)
        begin(YBLOCKS - HALO + e, False, e)

    def clear(at, carry):
        heat[pl.ds(pl.multiple_of(at * SUB, SUB), SUB), :] = zero
        return carry

    lax.fori_loop(0, heat.shape[0] // SUB, clear, 0, unroll=8)
    for move in moves:
        move.wait()
    low_at, high_at = (LOW[0] + LOW[1]) * ROW, LOW_ROWS + (HIGH[0] + HIGH[1]) * ROW
    for part in range(width_gy):
        dev = part_device(part, chips, j)
        for t in range(TILES):
            for which, by in enumerate((0, -1, 1)):
                tile = jnp.clip(i + by, 0, rows_gx - 1) * tiles + dev * TILES + t
                cell = (pos[1, tile] + 1) * 2 + pos[2, tile]
                local = window(which, cell, i, j, rows_gx)
                source, start, x, count = (
                    (sigmas.at[part], 0, HALO, TE),
                    (halos[part], low_at, HALO - 2, 2),
                    (halos[part], high_at, HALO + TE, 2),
                )[which]
                first = pl.multiple_of((local * SLABX + x) * SUB, SUB)
                for p in range(count):
                    rows = pl.ds(pl.multiple_of(first + p * SUB, SUB), SUB)
                    sigma = source[pl.ds(start + p * ROW + t, SUB, stride=TILES), :]
                    heat[rows, :] = sigma * slope[rows, :]

    def place_heat(at, carry):
        first = at - 1
        col, yq = lax.div(first * 4 + TE, TE), lax.rem(first * 4 + TE, TE) // 4
        for g in range(groups):
            cells = [
                heat[pl.ds(pl.multiple_of(((2 * col + c) * SLABX + g * SUB) * SUB, SUB) + yq, SUB, stride=SUB), :]
                for c in range(4)
            ]
            for r in range(4):
                block = 4 * first + r + HALO + 1
                q_ext[rows_of(block, g)] = pick([turned(cells[c], c - r - c % 2) for c in range(4)])
        return carry

    lax.fori_loop(0, HALF // 4 + 2, place_heat, 0, unroll=2)

    for step in range(CSWEEPS):
        src, dst = (state_a, state_b)[:: 1 if step % 2 == 0 else -1]

        def y_fluxes(block, now, ahead):
            closed = (low_y & (block == HALO - 1)) | (high_y & (block == HALO + HALF - 1))
            return [flux(now, ahead, g, closed) for g in range(groups)]

        def flux(now, other, g, closed=None):
            value = (now[1][g] + other[1][g]) * (other[0][g] - now[0][g])
            return value if closed is None else jnp.where(closed, 0.0, value)

        def advance(block, carry):
            now, before = carry
            ahead = load(src, block + 1)
            flux_y = y_fluxes(block, now, ahead)
            x_p, x_m = load(src, block, 1), load(src, block, -1)
            results = []
            for g in range(groups):
                temp, cond = now[0][g], now[1][g]
                up = flux(now, x_p, g, {0: low_x[0], groups - 1: high_x}.get(g))
                down = flux(now, x_m, g, {0: low_x[1]}.get(g))
                flux_z = (cond + roll(cond, -1, 1)) * (roll(temp, -1, 1) - temp)
                flux_z = jnp.where(no_z, 0.0, flux_z)
                div = (flux_y[g] - before[g]) + (up + down) + (flux_z - roll(flux_z, 1, 1))
                new = temp + DT * (0.5 * div + q_ext[rows_of(block + 1, g)])
                if step < CSWEEPS - 1:
                    rows = rows_of(block, g)
                    results.append((new, k0_all[rows] * inverse(1.0 + b_all[rows] * new * new)))
                else:
                    results.append((new,))
            for g in range(groups):
                store(dst, block, g, *results[g])
            return ahead, flux_y

        first, second = load(src, 0), load(src, 1)
        lax.fori_loop(1, YBLOCKS - 1, advance, (second, y_fluxes(0, first, second)), unroll=9)
    final = state_b if CSWEEPS % 2 else state_a

    def give_out(yq, carry):
        for g in range(TE // SUB):
            x = slice(g * SUB, (g + 1) * SUB)
            turns = []
            for r in range(4):
                value = final[both_of(HALO + 4 * yq + r, g, HALO)[0], :]
                turns.append([turned(value, by) for by in range(4)])
            for pair in range(2):
                even, odd = turns[2 * pair], turns[2 * pair + 1]
                lower = (2 * yq + pair) * LANES
                upper = lower + temp_out.shape[1] // 2
                temp_out[x, pl.ds(pl.multiple_of(lower, LANES), LANES)] = jnp.where(half, even[0], odd[2])
                temp_out[x, pl.ds(pl.multiple_of(upper, LANES), LANES)] = jnp.where(half, even[2], odd[0])
            for c in range(4):
                value = pick([turns[r][(r - c) % 4] for r in range(4)])
                blocks[pl.ds((c * TE + g * SUB) * SUB + yq, SUB, stride=SUB), :] = value
        return carry

    lax.fori_loop(0, HALF // 4, give_out, 0, unroll=2)
    places = []
    mate = j + 1 - 2 * lax.rem(j, 2)
    targets = [(mine, 0, j)] + [(across[d - 1], 0, j + 2 * d) for d in range(1, chips)]
    targets += [(bundle, d * TE * ROW, mate + 2 * d) for d in range(chips)]
    for target, first, to in targets:
        dev = lax.rem(to, width_gy)
        for t in range(TILES):
            tile = i * tiles + dev * TILES + t
            col = pos[1, tile] - 2 * j
            cell = jnp.clip(col, 0, 1) * 2 + pos[2, tile]
            places.append((target, first + t, cell, (col >= 0) & (col < 2)))

    def pack(p, carry):
        values = []
        for _, _, cell, here in places:
            value = blocks[pl.ds(pl.multiple_of((cell * TE + p) * SUB, SUB), SUB), :]
            values.append(jnp.where(here, value, 0.0))
        for (target, first, _, _), value in zip(places, values):
            target[pl.ds(pl.multiple_of(p * ROW, ROW) + first, SUB, stride=TILES), :] = value
        return carry

    lax.fori_loop(0, TE, pack, 0, unroll=4)


def shifted(value, axis, by, wrap=False):
    count = lax.axis_size(axis)
    pairs = [(d, (d + by) % count) for d in range(count) if wrap or 0 <= d + by < count]
    return lax.ppermute(value, axis, pairs)


def with_partner(value, axis, first):
    count = lax.axis_size(axis)
    pairs = [(d, d + 1) for d in range(first, count - 1, 2)]
    return lax.ppermute(value, axis, pairs + [(high, low) for low, high in pairs])


def from_mate(value):
    return lax.ppermute(value, "gy", [(d, d ^ 1) for d in range(lax.axis_size("gy"))])


def to_rows(value):
    return value.reshape(TILES, -1, LANES).transpose(1, 0, 2).reshape(-1, LANES)


def from_rows(value):
    return value.reshape(-1, TILES, LANES).transpose(1, 0, 2).reshape(TILES, -1)


def to_other_core(value, by):
    count = lax.axis_size("gy")
    return lax.ppermute(value, "gy", [(at, ((at ^ 1) + 2 * by) % count) for at in range(count)])


VMEM = pl.BlockSpec(memory_space=pltpu.VMEM)
SMEM = pl.BlockSpec(memory_space=pltpu.SMEM)
HBM = pl.BlockSpec(memory_space=pltpu.HBM)
ANY = pl.BlockSpec(memory_space=pl.ANY)
PARAMS = pltpu.CompilerParams(vmem_limit_bytes=32 * 1024 * 1024)


def on_device(
    phi_init,
    source,
    tile_mat,
    tile_pos,
    neighbours,
    sigma_table,
    temp_init,
    slab_mat,
    k0_table,
    beta_table,
):
    f32 = jnp.float32
    pos = tile_pos.T
    width_gy = lax.axis_size("gy")
    chips = width_gy // 2
    tiles = width_gy * TILES
    size_x, width = temp_init.shape
    edge_rows = width // LANES * SUB

    def rows(count):
        return jax.ShapeDtypeStruct((count, LANES), f32)

    ready, sigma, inner, outer = pl.pallas_call(
        prep_kernel,
        out_shape=(
            rows(2 * TE * ROW),
            rows(TE * ROW),
            rows(SIDE_ROWS + edge_rows),
            rows(SIDE_ROWS + edge_rows),
        ),
        in_specs=[SMEM] * 2 + [HBM] * 5,
        out_specs=(VMEM,) * 4,
        scratch_shapes=[
            pltpu.VMEM((TE * ROW, LANES), f32),
            pltpu.VMEM((TE * ROW, LANES), f32),
            pltpu.VMEM((TE * ROW, LANES), jnp.int32),
            pltpu.VMEM((2, SUB, width), f32),
            pltpu.VMEM((2, SUB, width), jnp.int32),
            pltpu.SemaphoreType.DMA((7,)),
        ],
        compiler_params=pltpu.CompilerParams(vmem_limit_bytes=62 * 1024 * 1024),
        name="prep",
    )(sigma_table, pos, to_rows(phi_init), to_rows(source), to_rows(tile_mat), temp_init, slab_mat)
    bodies = [ready] + [shifted(ready, "gy", 2 * d, True) for d in range(1, chips)]
    bodies += [from_mate(part) for part in bodies]
    inner, outer = with_partner(inner, "gx", 0), with_partner(outer, "gx", 1)

    halo = pl.pallas_call(
        relay_kernel,
        out_shape=rows(LOW_ROWS + HIGH_ROWS),
        in_specs=[VMEM] * 2,
        out_specs=VMEM,
        compiler_params=PARAMS,
        name="relay",
    )(inner, outer)
    halos = [halo] + [shifted(halo, "gy", 2 * d, True) for d in range(1, chips)]
    native = pltpu.VMEM((width // LANES * SLABX + SUB, LANES), f32)
    t_ext, k0_ext, b_ext, edge_in, packet = pl.pallas_call(
        slab_kernel,
        out_shape=(rows(SLAB_ROWS),) * 3 + (rows(HALO * SLABX), rows(TE * ROW + HALO * SLABX)),
        in_specs=[SMEM] * 3 + [VMEM] * 5,
        out_specs=(VMEM,) * 5,
        scratch_shapes=[native, native] + [pltpu.VMEM((HALO * SLABX, LANES), f32)] * 2,
        compiler_params=PARAMS,
        name="slab_prep",
    )(pos, k0_table, beta_table, temp_init, slab_mat, inner, outer, sigma)
    y_in = with_partner(edge_in, "gy", 0)
    sigmas = [sigma] + [shifted(sigma, "gy", 2 * d, True) for d in range(1, chips)]
    sigmas += [from_mate(sigma)] + [
        to_other_core(packet if d in (1, chips - 1) else sigma, d) for d in range(1, chips)
    ]
    *halos[1:], y_in = lax.optimization_barrier((*halos[1:], y_in))
    halos = halos + [from_mate(part) for part in halos]

    def fields(count):
        return pltpu.VMEM((2 * ROW0 + (width_gy + 1) * count * ROW, LANES), f32)

    pot, slope = pl.pallas_call(
        functools.partial(sweep_kernel, chips),
        out_shape=(rows(TE * ROW), rows(CELLS * SLABX * SUB)),
        in_specs=[SMEM] + [ANY] * (2 * width_gy),
        out_specs=(VMEM, VMEM),
        scratch_shapes=[
            pltpu.SMEM((3, 2 * (2 * width_gy + 2)), jnp.int32),
            pltpu.SMEM((3, tiles), jnp.int32),
            pltpu.SMEM((3 * tiles * 8,), jnp.int32),
            fields(TE), fields(TE), fields(LOW[0]), fields(LOW[0]), fields(HIGH[0]), fields(HIGH[0]),
            fields(TE), fields(LOW[1]), fields(HIGH[1]),
            pltpu.SemaphoreType.DMA((6 * width_gy,)),
        ],
        compiler_params=PARAMS,
        name="sweeps",
    )(pos, *bodies, *halos)

    temp, mine, bundle, *across = pl.pallas_call(
        functools.partial(slab_steps_kernel, chips),
        out_shape=(jax.ShapeDtypeStruct((size_x, width), f32), rows(TE * ROW), rows(chips * TE * ROW))
        + (rows(TE * ROW),) * (chips - 1),
        in_specs=[SMEM] * 3 + [ANY] * width_gy + [VMEM] * (width_gy + 5),
        out_specs=(VMEM,) * (2 + chips),
        scratch_shapes=[pltpu.VMEM((CELLS * SLABX * SUB, LANES), f32)]
        + [pltpu.VMEM((SLAB_ROWS + 3 * SLABX, LANES), f32)]
        + [pltpu.VMEM((2 * SLAB_ROWS, LANES), f32)] * 2
        + [pltpu.VMEM((SLAB_ROWS, LANES), f32)] * 2
        + [pltpu.VMEM((4 * TE * SUB, LANES), f32), pltpu.VMEM((width_gy, TE * ROW, LANES), f32)]
        + [pltpu.VMEM((2, HALO * SLABX, LANES), f32), pltpu.SemaphoreType.DMA((width_gy + 2,))],
        compiler_params=PARAMS,
        name="slab_steps",
    )(pos, k0_table, beta_table, *sigmas, *halos, slope, t_ext, k0_ext, b_ext, y_in)
    got = from_mate(bundle).reshape(chips, TE * ROW, LANES)
    tile_temps = mine + got[0]
    for d in range(1, chips):
        tile_temps = tile_temps + shifted(across[d - 1] + got[d], "gy", 2 * d, True)
    return from_rows(pot), temp, from_rows(tile_temps)


def solution(mesh):
    placed = (
        P(("gx", "gy"), None),
        P(("gx", "gy"), None),
        P(("gx", "gy"), None),
        P(),
        P(("gx", "gy"), None),
        P(),
        P("gx", "gy"),
        P("gx", "gy"),
        P(),
        P(),
    )
    return jax.shard_map(
        on_device,
        mesh=mesh,
        in_specs=placed,
        out_specs=(P(("gx", "gy"), None), P("gx", "gy"), P(("gx", "gy"), None)),
        check_vma=False,
    )
```
